32 devices in a mesh: dp: 4 (over z), ctx: 4 (over y, x), tp: 2 (over core).
Axes of the slice: x: 2, y: 2, z: 4, core: 2. Of those that a mesh axis runs over, the one named last changes fastest.
Arguments:
- activations: bfloat16 [4, 2048, 2048], P('dp', 'ctx'), may hold values from -6 to 6
- seg_ids: int32 [4, 2048], P('dp', 'ctx'), may hold values from 0 to 7, never falling along the last dimension, each value on 1 to 1024 neighbouring positions
- cotangent: bfloat16 [4, 2048, 2048], P('dp', 'ctx'), may hold values from -6 to 6
- q_weight: bfloat16 [2048, 256], P(('dp', 'ctx'), 'tp'), may hold values from -0.125 to 0.125
- k_weight: bfloat16 [2048, 256], P(('dp', 'ctx'), 'tp'), may hold values from -0.125 to 0.125
- v_weight: bfloat16 [2048, 2048], P(('dp', 'ctx'), 'tp'), may hold values from -0.125 to 0.125
- o_weight: bfloat16 [2048, 2048], P(('dp', 'ctx'), 'tp'), may hold values from -2 to 2
- gate_weight: bfloat16 [2048, 5632], P(('dp', 'ctx'), 'tp'), may hold values from -0.125 to 0.125
- up_weight: bfloat16 [2048, 5632], P(('dp', 'ctx'), 'tp'), may hold values from -0.125 to 0.125
- down_weight: bfloat16 [2048, 5632], P(('dp', 'ctx'), 'tp'), may hold values from -0.078125 to 0.078125
- attn_gain: bfloat16 [2048], P(('dp', 'ctx')), may hold values from 0.5 to 1.5
- mlp_gain: bfloat16 [2048], P(('dp', 'ctx')), may hold values from 0.5 to 1.5
Outputs:
- out_activations: bfloat16 [4, 2048, 2048], P('dp', 'ctx')
- grad_activations: float32 [4, 2048, 2048], P('dp', 'ctx')
- grad_q_weight: float32 [2048, 256], P(('dp', 'ctx'), 'tp')
- grad_k_weight: float32 [2048, 256], P(('dp', 'ctx'), 'tp')
- grad_v_weight: float32 [2048, 2048], P(('dp', 'ctx'), 'tp')
- grad_o_weight: float32 [2048, 2048], P(('dp', 'ctx'), 'tp')
- grad_gate_weight: float32 [2048, 5632], P(('dp', 'ctx'), 'tp')
- grad_up_weight: float32 [2048, 5632], P(('dp', 'ctx'), 'tp')
- grad_down_weight: float32 [2048, 5632], P(('dp', 'ctx'), 'tp')
- grad_attn_gain: float32 [2048], P(('dp', 'ctx'))
- grad_mlp_gain: float32 [2048], P(('dp', 'ctx'))
The draws below stay inside these ranges and needn't reach their ends.
Inputs may be any that keep to these rules, and one draw needn't show every extreme that they name: `seg_ids`: along each sequence the document ids never fall; a document holds 1 to 1024 tokens and one holds exactly 1024.
All inputs are finite; a program needn't handle non-finite values.
Results may differ from the reference program's by a relative error of at most 0.017.
Values may be sent and summed in bfloat16 or wider, within the bound.
A program may use at most 256 MiB of HBM per device.

```python
import math
import jax
import jax.numpy as jnp
import numpy as np
from jax import lax

D = 2048
H = 16
F = 16
DV = 128
FF = 5632
TOK_DEV = 512
FT = 273
SEQS = 4
LENGTH = 2048
DOCS = 8
DOC_MOST = 1024


def raised(drawn, key, source, target, shards_of, factor):
    def block_of(position):
        return (jnp.arange(drawn.shape[position]) // (drawn.shape[position] // shards_of)).reshape((-1,) + (1,) * (drawn.ndim - 1 - position))

    one_side = jax.random.permutation(key, shards_of)[block_of(target)]
    second = (block_of(target) + shards_of // 2) % shards_of
    return jnp.where((block_of(source) == one_side) | (block_of(source) == second), factor * drawn, drawn)


def level_of(own_key, extent, split, low, high):
    level = 1.0
    for dim, shards_of in split:
        steps = jax.random.uniform(jax.random.fold_in(jax.random.fold_in(own_key, 6), dim), (shards_of,), jnp.float32, low / len(split), high / len(split))
        level = level * jnp.repeat(jnp.exp(steps), extent[dim] // shards_of).reshape((-1,) + (1,) * (len(extent) - 1 - dim))
    return level


def profile(amount, total, limit, skew):
    portions = [(1 << 20) // math.isqrt(rank ** skew) + 1 for rank in range(2, amount + 1)]
    surplus, counts = total - limit - (amount - 1), [1] * (amount - 1)
    while surplus > 0:
        movable = [i for i in range(amount - 1) if counts[i] < limit]
        pool, remaining = sum([portions[i] for i in movable]), surplus
        for i in movable:
            addition = min(limit - counts[i], max(1, remaining * portions[i] // pool), surplus)
            counts[i] = counts[i] + addition
            surplus = surplus - addition
    return np.array([limit] + counts)


def ragged_sizes(rng, amount, total, limit, skew):
    if amount == 2:
        one = jax.random.randint(rng, (), max(1, total - limit), min(limit, total - 1) + 1)
        return jnp.stack([one, total - one])
    sizes = jnp.asarray(profile(amount, total, limit, skew), jnp.int32)
    pairs = (amount - 1) // 2
    donor, taker = sizes[1:1 + 2 * pairs:2], sizes[2:2 + 2 * pairs:2]
    room = jnp.minimum(donor - 1, limit - taker)
    shifted = jax.random.randint(jax.random.fold_in(rng, 1), (pairs,), 0, 1 << 20) % (room + 1)
    sizes = sizes.at[1:1 + 2 * pairs:2].set(donor - shifted).at[2:2 + 2 * pairs:2].set(taker + shifted)
    return sizes[jax.random.permutation(jax.random.fold_in(rng, 2), amount)]


def gaussian(stream_key, dims, scale, limit, pieces=(), kind=jnp.bfloat16):
    entries = scale * jax.random.normal(stream_key, dims, jnp.float32)
    if pieces:
        entries = entries * level_of(stream_key, dims, pieces, -0.22, 0.18)
    return jnp.clip(entries, -limit, limit).astype(kind)


def heavy_noise(key, dims, scale, most, pieces, heavy, held_as=jnp.bfloat16):
    values = scale * jax.random.normal(key, dims, jnp.float32)
    if pieces:
        values = values * level_of(key, dims, pieces, -0.22, 0.18)
    return jnp.clip(raised(values, jax.random.fold_in(key, 3), *heavy), -most, most).astype(held_as)


def setup_inputs(seed: int = 0) -> dict:
    keys = jax.random.split(jax.random.key(seed), 13)
    activations = gaussian(keys[0], (SEQS, LENGTH, D), 1.0, 6.0, ((0, 4), (1, 4)))
    seg_ids = jax.vmap(lambda own: jnp.searchsorted(jnp.cumsum(ragged_sizes(own, DOCS, LENGTH, DOC_MOST, 2)), jnp.arange(LENGTH), side="right"))(jax.random.split(keys[1], SEQS)).reshape((SEQS, LENGTH)).astype(jnp.int32)
    cotangent = heavy_noise(keys[2], (SEQS, LENGTH, D), 1.0, 6.0, ((0, 4), (1, 4)), (1, 2, 4, 2.0))
    q_weight = gaussian(keys[3], (D, H * F), D ** -0.5, 0.125, ((0, 16), (1, 2)))
    k_weight = gaussian(keys[4], (D, H * F), D ** -0.5, 0.125, ((0, 16), (1, 2)))
    v_weight = gaussian(keys[5], (D, H * DV), D ** -0.5, 0.125, ((0, 16), (1, 2)))
    o_weight = gaussian(keys[6], (D, H * DV), (max(1, H * DV // 256)) ** -0.5, 2.0, ((0, 16), (1, 2)))
    gate_weight = gaussian(keys[7], (D, FF), D ** -0.5, 0.125, ((0, 16), (1, 2)))
    up_weight = gaussian(keys[8], (D, FF), D ** -0.5, 0.125, ((0, 16), (1, 2)))
    down_weight = gaussian(keys[9], (D, FF), FF ** -0.5, 0.078125, ((0, 16), (1, 2)))
    attn_gain = jnp.clip(1.0 + 0.1 * jax.random.normal(keys[10], (D,), jnp.float32), 0.5, 1.5).astype(jnp.bfloat16)
    mlp_gain = jnp.clip(1.0 + 0.1 * jax.random.normal(keys[11], (D,), jnp.float32), 0.5, 1.5).astype(jnp.bfloat16)
    return {"activations": activations, "seg_ids": seg_ids, "cotangent": cotangent, "q_weight": q_weight, "k_weight": k_weight, "v_weight": v_weight, "o_weight": o_weight, "gate_weight": gate_weight, "up_weight": up_weight, "down_weight": down_weight, "attn_gain": attn_gain, "mlp_gain": mlp_gain}


EPSILON = 1e-05
PRECISE = lax.Precision.HIGHEST

@jax.custom_vjp
def low(v):
    return lax.optimization_barrier(v.astype(jnp.bfloat16)).astype(jnp.float32)

@jax.custom_vjp
def low_back(v):
    return v

def low_keep(v):
    return (low(v), None)

def low_pass(kept, grad):
    return (grad,)

def back_keep(v):
    return (v, None)

def back_low(kept, grad):
    return (low(grad),)
low.defvjp(low_keep, low_pass)
low_back.defvjp(back_keep, back_low)

def taylor(features_in):
    products = (features_in[..., :, None] * features_in[..., None, :]).reshape(features_in.shape[:-1] + (F * F,))
    constant = jnp.ones(features_in.shape[:-1] + (1,), jnp.float32)
    return jnp.concatenate([constant, features_in * F ** (-0.25), products * (2.0 * F) ** (-0.5)], axis=-1)

def rms_norm(layer_input_rows, gain_vector_row):
    multiplier_term = lax.rsqrt(lax.optimization_barrier(jnp.mean(layer_input_rows * layer_input_rows, axis=-1, keepdims=True)) + EPSILON)
    return layer_input_rows * multiplier_term * gain_vector_row

def block_attend(carried, block_inputs):
    prior_state, prior_total, last_seg = carried
    queries, key_heads, value_heads, segment = block_inputs
    scores = low_back(jnp.einsum('thf,shf->hts', queries, key_heads, precision=PRECISE) * F ** (-0.5))
    places = jnp.arange(queries.shape[0])
    visible = ((places[:, None] >= places[None, :]) & (segment[:, None] == segment[None, :])).astype(jnp.float32)
    weights = low(visible * (1.0 + scores + 0.5 * scores * scores))
    feat_q = taylor(queries)
    feat_k = taylor(key_heads)
    inherit = (segment == last_seg).astype(jnp.float32)
    numerator = low_back(jnp.einsum('hts,shd->thd', weights, value_heads, precision=PRECISE) + inherit[:, None, None] * jnp.einsum('thf,hfd->thd', feat_q, prior_state, precision=PRECISE))
    denominator = lax.optimization_barrier(jnp.sum(weights, axis=2)).T + inherit[:, None] * jnp.einsum('thf,hf->th', feat_q, prior_total, precision=PRECISE)
    ending = segment[-1]
    owned = (segment == ending).astype(jnp.float32)[:, None, None]
    local_state = jnp.einsum('thf,thd->hfd', feat_k * owned, value_heads, precision=PRECISE)
    local_total = lax.optimization_barrier(jnp.sum(feat_k * owned, axis=0))
    retain = (last_seg == ending).astype(jnp.float32)
    return ((local_state + retain * prior_state, local_total + retain * prior_total, ending), numerator / denominator[:, :, None])

def layer_one(layer_input_rows, segment, w_query, w_key, w_value, w_out, w_gate, w_up, w_down, first_norm_gain, second_norm_gain):
    length = layer_input_rows.shape[0]
    blocks = length // TOK_DEV
    first_normalized = low(rms_norm(layer_input_rows, first_norm_gain))
    queries = low(low_back(jnp.dot(first_normalized, w_query, precision=PRECISE)))
    key_rows = low(low_back(jnp.dot(first_normalized, w_key, precision=PRECISE)))
    value_rows = low(low_back(jnp.dot(first_normalized, w_value, precision=PRECISE)))
    start_carry = (jnp.zeros((H, FT, DV), jnp.float32), jnp.zeros((H, FT), jnp.float32), jnp.float32(-1.0))
    block_inputs = (queries.reshape(blocks, TOK_DEV, H, F), key_rows.reshape(blocks, TOK_DEV, H, F), value_rows.reshape(blocks, TOK_DEV, H, DV), segment.reshape(blocks, TOK_DEV))
    unused, mixed_heads = lax.scan(jax.checkpoint(block_attend), start_carry, block_inputs)
    heads_out = low(low_back(mixed_heads.reshape(length, H * DV)))
    residual_midpoint = layer_input_rows + low_back(jnp.dot(heads_out, w_out.T, precision=PRECISE))
    second_normalized = low(rms_norm(residual_midpoint, second_norm_gain))
    gate_value = low_back(jnp.dot(second_normalized, w_gate, precision=PRECISE))
    up_value = low_back(jnp.dot(second_normalized, w_up, precision=PRECISE))
    hidden = low(jax.nn.silu(gate_value) * up_value)
    return residual_midpoint + low_back(jnp.dot(hidden, w_down.T, precision=PRECISE))

def reference(activations, seg_ids, cotangent, q_weight, k_weight, v_weight, o_weight, gate_weight, up_weight, down_weight, attn_gain, mlp_gain):
    params = tuple((weight.astype(jnp.float32) for weight in (q_weight, k_weight, v_weight, o_weight, gate_weight, up_weight, down_weight, attn_gain, mlp_gain)))
    segments = seg_ids.astype(jnp.float32)

    def forward(all_inputs, *weights):

        def one_sequence(sequence_pair):
            return layer_one(sequence_pair[0], sequence_pair[1], *weights)
        return lax.map(jax.checkpoint(one_sequence), (all_inputs, segments))
    result, pullback = jax.vjp(forward, activations.astype(jnp.float32), *params)
    gradients = pullback(cotangent.astype(jnp.float32))
    return (result.astype(jnp.bfloat16), gradients[0], gradients[1], gradients[2], gradients[3], gradients[4], gradients[5], gradients[6], gradients[7], gradients[8], gradients[9])
```

```python
import jax
import jax.numpy as jnp
from jax import lax
from jax.experimental import pallas as pl
from jax.experimental.pallas import tpu as pltpu
from jax.sharding import PartitionSpec as P

F = 16
DV = 128


EPSILON = 1e-05
PRECISE = lax.Precision.HIGHEST
VMEM_MOST = 56 * 2**20


def prefix(x, axis, join, neutral, backward):
    count = lax.axis_size(axis)
    place = lax.axis_index(axis)
    ahead = count - 1 - place if backward else place
    gathered = jax.tree.map(
        lambda a, kind: lax.all_gather(a.astype(kind), axis),
        x,
        (jnp.bfloat16, jnp.bfloat16, jnp.bfloat16),
    )
    state = jax.tree.map(lambda a, e: jnp.zeros_like(a) + jnp.asarray(e, a.dtype), x, neutral)

    def one(lap, state):
        source = count - 1 - lap if backward else lap
        return join(
            state,
            jax.tree.map(
                lambda a, own: lax.dynamic_index_in_dim(a, source, 0, False).astype(own.dtype),
                gathered,
                x,
            ),
        )

    return lax.fori_loop(0, ahead, one, state)


def taylor(features_in):
    feature_count = features_in.shape[-1]
    products = (features_in[..., :, None] * features_in[..., None, :]).reshape(
        features_in.shape[:-1] + (feature_count * feature_count,)
    )
    constant = jnp.ones(features_in.shape[:-1] + (1,), jnp.float32)
    return jnp.concatenate(
        [
            constant,
            features_in * feature_count ** (-0.25),
            products * (2.0 * feature_count) ** (-0.5),
        ],
        axis=-1,
    )


def taylor_back(features_in, incoming_gradient):
    feature_count = features_in.shape[-1]
    linear = incoming_gradient[..., 1 : 1 + feature_count] * feature_count ** (-0.25)
    square = incoming_gradient[..., 1 + feature_count :].reshape(
        incoming_gradient.shape[:-1] + (feature_count, feature_count)
    )
    paired = jnp.einsum(
        "...ab,...b->...a", square + jnp.swapaxes(square, -1, -2), features_in, precision=PRECISE
    )
    return linear + paired * (2.0 * feature_count) ** (-0.5)


def norm_backward_step(incoming_gradient, unit_normalized_rows, multiplier_term, gain_vector_row):
    rescaled_rows = incoming_gradient * gain_vector_row
    return multiplier_term * (
        rescaled_rows
        - unit_normalized_rows
        * jnp.mean(rescaled_rows * unit_normalized_rows, axis=1, keepdims=True)
    )


def join_states(earlier, later_part):
    is_empty = later_part[2] < 0.0
    retain = jnp.where(is_empty | (earlier[2] == later_part[2]), 1.0, 0.0).astype(jnp.float32)
    return (
        later_part[0] + retain * earlier[0],
        later_part[1] + retain * earlier[1],
        jnp.where(is_empty, earlier[2], later_part[2]),
    )


def shards(
    activations,
    seg_ids,
    cotangent,
    q_weight,
    k_weight,
    v_weight,
    o_weight,
    gate_weight,
    up_weight,
    down_weight,
    attn_gain,
    mlp_gain,
):
    layer_input_rows = activations[0].astype(jnp.float32)
    segment = seg_ids[0].astype(jnp.float32)
    tokens = layer_input_rows.shape[0]
    head_count = q_weight.shape[1] // F
    w_query, w_key, w_value, w_out, first_norm_gain = (
        lax.all_gather(q_weight, ("dp", "ctx"), axis=0, tiled=True),
        lax.all_gather(k_weight, ("dp", "ctx"), axis=0, tiled=True),
        lax.all_gather(v_weight, ("dp", "ctx"), axis=0, tiled=True),
        lax.all_gather(o_weight, ("dp", "ctx"), axis=0, tiled=True),
        lax.all_gather(attn_gain, ("dp", "ctx"), axis=0, tiled=True),
    )
    first_inverse_scale = lax.rsqrt(
        jnp.mean(layer_input_rows * layer_input_rows, axis=1, keepdims=True) + EPSILON
    )
    first_unit_rows = layer_input_rows * first_inverse_scale
    first_normalized = (first_unit_rows * first_norm_gain.astype(jnp.float32)).astype(jnp.bfloat16)
    queries = (
        jnp.dot(first_normalized, w_query, preferred_element_type=jnp.float32)
        .astype(jnp.bfloat16)
        .reshape(tokens, head_count, F)
    )
    key_heads = (
        jnp.dot(first_normalized, w_key, preferred_element_type=jnp.float32)
        .astype(jnp.bfloat16)
        .reshape(tokens, head_count, F)
    )
    value_heads = (
        jnp.dot(first_normalized, w_value, preferred_element_type=jnp.float32)
        .astype(jnp.bfloat16)
        .reshape(tokens, head_count, DV)
    )
    w_gate, w_up, w_down, second_norm_gain = (
        lax.all_gather(gate_weight, ("dp", "ctx"), axis=0, tiled=True),
        lax.all_gather(up_weight, ("dp", "ctx"), axis=0, tiled=True),
        lax.all_gather(down_weight, ("dp", "ctx"), axis=0, tiled=True),
        lax.all_gather(mlp_gain, ("dp", "ctx"), axis=0, tiled=True),
    )
    scores = jnp.einsum(
        "thf,shf->hts", queries, key_heads, preferred_element_type=jnp.float32
    ) * F ** (-0.5)
    places = jnp.arange(tokens)
    visible = (
        (places[:, None] >= places[None, :]) & (segment[:, None] == segment[None, :])
    ).astype(jnp.float32)
    weights = (visible * (1.0 + scores + 0.5 * scores * scores)).astype(jnp.bfloat16)
    query_float = queries.astype(jnp.float32)
    key_float = key_heads.astype(jnp.float32)
    value_float = value_heads.astype(jnp.float32)
    feat_q = taylor(query_float)
    feat_k = taylor(key_float)
    ending = segment[-1]
    owned = (segment == ending).astype(jnp.float32)[:, None, None]
    local_state = jnp.einsum("thf,thd->hfd", feat_k * owned, value_float, precision=PRECISE)
    local_total = jnp.sum(feat_k * owned, axis=0)
    empty_state = (jnp.zeros_like(local_state), jnp.zeros_like(local_total), jnp.float32(-1.0))
    prior_state, prior_total, before = prefix(
        (local_state, local_total, ending), "ctx", join_states, empty_state, False
    )
    inherit = (segment == before).astype(jnp.float32)
    numerator = jnp.einsum(
        "hts,shd->thd", weights, value_heads, preferred_element_type=jnp.float32
    ) + inherit[:, None, None] * jnp.einsum("thf,hfd->thd", feat_q, prior_state, precision=PRECISE)
    denominator = jnp.sum(weights.astype(jnp.float32), axis=2).T + inherit[:, None] * jnp.einsum(
        "thf,hf->th", feat_q, prior_total, precision=PRECISE
    )
    mixed_heads = numerator / denominator[:, :, None]
    heads_out = mixed_heads.reshape(tokens, head_count * DV).astype(jnp.bfloat16)
    attn_out = lax.psum(
        jnp.einsum("tc,dc->td", heads_out, w_out, preferred_element_type=jnp.float32), "tp"
    )
    residual_midpoint = layer_input_rows + attn_out
    second_inverse_scale = lax.rsqrt(
        jnp.mean(residual_midpoint * residual_midpoint, axis=1, keepdims=True) + EPSILON
    )
    second_unit_rows = residual_midpoint * second_inverse_scale
    second_normalized = (second_unit_rows * second_norm_gain.astype(jnp.float32)).astype(
        jnp.bfloat16
    )
    gate_value = jnp.dot(second_normalized, w_gate, preferred_element_type=jnp.float32)
    up_value = jnp.dot(second_normalized, w_up, preferred_element_type=jnp.float32)
    sigmoid_gate = jax.nn.sigmoid(gate_value)
    hidden = (gate_value * sigmoid_gate * up_value).astype(jnp.bfloat16)
    mlp_out = lax.psum(
        jnp.einsum("tc,dc->td", hidden, w_down, preferred_element_type=jnp.float32).astype(
            jnp.bfloat16
        ),
        "tp",
    ).astype(jnp.float32)
    final_out = residual_midpoint + mlp_out
    grad_out = cotangent[0].astype(jnp.float32)
    grad_branch_two = cotangent[0]
    grad_w_down = jnp.einsum(
        "td,tc->dc", grad_branch_two, hidden, preferred_element_type=jnp.float32
    )
    grad_hidden = jnp.dot(grad_branch_two, w_down, preferred_element_type=jnp.float32)
    grad_gate = (
        grad_hidden * up_value * sigmoid_gate * (1.0 + gate_value * (1.0 - sigmoid_gate))
    ).astype(jnp.bfloat16)
    grad_up = (grad_hidden * gate_value * sigmoid_gate).astype(jnp.bfloat16)
    grad_w_gate = jnp.einsum(
        "td,tc->dc", second_normalized, grad_gate, preferred_element_type=jnp.float32
    )
    grad_w_up = jnp.einsum(
        "td,tc->dc", second_normalized, grad_up, preferred_element_type=jnp.float32
    )
    grad_normed_part = jnp.einsum(
        "tc,dc->td", grad_gate, w_gate, preferred_element_type=jnp.float32
    ) + jnp.einsum("tc,dc->td", grad_up, w_up, preferred_element_type=jnp.float32)
    second_normalized_gradient = lax.psum(grad_normed_part.astype(jnp.bfloat16), "tp").astype(
        jnp.float32
    )
    second_gain_gradient = jnp.sum(second_normalized_gradient * second_unit_rows, axis=0)
    grad_middle = grad_out + norm_backward_step(
        second_normalized_gradient,
        second_unit_rows,
        second_inverse_scale,
        second_norm_gain.astype(jnp.float32),
    )
    mlp_grads = (
        lax.psum_scatter(grad_w_gate, ("dp", "ctx"), scatter_dimension=0, tiled=True),
        lax.psum_scatter(grad_w_up, ("dp", "ctx"), scatter_dimension=0, tiled=True),
        lax.psum_scatter(grad_w_down, ("dp", "ctx"), scatter_dimension=0, tiled=True),
        lax.psum_scatter(second_gain_gradient, ("dp", "ctx"), scatter_dimension=0, tiled=True),
    )
    grad_branch_one = grad_middle.astype(jnp.bfloat16)
    grad_w_out = jnp.einsum(
        "td,tc->dc", grad_branch_one, heads_out, preferred_element_type=jnp.float32
    )
    grad_heads_low = jnp.dot(grad_branch_one, w_out, preferred_element_type=jnp.float32).astype(
        jnp.bfloat16
    )
    grad_mixed = (
        lax.optimization_barrier(grad_heads_low).astype(jnp.float32).reshape(tokens, head_count, DV)
    )
    numer_low = (grad_mixed / denominator[:, :, None]).astype(jnp.bfloat16)
    grad_numer = lax.optimization_barrier(numer_low).astype(jnp.float32)
    grad_denom = -jnp.sum(grad_mixed * mixed_heads, axis=2) / denominator
    grad_weights = (
        jnp.einsum("thd,shd->hts", numer_low, value_heads, preferred_element_type=jnp.float32)
        + grad_denom.T[:, :, None]
    )
    grad_scores = (grad_weights * visible * (1.0 + scores)).astype(jnp.bfloat16)
    grad_value = jnp.einsum("hts,thd->shd", weights, numer_low, preferred_element_type=jnp.float32)
    grad_query = jnp.einsum(
        "hts,shf->thf", grad_scores, key_heads, preferred_element_type=jnp.float32
    ) * F ** (-0.5)
    grad_key = jnp.einsum(
        "hts,thf->shf", grad_scores, queries, preferred_element_type=jnp.float32
    ) * F ** (-0.5)
    grad_feat_q = inherit[:, None, None] * (
        jnp.einsum("thd,hfd->thf", grad_numer, prior_state, precision=PRECISE)
        + grad_denom[:, :, None] * prior_total[None]
    )
    carried_state = jnp.einsum(
        "thf,thd->hfd", feat_q * inherit[:, None, None], grad_numer, precision=PRECISE
    )
    carried_total = jnp.sum(feat_q * (inherit[:, None] * grad_denom)[:, :, None], axis=0)
    starting = segment[0]
    later_state, later_total, after_seg = prefix(
        (carried_state, carried_total, starting), "ctx", join_states, empty_state, True
    )
    reached = (segment == after_seg).astype(jnp.float32)[:, None, None]
    grad_feat_k = reached * (
        jnp.einsum("hfd,thd->thf", later_state, value_float, precision=PRECISE) + later_total[None]
    )
    grad_value = grad_value + reached * jnp.einsum(
        "thf,hfd->thd", feat_k, later_state, precision=PRECISE
    )
    grad_query = grad_query + taylor_back(query_float, grad_feat_q)
    grad_key = grad_key + taylor_back(key_float, grad_feat_k)
    grad_query_low = grad_query.reshape(tokens, head_count * F).astype(jnp.bfloat16)
    grad_key_low = grad_key.reshape(tokens, head_count * F).astype(jnp.bfloat16)
    grad_value_low = grad_value.reshape(tokens, head_count * DV).astype(jnp.bfloat16)
    grad_w_query = jnp.einsum(
        "td,tc->dc", first_normalized, grad_query_low, preferred_element_type=jnp.float32
    )
    grad_w_key = jnp.einsum(
        "td,tc->dc", first_normalized, grad_key_low, preferred_element_type=jnp.float32
    )
    grad_w_value = jnp.einsum(
        "td,tc->dc", first_normalized, grad_value_low, preferred_element_type=jnp.float32
    )
    grad_normed_sum = (
        jnp.einsum("tc,dc->td", grad_query_low, w_query, preferred_element_type=jnp.float32)
        + jnp.einsum("tc,dc->td", grad_key_low, w_key, preferred_element_type=jnp.float32)
        + jnp.einsum("tc,dc->td", grad_value_low, w_value, preferred_element_type=jnp.float32)
    )
    first_normalized_gradient = lax.psum(grad_normed_sum.astype(jnp.bfloat16), "tp").astype(
        jnp.float32
    )
    first_gain_gradient = jnp.sum(first_normalized_gradient * first_unit_rows, axis=0)
    grad_inputs = grad_middle + norm_backward_step(
        first_normalized_gradient,
        first_unit_rows,
        first_inverse_scale,
        first_norm_gain.astype(jnp.float32),
    )
    attn_grads = (
        lax.psum_scatter(grad_w_query, ("dp", "ctx"), scatter_dimension=0, tiled=True),
        lax.psum_scatter(grad_w_key, ("dp", "ctx"), scatter_dimension=0, tiled=True),
        lax.psum_scatter(grad_w_value, ("dp", "ctx"), scatter_dimension=0, tiled=True),
        lax.psum_scatter(grad_w_out, ("dp", "ctx"), scatter_dimension=0, tiled=True),
        lax.psum_scatter(first_gain_gradient, ("dp", "ctx"), scatter_dimension=0, tiled=True),
    )
    return (
        final_out.astype(jnp.bfloat16)[None],
        grad_inputs[None],
        attn_grads[0],
        attn_grads[1],
        attn_grads[2],
        attn_grads[3],
        mlp_grads[0],
        mlp_grads[1],
        mlp_grads[2],
        attn_grads[4],
        mlp_grads[3],
    )


BLOCK = 512


def attention_forward(qkv, seg_rows, seg_cols, heads):
    tokens = qkv.shape[0]
    wide = heads * DV

    def kernel(x_ref, row_ref, col_ref, mixed_ref, denom_ref, low_ref, ext_ref):
        i = pl.program_id(0)

        @pl.when(i == 0)
        def _():
            for h in range(heads):
                ext_ref[:, 2 * h * DV : (2 * h + 1) * DV] = x_ref[:, h * DV : (h + 1) * DV]
                ext_ref[:, (2 * h + 1) * DV : (2 * h + 2) * DV] = jnp.ones(
                    (tokens, DV), jnp.bfloat16
                )

        base = pl.multiple_of(i * BLOCK, BLOCK)
        own = row_ref[pl.ds(base, BLOCK), :]
        place = lax.broadcasted_iota(jnp.int32, (BLOCK, BLOCK), 0) - lax.broadcasted_iota(
            jnp.int32, (BLOCK, BLOCK), 1
        )
        queries = [
            x_ref[pl.ds(base, BLOCK), wide + h * F : wide + (h + 1) * F] * jnp.bfloat16(F**-0.5)
            for h in range(heads)
        ]

        def step(j, sums):
            start = pl.multiple_of(j * BLOCK, BLOCK)
            visible = (place >= start - base) & (own == col_ref[:, pl.ds(start, BLOCK)])
            out = []
            for h in range(heads):
                keys = x_ref[
                    pl.ds(start, BLOCK),
                    wide + (heads + h) * F : wide + (heads + h + 1) * F,
                ]
                s = lax.dot_general(
                    queries[h], keys, (((1,), (1,)), ((), ())), preferred_element_type=jnp.float32
                )
                a = jnp.where(visible, (0.5 * s + 1.0) * s + 1.0, 0.0).astype(jnp.bfloat16)
                out.append(
                    sums[h]
                    + jnp.dot(
                        a,
                        ext_ref[pl.ds(start, BLOCK), 2 * h * DV : (2 * h + 2) * DV],
                        preferred_element_type=jnp.float32,
                    )
                )
            return tuple(out)

        sums = lax.fori_loop(
            0, i + 1, step, tuple(jnp.zeros((BLOCK, 2 * DV), jnp.float32) for _ in range(heads))
        )
        for h in range(heads):
            denom = sums[h][:, DV:]
            mixed = sums[h][:, :DV] / denom
            mixed_ref[:, h * DV : (h + 1) * DV] = mixed
            low_ref[:, h * DV : (h + 1) * DV] = mixed.astype(jnp.bfloat16)
            denom_ref[:, h : h + 1] = denom[:, :1]

    return pl.pallas_call(
        kernel,
        grid=(tokens // BLOCK,),
        in_specs=[
            pl.BlockSpec(qkv.shape, lambda i: (0, 0)),
            pl.BlockSpec((tokens, 1), lambda i: (0, 0)),
            pl.BlockSpec((1, tokens), lambda i: (0, 0)),
        ],
        out_specs=[
            pl.BlockSpec((BLOCK, wide), lambda i: (i, 0)),
            pl.BlockSpec((BLOCK, heads), lambda i: (i, 0)),
            pl.BlockSpec((BLOCK, wide), lambda i: (i, 0)),
        ],
        out_shape=[
            jax.ShapeDtypeStruct((tokens, wide), jnp.float32),
            jax.ShapeDtypeStruct((tokens, heads), jnp.float32),
            jax.ShapeDtypeStruct((tokens, wide), jnp.bfloat16),
        ],
        scratch_shapes=[pltpu.VMEM((tokens, 2 * wide), jnp.bfloat16)],
        compiler_params=pltpu.CompilerParams(vmem_limit_bytes=VMEM_MOST),
        cost_estimate=pl.CostEstimate(
            flops=tokens * tokens * heads * 400, bytes_accessed=tokens * wide * 12, transcendentals=0
        ),
        name="attn_forward",
    )(qkv, seg_rows, seg_cols)


def attention_backward(qkv, g_mixed, mixed, denom, seg_rows, seg_cols, heads):
    tokens = qkv.shape[0]
    wide = heads * DV
    blocks = tokens // BLOCK

    def kernel(
        x_ref, gm_ref, m_ref, d_ref, row_ref, col_ref, g_ref, gq_ref, numer_ref, gden_ref, key_ref
    ):
        j = pl.program_id(0)

        @pl.when(j == 0)
        def _():
            gq_ref[...] = jnp.zeros_like(gq_ref)
            for h in range(heads):
                part = pl.ds(h * DV, DV)
                gm = gm_ref[:, part].astype(jnp.float32)
                inverse = 1.0 / d_ref[:, h : h + 1]
                numer_ref[:, part] = (gm * inverse).astype(jnp.bfloat16)
                down = -jnp.sum(gm * m_ref[:, part], axis=1, keepdims=True) * inverse
                gden_ref[h : h + 1, :] = jnp.transpose(
                    jnp.broadcast_to(down, (tokens, 128)), (1, 0)
                )[:1, :]
            key_ref[...] = jnp.transpose(
                x_ref[:, wide : wide + 2 * heads * F].astype(jnp.float32), (1, 0)
            ).astype(jnp.bfloat16)

        start = pl.multiple_of(j * BLOCK, BLOCK)
        own = row_ref[pl.ds(start, BLOCK), :]
        place = lax.broadcasted_iota(jnp.int32, (BLOCK, BLOCK), 1) - lax.broadcasted_iota(
            jnp.int32, (BLOCK, BLOCK), 0
        )
        values = [x_ref[pl.ds(start, BLOCK), h * DV : (h + 1) * DV] for h in range(heads)]
        keys = [
            x_ref[pl.ds(start, BLOCK), wide + (heads + h) * F : wide + (heads + h + 1) * F]
            * jnp.bfloat16(F**-0.5)
            for h in range(heads)
        ]
        across = [
            key_ref[(heads + h) * F : (heads + h + 1) * F, pl.ds(start, BLOCK)]
            * jnp.bfloat16(F**-0.5)
            for h in range(heads)
        ]

        def step(i, sums):
            base = pl.multiple_of(i * BLOCK, BLOCK)
            visible = (place >= start - base) & (own == col_ref[:, pl.ds(base, BLOCK)])
            out = []
            for h in range(heads):
                queries = x_ref[pl.ds(base, BLOCK), wide + h * F : wide + (h + 1) * F]
                numer = numer_ref[pl.ds(base, BLOCK), h * DV : (h + 1) * DV]
                s = lax.dot_general(
                    keys[h], queries, (((1,), (1,)), ((), ())), preferred_element_type=jnp.float32
                )
                a = jnp.where(visible, (0.5 * s + 1.0) * s + 1.0, 0.0).astype(jnp.bfloat16)
                ga = (
                    lax.dot_general(
                        values[h],
                        numer,
                        (((1,), (1,)), ((), ())),
                        preferred_element_type=jnp.float32,
                    )
                    + gden_ref[h : h + 1, pl.ds(base, BLOCK)]
                )
                gs = jnp.where(visible, ga * (1.0 + s), 0.0).astype(jnp.bfloat16)
                gv = sums[2 * h] + jnp.dot(a, numer, preferred_element_type=jnp.float32)
                gk = sums[2 * h + 1] + jnp.dot(gs, queries, preferred_element_type=jnp.float32)
                gq_ref[h * F : (h + 1) * F, pl.ds(base, BLOCK)] += jnp.dot(
                    across[h], gs, preferred_element_type=jnp.float32
                )
                out += [gv, gk]
            return tuple(out)

        zeros = []
        for h in range(heads):
            zeros += [jnp.zeros((BLOCK, DV), jnp.float32), jnp.zeros((BLOCK, F), jnp.float32)]
        sums = lax.fori_loop(j, blocks, step, tuple(zeros))
        for h in range(heads):
            g_ref[pl.ds(start, BLOCK), h * DV : (h + 1) * DV] = sums[2 * h].astype(jnp.bfloat16)
            g_ref[
                pl.ds(start, BLOCK), wide + (heads + h) * F : wide + (heads + h + 1) * F
            ] = (sums[2 * h + 1] * F**-0.5).astype(jnp.bfloat16)

        @pl.when(j == blocks - 1)
        def _():
            g_ref[:, wide : wide + heads * F] = jnp.transpose(gq_ref[...], (1, 0)).astype(
                jnp.bfloat16
            )

    whole = lambda shape: pl.BlockSpec(shape, lambda j: (0, 0))
    return pl.pallas_call(
        kernel,
        grid=(blocks,),
        in_specs=[
            whole(qkv.shape),
            whole(g_mixed.shape),
            whole(mixed.shape),
            whole(denom.shape),
            whole((tokens, 1)),
            whole((1, tokens)),
        ],
        out_specs=whole(qkv.shape),
        out_shape=jax.ShapeDtypeStruct(qkv.shape, jnp.bfloat16),
        scratch_shapes=[
            pltpu.VMEM((heads * F, tokens), jnp.float32),
            pltpu.VMEM((tokens, wide), jnp.bfloat16),
            pltpu.VMEM((8, tokens), jnp.float32),
            pltpu.VMEM((2 * heads * F, tokens), jnp.bfloat16),
        ],
        compiler_params=pltpu.CompilerParams(vmem_limit_bytes=VMEM_MOST),
        cost_estimate=pl.CostEstimate(
            flops=tokens * tokens * heads * 800, bytes_accessed=tokens * wide * 12, transcendentals=0
        ),
        name="attn_backward",
    )(qkv, g_mixed, mixed, denom, seg_rows, seg_cols)


def by_columns(weight, parts):
    rows, columns = weight.shape
    return weight.reshape(rows, parts, columns // parts).transpose(1, 0, 2)


def to_owner(packed):
    summed = lax.psum_scatter(packed, "dp", scatter_dimension=0, tiled=True)
    parts = lax.axis_size("ctx")
    return lax.all_to_all(
        summed.reshape(parts, -1, packed.shape[1]), "ctx", 0, 0, tiled=True
    ).transpose(1, 0, 2)


def plane_shards(
    activations,
    seg_ids,
    cotangent,
    q_weight,
    k_weight,
    v_weight,
    o_weight,
    gate_weight,
    up_weight,
    down_weight,
    attn_gain,
    mlp_gain,
):
    parts = lax.axis_size("ctx")
    plane = ("ctx", "tp")
    heads = q_weight.shape[1] // F // parts
    wide = heads * DV
    narrow = heads * F
    units = gate_weight.shape[1] // parts
    rows = activations.shape[1] // lax.axis_size("tp")
    mine = lax.axis_index("tp") * rows
    f32, bf16 = jnp.float32, jnp.bfloat16

    def dot(a, b, ca, cb):
        return lax.dot_general(a, b, (((ca,), (cb,)), ((), ())), preferred_element_type=f32)

    def gather(own):
        return lax.all_gather(own, plane, axis=0, tiled=True)

    def scatter(partial):
        return lax.psum_scatter(
            partial.astype(bf16), plane, scatter_dimension=0, tiled=True
        ).astype(f32)

    def fetch(packed):
        mixed = lax.all_to_all(packed, "ctx", 0, 0, tiled=True)
        return lax.all_gather(mixed, "dp", axis=0, tiled=True).reshape(-1, packed.shape[2])

    gain_one = attn_gain.astype(f32)[:, None]
    gain_two = mlp_gain.astype(f32)[:, None]
    scaled = lambda w, g: (w.astype(f32) * g).astype(bf16)
    w_attn = fetch(
        jnp.concatenate(
            [
                by_columns(scaled(v_weight, gain_one), parts),
                by_columns(scaled(q_weight, gain_one), parts),
                by_columns(scaled(k_weight, gain_one), parts),
                by_columns(o_weight, parts),
            ],
            axis=2,
        )
    )
    w_mlp = fetch(
        jnp.concatenate(
            [
                by_columns(scaled(gate_weight, gain_two), parts),
                by_columns(scaled(up_weight, gain_two), parts),
                by_columns(down_weight, parts),
            ],
            axis=2,
        )
    )
    w_qkv, w_out = w_attn[:, : wide + 2 * narrow], w_attn[:, wide + 2 * narrow :]
    w_gate, w_up, w_down = w_mlp[:, :units], w_mlp[:, units : 2 * units], w_mlp[:, 2 * units :]

    x_own = lax.dynamic_slice_in_dim(activations[0], mine, rows, 0).astype(f32)
    r_one = lax.rsqrt(jnp.mean(x_own * x_own, axis=1, keepdims=True) + EPSILON)
    hat_one = x_own * r_one
    rows_one = gather(hat_one.astype(bf16))
    cot_own = lax.dynamic_slice_in_dim(cotangent[0], mine, rows, 0)
    cot = gather(cot_own)
    segments = lax.all_gather(seg_ids[0], "ctx", axis=0, tiled=True)
    seg_rows, seg_cols = segments[:, None], segments[None, :]

    qkv = dot(rows_one, w_qkv, 1, 0).astype(bf16)
    mixed, denom, heads_out = attention_forward(qkv, seg_rows, seg_cols, heads)
    middle = x_own + scatter(dot(heads_out, w_out, 1, 1))
    r_two = lax.rsqrt(jnp.mean(middle * middle, axis=1, keepdims=True) + EPSILON)
    hat_two = middle * r_two
    rows_two = gather(hat_two.astype(bf16))
    gate = dot(rows_two, w_gate, 1, 0)
    up = dot(rows_two, w_up, 1, 0)
    sig = jax.nn.sigmoid(gate)
    hidden = (gate * sig * up).astype(bf16)
    out_own = (middle + scatter(dot(hidden, w_down, 1, 1))).astype(bf16)
    out = lax.all_gather(out_own, "tp", axis=0, tiled=True)

    g_hidden = dot(cot, w_down, 1, 0)
    g_gate = (g_hidden * up * sig * (1.0 + gate * (1.0 - sig))).astype(bf16)
    g_up = (g_hidden * gate * sig).astype(bf16)
    e_two = scatter(dot(g_gate, w_gate, 1, 1) + dot(g_up, w_up, 1, 1))
    g_middle = cot_own.astype(f32) + r_two * (
        e_two - hat_two * jnp.mean(e_two * hat_two, axis=1, keepdims=True)
    )
    back_mlp = to_owner(
        jnp.concatenate(
            [dot(rows_two, g_gate, 0, 0), dot(rows_two, g_up, 0, 0), dot(cot, hidden, 0, 0)], axis=1
        ).astype(bf16)
    )
    branch = gather(g_middle.astype(bf16))
    g_mixed = dot(branch, w_out, 1, 0).astype(bf16)
    g_qkv = attention_backward(qkv, g_mixed, mixed, denom, seg_rows, seg_cols, heads)
    e_one = scatter(dot(g_qkv, w_qkv, 1, 1))
    g_x = g_middle + r_one * (e_one - hat_one * jnp.mean(e_one * hat_one, axis=1, keepdims=True))
    g_input = lax.all_gather(g_x, "tp", axis=0, tiled=True)
    back_attn = to_owner(
        jnp.concatenate([dot(rows_one, g_qkv, 0, 0), dot(branch, heads_out, 0, 0)], axis=1).astype(
            bf16
        )
    )

    def owned(back, start, width):
        return back[:, :, start : start + width].reshape(back.shape[0], -1).astype(f32)

    s_v = owned(back_attn, 0, wide)
    s_q = owned(back_attn, wide, narrow)
    s_k = owned(back_attn, wide + narrow, narrow)
    s_o = owned(back_attn, wide + 2 * narrow, wide)
    s_gate = owned(back_mlp, 0, units)
    s_up = owned(back_mlp, units, units)
    s_down = owned(back_mlp, 2 * units, units)
    along = lambda s, w: jnp.sum(s * w.astype(f32), axis=1)
    gains = lax.psum(
        jnp.stack(
            [
                along(s_q, q_weight) + along(s_k, k_weight) + along(s_v, v_weight),
                along(s_gate, gate_weight) + along(s_up, up_weight),
            ]
        ),
        "tp",
    )
    return (
        out[None],
        g_input[None],
        s_q * gain_one,
        s_k * gain_one,
        s_v * gain_one,
        s_o,
        s_gate * gain_two,
        s_up * gain_two,
        s_down,
        gains[0],
        gains[1],
    )


def layer(*arrays):
    heads = arrays[3].shape[1] // F
    plan = shards if heads % lax.axis_size("ctx") else plane_shards
    return plan(*arrays)


def solution(mesh):
    placed = (
        P("dp", "ctx", None),
        P("dp", "ctx"),
        P("dp", "ctx", None),
        P(("dp", "ctx"), "tp"),
        P(("dp", "ctx"), "tp"),
        P(("dp", "ctx"), "tp"),
        P(("dp", "ctx"), "tp"),
        P(("dp", "ctx"), "tp"),
        P(("dp", "ctx"), "tp"),
        P(("dp", "ctx"), "tp"),
        P(("dp", "ctx")),
        P(("dp", "ctx")),
    )
    return jax.shard_map(
        layer,
        mesh=mesh,
        in_specs=placed,
        out_specs=(
            P("dp", "ctx", None),
            P("dp", "ctx", None),
            P(("dp", "ctx"), "tp"),
            P(("dp", "ctx"), "tp"),
            P(("dp", "ctx"), "tp"),
            P(("dp", "ctx"), "tp"),
            P(("dp", "ctx"), "tp"),
            P(("dp", "ctx"), "tp"),
            P(("dp", "ctx"), "tp"),
            P(("dp", "ctx")),
            P(("dp", "ctx")),
        ),
        check_vma=False,
    )
```

```python
import jax
import jax.numpy as jnp
from jax import lax
from jax.experimental import pallas as pl
from jax.experimental.pallas import tpu as pltpu
from jax.sharding import PartitionSpec as P

F = 16
DV = 128


EPSILON = 1e-05
PRECISE = lax.Precision.HIGHEST
VMEM_MOST = 56 * 2**20


def prefix(x, axis, join, neutral, backward):
    count = lax.axis_size(axis)
    place = lax.axis_index(axis)
    ahead = count - 1 - place if backward else place
    gathered = jax.tree.map(
        lambda a, kind: lax.all_gather(a.astype(kind), axis),
        x,
        (jnp.bfloat16, jnp.bfloat16, jnp.bfloat16),
    )
    state = jax.tree.map(lambda a, e: jnp.zeros_like(a) + jnp.asarray(e, a.dtype), x, neutral)

    def one(lap, state):
        source = count - 1 - lap if backward else lap
        return join(
            state,
            jax.tree.map(
                lambda a, own: lax.dynamic_index_in_dim(a, source, 0, False).astype(own.dtype),
                gathered,
                x,
            ),
        )

    return lax.fori_loop(0, ahead, one, state)


def taylor(features_in):
    feature_count = features_in.shape[-1]
    products = (features_in[..., :, None] * features_in[..., None, :]).reshape(
        features_in.shape[:-1] + (feature_count * feature_count,)
    )
    constant = jnp.ones(features_in.shape[:-1] + (1,), jnp.float32)
    return jnp.concatenate(
        [
            constant,
            features_in * feature_count ** (-0.25),
            products * (2.0 * feature_count) ** (-0.5),
        ],
        axis=-1,
    )


def taylor_back(features_in, incoming_gradient):
    feature_count = features_in.shape[-1]
    linear = incoming_gradient[..., 1 : 1 + feature_count] * feature_count ** (-0.25)
    square = incoming_gradient[..., 1 + feature_count :].reshape(
        incoming_gradient.shape[:-1] + (feature_count, feature_count)
    )
    paired = jnp.einsum(
        "...ab,...b->...a", square + jnp.swapaxes(square, -1, -2), features_in, precision=PRECISE
    )
    return linear + paired * (2.0 * feature_count) ** (-0.5)


def norm_backward_step(incoming_gradient, unit_normalized_rows, multiplier_term, gain_vector_row):
    rescaled_rows = incoming_gradient * gain_vector_row
    return multiplier_term * (
        rescaled_rows
        - unit_normalized_rows
        * jnp.mean(rescaled_rows * unit_normalized_rows, axis=1, keepdims=True)
    )


def join_states(earlier, later_part):
    is_empty = later_part[2] < 0.0
    retain = jnp.where(is_empty | (earlier[2] == later_part[2]), 1.0, 0.0).astype(jnp.float32)
    return (
        later_part[0] + retain * earlier[0],
        later_part[1] + retain * earlier[1],
        jnp.where(is_empty, earlier[2], later_part[2]),
    )


def shards(
    activations,
    seg_ids,
    cotangent,
    q_weight,
    k_weight,
    v_weight,
    o_weight,
    gate_weight,
    up_weight,
    down_weight,
    attn_gain,
    mlp_gain,
):
    layer_input_rows = activations[0].astype(jnp.float32)
    segment = seg_ids[0].astype(jnp.float32)
    tokens = layer_input_rows.shape[0]
    head_count = q_weight.shape[1] // F
    w_query, w_key, w_value, w_out, first_norm_gain = (
        lax.all_gather(q_weight, ("dp", "ctx"), axis=0, tiled=True),
        lax.all_gather(k_weight, ("dp", "ctx"), axis=0, tiled=True),
        lax.all_gather(v_weight, ("dp", "ctx"), axis=0, tiled=True),
        lax.all_gather(o_weight, ("dp", "ctx"), axis=0, tiled=True),
        lax.all_gather(attn_gain, ("dp", "ctx"), axis=0, tiled=True),
    )
    first_inverse_scale = lax.rsqrt(
        jnp.mean(layer_input_rows * layer_input_rows, axis=1, keepdims=True) + EPSILON
    )
    first_unit_rows = layer_input_rows * first_inverse_scale
    first_normalized = (first_unit_rows * first_norm_gain.astype(jnp.float32)).astype(jnp.bfloat16)
    queries = (
        jnp.dot(first_normalized, w_query, preferred_element_type=jnp.float32)
        .astype(jnp.bfloat16)
        .reshape(tokens, head_count, F)
    )
    key_heads = (
        jnp.dot(first_normalized, w_key, preferred_element_type=jnp.float32)
        .astype(jnp.bfloat16)
        .reshape(tokens, head_count, F)
    )
    value_heads = (
        jnp.dot(first_normalized, w_value, preferred_element_type=jnp.float32)
        .astype(jnp.bfloat16)
        .reshape(tokens, head_count, DV)
    )
    w_gate, w_up, w_down, second_norm_gain = (
        lax.all_gather(gate_weight, ("dp", "ctx"), axis=0, tiled=True),
        lax.all_gather(up_weight, ("dp", "ctx"), axis=0, tiled=True),
        lax.all_gather(down_weight, ("dp", "ctx"), axis=0, tiled=True),
        lax.all_gather(mlp_gain, ("dp", "ctx"), axis=0, tiled=True),
    )
    scores = jnp.einsum(
        "thf,shf->hts", queries, key_heads, preferred_element_type=jnp.float32
    ) * F ** (-0.5)
    places = jnp.arange(tokens)
    visible = (
        (places[:, None] >= places[None, :]) & (segment[:, None] == segment[None, :])
    ).astype(jnp.float32)
    weights = (visible * (1.0 + scores + 0.5 * scores * scores)).astype(jnp.bfloat16)
    query_float = queries.astype(jnp.float32)
    key_float = key_heads.astype(jnp.float32)
    value_float = value_heads.astype(jnp.float32)
    feat_q = taylor(query_float)
    feat_k = taylor(key_float)
    ending = segment[-1]
    owned = (segment == ending).astype(jnp.float32)[:, None, None]
    local_state = jnp.einsum("thf,thd->hfd", feat_k * owned, value_float, precision=PRECISE)
    local_total = jnp.sum(feat_k * owned, axis=0)
    empty_state = (jnp.zeros_like(local_state), jnp.zeros_like(local_total), jnp.float32(-1.0))
    prior_state, prior_total, before = prefix(
        (local_state, local_total, ending), "ctx", join_states, empty_state, False
    )
    inherit = (segment == before).astype(jnp.float32)
    numerator = jnp.einsum(
        "hts,shd->thd", weights, value_heads, preferred_element_type=jnp.float32
    ) + inherit[:, None, None] * jnp.einsum("thf,hfd->thd", feat_q, prior_state, precision=PRECISE)
    denominator = jnp.sum(weights.astype(jnp.float32), axis=2).T + inherit[:, None] * jnp.einsum(
        "thf,hf->th", feat_q, prior_total, precision=PRECISE
    )
    mixed_heads = numerator / denominator[:, :, None]
    heads_out = mixed_heads.reshape(tokens, head_count * DV).astype(jnp.bfloat16)
    attn_out = lax.psum(
        jnp.einsum("tc,dc->td", heads_out, w_out, preferred_element_type=jnp.float32), "tp"
    )
    residual_midpoint = layer_input_rows + attn_out
    second_inverse_scale = lax.rsqrt(
        jnp.mean(residual_midpoint * residual_midpoint, axis=1, keepdims=True) + EPSILON
    )
    second_unit_rows = residual_midpoint * second_inverse_scale
    second_normalized = (second_unit_rows * second_norm_gain.astype(jnp.float32)).astype(
        jnp.bfloat16
    )
    gate_value = jnp.dot(second_normalized, w_gate, preferred_element_type=jnp.float32)
    up_value = jnp.dot(second_normalized, w_up, preferred_element_type=jnp.float32)
    sigmoid_gate = jax.nn.sigmoid(gate_value)
    hidden = (gate_value * sigmoid_gate * up_value).astype(jnp.bfloat16)
    mlp_out = lax.psum(
        jnp.einsum("tc,dc->td", hidden, w_down, preferred_element_type=jnp.float32).astype(
            jnp.bfloat16
        ),
        "tp",
    ).astype(jnp.float32)
    final_out = residual_midpoint + mlp_out
    grad_out = cotangent[0].astype(jnp.float32)
    grad_branch_two = cotangent[0]
    grad_w_down = jnp.einsum(
        "td,tc->dc", grad_branch_two, hidden, preferred_element_type=jnp.float32
    )
    grad_hidden = jnp.dot(grad_branch_two, w_down, preferred_element_type=jnp.float32)
    grad_gate = (
        grad_hidden * up_value * sigmoid_gate * (1.0 + gate_value * (1.0 - sigmoid_gate))
    ).astype(jnp.bfloat16)
    grad_up = (grad_hidden * gate_value * sigmoid_gate).astype(jnp.bfloat16)
    grad_w_gate = jnp.einsum(
        "td,tc->dc", second_normalized, grad_gate, preferred_element_type=jnp.float32
    )
    grad_w_up = jnp.einsum(
        "td,tc->dc", second_normalized, grad_up, preferred_element_type=jnp.float32
    )
    grad_normed_part = jnp.einsum(
        "tc,dc->td", grad_gate, w_gate, preferred_element_type=jnp.float32
    ) + jnp.einsum("tc,dc->td", grad_up, w_up, preferred_element_type=jnp.float32)
    second_normalized_gradient = lax.psum(grad_normed_part.astype(jnp.bfloat16), "tp").astype(
        jnp.float32
    )
    second_gain_gradient = jnp.sum(second_normalized_gradient * second_unit_rows, axis=0)
    grad_middle = grad_out + norm_backward_step(
        second_normalized_gradient,
        second_unit_rows,
        second_inverse_scale,
        second_norm_gain.astype(jnp.float32),
    )
    mlp_grads = (
        lax.psum_scatter(grad_w_gate, ("dp", "ctx"), scatter_dimension=0, tiled=True),
        lax.psum_scatter(grad_w_up, ("dp", "ctx"), scatter_dimension=0, tiled=True),
        lax.psum_scatter(grad_w_down, ("dp", "ctx"), scatter_dimension=0, tiled=True),
        lax.psum_scatter(second_gain_gradient, ("dp", "ctx"), scatter_dimension=0, tiled=True),
    )
    grad_branch_one = grad_middle.astype(jnp.bfloat16)
    grad_w_out = jnp.einsum(
        "td,tc->dc", grad_branch_one, heads_out, preferred_element_type=jnp.float32
    )
    grad_heads_low = jnp.dot(grad_branch_one, w_out, preferred_element_type=jnp.float32).astype(
        jnp.bfloat16
    )
    grad_mixed = (
        lax.optimization_barrier(grad_heads_low).astype(jnp.float32).reshape(tokens, head_count, DV)
    )
    numer_low = (grad_mixed / denominator[:, :, None]).astype(jnp.bfloat16)
    grad_numer = lax.optimization_barrier(numer_low).astype(jnp.float32)
    grad_denom = -jnp.sum(grad_mixed * mixed_heads, axis=2) / denominator
    grad_weights = (
        jnp.einsum("thd,shd->hts", numer_low, value_heads, preferred_element_type=jnp.float32)
        + grad_denom.T[:, :, None]
    )
    grad_scores = (grad_weights * visible * (1.0 + scores)).astype(jnp.bfloat16)
    grad_value = jnp.einsum("hts,thd->shd", weights, numer_low, preferred_element_type=jnp.float32)
    grad_query = jnp.einsum(
        "hts,shf->thf", grad_scores, key_heads, preferred_element_type=jnp.float32
    ) * F ** (-0.5)
    grad_key = jnp.einsum(
        "hts,thf->shf", grad_scores, queries, preferred_element_type=jnp.float32
    ) * F ** (-0.5)
    grad_feat_q = inherit[:, None, None] * (
        jnp.einsum("thd,hfd->thf", grad_numer, prior_state, precision=PRECISE)
        + grad_denom[:, :, None] * prior_total[None]
    )
    carried_state = jnp.einsum(
        "thf,thd->hfd", feat_q * inherit[:, None, None], grad_numer, precision=PRECISE
    )
    carried_total = jnp.sum(feat_q * (inherit[:, None] * grad_denom)[:, :, None], axis=0)
    starting = segment[0]
    later_state, later_total, after_seg = prefix(
        (carried_state, carried_total, starting), "ctx", join_states, empty_state, True
    )
    reached = (segment == after_seg).astype(jnp.float32)[:, None, None]
    grad_feat_k = reached * (
        jnp.einsum("hfd,thd->thf", later_state, value_float, precision=PRECISE) + later_total[None]
    )
    grad_value = grad_value + reached * jnp.einsum(
        "thf,hfd->thd", feat_k, later_state, precision=PRECISE
    )
    grad_query = grad_query + taylor_back(query_float, grad_feat_q)
    grad_key = grad_key + taylor_back(key_float, grad_feat_k)
    grad_query_low = grad_query.reshape(tokens, head_count * F).astype(jnp.bfloat16)
    grad_key_low = grad_key.reshape(tokens, head_count * F).astype(jnp.bfloat16)
    grad_value_low = grad_value.reshape(tokens, head_count * DV).astype(jnp.bfloat16)
    grad_w_query = jnp.einsum(
        "td,tc->dc", first_normalized, grad_query_low, preferred_element_type=jnp.float32
    )
    grad_w_key = jnp.einsum(
        "td,tc->dc", first_normalized, grad_key_low, preferred_element_type=jnp.float32
    )
    grad_w_value = jnp.einsum(
        "td,tc->dc", first_normalized, grad_value_low, preferred_element_type=jnp.float32
    )
    grad_normed_sum = (
        jnp.einsum("tc,dc->td", grad_query_low, w_query, preferred_element_type=jnp.float32)
        + jnp.einsum("tc,dc->td", grad_key_low, w_key, preferred_element_type=jnp.float32)
        + jnp.einsum("tc,dc->td", grad_value_low, w_value, preferred_element_type=jnp.float32)
    )
    first_normalized_gradient = lax.psum(grad_normed_sum.astype(jnp.bfloat16), "tp").astype(
        jnp.float32
    )
    first_gain_gradient = jnp.sum(first_normalized_gradient * first_unit_rows, axis=0)
    grad_inputs = grad_middle + norm_backward_step(
        first_normalized_gradient,
        first_unit_rows,
        first_inverse_scale,
        first_norm_gain.astype(jnp.float32),
    )
    attn_grads = (
        lax.psum_scatter(grad_w_query, ("dp", "ctx"), scatter_dimension=0, tiled=True),
        lax.psum_scatter(grad_w_key, ("dp", "ctx"), scatter_dimension=0, tiled=True),
        lax.psum_scatter(grad_w_value, ("dp", "ctx"), scatter_dimension=0, tiled=True),
        lax.psum_scatter(grad_w_out, ("dp", "ctx"), scatter_dimension=0, tiled=True),
        lax.psum_scatter(first_gain_gradient, ("dp", "ctx"), scatter_dimension=0, tiled=True),
    )
    return (
        final_out.astype(jnp.bfloat16)[None],
        grad_inputs[None],
        attn_grads[0],
        attn_grads[1],
        attn_grads[2],
        attn_grads[3],
        mlp_grads[0],
        mlp_grads[1],
        mlp_grads[2],
        attn_grads[4],
        mlp_grads[3],
    )


BLOCK = 512


def attention_forward(qkv, seg_rows, seg_cols, heads):
    tokens = qkv.shape[0]
    wide = heads * DV

    def kernel(x_ref, row_ref, col_ref, mixed_ref, denom_ref, low_ref, ext_ref):
        i = pl.program_id(0)

        @pl.when(i == 0)
        def _():
            for h in range(heads):
                ext_ref[:, 2 * h * DV : (2 * h + 1) * DV] = x_ref[:, h * DV : (h + 1) * DV]
                ext_ref[:, (2 * h + 1) * DV : (2 * h + 2) * DV] = jnp.ones(
                    (tokens, DV), jnp.bfloat16
                )

        base = pl.multiple_of(i * BLOCK, BLOCK)
        own = row_ref[pl.ds(base, BLOCK), :]
        place = lax.broadcasted_iota(jnp.int32, (BLOCK, BLOCK), 0) - lax.broadcasted_iota(
            jnp.int32, (BLOCK, BLOCK), 1
        )
        queries = [
            x_ref[pl.ds(base, BLOCK), wide + h * F : wide + (h + 1) * F] * jnp.bfloat16(F**-0.5)
            for h in range(heads)
        ]

        def step(j, sums):
            start = pl.multiple_of(j * BLOCK, BLOCK)
            visible = (place >= start - base) & (own == col_ref[:, pl.ds(start, BLOCK)])
            out = []
            for h in range(heads):
                keys = x_ref[
                    pl.ds(start, BLOCK),
                    wide + (heads + h) * F : wide + (heads + h + 1) * F,
                ]
                s = lax.dot_general(
                    queries[h], keys, (((1,), (1,)), ((), ())), preferred_element_type=jnp.float32
                )
                a = jnp.where(visible, (0.5 * s + 1.0) * s + 1.0, 0.0).astype(jnp.bfloat16)
                out.append(
                    sums[h]
                    + jnp.dot(
                        a,
                        ext_ref[pl.ds(start, BLOCK), 2 * h * DV : (2 * h + 2) * DV],
                        preferred_element_type=jnp.float32,
                    )
                )
            return tuple(out)

        sums = lax.fori_loop(
            0, i + 1, step, tuple(jnp.zeros((BLOCK, 2 * DV), jnp.float32) for _ in range(heads))
        )
        for h in range(heads):
            denom = sums[h][:, DV:]
            mixed = sums[h][:, :DV] / denom
            mixed_ref[:, h * DV : (h + 1) * DV] = mixed
            low_ref[:, h * DV : (h + 1) * DV] = mixed.astype(jnp.bfloat16)
            denom_ref[:, h : h + 1] = denom[:, :1]

    return pl.pallas_call(
        kernel,
        grid=(tokens // BLOCK,),
        in_specs=[
            pl.BlockSpec(qkv.shape, lambda i: (0, 0)),
            pl.BlockSpec((tokens, 1), lambda i: (0, 0)),
            pl.BlockSpec((1, tokens), lambda i: (0, 0)),
        ],
        out_specs=[
            pl.BlockSpec((BLOCK, wide), lambda i: (i, 0)),
            pl.BlockSpec((BLOCK, heads), lambda i: (i, 0)),
            pl.BlockSpec((BLOCK, wide), lambda i: (i, 0)),
        ],
        out_shape=[
            jax.ShapeDtypeStruct((tokens, wide), jnp.float32),
            jax.ShapeDtypeStruct((tokens, heads), jnp.float32),
            jax.ShapeDtypeStruct((tokens, wide), jnp.bfloat16),
        ],
        scratch_shapes=[pltpu.VMEM((tokens, 2 * wide), jnp.bfloat16)],
        compiler_params=pltpu.CompilerParams(vmem_limit_bytes=VMEM_MOST),
        cost_estimate=pl.CostEstimate(
            flops=tokens * tokens * heads * 400, bytes_accessed=tokens * wide * 12, transcendentals=0
        ),
        name="attn_forward",
    )(qkv, seg_rows, seg_cols)


def attention_backward(qkv, g_mixed, mixed, denom, seg_rows, seg_cols, heads):
    tokens = qkv.shape[0]
    wide = heads * DV
    blocks = tokens // BLOCK

    def kernel(
        x_ref, gm_ref, m_ref, d_ref, row_ref, col_ref, g_ref, gq_ref, numer_ref, gden_ref, key_ref
    ):
        j = pl.program_id(0)

        @pl.when(j == 0)
        def _():
            gq_ref[...] = jnp.zeros_like(gq_ref)
            for h in range(heads):
                part = pl.ds(h * DV, DV)
                gm = gm_ref[:, part].astype(jnp.float32)
                inverse = 1.0 / d_ref[:, h : h + 1]
                numer_ref[:, part] = (gm * inverse).astype(jnp.bfloat16)
                down = -jnp.sum(gm * m_ref[:, part], axis=1, keepdims=True) * inverse
                gden_ref[h : h + 1, :] = jnp.transpose(
                    jnp.broadcast_to(down, (tokens, 128)), (1, 0)
                )[:1, :]
            key_ref[...] = jnp.transpose(
                x_ref[:, wide : wide + 2 * heads * F].astype(jnp.float32), (1, 0)
            ).astype(jnp.bfloat16)

        start = pl.multiple_of(j * BLOCK, BLOCK)
        own = row_ref[pl.ds(start, BLOCK), :]
        place = lax.broadcasted_iota(jnp.int32, (BLOCK, BLOCK), 1) - lax.broadcasted_iota(
            jnp.int32, (BLOCK, BLOCK), 0
        )
        values = [x_ref[pl.ds(start, BLOCK), h * DV : (h + 1) * DV] for h in range(heads)]
        keys = [
            x_ref[pl.ds(start, BLOCK), wide + (heads + h) * F : wide + (heads + h + 1) * F]
            * jnp.bfloat16(F**-0.5)
            for h in range(heads)
        ]
        across = [
            key_ref[(heads + h) * F : (heads + h + 1) * F, pl.ds(start, BLOCK)]
            * jnp.bfloat16(F**-0.5)
            for h in range(heads)
        ]

        def step(i, sums):
            base = pl.multiple_of(i * BLOCK, BLOCK)
            visible = (place >= start - base) & (own == col_ref[:, pl.ds(base, BLOCK)])
            out = []
            for h in range(heads):
                queries = x_ref[pl.ds(base, BLOCK), wide + h * F : wide + (h + 1) * F]
                numer = numer_ref[pl.ds(base, BLOCK), h * DV : (h + 1) * DV]
                s = lax.dot_general(
                    keys[h], queries, (((1,), (1,)), ((), ())), preferred_element_type=jnp.float32
                )
                a = jnp.where(visible, (0.5 * s + 1.0) * s + 1.0, 0.0).astype(jnp.bfloat16)
                ga = (
                    lax.dot_general(
                        values[h],
                        numer,
                        (((1,), (1,)), ((), ())),
                        preferred_element_type=jnp.float32,
                    )
                    + gden_ref[h : h + 1, pl.ds(base, BLOCK)]
                )
                gs = jnp.where(visible, ga * (1.0 + s), 0.0).astype(jnp.bfloat16)
                gv = sums[2 * h] + jnp.dot(a, numer, preferred_element_type=jnp.float32)
                gk = sums[2 * h + 1] + jnp.dot(gs, queries, preferred_element_type=jnp.float32)
                gq_ref[h * F : (h + 1) * F, pl.ds(base, BLOCK)] += jnp.dot(
                    across[h], gs, preferred_element_type=jnp.float32
                )
                out += [gv, gk]
            return tuple(out)

        zeros = []
        for h in range(heads):
            zeros += [jnp.zeros((BLOCK, DV), jnp.float32), jnp.zeros((BLOCK, F), jnp.float32)]
        sums = lax.fori_loop(j, blocks, step, tuple(zeros))
        for h in range(heads):
            g_ref[pl.ds(start, BLOCK), h * DV : (h + 1) * DV] = sums[2 * h].astype(jnp.bfloat16)
            g_ref[
                pl.ds(start, BLOCK), wide + (heads + h) * F : wide + (heads + h + 1) * F
            ] = (sums[2 * h + 1] * F**-0.5).astype(jnp.bfloat16)

        @pl.when(j == blocks - 1)
        def _():
            g_ref[:, wide : wide + heads * F] = jnp.transpose(gq_ref[...], (1, 0)).astype(
                jnp.bfloat16
            )

    whole = lambda shape: pl.BlockSpec(shape, lambda j: (0, 0))
    return pl.pallas_call(
        kernel,
        grid=(blocks,),
        in_specs=[
            whole(qkv.shape),
            whole(g_mixed.shape),
            whole(mixed.shape),
            whole(denom.shape),
            whole((tokens, 1)),
            whole((1, tokens)),
        ],
        out_specs=whole(qkv.shape),
        out_shape=jax.ShapeDtypeStruct(qkv.shape, jnp.bfloat16),
        scratch_shapes=[
            pltpu.VMEM((heads * F, tokens), jnp.float32),
            pltpu.VMEM((tokens, wide), jnp.bfloat16),
            pltpu.VMEM((8, tokens), jnp.float32),
            pltpu.VMEM((2 * heads * F, tokens), jnp.bfloat16),
        ],
        compiler_params=pltpu.CompilerParams(vmem_limit_bytes=VMEM_MOST),
        cost_estimate=pl.CostEstimate(
            flops=tokens * tokens * heads * 800, bytes_accessed=tokens * wide * 12, transcendentals=0
        ),
        name="attn_backward",
    )(qkv, g_mixed, mixed, denom, seg_rows, seg_cols)


MESH = pl.DeviceIdType.MESH
BF16, F32 = jnp.bfloat16, jnp.float32


def dot(a, b, ca, cb):
    return lax.dot_general(a, b, (((ca,), (cb,)), ((), ())), preferred_element_type=F32)


def place_of():
    return lax.axis_index("dp"), lax.axis_index("ctx"), lax.axis_index("tp")


def beside(c, across):
    x, y = lax.rem(c, 2), lax.div(c, 2)
    return lax.rem(x + across % 2, 2) + 2 * lax.rem(y + across // 2, 2)


def greet(devices):
    barrier = pltpu.get_barrier_semaphore()
    for device in devices:
        pl.semaphore_signal(barrier, inc=1, device_id=device, device_id_type=MESH)
    pl.semaphore_wait(barrier, len(devices))


def remote(source, target, send, receive, k, device):
    return pltpu.make_async_remote_copy(
        src_ref=source,
        dst_ref=target,
        send_sem=send.at[k],
        recv_sem=receive.at[k],
        device_id=device,
        device_id_type=MESH,
    )


def gather_rows(buf, send, receive, piece=None, early=None):
    d, c, t = place_of()
    own = buf.shape[0] // 8
    half = own // 2
    to_x, to_y, to_t = (d, beside(c, 1), t), (d, beside(c, 2), t), (d, c, 1 - t)
    started = []

    def part(across, core, h):
        block = c if across == 0 else beside(c, across)
        start = (2 * block + core) * own + h * half
        return buf.at[pl.ds(pl.multiple_of(start, half), half)]

    def put(k, across, h, device):
        ref = part(across, t, h)
        copy = remote(ref, ref, send, receive, k, device)
        copy.start()
        started.append(copy)

    def got(k, across, core, h):
        ref = part(across, core, h)
        remote(ref, ref, send, receive, k, to_t).wait_recv()

    def work(across, core):
        if piece is not None:
            block = c if across == 0 else beside(c, across)
            piece(pl.multiple_of((2 * block + core) * own, own))

    put(0, 0, 0, to_x)
    put(1, 0, 1, to_y)
    put(2, 0, 1, to_x)
    put(3, 0, 0, to_y)
    put(6, 0, 0, to_t)
    put(7, 0, 1, to_t)
    if early is not None:
        early()
    work(0, t)
    got(6, 0, 1 - t, 0)
    got(7, 0, 1 - t, 1)
    work(0, 1 - t)
    got(0, 1, t, 0)
    put(4, 1, 0, to_y)
    put(8, 1, 0, to_t)
    got(1, 2, t, 1)
    put(5, 2, 1, to_x)
    put(9, 2, 1, to_t)
    got(2, 1, t, 1)
    put(10, 1, 1, to_t)
    got(3, 2, t, 0)
    put(11, 2, 0, to_t)
    work(1, t)
    work(2, t)
    got(8, 1, 1 - t, 0)
    got(10, 1, 1 - t, 1)
    work(1, 1 - t)
    got(9, 2, 1 - t, 1)
    got(11, 2, 1 - t, 0)
    work(2, 1 - t)
    got(4, 3, t, 0)
    put(12, 3, 0, to_t)
    got(5, 3, t, 1)
    put(13, 3, 1, to_t)
    work(3, t)
    got(12, 3, 1 - t, 0)
    got(13, 3, 1 - t, 1)
    work(3, 1 - t)
    for copy in started:
        copy.wait_send()


GATHER_COPIES = 14


def scatter_rows(piece, bufs, send, receive):
    to_core, from_core, kept, over, came = bufs
    d, c, t = place_of()
    own = kept.shape[1]
    half = own // 2
    to_x, to_y, to_t = (d, beside(c, 1), t), (d, beside(c, 2), t), (d, c, 1 - t)

    def link(k):
        return remote(over.at[k], came.at[k], send, receive, 4 + k, to_x if k % 2 == 0 else to_y)

    def core(i):
        return remote(to_core.at[i], from_core.at[i], send, receive, i, to_t)

    def ready(k, i, h, extra=None):
        rows = pl.ds(h * half, half)
        total = kept[i, rows, :]
        if extra is not None:
            total = total + came[extra].astype(F32)
        over[k] = total.astype(BF16)
        link(k).start()

    def step(p, carry):
        i = lax.div(p, 2)
        across = 3 - i
        x, y = lax.rem(c, 2), lax.div(c, 2)
        block = lax.rem(x + lax.rem(across, 2), 2) + 2 * lax.rem(y + lax.div(across, 2), 2)
        mine = lax.rem(p, 2)
        who = mine * t + (1 - mine) * (1 - t)
        piece(pl.multiple_of((2 * block + who) * own, own), kept.at[i])

        @pl.when(mine == 0)
        def _():
            to_core[i] = kept[i].astype(BF16)
            core(i).start()

        @pl.when(mine == 1)
        def _():
            core(i).wait_recv()
            kept[i] = kept[i] + from_core[i].astype(F32)

        @pl.when(p == 1)
        def _():
            ready(0, 0, 0)
            ready(1, 0, 1)

        @pl.when(p == 3)
        def _():
            ready(3, 1, 1)

        @pl.when(p == 5)
        def _():
            ready(2, 2, 0)
            link(1).wait_recv()
            ready(4, 2, 1, 1)
            link(0).wait_recv()
            ready(5, 1, 0, 0)

        return carry

    lax.fori_loop(0, 8, step, 0)
    for h, a, b in ((0, 2, 5), (1, 3, 4)):
        link(a).wait_recv()
        link(b).wait_recv()
        rows = pl.ds(h * half, half)
        kept[3, rows, :] = kept[3, rows, :] + (came[a].astype(F32) + came[b].astype(F32))
    for i in range(4):
        core(i).wait_send()
    for k in range(6):
        link(k).wait_send()


SCATTER_COPIES = 10


def scatter_scratch(own, width):
    return [
        pltpu.VMEM((4, own, width), BF16),
        pltpu.VMEM((4, own, width), BF16),
        pltpu.VMEM((4, own, width), F32),
        pltpu.VMEM((6, own // 2, width), BF16),
        pltpu.VMEM((6, own // 2, width), BF16),
    ]


def by_tiles(a, weights, out_ref, tile=512):
    width = out_ref.shape[1]

    @pl.loop(0, width // tile)
    def _(n):
        columns = pl.ds(pl.multiple_of(n * tile, tile), tile)
        total = None
        for x, w in zip(a, weights):
            term = dot(x, w[columns, :], 1, 1)
            total = term if total is None else total + term
        out_ref[:, columns] = total


def norm_parts(rows):
    scale = lax.rsqrt(jnp.mean(rows * rows, axis=1, keepdims=True) + EPSILON)
    return scale, rows * scale


def norm_back(e, hat, scale):
    return scale * (e - hat * jnp.mean(e * hat, axis=1, keepdims=True))


def call(kernel, name, collective, arrays, out_shape, scratch, spaces=None, out_spaces=None, flops=0):
    vmem = pl.BlockSpec(memory_space=pltpu.VMEM)
    moved = sum(a.size * a.dtype.itemsize for a in arrays)
    return pl.pallas_call(
        kernel,
        in_specs=spaces or [vmem] * len(arrays),
        out_specs=out_spaces or [vmem] * len(out_shape),
        out_shape=out_shape,
        scratch_shapes=scratch,
        compiler_params=pltpu.CompilerParams(
            collective_id=collective, has_side_effects=True, vmem_limit_bytes=VMEM_MOST
        ),
        cost_estimate=pl.CostEstimate(flops=flops, bytes_accessed=moved, transcendentals=0),
        name=name,
    )(*arrays)


def sems(count):
    return [pltpu.SemaphoreType.DMA((count,)), pltpu.SemaphoreType.DMA((count,))]


def depth(d, k):
    return lax.rem(d + k, lax.axis_size("dp"))


def front(x, seg, w_attn, w_mlp, tokens):
    width = x.shape[1]
    own = tokens // 8
    deep = lax.axis_size("dp")

    def kernel(
        x_ref, seg_ref, wa_ref, wm_ref, rows_ref, segs_ref, wa_out, wm_out,
        send, receive, small_send, small_receive, deep_send, deep_receive, here,
    ):
        d, c, t = place_of()
        greet(
            [(d, beside(c, k), t) for k in (1, 2, 3)]
            + [(d, c, 1 - t)]
            + [(depth(d, k), c, t) for k in range(1, deep)]
        )
        jobs = (
            (lambda block: wa_ref.at[block], lambda block: wa_out.at[d, block]),
            (lambda block: seg_ref.at[0], lambda block: segs_ref.at[block]),
            (lambda block: wm_ref.at[block], lambda block: wm_out.at[block]),
        )

        def local(n):
            return pltpu.make_async_copy(jobs[n][0](c), jobs[n][1](c), here.at[n])

        def out(n, k):
            return remote(
                jobs[n][0](beside(c, k)), jobs[n][1](c), small_send, small_receive,
                3 * n + k - 1, (d, beside(c, k), t),
            )

        def arrival(n, k):
            block = beside(c, k)
            return remote(
                jobs[n][0](block), jobs[n][1](block), small_send, small_receive,
                3 * n + k - 1, (d, block, t),
            )

        def along(k):
            return remote(
                wa_out.at[d], wa_out.at[d], deep_send, deep_receive, k - 1, (depth(d, k), c, t)
            )

        def from_depth(k):
            there = wa_out.at[depth(d, deep - k)]
            return remote(there, there, deep_send, deep_receive, k - 1, (depth(d, k), c, t))

        local(0).start()
        for k in (3, 1, 2):
            out(0, k).start()
        mine = pl.multiple_of((2 * c + t) * own, own)
        _, hat = norm_parts(x_ref[pl.ds(pl.multiple_of(t * own, own), own), :].astype(F32))
        rows_ref[pl.ds(mine, own), :] = hat.astype(BF16)

        def early():
            for n in (1, 2):
                local(n).start()
                for k in (3, 1, 2):
                    out(n, k).start()
            local(0).wait()
            for k in (1, 2, 3):
                arrival(0, k).wait_recv()
            for k in range(1, deep):
                along(k).start()

        gather_rows(rows_ref, send, receive, early=early)
        for n in (1, 2):
            local(n).wait()
            for k in (1, 2, 3):
                arrival(n, k).wait_recv()
        for k in range(1, deep):
            from_depth(k).wait_recv()
        for n in range(3):
            for k in (1, 2, 3):
                out(n, k).wait_send()
        for k in range(1, deep):
            along(k).wait_send()

    vmem, hbm = pl.BlockSpec(memory_space=pltpu.VMEM), pl.BlockSpec(memory_space=pl.ANY)
    return call(
        kernel,
        "front",
        1,
        (x, seg[None], w_attn, w_mlp),
        [
            jax.ShapeDtypeStruct((tokens, width), BF16),
            jax.ShapeDtypeStruct((4,) + seg.shape, seg.dtype),
            jax.ShapeDtypeStruct((deep,) + w_attn.shape, BF16),
            jax.ShapeDtypeStruct(w_mlp.shape, BF16),
        ],
        sems(GATHER_COPIES) + sems(9) + sems(deep - 1) + [pltpu.SemaphoreType.DMA((3,))],
        [vmem, hbm, hbm, hbm],
        [vmem, hbm, hbm, hbm],
    )


def cotangent_rows(cot, tokens):
    width = cot.shape[1]
    own = tokens // 8

    def kernel(x_ref, rows_ref, send, receive):
        d, c, t = place_of()
        greet([(d, beside(c, 1), t), (d, beside(c, 2), t), (d, c, 1 - t)])
        mine = pl.multiple_of((2 * c + t) * own, own)
        rows_ref[pl.ds(mine, own), :] = x_ref[pl.ds(pl.multiple_of(t * own, own), own), :]
        gather_rows(rows_ref, send, receive)

    return call(
        kernel, "cotangent_rows", 2, (cot,), [jax.ShapeDtypeStruct((tokens, width), BF16)],
        sems(GATHER_COPIES),
    )[0]


def to_middle(heads_out, w_out, x):
    tokens, width = heads_out.shape[0], x.shape[1]
    own = tokens // 8

    def kernel(h_ref, w_ref, x_ref, mid_ref, rows_ref, *rest):
        bufs, (s_send, s_receive, g_send, g_receive) = rest[:5], rest[5:]
        d, c, t = place_of()
        greet([(d, beside(c, 1), t), (d, beside(c, 2), t), (d, c, 1 - t)])

        def piece(start, out_ref):
            by_tiles([h_ref[pl.ds(start, own), :]], [w_ref], out_ref)

        scatter_rows(piece, bufs, s_send, s_receive)
        middle = bufs[2][3] + x_ref[pl.ds(pl.multiple_of(t * own, own), own), :].astype(F32)
        mid_ref[...] = middle
        _, hat = norm_parts(middle)
        rows_ref[pl.ds(pl.multiple_of((2 * c + t) * own, own), own), :] = hat.astype(BF16)
        gather_rows(rows_ref, g_send, g_receive)

    return call(
        kernel, "to_middle", 3, (heads_out, w_out, x),
        [jax.ShapeDtypeStruct((own, width), F32), jax.ShapeDtypeStruct((tokens, width), BF16)],
        scatter_scratch(own, width) + sems(SCATTER_COPIES) + sems(GATHER_COPIES),
        flops=2 * tokens * width * heads_out.shape[1],
    )


def feed_forward(rows_two, cot, middle, w_gate, w_up, w_down):
    tokens, width = rows_two.shape
    own = tokens // 8
    units = w_gate.shape[1]

    def kernel(
        rows_ref, cot_ref, mid_ref, g_ref, u_ref, d_ref, hid_ref, gg_ref, gu_ref, out_ref,
        row_buf, cot_buf, here, *rest,
    ):
        bufs, (s_send, s_receive, t_send, t_receive) = rest[:5], rest[5:]
        d, c, t = place_of()
        greet([(d, beside(c, 1), t), (d, beside(c, 2), t), (d, c, 1 - t)])

        def piece(start, out_ref):
            first = pltpu.make_async_copy(rows_ref.at[pl.ds(start, own)], row_buf, here.at[0])
            other = pltpu.make_async_copy(cot_ref.at[pl.ds(start, own)], cot_buf, here.at[1])
            first.start()
            other.start()
            first.wait()
            rows = row_buf[...]
            gate = dot(rows, g_ref[...], 1, 0)
            up = dot(rows, u_ref[...], 1, 0)
            other.wait()
            g_hidden = dot(cot_buf[...], d_ref[...], 1, 0)
            sig = jax.nn.sigmoid(gate)
            silu = gate * sig
            hidden = (silu * up).astype(BF16)
            hid_ref[pl.ds(start, own), :] = hidden
            gu_ref[pl.ds(start, own), :] = (g_hidden * silu).astype(BF16)
            gg_ref[pl.ds(start, own), :] = (
                g_hidden * up * sig * (1.0 + gate * (1.0 - sig))
            ).astype(BF16)
            by_tiles([hidden], [d_ref], out_ref)

        scatter_rows(piece, bufs, s_send, s_receive)
        place = out_ref.at[pl.ds(pl.multiple_of(t * own, own), own)]
        place[...] = (mid_ref[...] + bufs[2][3]).astype(BF16)
        copy = remote(place, place, t_send, t_receive, 0, (d, c, 1 - t))
        copy.start()
        copy.wait_send()
        there = out_ref.at[pl.ds(pl.multiple_of((1 - t) * own, own), own)]
        remote(there, there, t_send, t_receive, 0, (d, c, 1 - t)).wait_recv()

    vmem, hbm = pl.BlockSpec(memory_space=pltpu.VMEM), pl.BlockSpec(memory_space=pl.ANY)
    return call(
        kernel, "feed_forward", 4, (rows_two, cot, middle, w_gate, w_up, w_down),
        [jax.ShapeDtypeStruct((tokens, units), BF16)] * 3
        + [jax.ShapeDtypeStruct((2 * own, width), BF16)],
        [pltpu.VMEM((own, width), BF16), pltpu.VMEM((own, width), BF16), pltpu.SemaphoreType.DMA((2,))]
        + scatter_scratch(own, width) + sems(SCATTER_COPIES) + sems(1),
        [hbm, hbm, vmem, vmem, vmem, vmem],
        flops=8 * tokens * width * units,
    )


def to_branch(g_gate, g_up, w_gate, w_up, middle, cot, w_out):
    tokens, width = g_gate.shape[0], middle.shape[1]
    own = tokens // 8
    wide = w_out.shape[1]

    def kernel(gg_ref, gu_ref, g_ref, u_ref, mid_ref, cot_ref, w_ref, gm_ref, rows_ref, mix_ref, *rest):
        bufs, (s_send, s_receive, g_send, g_receive) = rest[:5], rest[5:]
        d, c, t = place_of()
        greet([(d, beside(c, 1), t), (d, beside(c, 2), t), (d, c, 1 - t)])

        def piece(start, out_ref):
            by_tiles(
                [gg_ref[pl.ds(start, own), :], gu_ref[pl.ds(start, own), :]], [g_ref, u_ref], out_ref
            )

        scatter_rows(piece, bufs, s_send, s_receive)
        scale, hat = norm_parts(mid_ref[...])
        g_middle = cot_ref[pl.ds(pl.multiple_of(t * own, own), own), :].astype(F32) + norm_back(
            bufs[2][3], hat, scale
        )
        gm_ref[...] = g_middle
        rows_ref[pl.ds(pl.multiple_of((2 * c + t) * own, own), own), :] = g_middle.astype(BF16)

        def mix(start):
            mix_ref[pl.ds(start, own), :] = dot(
                rows_ref[pl.ds(start, own), :], w_ref[...], 1, 0
            ).astype(BF16)

        gather_rows(rows_ref, g_send, g_receive, mix)

    return call(
        kernel, "to_branch", 5, (g_gate, g_up, w_gate, w_up, middle, cot, w_out),
        [
            jax.ShapeDtypeStruct((own, width), F32),
            jax.ShapeDtypeStruct((tokens, width), BF16),
            jax.ShapeDtypeStruct((tokens, wide), BF16),
        ],
        scatter_scratch(own, width) + sems(SCATTER_COPIES) + sems(GATHER_COPIES),
        flops=4 * tokens * width * (g_gate.shape[1] + wide),
    )


def to_input(g_qkv, w_qkv, x, g_middle, back, weights, gain, heads):
    tokens, width = g_qkv.shape[0], x.shape[1]
    own = tokens // 8
    deep = lax.axis_size("dp")
    across = back.shape[1]
    group = back.shape[0] // deep
    held = group // 4
    wide, narrow = heads * DV, heads * F

    def kernel(
        g_ref, w_ref, x_ref, gm_ref, back_ref, wq_ref, wk_ref, wv_ref, gain_ref,
        out_ref, gq_ref, gk_ref, gv_ref, go_ref, gg_ref, *rest,
    ):
        bufs, (s_send, s_receive, t_send, t_receive) = rest[:5], rest[5:9]
        terms, sums, parts, scalar, d_send, d_receive, p_send, p_receive = rest[9:]
        d, c, t = place_of()
        greet(
            [(d, beside(c, k), t) for k in (1, 2, 3)]
            + [(d, c, 1 - t)]
            + [(depth(d, k), c, t) for k in range(1, deep)]
        )

        def deeper(k):
            rows = pl.ds(pl.multiple_of(depth(d, k) * group, group), group)
            return remote(
                back_ref.at[rows], terms.at[k - 1], d_send, d_receive, k - 1, (depth(d, k), c, t)
            )

        def to_block(k):
            rows = pl.ds(pl.multiple_of(beside(c, k) * held, held), held)
            return remote(
                sums.at[rows], parts.at[c], p_send, p_receive, k - 1, (d, beside(c, k), t)
            )

        def from_block(k):
            there = parts.at[beside(c, k)]
            return remote(there, there, p_send, p_receive, k - 1, (d, beside(c, k), t))

        for k in (2, 1, 3)[: deep - 1] if deep == 4 else range(1, deep):
            deeper(k).start()

        def piece(start, ref):
            by_tiles([g_ref[pl.ds(start, own), :]], [w_ref], ref)

        scatter_rows(piece, bufs, s_send, s_receive)
        scale, hat = norm_parts(x_ref[pl.ds(pl.multiple_of(t * own, own), own), :].astype(F32))
        place = out_ref.at[pl.ds(pl.multiple_of(t * own, own), own)]
        place[...] = gm_ref[...] + norm_back(bufs[2][3], hat, scale)
        copy = remote(place, place, t_send, t_receive, 0, (d, c, 1 - t))
        copy.start()

        for k in range(1, deep):
            deeper(k).wait_recv()
        rows = pl.ds(pl.multiple_of(d * group, group), group)
        total = back_ref[rows, :].astype(F32)
        for k in range(1, deep):
            total = total + terms[k - 1].astype(F32)
        sums[...] = total.astype(BF16)
        for k in (3, 1, 2):
            to_block(k).start()
        parts[c] = sums[pl.ds(pl.multiple_of(c * held, held), held), :]
        for k in (1, 2, 3):
            from_block(k).wait_recv()
        gain_column = gain_ref[...]

        def owned(start, count):
            return jnp.concatenate(
                [parts[b][:, start : start + count].astype(F32) for b in range(4)], axis=1
            )

        own_term = jnp.zeros((held, 1), F32)
        for ref, weight, start, count in (
            (gv_ref, wv_ref, 0, wide),
            (gq_ref, wq_ref, wide, narrow),
            (gk_ref, wk_ref, wide + narrow, narrow),
        ):
            s = owned(start, count)
            own_term = own_term + jnp.sum(s * weight[...].astype(F32), axis=1, keepdims=True)
            ref[...] = s * gain_column
        go_ref[...] = owned(wide + 2 * narrow, wide)
        scalar[0] = jnp.broadcast_to(own_term, (held, 128))
        swap = remote(scalar.at[0], scalar.at[1], t_send, t_receive, 1, (d, c, 1 - t))
        swap.start()
        swap.wait()
        gg_ref[...] = own_term + scalar[1][:, :1]

        copy.wait_send()
        there = out_ref.at[pl.ds(pl.multiple_of((1 - t) * own, own), own)]
        remote(there, there, t_send, t_receive, 0, (d, c, 1 - t)).wait_recv()
        for k in range(1, deep):
            deeper(k).wait_send()
        for k in (1, 2, 3):
            to_block(k).wait_send()

    w_q, w_k, w_v = weights
    return call(
        kernel, "to_input", 6, (g_qkv, w_qkv, x, g_middle, back, w_q, w_k, w_v, gain),
        [
            jax.ShapeDtypeStruct((2 * own, width), F32),
            jax.ShapeDtypeStruct(w_q.shape, F32),
            jax.ShapeDtypeStruct(w_k.shape, F32),
            jax.ShapeDtypeStruct(w_v.shape, F32),
            jax.ShapeDtypeStruct(w_v.shape, F32),
            jax.ShapeDtypeStruct((held, 1), F32),
        ],
        scatter_scratch(own, width) + sems(SCATTER_COPIES) + sems(2)
        + [
            pltpu.VMEM((deep - 1, group, across), BF16),
            pltpu.VMEM((group, across), BF16),
            pltpu.VMEM((4, held, across), BF16),
            pltpu.VMEM((2, held, 128), F32),
        ]
        + sems(deep - 1) + sems(3),
        flops=2 * tokens * width * g_qkv.shape[1],
    )


def by_columns(weight, parts):
    rows, columns = weight.shape
    return weight.reshape(rows, parts, columns // parts).transpose(1, 0, 2)


def to_owner(packed):
    summed = lax.psum_scatter(packed, "dp", scatter_dimension=0, tiled=True)
    parts = lax.axis_size("ctx")
    return lax.all_to_all(
        summed.reshape(parts, -1, packed.shape[1]), "ctx", 0, 0, tiled=True
    ).transpose(1, 0, 2)


def plane_shards(
    activations,
    seg_ids,
    cotangent,
    q_weight,
    k_weight,
    v_weight,
    o_weight,
    gate_weight,
    up_weight,
    down_weight,
    attn_gain,
    mlp_gain,
):
    parts = lax.axis_size("ctx")
    heads = q_weight.shape[1] // F // parts
    wide = heads * DV
    narrow = heads * F
    units = gate_weight.shape[1] // parts
    tokens = activations.shape[1] * parts
    x, cot_block = activations[0], cotangent[0]

    gain_one = attn_gain.astype(F32)[:, None]
    gain_two = mlp_gain.astype(F32)[:, None]
    scaled = lambda w, g: (w.astype(F32) * g).astype(BF16)
    cut_attn = jnp.concatenate(
        [
            by_columns(scaled(v_weight, gain_one), parts),
            by_columns(scaled(q_weight, gain_one), parts),
            by_columns(scaled(k_weight, gain_one), parts),
            by_columns(o_weight, parts),
        ],
        axis=2,
    )
    cut_mlp = jnp.concatenate(
        [
            by_columns(scaled(gate_weight, gain_two), parts),
            by_columns(scaled(up_weight, gain_two), parts),
            by_columns(down_weight, parts),
        ],
        axis=2,
    )
    rows_one, segments, w_attn, cut_mlp = front(x, seg_ids, cut_attn, cut_mlp, tokens)
    w_attn = w_attn.reshape(-1, w_attn.shape[3])
    w_mlp = lax.all_gather(cut_mlp, "dp", axis=0, tiled=True).reshape(-1, cut_mlp.shape[2])
    w_qkv, w_out = w_attn[:, : wide + 2 * narrow], w_attn[:, wide + 2 * narrow :]
    w_gate, w_up, w_down = w_mlp[:, :units], w_mlp[:, units : 2 * units], w_mlp[:, 2 * units :]
    cot = cotangent_rows(cot_block, tokens)
    seg_rows, seg_cols = segments.reshape(tokens, 1), segments.reshape(1, tokens)

    qkv = dot(rows_one, w_qkv, 1, 0).astype(BF16)
    mixed, denom, heads_out = attention_forward(qkv, seg_rows, seg_cols, heads)
    middle, rows_two = to_middle(heads_out, w_out, x)
    hidden, g_gate, g_up, out = feed_forward(rows_two, cot, middle, w_gate, w_up, w_down)
    back_mlp = jnp.concatenate(
        [dot(rows_two, g_gate, 0, 0), dot(rows_two, g_up, 0, 0), dot(cot, hidden, 0, 0)], axis=1
    ).astype(BF16)
    g_gate, back_mlp = lax.optimization_barrier((g_gate, back_mlp))
    back_mlp = to_owner(back_mlp)
    g_middle, branch, g_mixed = to_branch(g_gate, g_up, w_gate, w_up, middle, cot_block, w_out)
    g_qkv = attention_backward(qkv, g_mixed, mixed, denom, seg_rows, seg_cols, heads)
    back_attn = jnp.concatenate(
        [dot(rows_one, g_qkv, 0, 0), dot(branch, heads_out, 0, 0)], axis=1
    ).astype(BF16)
    g_input, s_q, s_k, s_v, s_o, attn_row = to_input(
        g_qkv, w_qkv, x, g_middle, back_attn, (q_weight, k_weight, v_weight), gain_one, heads
    )

    def owned(back, start, width):
        return back[:, :, start : start + width].reshape(back.shape[0], -1).astype(F32)

    s_gate = owned(back_mlp, 0, units)
    s_up = owned(back_mlp, units, units)
    s_down = owned(back_mlp, 2 * units, units)
    along = lambda s, w: jnp.sum(s * w.astype(F32), axis=1)
    mlp_row = lax.psum(along(s_gate, gate_weight) + along(s_up, up_weight), "tp")
    return (
        out[None],
        g_input[None],
        s_q,
        s_k,
        s_v,
        s_o,
        s_gate * gain_two,
        s_up * gain_two,
        s_down,
        attn_row[:, 0],
        mlp_row,
    )


def layer(*arrays):
    heads = arrays[3].shape[1] // F
    plan = shards if heads % lax.axis_size("ctx") else plane_shards
    return plan(*arrays)


def solution(mesh):
    placed = (
        P("dp", "ctx", None),
        P("dp", "ctx"),
        P("dp", "ctx", None),
        P(("dp", "ctx"), "tp"),
        P(("dp", "ctx"), "tp"),
        P(("dp", "ctx"), "tp"),
        P(("dp", "ctx"), "tp"),
        P(("dp", "ctx"), "tp"),
        P(("dp", "ctx"), "tp"),
        P(("dp", "ctx"), "tp"),
        P(("dp", "ctx")),
        P(("dp", "ctx")),
    )
    return jax.shard_map(
        layer,
        mesh=mesh,
        in_specs=placed,
        out_specs=(
            P("dp", "ctx", None),
            P("dp", "ctx", None),
            P(("dp", "ctx"), "tp"),
            P(("dp", "ctx"), "tp"),
            P(("dp", "ctx"), "tp"),
            P(("dp", "ctx"), "tp"),
            P(("dp", "ctx"), "tp"),
            P(("dp", "ctx"), "tp"),
            P(("dp", "ctx"), "tp"),
            P(("dp", "ctx")),
            P(("dp", "ctx")),
        ),
        check_vma=False,
    )
```

```python
import jax
import jax.numpy as jnp
from jax import lax
from jax.experimental import pallas as pl
from jax.experimental.pallas import tpu as pltpu
from jax.sharding import PartitionSpec as P

F = 16
DV = 128


EPSILON = 1e-05
PRECISE = lax.Precision.HIGHEST
VMEM_MOST = 60 * 2**20


def prefix(x, axis, join, neutral, backward):
    count = lax.axis_size(axis)
    place = lax.axis_index(axis)
    ahead = count - 1 - place if backward else place
    gathered = jax.tree.map(
        lambda a, kind: lax.all_gather(a.astype(kind), axis),
        x,
        (jnp.bfloat16, jnp.bfloat16, jnp.bfloat16),
    )
    state = jax.tree.map(lambda a, e: jnp.zeros_like(a) + jnp.asarray(e, a.dtype), x, neutral)

    def one(lap, state):
        source = count - 1 - lap if backward else lap
        return join(
            state,
            jax.tree.map(
                lambda a, own: lax.dynamic_index_in_dim(a, source, 0, False).astype(own.dtype),
                gathered,
                x,
            ),
        )

    return lax.fori_loop(0, ahead, one, state)


def taylor(features_in):
    feature_count = features_in.shape[-1]
    products = (features_in[..., :, None] * features_in[..., None, :]).reshape(
        features_in.shape[:-1] + (feature_count * feature_count,)
    )
    constant = jnp.ones(features_in.shape[:-1] + (1,), jnp.float32)
    return jnp.concatenate(
        [
            constant,
            features_in * feature_count ** (-0.25),
            products * (2.0 * feature_count) ** (-0.5),
        ],
        axis=-1,
    )


def taylor_back(features_in, incoming_gradient):
    feature_count = features_in.shape[-1]
    linear = incoming_gradient[..., 1 : 1 + feature_count] * feature_count ** (-0.25)
    square = incoming_gradient[..., 1 + feature_count :].reshape(
        incoming_gradient.shape[:-1] + (feature_count, feature_count)
    )
    paired = jnp.einsum(
        "...ab,...b->...a", square + jnp.swapaxes(square, -1, -2), features_in, precision=PRECISE
    )
    return linear + paired * (2.0 * feature_count) ** (-0.5)


def norm_backward_step(incoming_gradient, unit_normalized_rows, multiplier_term, gain_vector_row):
    rescaled_rows = incoming_gradient * gain_vector_row
    return multiplier_term * (
        rescaled_rows
        - unit_normalized_rows
        * jnp.mean(rescaled_rows * unit_normalized_rows, axis=1, keepdims=True)
    )


def join_states(earlier, later_part):
    is_empty = later_part[2] < 0.0
    retain = jnp.where(is_empty | (earlier[2] == later_part[2]), 1.0, 0.0).astype(jnp.float32)
    return (
        later_part[0] + retain * earlier[0],
        later_part[1] + retain * earlier[1],
        jnp.where(is_empty, earlier[2], later_part[2]),
    )


def shards(
    activations,
    seg_ids,
    cotangent,
    q_weight,
    k_weight,
    v_weight,
    o_weight,
    gate_weight,
    up_weight,
    down_weight,
    attn_gain,
    mlp_gain,
):
    layer_input_rows = activations[0].astype(jnp.float32)
    segment = seg_ids[0].astype(jnp.float32)
    tokens = layer_input_rows.shape[0]
    head_count = q_weight.shape[1] // F
    w_query, w_key, w_value, w_out, first_norm_gain = (
        lax.all_gather(q_weight, ("dp", "ctx"), axis=0, tiled=True),
        lax.all_gather(k_weight, ("dp", "ctx"), axis=0, tiled=True),
        lax.all_gather(v_weight, ("dp", "ctx"), axis=0, tiled=True),
        lax.all_gather(o_weight, ("dp", "ctx"), axis=0, tiled=True),
        lax.all_gather(attn_gain, ("dp", "ctx"), axis=0, tiled=True),
    )
    first_inverse_scale = lax.rsqrt(
        jnp.mean(layer_input_rows * layer_input_rows, axis=1, keepdims=True) + EPSILON
    )
    first_unit_rows = layer_input_rows * first_inverse_scale
    first_normalized = (first_unit_rows * first_norm_gain.astype(jnp.float32)).astype(jnp.bfloat16)
    queries = (
        jnp.dot(first_normalized, w_query, preferred_element_type=jnp.float32)
        .astype(jnp.bfloat16)
        .reshape(tokens, head_count, F)
    )
    key_heads = (
        jnp.dot(first_normalized, w_key, preferred_element_type=jnp.float32)
        .astype(jnp.bfloat16)
        .reshape(tokens, head_count, F)
    )
    value_heads = (
        jnp.dot(first_normalized, w_value, preferred_element_type=jnp.float32)
        .astype(jnp.bfloat16)
        .reshape(tokens, head_count, DV)
    )
    w_gate, w_up, w_down, second_norm_gain = (
        lax.all_gather(gate_weight, ("dp", "ctx"), axis=0, tiled=True),
        lax.all_gather(up_weight, ("dp", "ctx"), axis=0, tiled=True),
        lax.all_gather(down_weight, ("dp", "ctx"), axis=0, tiled=True),
        lax.all_gather(mlp_gain, ("dp", "ctx"), axis=0, tiled=True),
    )
    scores = jnp.einsum(
        "thf,shf->hts", queries, key_heads, preferred_element_type=jnp.float32
    ) * F ** (-0.5)
    places = jnp.arange(tokens)
    visible = (
        (places[:, None] >= places[None, :]) & (segment[:, None] == segment[None, :])
    ).astype(jnp.float32)
    weights = (visible * (1.0 + scores + 0.5 * scores * scores)).astype(jnp.bfloat16)
    query_float = queries.astype(jnp.float32)
    key_float = key_heads.astype(jnp.float32)
    value_float = value_heads.astype(jnp.float32)
    feat_q = taylor(query_float)
    feat_k = taylor(key_float)
    ending = segment[-1]
    owned = (segment == ending).astype(jnp.float32)[:, None, None]
    local_state = jnp.einsum("thf,thd->hfd", feat_k * owned, value_float, precision=PRECISE)
    local_total = jnp.sum(feat_k * owned, axis=0)
    empty_state = (jnp.zeros_like(local_state), jnp.zeros_like(local_total), jnp.float32(-1.0))
    prior_state, prior_total, before = prefix(
        (local_state, local_total, ending), "ctx", join_states, empty_state, False
    )
    inherit = (segment == before).astype(jnp.float32)
    numerator = jnp.einsum(
        "hts,shd->thd", weights, value_heads, preferred_element_type=jnp.float32
    ) + inherit[:, None, None] * jnp.einsum("thf,hfd->thd", feat_q, prior_state, precision=PRECISE)
    denominator = jnp.sum(weights.astype(jnp.float32), axis=2).T + inherit[:, None] * jnp.einsum(
        "thf,hf->th", feat_q, prior_total, precision=PRECISE
    )
    mixed_heads = numerator / denominator[:, :, None]
    heads_out = mixed_heads.reshape(tokens, head_count * DV).astype(jnp.bfloat16)
    attn_out = lax.psum(
        jnp.einsum("tc,dc->td", heads_out, w_out, preferred_element_type=jnp.float32), "tp"
    )
    residual_midpoint = layer_input_rows + attn_out
    second_inverse_scale = lax.rsqrt(
        jnp.mean(residual_midpoint * residual_midpoint, axis=1, keepdims=True) + EPSILON
    )
    second_unit_rows = residual_midpoint * second_inverse_scale
    second_normalized = (second_unit_rows * second_norm_gain.astype(jnp.float32)).astype(
        jnp.bfloat16
    )
    gate_value = jnp.dot(second_normalized, w_gate, preferred_element_type=jnp.float32)
    up_value = jnp.dot(second_normalized, w_up, preferred_element_type=jnp.float32)
    sigmoid_gate = jax.nn.sigmoid(gate_value)
    hidden = (gate_value * sigmoid_gate * up_value).astype(jnp.bfloat16)
    mlp_out = lax.psum(
        jnp.einsum("tc,dc->td", hidden, w_down, preferred_element_type=jnp.float32).astype(
            jnp.bfloat16
        ),
        "tp",
    ).astype(jnp.float32)
    final_out = residual_midpoint + mlp_out
    grad_out = cotangent[0].astype(jnp.float32)
    grad_branch_two = cotangent[0]
    grad_w_down = jnp.einsum(
        "td,tc->dc", grad_branch_two, hidden, preferred_element_type=jnp.float32
    )
    grad_hidden = jnp.dot(grad_branch_two, w_down, preferred_element_type=jnp.float32)
    grad_gate = (
        grad_hidden * up_value * sigmoid_gate * (1.0 + gate_value * (1.0 - sigmoid_gate))
    ).astype(jnp.bfloat16)
    grad_up = (grad_hidden * gate_value * sigmoid_gate).astype(jnp.bfloat16)
    grad_w_gate = jnp.einsum(
        "td,tc->dc", second_normalized, grad_gate, preferred_element_type=jnp.float32
    )
    grad_w_up = jnp.einsum(
        "td,tc->dc", second_normalized, grad_up, preferred_element_type=jnp.float32
    )
    grad_normed_part = jnp.einsum(
        "tc,dc->td", grad_gate, w_gate, preferred_element_type=jnp.float32
    ) + jnp.einsum("tc,dc->td", grad_up, w_up, preferred_element_type=jnp.float32)
    second_normalized_gradient = lax.psum(grad_normed_part.astype(jnp.bfloat16), "tp").astype(
        jnp.float32
    )
    second_gain_gradient = jnp.sum(second_normalized_gradient * second_unit_rows, axis=0)
    grad_middle = grad_out + norm_backward_step(
        second_normalized_gradient,
        second_unit_rows,
        second_inverse_scale,
        second_norm_gain.astype(jnp.float32),
    )
    mlp_grads = (
        lax.psum_scatter(grad_w_gate, ("dp", "ctx"), scatter_dimension=0, tiled=True),
        lax.psum_scatter(grad_w_up, ("dp", "ctx"), scatter_dimension=0, tiled=True),
        lax.psum_scatter(grad_w_down, ("dp", "ctx"), scatter_dimension=0, tiled=True),
        lax.psum_scatter(second_gain_gradient, ("dp", "ctx"), scatter_dimension=0, tiled=True),
    )
    grad_branch_one = grad_middle.astype(jnp.bfloat16)
    grad_w_out = jnp.einsum(
        "td,tc->dc", grad_branch_one, heads_out, preferred_element_type=jnp.float32
    )
    grad_heads_low = jnp.dot(grad_branch_one, w_out, preferred_element_type=jnp.float32).astype(
        jnp.bfloat16
    )
    grad_mixed = (
        lax.optimization_barrier(grad_heads_low).astype(jnp.float32).reshape(tokens, head_count, DV)
    )
    numer_low = (grad_mixed / denominator[:, :, None]).astype(jnp.bfloat16)
    grad_numer = lax.optimization_barrier(numer_low).astype(jnp.float32)
    grad_denom = -jnp.sum(grad_mixed * mixed_heads, axis=2) / denominator
    grad_weights = (
        jnp.einsum("thd,shd->hts", numer_low, value_heads, preferred_element_type=jnp.float32)
        + grad_denom.T[:, :, None]
    )
    grad_scores = (grad_weights * visible * (1.0 + scores)).astype(jnp.bfloat16)
    grad_value = jnp.einsum("hts,thd->shd", weights, numer_low, preferred_element_type=jnp.float32)
    grad_query = jnp.einsum(
        "hts,shf->thf", grad_scores, key_heads, preferred_element_type=jnp.float32
    ) * F ** (-0.5)
    grad_key = jnp.einsum(
        "hts,thf->shf", grad_scores, queries, preferred_element_type=jnp.float32
    ) * F ** (-0.5)
    grad_feat_q = inherit[:, None, None] * (
        jnp.einsum("thd,hfd->thf", grad_numer, prior_state, precision=PRECISE)
        + grad_denom[:, :, None] * prior_total[None]
    )
    carried_state = jnp.einsum(
        "thf,thd->hfd", feat_q * inherit[:, None, None], grad_numer, precision=PRECISE
    )
    carried_total = jnp.sum(feat_q * (inherit[:, None] * grad_denom)[:, :, None], axis=0)
    starting = segment[0]
    later_state, later_total, after_seg = prefix(
        (carried_state, carried_total, starting), "ctx", join_states, empty_state, True
    )
    reached = (segment == after_seg).astype(jnp.float32)[:, None, None]
    grad_feat_k = reached * (
        jnp.einsum("hfd,thd->thf", later_state, value_float, precision=PRECISE) + later_total[None]
    )
    grad_value = grad_value + reached * jnp.einsum(
        "thf,hfd->thd", feat_k, later_state, precision=PRECISE
    )
    grad_query = grad_query + taylor_back(query_float, grad_feat_q)
    grad_key = grad_key + taylor_back(key_float, grad_feat_k)
    grad_query_low = grad_query.reshape(tokens, head_count * F).astype(jnp.bfloat16)
    grad_key_low = grad_key.reshape(tokens, head_count * F).astype(jnp.bfloat16)
    grad_value_low = grad_value.reshape(tokens, head_count * DV).astype(jnp.bfloat16)
    grad_w_query = jnp.einsum(
        "td,tc->dc", first_normalized, grad_query_low, preferred_element_type=jnp.float32
    )
    grad_w_key = jnp.einsum(
        "td,tc->dc", first_normalized, grad_key_low, preferred_element_type=jnp.float32
    )
    grad_w_value = jnp.einsum(
        "td,tc->dc", first_normalized, grad_value_low, preferred_element_type=jnp.float32
    )
    grad_normed_sum = (
        jnp.einsum("tc,dc->td", grad_query_low, w_query, preferred_element_type=jnp.float32)
        + jnp.einsum("tc,dc->td", grad_key_low, w_key, preferred_element_type=jnp.float32)
        + jnp.einsum("tc,dc->td", grad_value_low, w_value, preferred_element_type=jnp.float32)
    )
    first_normalized_gradient = lax.psum(grad_normed_sum.astype(jnp.bfloat16), "tp").astype(
        jnp.float32
    )
    first_gain_gradient = jnp.sum(first_normalized_gradient * first_unit_rows, axis=0)
    grad_inputs = grad_middle + norm_backward_step(
        first_normalized_gradient,
        first_unit_rows,
        first_inverse_scale,
        first_norm_gain.astype(jnp.float32),
    )
    attn_grads = (
        lax.psum_scatter(grad_w_query, ("dp", "ctx"), scatter_dimension=0, tiled=True),
        lax.psum_scatter(grad_w_key, ("dp", "ctx"), scatter_dimension=0, tiled=True),
        lax.psum_scatter(grad_w_value, ("dp", "ctx"), scatter_dimension=0, tiled=True),
        lax.psum_scatter(grad_w_out, ("dp", "ctx"), scatter_dimension=0, tiled=True),
        lax.psum_scatter(first_gain_gradient, ("dp", "ctx"), scatter_dimension=0, tiled=True),
    )
    return (
        final_out.astype(jnp.bfloat16)[None],
        grad_inputs[None],
        attn_grads[0],
        attn_grads[1],
        attn_grads[2],
        attn_grads[3],
        mlp_grads[0],
        mlp_grads[1],
        mlp_grads[2],
        attn_grads[4],
        mlp_grads[3],
    )


BLOCK = 512


MESH = pl.DeviceIdType.MESH
BF16, F32 = jnp.bfloat16, jnp.float32


def dot(a, b, ca, cb):
    return lax.dot_general(a, b, (((ca,), (cb,)), ((), ())), preferred_element_type=F32)


def place_of():
    return lax.axis_index("dp"), lax.axis_index("ctx"), lax.axis_index("tp")


def beside(c, across):
    x, y = lax.rem(c, 2), lax.div(c, 2)
    return lax.rem(x + across % 2, 2) + 2 * lax.rem(y + across // 2, 2)


def greet(devices):
    barrier = pltpu.get_barrier_semaphore()
    for device in devices:
        pl.semaphore_signal(barrier, inc=1, device_id=device, device_id_type=MESH)
    pl.semaphore_wait(barrier, len(devices))


def remote(source, target, send, receive, k, device):
    return pltpu.make_async_remote_copy(
        src_ref=source,
        dst_ref=target,
        send_sem=send.at[k],
        recv_sem=receive.at[k],
        device_id=device,
        device_id_type=MESH,
    )


def gather_rows(buf, send, receive, piece=None, early=None, middle=None, late=None):
    d, c, t = place_of()
    own = buf.shape[0] // 8
    half = own // 2
    to_x, to_y, to_t = (d, beside(c, 1), t), (d, beside(c, 2), t), (d, c, 1 - t)
    started = []

    def part(across, core, h):
        block = c if across == 0 else beside(c, across)
        start = (2 * block + core) * own + h * half
        return buf.at[pl.ds(pl.multiple_of(start, half), half)]

    def put(k, across, h, device):
        ref = part(across, t, h)
        copy = remote(ref, ref, send, receive, k, device)
        copy.start()
        started.append(copy)

    def got(k, across, core, h):
        ref = part(across, core, h)
        remote(ref, ref, send, receive, k, to_t).wait_recv()

    def work(across, core):
        if piece is not None:
            block = c if across == 0 else beside(c, across)
            piece(pl.multiple_of((2 * block + core) * own, own))

    put(0, 0, 0, to_x)
    put(1, 0, 1, to_y)
    put(2, 0, 1, to_x)
    put(3, 0, 0, to_y)
    put(6, 0, 0, to_t)
    put(7, 0, 1, to_t)
    if early is not None:
        early()
    work(0, t)
    got(6, 0, 1 - t, 0)
    got(7, 0, 1 - t, 1)
    work(0, 1 - t)
    got(0, 1, t, 0)
    put(4, 1, 0, to_y)
    put(8, 1, 0, to_t)
    got(1, 2, t, 1)
    put(5, 2, 1, to_x)
    put(9, 2, 1, to_t)
    if middle is not None:
        middle()
    got(2, 1, t, 1)
    put(10, 1, 1, to_t)
    got(3, 2, t, 0)
    put(11, 2, 0, to_t)
    if late is not None:
        late()
    work(1, t)
    work(2, t)
    got(8, 1, 1 - t, 0)
    got(10, 1, 1 - t, 1)
    work(1, 1 - t)
    got(9, 2, 1 - t, 1)
    got(11, 2, 1 - t, 0)
    work(2, 1 - t)
    got(4, 3, t, 0)
    put(12, 3, 0, to_t)
    got(5, 3, t, 1)
    put(13, 3, 1, to_t)
    work(3, t)
    got(12, 3, 1 - t, 0)
    got(13, 3, 1 - t, 1)
    work(3, 1 - t)
    for copy in started:
        copy.wait_send()


GATHER_COPIES = 14


def scatter_rows(terms, bufs, send, receive, fill=None):
    to_core, from_core, kept, over, came, stage = bufs
    d, c, t = place_of()
    own, width = kept.shape[1:]
    half = own // 2
    tile = stage.shape[1]
    to_x, to_y, to_t = (d, beside(c, 1), t), (d, beside(c, 2), t), (d, c, 1 - t)

    def link(k):
        return remote(over.at[k], came.at[k], send, receive, 4 + k, to_x if k % 2 == 0 else to_y)

    def core(i):
        return remote(to_core.at[lax.rem(i, 2)], from_core.at[i], send, receive, i, to_t)

    def total(i, h, *extra):
        rows = pl.ds(h * half, half)
        out = kept[i % 3, rows, :]
        for k in extra:
            out = out + came[k].astype(F32)
        return out

    def ready(k, i, h, *extra):
        over[k] = total(i, h, *extra).astype(BF16)

    def joined(i):
        core(i).wait_recv()
        slot = lax.rem(i, 3)
        kept[slot] = kept[slot] + from_core[i].astype(F32)

    def step(i, carry):
        across = 3 - i
        x, y = lax.rem(c, 2), lax.div(c, 2)
        block = lax.rem(x + lax.rem(across, 2), 2) + 2 * lax.rem(y + lax.div(across, 2), 2)
        pairs = terms(i, pl.multiple_of(2 * block * own, 2 * own))

        @pl.when(i >= 2)
        def _():
            core(i - 2).wait_send()

        @pl.loop(0, width // tile)
        def _(n):
            columns = pl.ds(pl.multiple_of(n * tile, tile), tile)
            out = None
            for rows, matrix, part in pairs:
                term = dot(rows, matrix[columns, part], 1, 1)
                out = term if out is None else out + term
            stage[...] = out
            to_core[lax.rem(i, 2), :, columns] = stage[
                pl.ds(pl.multiple_of((1 - t) * own, own), own), :
            ].astype(BF16)
            kept[lax.rem(i, 3), :, columns] = stage[pl.ds(pl.multiple_of(t * own, own), own), :]

        core(i).start()

        @pl.when(i == 0)
        def _():
            joined(0)
            ready(0, 0, 0)
            link(0).start()
            ready(1, 0, 1)
            link(1).start()

        @pl.when(i == 2)
        def _():
            joined(1)
            ready(3, 1, 1)
            link(3).start()

        return carry

    lax.fori_loop(0, 4, step, 0)
    joined(2)
    ready(2, 2, 0)
    link(2).start()
    if fill is not None:
        fill(0)
    link(0).wait_recv()
    link(1).wait_recv()
    ready(4, 2, 1, 1)
    ready(5, 1, 0, 0)
    link(4).start()
    link(5).start()
    joined(3)
    if fill is not None:
        fill(1)
    for k in (2, 3, 4, 5):
        link(k).wait_recv()
    core(2).wait_send()
    core(3).wait_send()
    for k in range(6):
        link(k).wait_send()
    return jnp.concatenate([total(3, 0, 2, 5), total(3, 1, 3, 4)], axis=0)


SCATTER_COPIES = 10


def scatter_scratch(own, width):
    return [
        pltpu.VMEM((2, own, width), BF16),
        pltpu.VMEM((4, own, width), BF16),
        pltpu.VMEM((3, own, width), F32),
        pltpu.VMEM((6, own // 2, width), BF16),
        pltpu.VMEM((6, own // 2, width), BF16),
        pltpu.VMEM((2 * own, width // 2), F32),
    ]


def norm_parts(rows):
    scale = lax.rsqrt(jnp.mean(rows * rows, axis=1, keepdims=True) + EPSILON)
    return scale, rows * scale


def norm_back(e, hat, scale):
    return scale * (e - hat * jnp.mean(e * hat, axis=1, keepdims=True))


def call(kernel, name, collective, arrays, out_shape, scratch, spaces=None, out_spaces=None, flops=0):
    vmem = pl.BlockSpec(memory_space=pltpu.VMEM)
    moved = sum(a.size * a.dtype.itemsize for a in arrays)
    return pl.pallas_call(
        kernel,
        in_specs=spaces or [vmem] * len(arrays),
        out_specs=out_spaces or [vmem] * len(out_shape),
        out_shape=out_shape,
        scratch_shapes=scratch,
        compiler_params=pltpu.CompilerParams(
            collective_id=collective, has_side_effects=True, vmem_limit_bytes=VMEM_MOST
        ),
        cost_estimate=pl.CostEstimate(flops=flops, bytes_accessed=moved, transcendentals=0),
        name=name,
    )(*arrays)


def sems(count):
    return [pltpu.SemaphoreType.DMA((count,)), pltpu.SemaphoreType.DMA((count,))]


def depth(d, k):
    return lax.rem(d + k, lax.axis_size("dp"))


def columns(ref, gain, start, count):
    low = start // 128 * 128
    high = -(-(start + count) // 128) * 128
    value = ref[:, low:high].astype(F32)
    if gain is not None:
        value = value * gain
    return value[:, start - low : start - low + count]


def whole_tiles(count):
    return -(-count // 128) * 128


def front(x, seg, weights, gains, tokens, heads):
    width = x.shape[1]
    own = tokens // 8
    deep = lax.axis_size("dp")
    held, units = weights[4].shape[0], weights[4].shape[1] // 4
    wide, narrow = heads * DV, heads * F
    main = units // 128 * 128
    packed = 2 * wide + 2 * narrow

    def kernel(
        x_ref, seg_ref, q_ref, k_ref, v_ref, o_ref, g_ref, u_ref, one_ref, two_ref,
        rows_ref, segs_ref, wa_out, wg_out,
        cut_a, cut_g,
        send, receive, small_send, small_receive, deep_send, deep_receive, here,
    ):
        d, c, t = place_of()
        jobs = (
            (lambda block: cut_a.at[block], lambda block: wa_out.at[d, block]),
            (lambda block: seg_ref.at[0], lambda block: segs_ref.at[block]),
            (lambda block: cut_g.at[block], lambda block: wg_out.at[block]),
        )

        def local(n):
            return pltpu.make_async_copy(jobs[n][0](c), jobs[n][1](c), here.at[n])

        def out(n, k):
            return remote(
                jobs[n][0](beside(c, k)), jobs[n][1](c), small_send, small_receive,
                3 * n + k - 1, (d, beside(c, k), t),
            )

        def arrival(n, k):
            block = beside(c, k)
            return remote(
                jobs[n][0](block), jobs[n][1](block), small_send, small_receive,
                3 * n + k - 1, (d, block, t),
            )

        def along(k):
            return remote(
                wa_out.at[d], wa_out.at[d], deep_send, deep_receive, k - 1, (depth(d, k), c, t)
            )

        def from_depth(k):
            there = wa_out.at[depth(d, deep - k)]
            return remote(there, there, deep_send, deep_receive, k - 1, (depth(d, k), c, t))

        one, two = one_ref[...], two_ref[...]
        for b in range(4):
            cut_a[b, :, :wide] = columns(v_ref, one, b * wide, wide).astype(BF16)
            cut_a[b, :, wide : 2 * wide] = o_ref[:, b * wide : (b + 1) * wide]
            cut_a[b, :, 2 * wide :] = jnp.concatenate(
                [columns(ref, one, b * narrow, narrow) for ref in (q_ref, k_ref)], axis=1
            ).astype(BF16)
        greet(
            [(d, beside(c, k), t) for k in (1, 2, 3)]
            + [(d, c, 1 - t)]
            + [(depth(d, k), c, t) for k in range(1, deep)]
        )
        local(0).start()
        for k in (3, 1, 2):
            out(0, k).start()
        mine = pl.multiple_of((2 * c + t) * own, own)
        _, hat = norm_parts(x_ref[pl.ds(pl.multiple_of(t * own, own), own), :].astype(F32))
        rows_ref[pl.ds(mine, own), :] = hat.astype(BF16)

        def early():
            for b in range(4):
                start = b * units
                cut_g[b, :, :main] = columns(g_ref, two, start, main).astype(BF16)
                cut_g[b, :, main : 2 * main] = columns(u_ref, two, start, main).astype(BF16)
                if main < units:
                    cut_g[b, :, 2 * main :] = jnp.concatenate(
                        [columns(r, two, start + main, units - main) for r in (g_ref, u_ref)],
                        axis=1,
                    ).astype(BF16)
            local(0).wait()
            for k in (1, 2, 3):
                arrival(0, k).wait_recv()
            for k in range(1, deep):
                along(k).start()
            for n in (1, 2):
                local(n).start()
                for k in (3, 1, 2):
                    out(n, k).start()

        gather_rows(rows_ref, send, receive, early=early)
        for n in (1, 2):
            local(n).wait()
            for k in (1, 2, 3):
                arrival(n, k).wait_recv()
        for k in range(1, deep):
            from_depth(k).wait_recv()
        for n in range(3):
            for k in (1, 2, 3):
                out(n, k).wait_send()
        for k in range(1, deep):
            along(k).wait_send()

    vmem, hbm = pl.BlockSpec(memory_space=pltpu.VMEM), pl.BlockSpec(memory_space=pl.ANY)
    return call(
        kernel,
        "front",
        1,
        (x, seg[None]) + tuple(weights) + tuple(gains),
        [
            jax.ShapeDtypeStruct((tokens, width), BF16),
            jax.ShapeDtypeStruct((4,) + seg.shape, seg.dtype),
            jax.ShapeDtypeStruct((deep, 4, held, packed), BF16),
            jax.ShapeDtypeStruct((4, held, 2 * units), BF16),
        ],
        [
            pltpu.VMEM((4, held, packed), BF16),
            pltpu.VMEM((4, held, 2 * units), BF16),
        ]
        + sems(GATHER_COPIES) + sems(9) + sems(deep - 1) + [pltpu.SemaphoreType.DMA((3,))],
        [vmem, hbm] + [vmem] * 8,
        [vmem, hbm, hbm, hbm],
    )


def apart(tokens):
    return (tokens // 2 - 2) // BLOCK + 2


def first_seen(i, tokens):
    return jnp.maximum(i - apart(tokens) + 1, 0)


def attend_back(qkv, g_mixed, mixed, denom, seg_rows, seg_cols, branch, heads_out, heads):
    tokens, width = branch.shape
    wide, narrow = heads * DV, heads * F
    blocks = tokens // BLOCK
    deep = lax.axis_size("dp")
    group = width // deep

    def kernel(
        x_ref, gm_ref, m_ref, d_ref, row_ref, col_ref, br_ref, h_ref, g_ref, sum_ref,
        gq_ref, numer_ref, gden_ref, key_ref, back_ref, came, br_buf, load, send, receive,
    ):
        d, c, t = place_of()

        def fetch(n):
            part = pl.ds(pl.multiple_of(depth(d, n + 1) * group, group), group)
            slot = lax.rem(n, 2)
            return pltpu.make_async_copy(br_ref.at[:, part], br_buf.at[slot], load.at[slot])

        def deeper(n):
            return remote(
                back_ref.at[n], came.at[n], send, receive, n, (depth(d, n + 1), c, t)
            )

        fetch(0).start()
        greet([(depth(d, k), c, t) for k in range(1, deep)])

        def plane(n, carry):
            @pl.when(n < deep - 1)
            def _():
                fetch(n + 1).start()

            fetch(n).wait()
            back_ref[n] = dot(br_buf[lax.rem(n, 2)], h_ref[...], 0, 0).astype(BF16)

            @pl.when(n < deep - 1)
            def _():
                deeper(n).start()

            return carry

        lax.fori_loop(0, deep, plane, 0)

        gq_ref[...] = jnp.zeros_like(gq_ref)
        for h in range(heads):
            part = pl.ds(h * DV, DV)
            gm = gm_ref[:, part].astype(F32)
            inverse = 1.0 / d_ref[:, h : h + 1]
            numer_ref[:, part] = (gm * inverse).astype(BF16)
            down = -jnp.sum(gm * m_ref[:, part], axis=1, keepdims=True) * inverse
            gden_ref[h : h + 1, :] = jnp.transpose(jnp.broadcast_to(down, (tokens, 128)), (1, 0))[:1]
        key_ref[...] = jnp.transpose(x_ref[:, wide : wide + 2 * narrow].astype(F32), (1, 0)).astype(
            BF16
        )
        place = lax.broadcasted_iota(jnp.int32, (BLOCK, BLOCK), 1) - lax.broadcasted_iota(
            jnp.int32, (BLOCK, BLOCK), 0
        )
        tempered = BF16(F**-0.5)

        @pl.loop(0, blocks)
        def _(j):
            start = pl.multiple_of(j * BLOCK, BLOCK)
            own = row_ref[pl.ds(start, BLOCK), :]
            values = [x_ref[pl.ds(start, BLOCK), h * DV : (h + 1) * DV] for h in range(heads)]
            keys = [
                x_ref[pl.ds(start, BLOCK), wide + (heads + h) * F : wide + (heads + h + 1) * F]
                * tempered
                for h in range(heads)
            ]
            across = [
                key_ref[(heads + h) * F : (heads + h + 1) * F, pl.ds(start, BLOCK)] * tempered
                for h in range(heads)
            ]

            def step(i, sums):
                base = pl.multiple_of(i * BLOCK, BLOCK)
                visible = (place >= start - base) & (own == col_ref[:, pl.ds(base, BLOCK)])
                out = []
                for h in range(heads):
                    queries = x_ref[pl.ds(base, BLOCK), wide + h * F : wide + (h + 1) * F]
                    numer = numer_ref[pl.ds(base, BLOCK), h * DV : (h + 1) * DV]
                    s = dot(keys[h], queries, 1, 1)
                    a = jnp.where(visible, (0.5 * s + 1.0) * s + 1.0, 0.0).astype(BF16)
                    ga = dot(values[h], numer, 1, 1) + gden_ref[h : h + 1, pl.ds(base, BLOCK)]
                    gs = jnp.where(visible, ga * (1.0 + s), 0.0).astype(BF16)
                    gq_ref[h * F : (h + 1) * F, pl.ds(base, BLOCK)] += dot(across[h], gs, 1, 0)
                    out += [sums[2 * h] + dot(a, numer, 1, 0), sums[2 * h + 1] + dot(gs, queries, 1, 0)]
                return tuple(out)

            zeros = []
            for h in range(heads):
                zeros += [jnp.zeros((BLOCK, DV), F32), jnp.zeros((BLOCK, F), F32)]
            sums = lax.fori_loop(
                j, jnp.minimum(j + apart(tokens), blocks), step, tuple(zeros)
            )
            for h in range(heads):
                g_ref[pl.ds(start, BLOCK), h * DV : (h + 1) * DV] = sums[2 * h].astype(BF16)
                g_ref[
                    pl.ds(start, BLOCK), wide + (heads + h) * F : wide + (heads + h + 1) * F
                ] = (sums[2 * h + 1] * F**-0.5).astype(BF16)

        g_ref[:, wide : wide + narrow] = jnp.transpose(gq_ref[...], (1, 0)).astype(BF16)
        total = back_ref[deep - 1].astype(F32)
        for n in range(deep - 1):
            deeper(n).wait_recv()
            total = total + came[n].astype(F32)
        sum_ref[...] = total.astype(BF16)
        for n in range(deep - 1):
            deeper(n).wait_send()

    vmem, hbm = pl.BlockSpec(memory_space=pltpu.VMEM), pl.BlockSpec(memory_space=pl.ANY)
    return call(
        kernel, "attend_back", 7,
        (qkv, g_mixed, mixed, denom, seg_rows, seg_cols, branch, heads_out),
        [jax.ShapeDtypeStruct(qkv.shape, BF16), jax.ShapeDtypeStruct((group, wide), BF16)],
        [
            pltpu.VMEM((narrow, tokens), F32),
            pltpu.VMEM((tokens, wide), BF16),
            pltpu.VMEM((8, tokens), F32),
            pltpu.VMEM((2 * narrow, tokens), BF16),
            pltpu.VMEM((deep, group, wide), BF16),
            pltpu.VMEM((deep - 1, group, wide), BF16),
            pltpu.VMEM((2, tokens, group), BF16),
            pltpu.SemaphoreType.DMA((2,)),
        ]
        + sems(deep - 1),
        [vmem] * 6 + [hbm, vmem],
    )


def attend_block(i, x_ref, ext_ref, row_ref, col_ref, mixed_ref, denom_ref, low_ref, heads):
    wide = heads * DV
    base = pl.multiple_of(i * BLOCK, BLOCK)
    own = row_ref[pl.ds(base, BLOCK), :]
    place = lax.broadcasted_iota(jnp.int32, (BLOCK, BLOCK), 0) - lax.broadcasted_iota(
        jnp.int32, (BLOCK, BLOCK), 1
    )
    queries = [
        x_ref[pl.ds(base, BLOCK), wide + h * F : wide + (h + 1) * F] * jnp.bfloat16(F**-0.5)
        for h in range(heads)
    ]

    def step(j, sums):
        start = pl.multiple_of(j * BLOCK, BLOCK)
        visible = (place >= start - base) & (own == col_ref[:, pl.ds(start, BLOCK)])
        out = []
        for h in range(heads):
            keys = x_ref[
                pl.ds(start, BLOCK), wide + (heads + h) * F : wide + (heads + h + 1) * F
            ]
            s = dot(queries[h], keys, 1, 1)
            a = jnp.where(visible, (0.5 * s + 1.0) * s + 1.0, 0.0).astype(BF16)
            out.append(
                sums[h] + dot(a, ext_ref[pl.ds(start, BLOCK), 2 * h * DV : (2 * h + 2) * DV], 1, 0)
            )
        return tuple(out)

    sums = lax.fori_loop(
        first_seen(i, x_ref.shape[0]),
        i + 1,
        step,
        tuple(jnp.zeros((BLOCK, 2 * DV), F32) for _ in range(heads)),
    )
    for h in range(heads):
        denom = sums[h][:, DV:]
        mixed = sums[h][:, :DV] / denom
        mixed_ref[pl.ds(base, BLOCK), h * DV : (h + 1) * DV] = mixed
        low_ref[pl.ds(base, BLOCK), h * DV : (h + 1) * DV] = mixed.astype(BF16)
        denom_ref[pl.ds(base, BLOCK), h : h + 1] = denom[:, :1]


def attend(rows_one, w_attn, seg_rows, seg_cols, cot, w_down, heads):
    tokens, width = rows_one.shape
    own = tokens // 8
    wide, narrow = heads * DV, heads * F
    held, units = w_down.shape[0], w_down.shape[1] // 4
    filled = whole_tiles(units)

    def kernel(
        x_ref, w_ref, row_ref, col_ref, cot_ref, d_ref,
        qkv_ref, mixed_ref, denom_ref, low_ref, rows_ref, wd_out,
        ext_ref, cut, send, receive, d_send, d_receive, here,
    ):
        d, c, t = place_of()

        def out(k):
            return remote(
                cut.at[beside(c, k)], wd_out.at[c], d_send, d_receive, k - 1, (d, beside(c, k), t)
            )

        def arrival(k):
            there = wd_out.at[beside(c, k)]
            return remote(there, there, d_send, d_receive, k - 1, (d, beside(c, k), t))

        local = pltpu.make_async_copy(cut.at[c], wd_out.at[c], here.at[0])
        for b in range(4):
            part = columns(d_ref, None, b * units, units)
            if units < filled:
                part = jnp.concatenate([part, jnp.zeros((held, filled - units), F32)], axis=1)
            cut[b] = part.astype(BF16)
        greet([(d, beside(c, k), t) for k in (1, 2, 3)] + [(d, c, 1 - t)])
        mine = pl.multiple_of((2 * c + t) * own, own)
        rows_ref[pl.ds(mine, own), :] = cot_ref[
            pl.ds(pl.multiple_of(t * own, own), own), : width // 2
        ]

        def blocks(first, last):
            @pl.loop(first, last)
            def _(i):
                attend_block(
                    i, qkv_ref, ext_ref, row_ref, col_ref, mixed_ref, denom_ref, low_ref, heads
                )

        def early():
            local.start()
            for k in (3, 1, 2):
                out(k).start()

            @pl.loop(0, tokens // BLOCK)
            def _(n):
                rows = pl.ds(pl.multiple_of(n * BLOCK, BLOCK), BLOCK)
                values = dot(x_ref[rows, :], w_ref[:, :wide], 1, 0).astype(BF16)
                qkv_ref[rows, :wide] = values
                qkv_ref[rows, wide:] = dot(x_ref[rows, :], w_ref[:, 2 * wide :], 1, 0).astype(BF16)
                for h in range(heads):
                    ext_ref[rows, 2 * h * DV : (2 * h + 1) * DV] = values[:, h * DV : (h + 1) * DV]
                    ext_ref[rows, (2 * h + 1) * DV : (2 * h + 2) * DV] = jnp.ones((BLOCK, DV), BF16)

        gather_rows(
            rows_ref, send, receive, early=early,
            middle=lambda: blocks(0, tokens // BLOCK // 2),
            late=lambda: blocks(tokens // BLOCK // 2, tokens // BLOCK),
        )
        local.wait()
        for k in (1, 2, 3):
            arrival(k).wait_recv()
            out(k).wait_send()

    vmem, hbm = pl.BlockSpec(memory_space=pltpu.VMEM), pl.BlockSpec(memory_space=pl.ANY)
    return call(
        kernel, "attend", 2, (rows_one, w_attn, seg_rows, seg_cols, cot, w_down),
        [
            jax.ShapeDtypeStruct((tokens, wide + 2 * narrow), BF16),
            jax.ShapeDtypeStruct((tokens, wide), F32),
            jax.ShapeDtypeStruct((tokens, heads), F32),
            jax.ShapeDtypeStruct((tokens, wide), BF16),
            jax.ShapeDtypeStruct((tokens, width // 2), BF16),
            jax.ShapeDtypeStruct((4, held, filled), BF16),
        ],
        [pltpu.VMEM((tokens, 2 * wide), BF16), pltpu.VMEM((4, held, filled), BF16)]
        + sems(GATHER_COPIES) + sems(3) + [pltpu.SemaphoreType.DMA((1,))],
        None,
        [vmem] * 5 + [hbm],
    )


def to_middle(heads_out, w_attn, x):
    tokens, width = heads_out.shape[0], x.shape[1]
    own = tokens // 8
    wide = heads_out.shape[1]

    def kernel(h_ref, w_ref, x_ref, mid_ref, rows_ref, *rest):
        bufs, (s_send, s_receive, g_send, g_receive) = rest[:6], rest[6:]
        d, c, t = place_of()
        greet([(d, beside(c, 1), t), (d, beside(c, 2), t), (d, c, 1 - t)])

        def terms(i, start):
            return [(h_ref[pl.ds(start, 2 * own), :], w_ref, slice(wide, 2 * wide))]

        total = scatter_rows(terms, bufs, s_send, s_receive)
        middle = total + x_ref[pl.ds(pl.multiple_of(t * own, own), own), :].astype(F32)
        mid_ref[...] = middle
        _, hat = norm_parts(middle)
        rows_ref[pl.ds(pl.multiple_of((2 * c + t) * own, own), own), :] = hat.astype(BF16)
        gather_rows(rows_ref, g_send, g_receive)

    return call(
        kernel, "to_middle", 3, (heads_out, w_attn, x),
        [jax.ShapeDtypeStruct((own, width), F32), jax.ShapeDtypeStruct((tokens, width), BF16)],
        scatter_scratch(own, width) + sems(SCATTER_COPIES) + sems(GATHER_COPIES),
        flops=2 * tokens * width * heads_out.shape[1],
    )


def gate_up(rows_two, w_both, cot):
    tokens, width = rows_two.shape
    own = tokens // 8
    units = w_both.shape[1] // 2
    main = units // 128 * 128
    count = tokens // BLOCK

    def kernel(
        x_ref, w_ref, cot_ref, hid_out, slope_out, silu_out, rows_ref,
        x_buf, w_buf, hid_ref, slope_ref, silu_ref, load, store, send, receive,
    ):
        d, c, t = place_of()

        def fetch(i):
            rows = pl.ds(pl.multiple_of(i * BLOCK, BLOCK), BLOCK)
            slot = lax.rem(i, 2)
            return pltpu.make_async_copy(x_ref.at[rows], x_buf.at[slot], load.at[slot])

        def given(i):
            rows = pl.ds(pl.multiple_of(i * BLOCK, BLOCK), BLOCK)
            slot = lax.rem(i, 2)
            return [
                pltpu.make_async_copy(source.at[slot], target.at[rows], store.at[n, slot])
                for n, (source, target) in enumerate(
                    ((hid_ref, hid_out), (slope_ref, slope_out), (silu_ref, silu_out))
                )
            ]

        weights = pltpu.make_async_copy(w_ref, w_buf, load.at[2])
        weights.start()
        fetch(0).start()
        greet([(d, beside(c, 1), t), (d, beside(c, 2), t), (d, c, 1 - t)])
        mine = pl.multiple_of((2 * c + t) * own, own)
        rows_ref[pl.ds(mine, own), :] = cot_ref[
            pl.ds(pl.multiple_of(t * own, own), own), width // 2 :
        ]

        def blocks(first, last):
            @pl.loop(first, last)
            def _(i):
                slot = lax.rem(i, 2)

                @pl.when(i + 1 < count)
                def _():
                    fetch(i + 1).start()

                fetch(i).wait()
                both = dot(x_buf[slot], w_buf[...], 1, 0)

                @pl.when(i >= 2)
                def _():
                    for copy in given(i - 2):
                        copy.wait()

                def act(gate, up, part):
                    sig = jax.nn.sigmoid(gate)
                    silu = gate * sig
                    hid_ref[slot, :, part] = (silu * up).astype(BF16)
                    slope_ref[slot, :, part] = (up * sig * (1.0 + gate * (1.0 - sig))).astype(BF16)
                    silu_ref[slot, :, part] = silu.astype(BF16)

                act(both[:, :main], both[:, main : 2 * main], slice(0, main))
                if main < units:
                    act(
                        both[:, 2 * main : main + units],
                        both[:, main + units :],
                        slice(main, units),
                    )
                for copy in given(i):
                    copy.start()

        def early():
            weights.wait()
            blocks(0, 1)

        gather_rows(
            rows_ref, send, receive, early=early,
            middle=lambda: blocks(1, count // 2), late=lambda: blocks(count // 2, count),
        )
        for i in (count - 2, count - 1):
            for copy in given(i):
                copy.wait()

    vmem, hbm = pl.BlockSpec(memory_space=pltpu.VMEM), pl.BlockSpec(memory_space=pl.ANY)
    return call(
        kernel, "gate_up", 8, (rows_two, w_both, cot),
        [jax.ShapeDtypeStruct((tokens, units), BF16)] * 3
        + [jax.ShapeDtypeStruct((tokens, width // 2), BF16)],
        [
            pltpu.VMEM((2, BLOCK, width), BF16),
            pltpu.VMEM(w_both.shape, BF16),
            pltpu.VMEM((2, BLOCK, units), BF16),
            pltpu.VMEM((2, BLOCK, units), BF16),
            pltpu.VMEM((2, BLOCK, units), BF16),
            pltpu.SemaphoreType.DMA((3,)),
            pltpu.SemaphoreType.DMA((3, 2)),
        ]
        + sems(GATHER_COPIES),
        [hbm, hbm, vmem],
        [hbm, hbm, hbm, vmem],
        flops=4 * tokens * width * units,
    )


def feed_forward(hidden, slope, silu, cot_low, cot_high, middle, w_down, rows_two):
    tokens, width = rows_two.shape
    own = tokens // 8
    units = hidden.shape[1]
    main = units // 128 * 128
    tile = 256
    part_width = width // 2

    def kernel(
        hid_ref, slope_ref, silu_ref, low_ref, high_ref, mid_ref, d_ref, two_ref,
        g_out, out_ref, grad_ref,
        hid_buf, slope_buf, silu_buf, low_buf, high_buf, d_buf, g_ref, here, g_store,
        cols, out, load, store, *rest,
    ):
        bufs, (s_send, s_receive, t_send, t_receive) = rest[:6], rest[6:]
        d, c, t = place_of()

        def block_rows(i):
            across = 3 - i
            x, y = lax.rem(c, 2), lax.div(c, 2)
            block = lax.rem(x + lax.rem(across, 2), 2) + 2 * lax.rem(y + lax.div(across, 2), 2)
            return pl.ds(pl.multiple_of(2 * block * own, 2 * own), 2 * own)

        def fetch(i):
            part = block_rows(i)
            return [
                pltpu.make_async_copy(source.at[part], target, here.at[n])
                for n, (source, target) in enumerate(
                    (
                        (low_ref, low_buf),
                        (high_ref, high_buf),
                        (slope_ref, slope_buf),
                        (silu_ref, silu_buf),
                    )
                )
            ]

        def fetch_hidden(i):
            return pltpu.make_async_copy(hid_ref.at[block_rows(i)], hid_buf, here.at[4])

        def g_given(i):
            part = block_rows(i)
            return pltpu.make_async_copy(g_ref.at[part], g_out.at[part], g_store.at[i])

        weights = pltpu.make_async_copy(d_ref, d_buf, here.at[5])
        weights.start()
        for copy in fetch(0):
            copy.start()

        def wanted(n):
            part = pl.ds(pl.multiple_of(n * tile, tile), tile)
            slot = lax.rem(n, 2)
            return pltpu.make_async_copy(two_ref.at[:, part], cols.at[slot], load.at[slot])

        def given(n):
            part = pl.ds(pl.multiple_of(n * tile, tile), tile)
            slot = lax.rem(n, 2)
            return pltpu.make_async_copy(out.at[slot], grad_ref.at[part], store.at[slot])

        last = width // tile

        def tiles(first, end):
            @pl.loop(first, end)
            def _(n):
                wanted(n).wait()

                @pl.when(n + 1 < last)
                def _():
                    wanted(n + 1).start()

                @pl.when(n >= 2)
                def _():
                    given(n - 2).wait()

                slot = lax.rem(n, 2)
                out[slot] = dot(cols[slot], g_ref[...], 0, 0).astype(BF16)
                given(n).start()

        wanted(0).start()
        greet([(d, beside(c, 1), t), (d, beside(c, 2), t), (d, c, 1 - t)])
        weights.wait()

        def terms(i, start):
            part = pl.ds(start, 2 * own)
            fetch_hidden(i).start()
            for copy in fetch(i):
                copy.wait()
            g_hidden = dot(low_buf[...], d_buf[:part_width, :units], 1, 0) + dot(
                high_buf[...], d_buf[part_width:, :units], 1, 0
            )
            gg = g_hidden * slope_buf[...].astype(F32)
            gu = g_hidden * silu_buf[...].astype(F32)
            g_ref[part, :main] = gg[:, :main].astype(BF16)
            g_ref[part, main : 2 * main] = gu[:, :main].astype(BF16)
            if main < units:
                g_ref[part, 2 * main :] = jnp.concatenate(
                    [gg[:, main:], gu[:, main:]], axis=1
                ).astype(BF16)
            g_given(i).start()

            @pl.when(i < 3)
            def _():
                for copy in fetch(i + 1):
                    copy.start()

            fetch_hidden(i).wait()
            return [(hid_buf[...], d_buf, slice(0, units))]

        def fill(n):
            if n == 0:
                tiles(0, 2)
            else:
                tiles(2, last)

        total = scatter_rows(terms, bufs, s_send, s_receive, fill)
        place = out_ref.at[pl.ds(pl.multiple_of(t * own, own), own)]
        place[...] = (mid_ref[...] + total).astype(BF16)
        copy = remote(place, place, t_send, t_receive, 0, (d, c, 1 - t))
        copy.start()
        copy.wait_send()
        there = out_ref.at[pl.ds(pl.multiple_of((1 - t) * own, own), own)]
        remote(there, there, t_send, t_receive, 0, (d, c, 1 - t)).wait_recv()
        given(last - 2).wait()
        given(last - 1).wait()
        for i in range(4):
            g_given(i).wait()

    vmem, hbm = pl.BlockSpec(memory_space=pltpu.VMEM), pl.BlockSpec(memory_space=pl.ANY)
    return call(
        kernel, "feed_forward", 4,
        (hidden, slope, silu, cot_low, cot_high, middle, w_down, rows_two),
        [
            jax.ShapeDtypeStruct((tokens, 2 * units), BF16),
            jax.ShapeDtypeStruct((2 * own, width), BF16),
            jax.ShapeDtypeStruct((width, 2 * units), BF16),
        ],
        [
            pltpu.VMEM((2 * own, units), BF16),
            pltpu.VMEM((2 * own, units), BF16),
            pltpu.VMEM((2 * own, units), BF16),
            pltpu.VMEM((2 * own, part_width), BF16),
            pltpu.VMEM((2 * own, part_width), BF16),
            pltpu.VMEM(w_down.shape, BF16),
            pltpu.VMEM((tokens, 2 * units), BF16),
            pltpu.SemaphoreType.DMA((6,)),
            pltpu.SemaphoreType.DMA((4,)),
            pltpu.VMEM((2, tokens, tile), BF16),
            pltpu.VMEM((2, tile, 2 * units), BF16),
            pltpu.SemaphoreType.DMA((2,)),
            pltpu.SemaphoreType.DMA((2,)),
        ]
        + scatter_scratch(own, width) + sems(SCATTER_COPIES) + sems(1),
        [hbm] * 5 + [vmem, hbm, hbm],
        [hbm, vmem, hbm],
        flops=8 * tokens * width * units,
    )


def to_branch(g_both, w_both, middle, cot, w_attn, wide):
    tokens, width = g_both.shape[0], middle.shape[1]
    own = tokens // 8

    def kernel(
        g_ref, w_ref, mid_ref, cot_ref, o_ref, gm_ref, rows_ref, mix_ref, g_buf, w_buf, load, *rest
    ):
        bufs, (s_send, s_receive, g_send, g_receive) = rest[:6], rest[6:]
        d, c, t = place_of()

        def fetch(i):
            across = 3 - i
            x, y = lax.rem(c, 2), lax.div(c, 2)
            block = lax.rem(x + lax.rem(across, 2), 2) + 2 * lax.rem(y + lax.div(across, 2), 2)
            part = pl.ds(pl.multiple_of(2 * block * own, 2 * own), 2 * own)
            slot = lax.rem(i, 2)
            return pltpu.make_async_copy(g_ref.at[part], g_buf.at[slot], load.at[slot])

        weights = pltpu.make_async_copy(w_ref, w_buf, load.at[2])
        weights.start()
        fetch(0).start()
        greet([(d, beside(c, 1), t), (d, beside(c, 2), t), (d, c, 1 - t)])
        weights.wait()

        def terms(i, start):
            fetch(i).wait()

            @pl.when(i < 3)
            def _():
                fetch(i + 1).start()

            return [(g_buf[lax.rem(i, 2)], w_buf, slice(None))]

        total = scatter_rows(terms, bufs, s_send, s_receive)
        scale, hat = norm_parts(mid_ref[...])
        g_middle = cot_ref[pl.ds(pl.multiple_of(t * own, own), own), :].astype(F32) + norm_back(
            total, hat, scale
        )
        gm_ref[...] = g_middle
        rows_ref[pl.ds(pl.multiple_of((2 * c + t) * own, own), own), :] = g_middle.astype(BF16)

        def mix(start):
            mix_ref[pl.ds(start, own), :] = dot(
                rows_ref[pl.ds(start, own), :], o_ref[:, wide : 2 * wide], 1, 0
            ).astype(BF16)

        gather_rows(rows_ref, g_send, g_receive, mix)

    return call(
        kernel, "to_branch", 5, (g_both, w_both, middle, cot, w_attn),
        [
            jax.ShapeDtypeStruct((own, width), F32),
            jax.ShapeDtypeStruct((tokens, width), BF16),
            jax.ShapeDtypeStruct((tokens, wide), BF16),
        ],
        [
            pltpu.VMEM((2, 2 * own, g_both.shape[1]), BF16),
            pltpu.VMEM(w_both.shape, BF16),
            pltpu.SemaphoreType.DMA((3,)),
        ]
        + scatter_scratch(own, width) + sems(SCATTER_COPIES) + sems(GATHER_COPIES),
        [pl.BlockSpec(memory_space=pl.ANY)] * 2 + [pl.BlockSpec(memory_space=pltpu.VMEM)] * 3,
        flops=4 * tokens * width * (g_both.shape[1] // 2 + wide),
    )


def as_row(column):
    return jnp.transpose(jnp.broadcast_to(column, (column.shape[0], 128)), (1, 0))[:8]


def to_input(
    g_qkv, w_attn, x, g_middle, rows_one, sum_out, sum_both, sum_down, weights, gains, heads
):
    tokens, width = g_qkv.shape[0], x.shape[1]
    own = tokens // 8
    deep = lax.axis_size("dp")
    across = g_qkv.shape[1]
    group = width // deep
    held = group // 4
    wide, narrow = heads * DV, heads * F
    both, units = sum_both.shape[1], sum_down.shape[1]
    main = units // 128 * 128

    def kernel(
        g_ref, w_ref, x_ref, gm_ref, one_ref, so_ref, both_ref, down_ref,
        wq_ref, wk_ref, wv_ref, wg_ref, wu_ref, gain_ref, gain_two_ref,
        out_ref, gq_ref, gk_ref, gv_ref, go_ref, gg_ref, gu_ref, gd_ref, row_ref, row_two_ref,
        *rest,
    ):
        bufs, (s_send, s_receive, t_send, t_receive) = rest[:6], rest[6:10]
        (
            came_deep, sums, parts_a, parts_b, parts_d, parts_o, scalar, back_ref, one_buf, load,
            d_send, d_receive, p_send, p_receive,
        ) = rest[10:]
        d, c, t = place_of()

        def fetch(n):
            part = pl.ds(pl.multiple_of(depth(d, n + 1) * group, group), group)
            slot = lax.rem(n, 2)
            return pltpu.make_async_copy(one_ref.at[:, part], one_buf.at[slot], load.at[slot])

        fetch(0).start()
        greet(
            [(d, beside(c, k), t) for k in (1, 2, 3)]
            + [(d, c, 1 - t)]
            + [(depth(d, k), c, t) for k in range(1, deep)]
        )

        def deeper(k):
            rows = pl.ds(pl.multiple_of(depth(d, k) * group, group), group)
            return remote(
                back_ref.at[rows], came_deep.at[k - 1], d_send, d_receive, k - 1,
                (depth(d, k), c, t),
            )

        jobs = ((sums, parts_a), (both_ref, parts_b), (down_ref, parts_d), (so_ref, parts_o))

        def rows_of(block):
            return pl.ds(pl.multiple_of(block * held, held), held)

        def to_block(n, k):
            source, target = jobs[n]
            return remote(
                source.at[rows_of(beside(c, k))], target.at[c], p_send, p_receive, 3 * n + k - 1,
                (d, beside(c, k), t),
            )

        def from_block(n, k):
            there = jobs[n][1].at[beside(c, k)]
            return remote(there, there, p_send, p_receive, 3 * n + k - 1, (d, beside(c, k), t))

        def at_home(n):
            source, target = jobs[n]
            return pltpu.make_async_copy(source.at[rows_of(c)], target.at[c], load.at[n + 1])

        def plane(n, carry):
            rows = pl.ds(pl.multiple_of(depth(d, n + 1) * group, group), group)

            @pl.when(n < deep - 1)
            def _():
                fetch(n + 1).start()

            fetch(n).wait()
            back_ref[rows, :] = dot(one_buf[lax.rem(n, 2)], g_ref[...], 0, 0).astype(BF16)

            @pl.when(n < deep - 1)
            def _():
                remote(
                    back_ref.at[rows], came_deep.at[n], d_send, d_receive, n,
                    (depth(d, n + 1), c, t),
                ).start()

            return carry

        lax.fori_loop(0, deep, plane, 0)

        def terms(i, start):
            part = pl.ds(start, 2 * own)
            return [
                (g_ref[part, :wide], w_ref, slice(0, wide)),
                (g_ref[part, wide:], w_ref, slice(2 * wide, None)),
            ]

        def fill(n):
            if n == 0:
                for job in (1, 2, 3):
                    for k in (3, 1, 2):
                        to_block(job, k).start()
                    at_home(job).start()

        e_one = scatter_rows(terms, bufs, s_send, s_receive, fill)
        scale, hat = norm_parts(x_ref[pl.ds(pl.multiple_of(t * own, own), own), :].astype(F32))
        place = out_ref.at[pl.ds(pl.multiple_of(t * own, own), own)]
        place[...] = gm_ref[...] + norm_back(e_one, hat, scale)
        copy = remote(place, place, t_send, t_receive, 0, (d, c, 1 - t))
        copy.start()

        for n in (1, 2, 3):
            at_home(n).wait()
            for k in (1, 2, 3):
                from_block(n, k).wait_recv()
        gain_two = gain_two_ref[...]
        for b in range(4):
            whole = parts_b[b].astype(F32)
            for ref, first, rest_of in (
                (gg_ref, 0, 2 * main),
                (gu_ref, main, main + units),
            ):
                s = whole[:, first : first + main]
                if main < units:
                    s = jnp.concatenate([s, whole[:, rest_of : rest_of + units - main]], axis=1)
                ref[:, b * units : (b + 1) * units] = s * gain_two
            gd_ref[:, b * units : (b + 1) * units] = parts_d[b].astype(F32)
            go_ref[:, b * wide : (b + 1) * wide] = parts_o[b].astype(F32)
        term_two = (
            jnp.sum(gg_ref[...] * wg_ref[...].astype(F32), axis=1, keepdims=True)
            + jnp.sum(gu_ref[...] * wu_ref[...].astype(F32), axis=1, keepdims=True)
        ) / gain_two

        for k in range(1, deep):
            deeper(k).wait_recv()
        mine = pl.ds(pl.multiple_of(d * group, group), group)
        total = back_ref[mine, :].astype(F32)
        for k in range(1, deep):
            total = total + came_deep[k - 1].astype(F32)
        sums[...] = total.astype(BF16)
        for k in (3, 1, 2):
            to_block(0, k).start()
        parts_a[c] = sums[rows_of(c), :]
        for k in (1, 2, 3):
            from_block(0, k).wait_recv()
        gain_one = gain_ref[...]

        def owned(start, count):
            return jnp.concatenate(
                [parts_a[b][:, start : start + count].astype(F32) for b in range(4)], axis=1
            )

        term_one = jnp.zeros((held, 1), F32)
        for ref, weight, start, count in (
            (gv_ref, wv_ref, 0, wide),
            (gq_ref, wq_ref, wide, narrow),
            (gk_ref, wk_ref, wide + narrow, narrow),
        ):
            s = owned(start, count)
            term_one = term_one + jnp.sum(s * weight[...].astype(F32), axis=1, keepdims=True)
            ref[...] = s * gain_one
        scalar[0, 0] = as_row(term_one)
        scalar[0, 1] = as_row(term_two)
        swap = remote(scalar.at[0], scalar.at[1], t_send, t_receive, 1, (d, c, 1 - t))
        swap.start()
        swap.wait()
        row_ref[...] = (scalar[0, 0] + scalar[1, 0])[:1]
        row_two_ref[...] = (scalar[0, 1] + scalar[1, 1])[:1]

        copy.wait_send()
        there = out_ref.at[pl.ds(pl.multiple_of((1 - t) * own, own), own)]
        remote(there, there, t_send, t_receive, 0, (d, c, 1 - t)).wait_recv()
        for k in range(1, deep):
            deeper(k).wait_send()
        for n in range(4):
            for k in (1, 2, 3):
                to_block(n, k).wait_send()

    w_q, w_k, w_v, w_gate, w_up = weights
    vmem, hbm = pl.BlockSpec(memory_space=pltpu.VMEM), pl.BlockSpec(memory_space=pl.ANY)
    return call(
        kernel, "to_input", 6,
        (g_qkv, w_attn, x, g_middle, rows_one, sum_out, sum_both, sum_down)
        + tuple(weights) + tuple(gains),
        [jax.ShapeDtypeStruct((2 * own, width), F32)]
        + [jax.ShapeDtypeStruct(w.shape, F32) for w in (w_q, w_k, w_v, w_v, w_gate, w_up, w_up)]
        + [jax.ShapeDtypeStruct((1, held), F32)] * 2,
        scatter_scratch(own, width) + sems(SCATTER_COPIES) + sems(2)
        + [
            pltpu.VMEM((deep - 1, group, across), BF16),
            pltpu.VMEM((group, across), BF16),
            pltpu.VMEM((4, held, across), BF16),
            pltpu.VMEM((4, held, both), BF16),
            pltpu.VMEM((4, held, units), BF16),
            pltpu.VMEM((4, held, wide), BF16),
            pltpu.VMEM((2, 2, 8, held), F32),
            pltpu.VMEM((width, across), BF16),
            pltpu.VMEM((2, tokens, group), BF16),
            pltpu.SemaphoreType.DMA((5,)),
        ]
        + sems(deep - 1) + sems(12),
        [vmem] * 4 + [hbm] * 4 + [vmem] * 7,
        flops=2 * tokens * width * g_qkv.shape[1],
    )


def plane_shards(
    activations,
    seg_ids,
    cotangent,
    q_weight,
    k_weight,
    v_weight,
    o_weight,
    gate_weight,
    up_weight,
    down_weight,
    attn_gain,
    mlp_gain,
):
    parts = lax.axis_size("ctx")
    heads = q_weight.shape[1] // F // parts
    tokens = activations.shape[1] * parts
    x, cot_block = activations[0], cotangent[0]
    gain_one = attn_gain.astype(F32)[:, None]
    gain_two = mlp_gain.astype(F32)[:, None]
    rows_one, segments, w_attn, cut_both = front(
        x,
        seg_ids,
        (q_weight, k_weight, v_weight, o_weight, gate_weight, up_weight),
        (gain_one, gain_two),
        tokens,
        heads,
    )
    w_attn = w_attn.reshape(-1, w_attn.shape[3])
    w_both = lax.all_gather(cut_both, "dp", axis=0, tiled=True).reshape(-1, cut_both.shape[2])
    seg_rows, seg_cols = segments.reshape(tokens, 1), segments.reshape(1, tokens)
    qkv, mixed, denom, heads_out, cot_low, cut_down = attend(
        rows_one, w_attn, seg_rows, seg_cols, cot_block, down_weight, heads
    )
    w_down = lax.all_gather(cut_down, "dp", axis=0, tiled=True).reshape(-1, cut_down.shape[2])
    middle, rows_two = to_middle(heads_out, w_attn, x)
    hidden, slope, silu, cot_high = gate_up(rows_two, w_both, cot_block)
    back_down = jnp.concatenate([dot(cot_low, hidden, 0, 0), dot(cot_high, hidden, 0, 0)]).astype(
        BF16
    )
    w_down, back_down = lax.optimization_barrier((w_down, back_down))
    sum_down = lax.psum_scatter(back_down, "dp", scatter_dimension=0, tiled=True)
    g_both, out, back_both = feed_forward(
        hidden, slope, silu, cot_low, cot_high, middle, w_down, rows_two
    )
    sum_both = lax.psum_scatter(back_both, "dp", scatter_dimension=0, tiled=True)
    g_middle, branch, g_mixed = to_branch(g_both, w_both, middle, cot_block, w_attn, heads * DV)
    g_qkv, sum_out = attend_back(
        qkv, g_mixed, mixed, denom, seg_rows, seg_cols, branch, heads_out, heads
    )
    g_input, s_q, s_k, s_v, s_o, s_gate, s_up, s_down, attn_row, mlp_row = to_input(
        g_qkv,
        w_attn,
        x,
        g_middle,
        rows_one,
        sum_out,
        sum_both,
        sum_down,
        (q_weight, k_weight, v_weight, gate_weight, up_weight),
        (gain_one, gain_two),
        heads,
    )
    return (
        out[None],
        g_input[None],
        s_q,
        s_k,
        s_v,
        s_o,
        s_gate,
        s_up,
        s_down,
        attn_row[0],
        mlp_row[0],
    )


def layer(*arrays):
    heads = arrays[3].shape[1] // F
    plan = shards if heads % lax.axis_size("ctx") else plane_shards
    return plan(*arrays)


def solution(mesh):
    placed = (
        P("dp", "ctx", None),
        P("dp", "ctx"),
        P("dp", "ctx", None),
        P(("dp", "ctx"), "tp"),
        P(("dp", "ctx"), "tp"),
        P(("dp", "ctx"), "tp"),
        P(("dp", "ctx"), "tp"),
        P(("dp", "ctx"), "tp"),
        P(("dp", "ctx"), "tp"),
        P(("dp", "ctx"), "tp"),
        P(("dp", "ctx")),
        P(("dp", "ctx")),
    )
    return jax.shard_map(
        layer,
        mesh=mesh,
        in_specs=placed,
        out_specs=(
            P("dp", "ctx", None),
            P("dp", "ctx", None),
            P(("dp", "ctx"), "tp"),
            P(("dp", "ctx"), "tp"),
            P(("dp", "ctx"), "tp"),
            P(("dp", "ctx"), "tp"),
            P(("dp", "ctx"), "tp"),
            P(("dp", "ctx"), "tp"),
            P(("dp", "ctx"), "tp"),
            P(("dp", "ctx")),
            P(("dp", "ctx")),
        ),
        check_vma=False,
    )
```

```python
import jax
import jax.numpy as jnp
from jax import lax
from jax.experimental import pallas as pl
from jax.experimental.pallas import tpu as pltpu
from jax.sharding import PartitionSpec as P

F = 16
DV = 128


EPSILON = 1e-05
PRECISE = lax.Precision.HIGHEST
VMEM_MOST = 60 * 2**20


def prefix(x, axis, join, neutral, backward):
    count = lax.axis_size(axis)
    place = lax.axis_index(axis)
    ahead = count - 1 - place if backward else place
    gathered = jax.tree.map(
        lambda a, kind: lax.all_gather(a.astype(kind), axis),
        x,
        (jnp.bfloat16, jnp.bfloat16, jnp.bfloat16),
    )
    state = jax.tree.map(lambda a, e: jnp.zeros_like(a) + jnp.asarray(e, a.dtype), x, neutral)

    def one(lap, state):
        source = count - 1 - lap if backward else lap
        return join(
            state,
            jax.tree.map(
                lambda a, own: lax.dynamic_index_in_dim(a, source, 0, False).astype(own.dtype),
                gathered,
                x,
            ),
        )

    return lax.fori_loop(0, ahead, one, state)


def taylor(features_in):
    feature_count = features_in.shape[-1]
    products = (features_in[..., :, None] * features_in[..., None, :]).reshape(
        features_in.shape[:-1] + (feature_count * feature_count,)
    )
    constant = jnp.ones(features_in.shape[:-1] + (1,), jnp.float32)
    return jnp.concatenate(
        [
            constant,
            features_in * feature_count ** (-0.25),
            products * (2.0 * feature_count) ** (-0.5),
        ],
        axis=-1,
    )


def taylor_back(features_in, incoming_gradient):
    feature_count = features_in.shape[-1]
    linear = incoming_gradient[..., 1 : 1 + feature_count] * feature_count ** (-0.25)
    square = incoming_gradient[..., 1 + feature_count :].reshape(
        incoming_gradient.shape[:-1] + (feature_count, feature_count)
    )
    paired = jnp.einsum(
        "...ab,...b->...a", square + jnp.swapaxes(square, -1, -2), features_in, precision=PRECISE
    )
    return linear + paired * (2.0 * feature_count) ** (-0.5)


def norm_backward_step(incoming_gradient, unit_normalized_rows, multiplier_term, gain_vector_row):
    rescaled_rows = incoming_gradient * gain_vector_row
    return multiplier_term * (
        rescaled_rows
        - unit_normalized_rows
        * jnp.mean(rescaled_rows * unit_normalized_rows, axis=1, keepdims=True)
    )


def join_states(earlier, later_part):
    is_empty = later_part[2] < 0.0
    retain = jnp.where(is_empty | (earlier[2] == later_part[2]), 1.0, 0.0).astype(jnp.float32)
    return (
        later_part[0] + retain * earlier[0],
        later_part[1] + retain * earlier[1],
        jnp.where(is_empty, earlier[2], later_part[2]),
    )


def shards(
    activations,
    seg_ids,
    cotangent,
    q_weight,
    k_weight,
    v_weight,
    o_weight,
    gate_weight,
    up_weight,
    down_weight,
    attn_gain,
    mlp_gain,
):
    layer_input_rows = activations[0].astype(jnp.float32)
    segment = seg_ids[0].astype(jnp.float32)
    tokens = layer_input_rows.shape[0]
    head_count = q_weight.shape[1] // F
    w_query, w_key, w_value, w_out, first_norm_gain = (
        lax.all_gather(q_weight, ("dp", "ctx"), axis=0, tiled=True),
        lax.all_gather(k_weight, ("dp", "ctx"), axis=0, tiled=True),
        lax.all_gather(v_weight, ("dp", "ctx"), axis=0, tiled=True),
        lax.all_gather(o_weight, ("dp", "ctx"), axis=0, tiled=True),
        lax.all_gather(attn_gain, ("dp", "ctx"), axis=0, tiled=True),
    )
    first_inverse_scale = lax.rsqrt(
        jnp.mean(layer_input_rows * layer_input_rows, axis=1, keepdims=True) + EPSILON
    )
    first_unit_rows = layer_input_rows * first_inverse_scale
    first_normalized = (first_unit_rows * first_norm_gain.astype(jnp.float32)).astype(jnp.bfloat16)
    queries = (
        jnp.dot(first_normalized, w_query, preferred_element_type=jnp.float32)
        .astype(jnp.bfloat16)
        .reshape(tokens, head_count, F)
    )
    key_heads = (
        jnp.dot(first_normalized, w_key, preferred_element_type=jnp.float32)
        .astype(jnp.bfloat16)
        .reshape(tokens, head_count, F)
    )
    value_heads = (
        jnp.dot(first_normalized, w_value, preferred_element_type=jnp.float32)
        .astype(jnp.bfloat16)
        .reshape(tokens, head_count, DV)
    )
    w_gate, w_up, w_down, second_norm_gain = (
        lax.all_gather(gate_weight, ("dp", "ctx"), axis=0, tiled=True),
        lax.all_gather(up_weight, ("dp", "ctx"), axis=0, tiled=True),
        lax.all_gather(down_weight, ("dp", "ctx"), axis=0, tiled=True),
        lax.all_gather(mlp_gain, ("dp", "ctx"), axis=0, tiled=True),
    )
    scores = jnp.einsum(
        "thf,shf->hts", queries, key_heads, preferred_element_type=jnp.float32
    ) * F ** (-0.5)
    places = jnp.arange(tokens)
    visible = (
        (places[:, None] >= places[None, :]) & (segment[:, None] == segment[None, :])
    ).astype(jnp.float32)
    weights = (visible * (1.0 + scores + 0.5 * scores * scores)).astype(jnp.bfloat16)
    query_float = queries.astype(jnp.float32)
    key_float = key_heads.astype(jnp.float32)
    value_float = value_heads.astype(jnp.float32)
    feat_q = taylor(query_float)
    feat_k = taylor(key_float)
    ending = segment[-1]
    owned = (segment == ending).astype(jnp.float32)[:, None, None]
    local_state = jnp.einsum("thf,thd->hfd", feat_k * owned, value_float, precision=PRECISE)
    local_total = jnp.sum(feat_k * owned, axis=0)
    empty_state = (jnp.zeros_like(local_state), jnp.zeros_like(local_total), jnp.float32(-1.0))
    prior_state, prior_total, before = prefix(
        (local_state, local_total, ending), "ctx", join_states, empty_state, False
    )
    inherit = (segment == before).astype(jnp.float32)
    numerator = jnp.einsum(
        "hts,shd->thd", weights, value_heads, preferred_element_type=jnp.float32
    ) + inherit[:, None, None] * jnp.einsum("thf,hfd->thd", feat_q, prior_state, precision=PRECISE)
    denominator = jnp.sum(weights.astype(jnp.float32), axis=2).T + inherit[:, None] * jnp.einsum(
        "thf,hf->th", feat_q, prior_total, precision=PRECISE
    )
    mixed_heads = numerator / denominator[:, :, None]
    heads_out = mixed_heads.reshape(tokens, head_count * DV).astype(jnp.bfloat16)
    attn_out = lax.psum(
        jnp.einsum("tc,dc->td", heads_out, w_out, preferred_element_type=jnp.float32), "tp"
    )
    residual_midpoint = layer_input_rows + attn_out
    second_inverse_scale = lax.rsqrt(
        jnp.mean(residual_midpoint * residual_midpoint, axis=1, keepdims=True) + EPSILON
    )
    second_unit_rows = residual_midpoint * second_inverse_scale
    second_normalized = (second_unit_rows * second_norm_gain.astype(jnp.float32)).astype(
        jnp.bfloat16
    )
    gate_value = jnp.dot(second_normalized, w_gate, preferred_element_type=jnp.float32)
    up_value = jnp.dot(second_normalized, w_up, preferred_element_type=jnp.float32)
    sigmoid_gate = jax.nn.sigmoid(gate_value)
    hidden = (gate_value * sigmoid_gate * up_value).astype(jnp.bfloat16)
    mlp_out = lax.psum(
        jnp.einsum("tc,dc->td", hidden, w_down, preferred_element_type=jnp.float32).astype(
            jnp.bfloat16
        ),
        "tp",
    ).astype(jnp.float32)
    final_out = residual_midpoint + mlp_out
    grad_out = cotangent[0].astype(jnp.float32)
    grad_branch_two = cotangent[0]
    grad_w_down = jnp.einsum(
        "td,tc->dc", grad_branch_two, hidden, preferred_element_type=jnp.float32
    )
    grad_hidden = jnp.dot(grad_branch_two, w_down, preferred_element_type=jnp.float32)
    grad_gate = (
        grad_hidden * up_value * sigmoid_gate * (1.0 + gate_value * (1.0 - sigmoid_gate))
    ).astype(jnp.bfloat16)
    grad_up = (grad_hidden * gate_value * sigmoid_gate).astype(jnp.bfloat16)
    grad_w_gate = jnp.einsum(
        "td,tc->dc", second_normalized, grad_gate, preferred_element_type=jnp.float32
    )
    grad_w_up = jnp.einsum(
        "td,tc->dc", second_normalized, grad_up, preferred_element_type=jnp.float32
    )
    grad_normed_part = jnp.einsum(
        "tc,dc->td", grad_gate, w_gate, preferred_element_type=jnp.float32
    ) + jnp.einsum("tc,dc->td", grad_up, w_up, preferred_element_type=jnp.float32)
    second_normalized_gradient = lax.psum(grad_normed_part.astype(jnp.bfloat16), "tp").astype(
        jnp.float32
    )
    second_gain_gradient = jnp.sum(second_normalized_gradient * second_unit_rows, axis=0)
    grad_middle = grad_out + norm_backward_step(
        second_normalized_gradient,
        second_unit_rows,
        second_inverse_scale,
        second_norm_gain.astype(jnp.float32),
    )
    mlp_grads = (
        lax.psum_scatter(grad_w_gate, ("dp", "ctx"), scatter_dimension=0, tiled=True),
        lax.psum_scatter(grad_w_up, ("dp", "ctx"), scatter_dimension=0, tiled=True),
        lax.psum_scatter(grad_w_down, ("dp", "ctx"), scatter_dimension=0, tiled=True),
        lax.psum_scatter(second_gain_gradient, ("dp", "ctx"), scatter_dimension=0, tiled=True),
    )
    grad_branch_one = grad_middle.astype(jnp.bfloat16)
    grad_w_out = jnp.einsum(
        "td,tc->dc", grad_branch_one, heads_out, preferred_element_type=jnp.float32
    )
    grad_heads_low = jnp.dot(grad_branch_one, w_out, preferred_element_type=jnp.float32).astype(
        jnp.bfloat16
    )
    grad_mixed = (
        lax.optimization_barrier(grad_heads_low).astype(jnp.float32).reshape(tokens, head_count, DV)
    )
    numer_low = (grad_mixed / denominator[:, :, None]).astype(jnp.bfloat16)
    grad_numer = lax.optimization_barrier(numer_low).astype(jnp.float32)
    grad_denom = -jnp.sum(grad_mixed * mixed_heads, axis=2) / denominator
    grad_weights = (
        jnp.einsum("thd,shd->hts", numer_low, value_heads, preferred_element_type=jnp.float32)
        + grad_denom.T[:, :, None]
    )
    grad_scores = (grad_weights * visible * (1.0 + scores)).astype(jnp.bfloat16)
    grad_value = jnp.einsum("hts,thd->shd", weights, numer_low, preferred_element_type=jnp.float32)
    grad_query = jnp.einsum(
        "hts,shf->thf", grad_scores, key_heads, preferred_element_type=jnp.float32
    ) * F ** (-0.5)
    grad_key = jnp.einsum(
        "hts,thf->shf", grad_scores, queries, preferred_element_type=jnp.float32
    ) * F ** (-0.5)
    grad_feat_q = inherit[:, None, None] * (
        jnp.einsum("thd,hfd->thf", grad_numer, prior_state, precision=PRECISE)
        + grad_denom[:, :, None] * prior_total[None]
    )
    carried_state = jnp.einsum(
        "thf,thd->hfd", feat_q * inherit[:, None, None], grad_numer, precision=PRECISE
    )
    carried_total = jnp.sum(feat_q * (inherit[:, None] * grad_denom)[:, :, None], axis=0)
    starting = segment[0]
    later_state, later_total, after_seg = prefix(
        (carried_state, carried_total, starting), "ctx", join_states, empty_state, True
    )
    reached = (segment == after_seg).astype(jnp.float32)[:, None, None]
    grad_feat_k = reached * (
        jnp.einsum("hfd,thd->thf", later_state, value_float, precision=PRECISE) + later_total[None]
    )
    grad_value = grad_value + reached * jnp.einsum(
        "thf,hfd->thd", feat_k, later_state, precision=PRECISE
    )
    grad_query = grad_query + taylor_back(query_float, grad_feat_q)
    grad_key = grad_key + taylor_back(key_float, grad_feat_k)
    grad_query_low = grad_query.reshape(tokens, head_count * F).astype(jnp.bfloat16)
    grad_key_low = grad_key.reshape(tokens, head_count * F).astype(jnp.bfloat16)
    grad_value_low = grad_value.reshape(tokens, head_count * DV).astype(jnp.bfloat16)
    grad_w_query = jnp.einsum(
        "td,tc->dc", first_normalized, grad_query_low, preferred_element_type=jnp.float32
    )
    grad_w_key = jnp.einsum(
        "td,tc->dc", first_normalized, grad_key_low, preferred_element_type=jnp.float32
    )
    grad_w_value = jnp.einsum(
        "td,tc->dc", first_normalized, grad_value_low, preferred_element_type=jnp.float32
    )
    grad_normed_sum = (
        jnp.einsum("tc,dc->td", grad_query_low, w_query, preferred_element_type=jnp.float32)
        + jnp.einsum("tc,dc->td", grad_key_low, w_key, preferred_element_type=jnp.float32)
        + jnp.einsum("tc,dc->td", grad_value_low, w_value, preferred_element_type=jnp.float32)
    )
    first_normalized_gradient = lax.psum(grad_normed_sum.astype(jnp.bfloat16), "tp").astype(
        jnp.float32
    )
    first_gain_gradient = jnp.sum(first_normalized_gradient * first_unit_rows, axis=0)
    grad_inputs = grad_middle + norm_backward_step(
        first_normalized_gradient,
        first_unit_rows,
        first_inverse_scale,
        first_norm_gain.astype(jnp.float32),
    )
    attn_grads = (
        lax.psum_scatter(grad_w_query, ("dp", "ctx"), scatter_dimension=0, tiled=True),
        lax.psum_scatter(grad_w_key, ("dp", "ctx"), scatter_dimension=0, tiled=True),
        lax.psum_scatter(grad_w_value, ("dp", "ctx"), scatter_dimension=0, tiled=True),
        lax.psum_scatter(grad_w_out, ("dp", "ctx"), scatter_dimension=0, tiled=True),
        lax.psum_scatter(first_gain_gradient, ("dp", "ctx"), scatter_dimension=0, tiled=True),
    )
    return (
        final_out.astype(jnp.bfloat16)[None],
        grad_inputs[None],
        attn_grads[0],
        attn_grads[1],
        attn_grads[2],
        attn_grads[3],
        mlp_grads[0],
        mlp_grads[1],
        mlp_grads[2],
        attn_grads[4],
        mlp_grads[3],
    )


BLOCK = 512


MESH = pl.DeviceIdType.MESH
BF16, F32 = jnp.bfloat16, jnp.float32


def dot(a, b, ca, cb):
    return lax.dot_general(a, b, (((ca,), (cb,)), ((), ())), preferred_element_type=F32)


def place_of():
    return lax.axis_index("dp"), lax.axis_index("ctx"), lax.axis_index("tp")


def beside(c, across):
    x, y = lax.rem(c, 2), lax.div(c, 2)
    return lax.rem(x + across % 2, 2) + 2 * lax.rem(y + across // 2, 2)


def say(devices):
    barrier = pltpu.get_barrier_semaphore()
    for device in devices:
        pl.semaphore_signal(barrier, inc=1, device_id=device, device_id_type=MESH)


def hear(count):
    pl.semaphore_wait(pltpu.get_barrier_semaphore(), count)


def greet(devices):
    say(devices)
    hear(len(devices))


def around():
    d, c, t = place_of()
    return [(d, beside(c, 1), t), (d, beside(c, 2), t), (d, c, 1 - t)]


def remote(source, target, send, receive, k, device):
    return pltpu.make_async_remote_copy(
        src_ref=source,
        dst_ref=target,
        send_sem=send.at[k],
        recv_sem=receive.at[k],
        device_id=device,
        device_id_type=MESH,
    )


def gather_rows(
    buf, out, send, receive, store, piece=None, early=None, middle=None, late=None
):
    d, c, t = place_of()
    own = buf.shape[0] // 8
    half = own // 2
    to_x, to_y, to_t = (d, beside(c, 1), t), (d, beside(c, 2), t), (d, c, 1 - t)
    started = []

    def part(across, core, h):
        block = c if across == 0 else beside(c, across)
        start = (2 * block + core) * own + h * half
        return buf.at[pl.ds(pl.multiple_of(start, half), half)]

    def put(k, across, h, device):
        ref = part(across, t, h)
        copy = remote(ref, ref, send, receive, k, device)
        copy.start()
        started.append(copy)

    def got(k, across, core, h):
        ref = part(across, core, h)
        remote(ref, ref, send, receive, k, to_t).wait_recv()

    stored = []

    def work(across, core):
        block = c if across == 0 else beside(c, across)
        start = pl.multiple_of((2 * block + core) * own, own)
        rows = pl.ds(start, own)
        copy = pltpu.make_async_copy(buf.at[rows], out.at[rows], store.at[len(stored)])
        copy.start()
        stored.append(copy)
        if piece is not None:
            piece(start)

    put(0, 0, 0, to_x)
    put(1, 0, 1, to_y)
    put(2, 0, 1, to_x)
    put(3, 0, 0, to_y)
    put(6, 0, 0, to_t)
    put(7, 0, 1, to_t)
    if early is not None:
        early()
    work(0, t)
    got(6, 0, 1 - t, 0)
    got(7, 0, 1 - t, 1)
    work(0, 1 - t)
    got(0, 1, t, 0)
    put(4, 1, 0, to_y)
    put(8, 1, 0, to_t)
    got(1, 2, t, 1)
    put(5, 2, 1, to_x)
    put(9, 2, 1, to_t)
    if middle is not None:
        middle()
    got(2, 1, t, 1)
    put(10, 1, 1, to_t)
    got(3, 2, t, 0)
    put(11, 2, 0, to_t)
    if late is not None:
        late()
    work(1, t)
    work(2, t)
    got(8, 1, 1 - t, 0)
    got(10, 1, 1 - t, 1)
    work(1, 1 - t)
    got(9, 2, 1 - t, 1)
    got(11, 2, 1 - t, 0)
    work(2, 1 - t)
    got(4, 3, t, 0)
    put(12, 3, 0, to_t)
    got(5, 3, t, 1)
    put(13, 3, 1, to_t)
    work(3, t)
    got(12, 3, 1 - t, 0)
    got(13, 3, 1 - t, 1)
    work(3, 1 - t)
    for copy in started:
        copy.wait_send()
    for copy in stored:
        copy.wait()


GATHER_COPIES = 14


def gather_scratch(tokens, width):
    return (
        [pltpu.VMEM((tokens, width), BF16)]
        + sems(GATHER_COPIES)
        + [pltpu.SemaphoreType.DMA((8,))]
    )


def exchange(jobs, held, send, receive, local):
    d, c, t = place_of()

    def rows_of(block):
        return pl.ds(pl.multiple_of(block * held, held), held)

    def to_block(n, k):
        source, target = jobs[n]
        return remote(
            source.at[rows_of(beside(c, k))], target.at[c], send, receive, 3 * n + k - 1,
            (d, beside(c, k), t),
        )

    def from_block(n, k):
        there = jobs[n][1].at[beside(c, k)]
        return remote(there, there, send, receive, 3 * n + k - 1, (d, beside(c, k), t))

    def at_home(n):
        source, target = jobs[n]
        return pltpu.make_async_copy(source.at[rows_of(c)], target.at[c], local.at[n])

    def hand_on(n):
        for k in (3, 1, 2):
            to_block(n, k).start()
        at_home(n).start()

    def landed(n):
        at_home(n).wait()
        for k in (1, 2, 3):
            from_block(n, k).wait_recv()
            to_block(n, k).wait_send()

    return hand_on, landed


def scatter_order(i):
    c = lax.axis_index("ctx")
    across = 3 - i
    x, y = lax.rem(c, 2), lax.div(c, 2)
    return lax.rem(x + lax.rem(across, 2), 2) + 2 * lax.rem(y + lax.div(across, 2), 2)


def scatter_rows(terms, bufs, send, receive, enter, fill=None):
    to_core, from_core, kept, over, came, stage = bufs
    d, c, t = place_of()
    own, tile = kept.shape[2:]
    half = own // 2
    to_x, to_y, to_t = (d, beside(c, 1), t), (d, beside(c, 2), t), (d, c, 1 - t)

    def link(k, n):
        return remote(
            over.at[k, n], came.at[k, n], send, receive, 8 + 2 * k + n, to_x if k % 2 == 0 else to_y
        )

    def core(i, n):
        return remote(to_core.at[lax.rem(i, 2), n], from_core.at[i, n], send, receive, 2 * i + n, to_t)

    def total(i, h, n, *extra):
        out = kept[i % 3, n, pl.ds(h * half, half), :]
        for k in extra:
            out = out + came[k, n].astype(F32)
        return out

    def go(k, i, h, n, *extra):
        over[k, n] = total(i, h, n, *extra).astype(BF16)
        link(k, n).start()

    def joined(i, n):
        core(i, n).wait_recv()
        kept[lax.rem(i, 3), n] = kept[lax.rem(i, 3), n] + from_core[i, n].astype(F32)

    def product(pairs, i, n):
        columns = pl.ds(n * tile, tile)
        theirs = pl.ds(pl.multiple_of((1 - t) * own, own), own)
        mine = pl.ds(pl.multiple_of(t * own, own), own)
        if not isinstance(pairs, list):
            to_core[lax.rem(i, 2), n] = pairs[theirs, columns]
            kept[lax.rem(i, 3), n] = pairs[mine, columns].astype(F32)
            return
        out = None
        for rows, matrix, part in pairs:
            term = dot(rows, matrix[columns, part], 1, 1)
            out = term if out is None else out + term
        stage[...] = out
        to_core[lax.rem(i, 2), n] = stage[theirs, :].astype(BF16)
        kept[lax.rem(i, 3), n] = stage[mine, :]

    def begin(i):
        return pl.multiple_of(2 * scatter_order(i) * own, 2 * own)

    pairs = terms(0, begin(0))
    product(pairs, 0, 0)
    enter()
    core(0, 0).start()
    product(pairs, 0, 1)
    core(0, 1).start()
    for n in (0, 1):
        joined(0, n)
        go(0, 0, 0, n)
        go(1, 0, 1, n)

    def step(i, carry):
        pairs = terms(i, begin(i))

        @pl.when(i >= 2)
        def _():
            for n in (0, 1):
                core(i - 2, n).wait_send()

        for n in (0, 1):
            product(pairs, i, n)
            core(i, n).start()

        @pl.when(i == 2)
        def _():
            for n in (0, 1):
                joined(1, n)
                go(3, 1, 1, n)

        return carry

    lax.fori_loop(1, 4, step, 0)
    for n in (0, 1):
        joined(2, n)
        go(2, 2, 0, n)
    if fill is not None:
        fill(0)
    for n in (0, 1):
        link(0, n).wait_recv()
        link(1, n).wait_recv()
        go(4, 2, 1, n, 1)
        go(5, 1, 0, n, 0)
    for n in (0, 1):
        joined(3, n)
    if fill is not None:
        fill(1)
    for n in (0, 1):
        for k in (2, 3, 4, 5):
            link(k, n).wait_recv()
        core(2, n).wait_send()
        core(3, n).wait_send()
        for k in range(6):
            link(k, n).wait_send()
    return jnp.concatenate(
        [
            jnp.concatenate([total(3, 0, n, 2, 5), total(3, 1, n, 3, 4)], axis=0)
            for n in (0, 1)
        ],
        axis=1,
    )


SCATTER_COPIES = 20


def scatter_scratch(own, width):
    tile = width // 2
    return [
        pltpu.VMEM((2, 2, own, tile), BF16),
        pltpu.VMEM((4, 2, own, tile), BF16),
        pltpu.VMEM((3, 2, own, tile), F32),
        pltpu.VMEM((6, 2, own // 2, tile), BF16),
        pltpu.VMEM((6, 2, own // 2, tile), BF16),
        pltpu.VMEM((2 * own, tile), F32),
    ]


def norm_parts(rows):
    scale = lax.rsqrt(jnp.mean(rows * rows, axis=1, keepdims=True) + EPSILON)
    return scale, rows * scale


def norm_back(e, hat, scale):
    return scale * (e - hat * jnp.mean(e * hat, axis=1, keepdims=True))


def call(kernel, name, collective, arrays, out_shape, scratch, spaces=None, out_spaces=None, flops=0):
    vmem = pl.BlockSpec(memory_space=pltpu.VMEM)
    moved = sum(a.size * a.dtype.itemsize for a in arrays)
    return pl.pallas_call(
        kernel,
        in_specs=spaces or [vmem] * len(arrays),
        out_specs=out_spaces or [vmem] * len(out_shape),
        out_shape=out_shape,
        scratch_shapes=scratch,
        compiler_params=pltpu.CompilerParams(
            collective_id=collective, has_side_effects=True, vmem_limit_bytes=VMEM_MOST
        ),
        cost_estimate=pl.CostEstimate(flops=flops, bytes_accessed=moved, transcendentals=0),
        name=name,
    )(*arrays)


def sems(count):
    return [pltpu.SemaphoreType.DMA((count,)), pltpu.SemaphoreType.DMA((count,))]


def depth(d, k):
    return lax.rem(d + k, lax.axis_size("dp"))


def columns(ref, gain, start, count):
    low = start // 128 * 128
    high = -(-(start + count) // 128) * 128
    value = ref[:, low:high].astype(F32)
    if gain is not None:
        value = value * gain
    return value[:, start - low : start - low + count]


def whole_tiles(count):
    return -(-count // 128) * 128


def front(x, seg, weights, gains, tokens, heads):
    width = x.shape[1]
    own = tokens // 8
    deep = lax.axis_size("dp")
    held, units = weights[4].shape[0], weights[4].shape[1] // 4
    wide, narrow = heads * DV, heads * F
    main = units // 128 * 128
    packed = 2 * wide + 2 * narrow

    def kernel(
        x_ref, seg_ref, q_ref, k_ref, v_ref, o_ref, g_ref, u_ref, one_ref, two_ref,
        rows_out, segs_ref, wa_out, wg_out,
        cut_a, cut_g, rows_ref, send, receive, store, small_send, small_receive, deep_send, deep_receive, here,
    ):
        d, c, t = place_of()
        jobs = (
            (lambda block: cut_a.at[block], lambda block: wa_out.at[d, block]),
            (lambda block: seg_ref.at[0], lambda block: segs_ref.at[block]),
            (lambda block: cut_g.at[block], lambda block: wg_out.at[block]),
        )

        def local(n):
            return pltpu.make_async_copy(jobs[n][0](c), jobs[n][1](c), here.at[n])

        def out(n, k):
            return remote(
                jobs[n][0](beside(c, k)), jobs[n][1](c), small_send, small_receive,
                3 * n + k - 1, (d, beside(c, k), t),
            )

        def arrival(n, k):
            block = beside(c, k)
            return remote(
                jobs[n][0](block), jobs[n][1](block), small_send, small_receive,
                3 * n + k - 1, (d, block, t),
            )

        def along(k):
            return remote(
                wa_out.at[d], wa_out.at[d], deep_send, deep_receive, k - 1, (depth(d, k), c, t)
            )

        def from_depth(k):
            there = wa_out.at[depth(d, deep - k)]
            return remote(there, there, deep_send, deep_receive, k - 1, (depth(d, k), c, t))

        one, two = one_ref[...], two_ref[...]
        met = (
            [(d, beside(c, k), t) for k in (1, 2, 3)]
            + [(d, c, 1 - t)]
            + [(depth(d, k), c, t) for k in range(1, deep)]
        )
        say(met)
        for b in range(4):
            cut_a[b, :, :wide] = columns(v_ref, one, b * wide, wide).astype(BF16)
            cut_a[b, :, wide : 2 * wide] = o_ref[:, b * wide : (b + 1) * wide]
            cut_a[b, :, 2 * wide :] = jnp.concatenate(
                [columns(ref, one, b * narrow, narrow) for ref in (q_ref, k_ref)], axis=1
            ).astype(BF16)
        hear(len(met))
        local(0).start()
        for k in (3, 1, 2):
            out(0, k).start()
        mine = pl.multiple_of((2 * c + t) * own, own)
        _, hat = norm_parts(x_ref[pl.ds(pl.multiple_of(t * own, own), own), :].astype(F32))
        rows_ref[pl.ds(mine, own), :] = hat.astype(BF16)

        def early():
            for b in range(4):
                start = b * units
                cut_g[b, :, :main] = columns(g_ref, two, start, main).astype(BF16)
                cut_g[b, :, main : 2 * main] = columns(u_ref, two, start, main).astype(BF16)
                if main < units:
                    cut_g[b, :, 2 * main :] = jnp.concatenate(
                        [columns(r, two, start + main, units - main) for r in (g_ref, u_ref)],
                        axis=1,
                    ).astype(BF16)
            local(0).wait()
            for k in (1, 2, 3):
                arrival(0, k).wait_recv()
            for k in range(1, deep):
                along(k).start()
            for n in (1, 2):
                local(n).start()
                for k in (3, 1, 2):
                    out(n, k).start()

        gather_rows(rows_ref, rows_out, send, receive, store, early=early)
        for n in (1, 2):
            local(n).wait()
            for k in (1, 2, 3):
                arrival(n, k).wait_recv()
        for k in range(1, deep):
            from_depth(k).wait_recv()
        for n in range(3):
            for k in (1, 2, 3):
                out(n, k).wait_send()
        for k in range(1, deep):
            along(k).wait_send()

    vmem, hbm = pl.BlockSpec(memory_space=pltpu.VMEM), pl.BlockSpec(memory_space=pl.ANY)
    return call(
        kernel,
        "front",
        1,
        (x, seg[None]) + tuple(weights) + tuple(gains),
        [
            jax.ShapeDtypeStruct((tokens, width), BF16),
            jax.ShapeDtypeStruct((4,) + seg.shape, seg.dtype),
            jax.ShapeDtypeStruct((deep, 4, held, packed), BF16),
            jax.ShapeDtypeStruct((4, held, 2 * units), BF16),
        ],
        [
            pltpu.VMEM((4, held, packed), BF16),
            pltpu.VMEM((4, held, 2 * units), BF16),
        ]
        + gather_scratch(tokens, width) + sems(9) + sems(deep - 1) + [pltpu.SemaphoreType.DMA((3,))],
        [vmem, hbm] + [vmem] * 8,
        [hbm, hbm, hbm, hbm],
    )


def apart(tokens):
    return (tokens // 2 - 2) // BLOCK + 2


def first_seen(i, tokens):
    return jnp.maximum(i - apart(tokens) + 1, 0)


def attend_back(
    qkv, g_mixed, mixed, denom, seg_rows, seg_cols, branch, heads_out, out_terms, middle, sum_down, heads
):
    tokens, width = branch.shape
    wide, narrow = heads * DV, heads * F
    blocks = tokens // BLOCK
    deep = lax.axis_size("dp")
    group = width // deep
    own = tokens // 8
    held, units = sum_down.shape[0] // 4, sum_down.shape[1]

    def kernel(
        x_ref, gm_ref, m_ref, d_ref, row_ref, col_ref, br_ref, h_ref, term_ref, mid_ref, down_ref,
        g_ref, out_ref, go_ref, gd_ref,
        gq_ref, numer_ref, gden_ref, key_ref, back_ref, came, br_buf, load, send, receive,
        term_buf, term_load, sums, parts_o, parts_d, p_send, p_receive, local, *rest,
    ):
        bufs, (s_send, s_receive, t_send, t_receive) = rest[:6], rest[6:]
        d, c, t = place_of()
        hand_on, landed = exchange(
            ((sums, parts_o), (down_ref, parts_d)), held, p_send, p_receive, local
        )

        def fetch_terms(i):
            part = pl.ds(pl.multiple_of(2 * scatter_order(i) * own, 2 * own), 2 * own)
            slot = lax.rem(i, 2)
            return pltpu.make_async_copy(term_ref.at[part], term_buf.at[slot], term_load.at[slot])

        fetch_terms(0).start()

        def fetch(n):
            part = pl.ds(pl.multiple_of(depth(d, n + 1) * group, group), group)
            slot = lax.rem(n, 2)
            return pltpu.make_async_copy(br_ref.at[:, part], br_buf.at[slot], load.at[slot])

        def deeper(n):
            return remote(
                back_ref.at[n], came.at[n], send, receive, n, (depth(d, n + 1), c, t)
            )

        fetch(0).start()
        met = (
            around()
            + [(d, beside(c, 3), t)]
            + [(depth(d, k), c, t) for k in range(1, deep)]
        )
        say(met)

        def plane(n, carry):
            @pl.when(n < deep - 1)
            def _():
                fetch(n + 1).start()

            fetch(n).wait()
            back_ref[n] = dot(br_buf[lax.rem(n, 2)], h_ref[...], 0, 0).astype(BF16)

            @pl.when(n < deep - 1)
            def _():
                deeper(n).start()

            return carry

        def prepare():
            gq_ref[...] = jnp.zeros_like(gq_ref)
            for h in range(heads):
                part = pl.ds(h * DV, DV)
                gm = gm_ref[:, part].astype(F32)
                inverse = 1.0 / d_ref[:, h : h + 1]
                numer_ref[:, part] = (gm * inverse).astype(BF16)
                down = -jnp.sum(gm * m_ref[:, part], axis=1, keepdims=True) * inverse
                gden_ref[h : h + 1, :] = jnp.transpose(
                    jnp.broadcast_to(down, (tokens, 128)), (1, 0)
                )[:1]
            key_ref[...] = jnp.transpose(
                x_ref[:, wide : wide + 2 * narrow].astype(F32), (1, 0)
            ).astype(BF16)

        place = lax.broadcasted_iota(jnp.int32, (BLOCK, BLOCK), 1) - lax.broadcasted_iota(
            jnp.int32, (BLOCK, BLOCK), 0
        )
        tempered = BF16(F**-0.5)

        def one_block(j):
            start = pl.multiple_of(j * BLOCK, BLOCK)
            ids = row_ref[pl.ds(start, BLOCK), :]
            values = [x_ref[pl.ds(start, BLOCK), h * DV : (h + 1) * DV] for h in range(heads)]
            keys = [
                x_ref[pl.ds(start, BLOCK), wide + (heads + h) * F : wide + (heads + h + 1) * F]
                * tempered
                for h in range(heads)
            ]
            across = [
                key_ref[(heads + h) * F : (heads + h + 1) * F, pl.ds(start, BLOCK)] * tempered
                for h in range(heads)
            ]

            def step(i, sums):
                base = pl.multiple_of(i * BLOCK, BLOCK)
                visible = (place >= start - base) & (ids == col_ref[:, pl.ds(base, BLOCK)])
                out = []
                for h in range(heads):
                    queries = x_ref[pl.ds(base, BLOCK), wide + h * F : wide + (h + 1) * F]
                    numer = numer_ref[pl.ds(base, BLOCK), h * DV : (h + 1) * DV]
                    s = dot(keys[h], queries, 1, 1)
                    a = jnp.where(visible, (0.5 * s + 1.0) * s + 1.0, 0.0).astype(BF16)
                    ga = dot(values[h], numer, 1, 1) + gden_ref[h : h + 1, pl.ds(base, BLOCK)]
                    gs = jnp.where(visible, ga * (1.0 + s), 0.0).astype(BF16)
                    gq_ref[h * F : (h + 1) * F, pl.ds(base, BLOCK)] += dot(across[h], gs, 1, 0)
                    out += [sums[2 * h] + dot(a, numer, 1, 0), sums[2 * h + 1] + dot(gs, queries, 1, 0)]
                return tuple(out)

            zeros = []
            for h in range(heads):
                zeros += [jnp.zeros((BLOCK, DV), F32), jnp.zeros((BLOCK, F), F32)]
            sums = lax.fori_loop(
                j, jnp.minimum(j + apart(tokens), blocks), step, tuple(zeros)
            )
            for h in range(heads):
                g_ref[pl.ds(start, BLOCK), h * DV : (h + 1) * DV] = sums[2 * h].astype(BF16)
                g_ref[
                    pl.ds(start, BLOCK), wide + (heads + h) * F : wide + (heads + h + 1) * F
                ] = (sums[2 * h + 1] * F**-0.5).astype(BF16)

        def terms(i, start):
            fetch_terms(i).wait()

            @pl.when(i < 3)
            def _():
                fetch_terms(i + 1).start()

            return term_buf.at[lax.rem(i, 2)]

        def fill(n):
            if n == 0:
                lax.fori_loop(0, deep, plane, 0)
                hand_on(1)
                prepare()
                pl.loop(0, 1)(one_block)
            else:
                pl.loop(1, blocks)(one_block)

        moved = scatter_rows(terms, bufs, s_send, s_receive, lambda: hear(len(met)), fill)
        here = out_ref.at[pl.ds(pl.multiple_of(t * own, own), own)]
        here[...] = (mid_ref[...] + moved).astype(BF16)
        copy = remote(here, here, t_send, t_receive, 0, (d, c, 1 - t))
        copy.start()
        g_ref[:, wide : wide + narrow] = jnp.transpose(gq_ref[...], (1, 0)).astype(BF16)
        total = back_ref[deep - 1].astype(F32)
        for n in range(deep - 1):
            deeper(n).wait_recv()
            total = total + came[n].astype(F32)
        sums[...] = total.astype(BF16)
        hand_on(0)
        landed(1)
        for b in range(4):
            gd_ref[:, b * units : (b + 1) * units] = parts_d[b].astype(F32)
        landed(0)
        for b in range(4):
            go_ref[:, b * wide : (b + 1) * wide] = parts_o[b].astype(F32)
        for n in range(deep - 1):
            deeper(n).wait_send()
        copy.wait_send()
        there = out_ref.at[pl.ds(pl.multiple_of((1 - t) * own, own), own)]
        remote(there, there, t_send, t_receive, 0, (d, c, 1 - t)).wait_recv()

    vmem, hbm = pl.BlockSpec(memory_space=pltpu.VMEM), pl.BlockSpec(memory_space=pl.ANY)
    return call(
        kernel, "attend_back", 7,
        (
            qkv, g_mixed, mixed, denom, seg_rows, seg_cols, branch, heads_out, out_terms, middle,
            sum_down,
        ),
        [
            jax.ShapeDtypeStruct(qkv.shape, BF16),
            jax.ShapeDtypeStruct((2 * own, width), BF16),
            jax.ShapeDtypeStruct((held, 4 * wide), F32),
            jax.ShapeDtypeStruct((held, 4 * units), F32),
        ],
        [
            pltpu.VMEM((narrow, tokens), F32),
            pltpu.VMEM((tokens, wide), BF16),
            pltpu.VMEM((8, tokens), F32),
            pltpu.VMEM((2 * narrow, tokens), BF16),
            pltpu.VMEM((deep, group, wide), BF16),
            pltpu.VMEM((deep - 1, group, wide), BF16),
            pltpu.VMEM((2, tokens, group), BF16),
            pltpu.SemaphoreType.DMA((2,)),
        ]
        + sems(deep - 1)
        + [pltpu.VMEM((2, 2 * own, width), BF16), pltpu.SemaphoreType.DMA((2,))]
        + [
            pltpu.VMEM((group, wide), BF16),
            pltpu.VMEM((4, held, wide), BF16),
            pltpu.VMEM((4, held, units), BF16),
        ]
        + sems(6) + [pltpu.SemaphoreType.DMA((2,))]
        + scatter_scratch(own, width) + sems(SCATTER_COPIES) + sems(1),
        [vmem] * 6 + [hbm, vmem, hbm, vmem, hbm],
    )


def attend_block(i, x_ref, ext_ref, row_ref, col_ref, mixed_ref, denom_ref, low_ref, heads):
    wide = heads * DV
    base = pl.multiple_of(i * BLOCK, BLOCK)
    own = row_ref[pl.ds(base, BLOCK), :]
    place = lax.broadcasted_iota(jnp.int32, (BLOCK, BLOCK), 0) - lax.broadcasted_iota(
        jnp.int32, (BLOCK, BLOCK), 1
    )
    queries = [
        x_ref[pl.ds(base, BLOCK), wide + h * F : wide + (h + 1) * F] * jnp.bfloat16(F**-0.5)
        for h in range(heads)
    ]

    def step(j, sums):
        start = pl.multiple_of(j * BLOCK, BLOCK)
        visible = (place >= start - base) & (own == col_ref[:, pl.ds(start, BLOCK)])
        out = []
        for h in range(heads):
            keys = x_ref[
                pl.ds(start, BLOCK), wide + (heads + h) * F : wide + (heads + h + 1) * F
            ]
            s = dot(queries[h], keys, 1, 1)
            a = jnp.where(visible, (0.5 * s + 1.0) * s + 1.0, 0.0).astype(BF16)
            out.append(
                sums[h] + dot(a, ext_ref[pl.ds(start, BLOCK), 2 * h * DV : (2 * h + 2) * DV], 1, 0)
            )
        return tuple(out)

    sums = lax.fori_loop(
        first_seen(i, x_ref.shape[0]),
        i + 1,
        step,
        tuple(jnp.zeros((BLOCK, 2 * DV), F32) for _ in range(heads)),
    )
    for h in range(heads):
        denom = sums[h][:, DV:]
        mixed = sums[h][:, :DV] / denom
        mixed_ref[pl.ds(base, BLOCK), h * DV : (h + 1) * DV] = mixed
        low_ref[pl.ds(base, BLOCK), h * DV : (h + 1) * DV] = mixed.astype(BF16)
        denom_ref[pl.ds(base, BLOCK), h : h + 1] = denom[:, :1]


def attend(rows_one, w_attn, seg_rows, seg_cols, cot, w_down, heads):
    tokens, width = rows_one.shape
    own = tokens // 8
    wide, narrow = heads * DV, heads * F
    held, units = w_down.shape[0], w_down.shape[1] // 4
    filled = whole_tiles(units)

    def kernel(
        x_ref, w_ref, row_ref, col_ref, cot_ref, d_ref,
        qkv_ref, mixed_ref, denom_ref, low_ref, rows_out, wd_out,
        ext_ref, cut, rows_ref, send, receive, store, d_send, d_receive, here,
    ):
        d, c, t = place_of()

        def out(k):
            return remote(
                cut.at[beside(c, k)], wd_out.at[c], d_send, d_receive, k - 1, (d, beside(c, k), t)
            )

        def arrival(k):
            there = wd_out.at[beside(c, k)]
            return remote(there, there, d_send, d_receive, k - 1, (d, beside(c, k), t))

        local = pltpu.make_async_copy(cut.at[c], wd_out.at[c], here.at[0])
        met = [(d, beside(c, k), t) for k in (1, 2, 3)] + [(d, c, 1 - t)]
        say(met)
        for b in range(4):
            part = columns(d_ref, None, b * units, units)
            if units < filled:
                part = jnp.concatenate([part, jnp.zeros((held, filled - units), F32)], axis=1)
            cut[b] = part.astype(BF16)
        mine = pl.multiple_of((2 * c + t) * own, own)
        hear(len(met))
        rows_ref[pl.ds(mine, own), :] = cot_ref[
            pl.ds(pl.multiple_of(t * own, own), own), : width // 2
        ]

        def blocks(first, last):
            @pl.loop(first, last)
            def _(i):
                attend_block(
                    i, qkv_ref, ext_ref, row_ref, col_ref, mixed_ref, denom_ref, low_ref, heads
                )

        def early():
            local.start()
            for k in (3, 1, 2):
                out(k).start()

            @pl.loop(0, tokens // BLOCK)
            def _(n):
                rows = pl.ds(pl.multiple_of(n * BLOCK, BLOCK), BLOCK)
                values = dot(x_ref[rows, :], w_ref[:, :wide], 1, 0).astype(BF16)
                qkv_ref[rows, :wide] = values
                qkv_ref[rows, wide:] = dot(x_ref[rows, :], w_ref[:, 2 * wide :], 1, 0).astype(BF16)
                for h in range(heads):
                    ext_ref[rows, 2 * h * DV : (2 * h + 1) * DV] = values[:, h * DV : (h + 1) * DV]
                    ext_ref[rows, (2 * h + 1) * DV : (2 * h + 2) * DV] = jnp.ones((BLOCK, DV), BF16)

        gather_rows(
            rows_ref, rows_out, send, receive, store, early=early,
            middle=lambda: blocks(0, tokens // BLOCK // 2),
            late=lambda: blocks(tokens // BLOCK // 2, tokens // BLOCK),
        )
        local.wait()
        for k in (1, 2, 3):
            arrival(k).wait_recv()
            out(k).wait_send()

    vmem, hbm = pl.BlockSpec(memory_space=pltpu.VMEM), pl.BlockSpec(memory_space=pl.ANY)
    return call(
        kernel, "attend", 2, (rows_one, w_attn, seg_rows, seg_cols, cot, w_down),
        [
            jax.ShapeDtypeStruct((tokens, wide + 2 * narrow), BF16),
            jax.ShapeDtypeStruct((tokens, wide), F32),
            jax.ShapeDtypeStruct((tokens, heads), F32),
            jax.ShapeDtypeStruct((tokens, wide), BF16),
            jax.ShapeDtypeStruct((tokens, width // 2), BF16),
            jax.ShapeDtypeStruct((4, held, filled), BF16),
        ],
        [pltpu.VMEM((tokens, 2 * wide), BF16), pltpu.VMEM((4, held, filled), BF16)]
        + gather_scratch(tokens, width // 2) + sems(3) + [pltpu.SemaphoreType.DMA((1,))],
        None,
        [vmem] * 4 + [hbm, hbm],
    )


def to_middle(heads_out, w_attn, x):
    tokens, width = heads_out.shape[0], x.shape[1]
    own = tokens // 8
    wide = heads_out.shape[1]

    def kernel(h_ref, w_ref, x_ref, mid_ref, rows_out, *rest):
        bufs, (s_send, s_receive, rows_ref, g_send, g_receive, store) = rest[:6], rest[6:]
        d, c, t = place_of()
        say(around())

        def terms(i, start):
            return [(h_ref[pl.ds(start, 2 * own), :], w_ref, slice(wide, 2 * wide))]

        total = scatter_rows(terms, bufs, s_send, s_receive, lambda: hear(3))
        middle = total + x_ref[pl.ds(pl.multiple_of(t * own, own), own), :].astype(F32)
        mid_ref[...] = middle
        _, hat = norm_parts(middle)
        rows_ref[pl.ds(pl.multiple_of((2 * c + t) * own, own), own), :] = hat.astype(BF16)
        gather_rows(rows_ref, rows_out, g_send, g_receive, store)

    return call(
        kernel, "to_middle", 3, (heads_out, w_attn, x),
        [jax.ShapeDtypeStruct((own, width), F32), jax.ShapeDtypeStruct((tokens, width), BF16)],
        scatter_scratch(own, width) + sems(SCATTER_COPIES) + gather_scratch(tokens, width),
        None,
        [pl.BlockSpec(memory_space=pltpu.VMEM), pl.BlockSpec(memory_space=pl.ANY)],
        flops=2 * tokens * width * heads_out.shape[1],
    )


def gate_up(rows_two, w_both, cot, cot_low):
    tokens, width = rows_two.shape
    own = tokens // 8
    units = w_both.shape[1] // 2
    main = units // 128 * 128
    count = tokens // BLOCK
    tile = 256

    def kernel(
        x_ref, w_ref, cot_ref, low_ref, hid_out, slope_out, silu_out, rows_out, down_out,
        x_buf, w_buf, low_buf, hid_ref, slope_ref, silu_ref, down_buf, load, store, down_store,
        rows_ref, send, receive, row_store,
    ):
        d, c, t = place_of()

        def fetch(i):
            rows = pl.ds(pl.multiple_of(i * BLOCK, BLOCK), BLOCK)
            slot = lax.rem(i, 2)
            return pltpu.make_async_copy(x_ref.at[rows], x_buf.at[slot], load.at[slot])

        def given(i):
            rows = pl.ds(pl.multiple_of(i * BLOCK, BLOCK), BLOCK)
            slot = lax.rem(i, 2)
            return [
                pltpu.make_async_copy(source, target.at[rows], store.at[n, slot])
                for n, (source, target) in enumerate(
                    (
                        (hid_ref.at[rows], hid_out),
                        (slope_ref.at[slot], slope_out),
                        (silu_ref.at[slot], silu_out),
                    )
                )
            ]

        weights = pltpu.make_async_copy(w_ref, w_buf, load.at[2])
        weights.start()
        fetch(0).start()
        low_copy = pltpu.make_async_copy(low_ref, low_buf, load.at[3])
        low_copy.start()
        greet(around())
        mine = pl.multiple_of((2 * c + t) * own, own)
        rows_ref[pl.ds(mine, own), :] = cot_ref[
            pl.ds(pl.multiple_of(t * own, own), own), width // 2 :
        ]

        def blocks(first, last):
            @pl.loop(first, last)
            def _(i):
                slot = lax.rem(i, 2)

                @pl.when(i + 1 < count)
                def _():
                    fetch(i + 1).start()

                fetch(i).wait()
                both = dot(x_buf[slot], w_buf[...], 1, 0)

                @pl.when(i >= 2)
                def _():
                    for copy in given(i - 2):
                        copy.wait()

                def act(gate, up, part):
                    sig = jax.nn.sigmoid(gate)
                    silu = gate * sig
                    hid_ref[pl.ds(pl.multiple_of(i * BLOCK, BLOCK), BLOCK), part] = (
                        silu * up
                    ).astype(BF16)
                    slope_ref[slot, :, part] = (up * sig * (1.0 + gate * (1.0 - sig))).astype(BF16)
                    silu_ref[slot, :, part] = silu.astype(BF16)

                act(both[:, :main], both[:, main : 2 * main], slice(0, main))
                if main < units:
                    act(
                        both[:, 2 * main : main + units],
                        both[:, main + units :],
                        slice(main, units),
                    )
                for copy in given(i):
                    copy.start()

        per = width // 2 // tile

        def down_given(base, n):
            slot = lax.rem(n, 2)
            rows = pl.ds(pl.multiple_of(base + n * tile, tile), tile)
            return pltpu.make_async_copy(down_buf.at[slot], down_out.at[rows], down_store.at[slot])

        def down_tiles(source, base, end):
            @pl.loop(0, end)
            def _(n):
                @pl.when(n >= 2)
                def _():
                    down_given(base, n - 2).wait()

                part = pl.ds(pl.multiple_of(n * tile, tile), tile)
                down_buf[lax.rem(n, 2)] = dot(source[:, part], hid_ref[...], 0, 0).astype(BF16)
                down_given(base, n).start()

        def early():
            weights.wait()
            blocks(0, 1)

        def later():
            blocks(count // 2, count)
            low_copy.wait()
            down_tiles(low_buf, 0, per)
            for n in (per - 2, per - 1):
                down_given(0, n).wait()

        gather_rows(
            rows_ref, rows_out, send, receive, row_store, early=early,
            middle=lambda: blocks(1, count // 2), late=later,
        )
        down_tiles(rows_ref, width // 2, per)
        for n in (per - 2, per - 1):
            down_given(width // 2, n).wait()
        for i in (count - 2, count - 1):
            for copy in given(i):
                copy.wait()

    vmem, hbm = pl.BlockSpec(memory_space=pltpu.VMEM), pl.BlockSpec(memory_space=pl.ANY)
    return call(
        kernel, "gate_up", 8, (rows_two, w_both, cot, cot_low),
        [jax.ShapeDtypeStruct((tokens, units), BF16)] * 3
        + [
            jax.ShapeDtypeStruct((tokens, width // 2), BF16),
            jax.ShapeDtypeStruct((width, units), BF16),
        ],
        [
            pltpu.VMEM((2, BLOCK, width), BF16),
            pltpu.VMEM(w_both.shape, BF16),
            pltpu.VMEM(cot_low.shape, BF16),
            pltpu.VMEM((tokens, units), BF16),
            pltpu.VMEM((2, BLOCK, units), BF16),
            pltpu.VMEM((2, BLOCK, units), BF16),
            pltpu.VMEM((2, tile, units), BF16),
            pltpu.SemaphoreType.DMA((4,)),
            pltpu.SemaphoreType.DMA((3, 2)),
            pltpu.SemaphoreType.DMA((2,)),
        ]
        + gather_scratch(tokens, width // 2),
        [hbm, hbm, vmem, hbm],
        [hbm] * 5,
        flops=4 * tokens * width * units,
    )


def feed_forward(slope, silu, cot_low, cot_high, w_down, rows_two):
    tokens, width = rows_two.shape
    units = slope.shape[1]
    main = units // 128 * 128
    tile = 256
    part_width = width // 2
    count = tokens // BLOCK

    def kernel(
        slope_ref, silu_ref, low_ref, high_ref, d_ref, two_ref, g_out, grad_ref,
        slope_buf, silu_buf, low_buf, high_buf, d_buf, g_ref, here, g_store, cols, out, load, store,
    ):
        def rows(i):
            return pl.ds(pl.multiple_of(i * BLOCK, BLOCK), BLOCK)

        def fetch(i):
            slot = lax.rem(i, 2)
            return [
                pltpu.make_async_copy(source.at[rows(i)], target.at[slot], here.at[n, slot])
                for n, (source, target) in enumerate(
                    (
                        (low_ref, low_buf),
                        (high_ref, high_buf),
                        (slope_ref, slope_buf),
                        (silu_ref, silu_buf),
                    )
                )
            ]

        def g_given(i):
            return pltpu.make_async_copy(g_ref.at[rows(i)], g_out.at[rows(i)], g_store.at[i])

        def wanted(n):
            part = pl.ds(pl.multiple_of(n * tile, tile), tile)
            slot = lax.rem(n, 2)
            return pltpu.make_async_copy(two_ref.at[:, part], cols.at[slot], load.at[slot])

        def given(n):
            part = pl.ds(pl.multiple_of(n * tile, tile), tile)
            slot = lax.rem(n, 2)
            return pltpu.make_async_copy(out.at[slot], grad_ref.at[part], store.at[slot])

        weights = pltpu.make_async_copy(d_ref, d_buf, load.at[2])
        weights.start()
        for copy in fetch(0):
            copy.start()
        wanted(0).start()
        weights.wait()

        @pl.loop(0, count)
        def _(i):
            slot = lax.rem(i, 2)

            @pl.when(i + 1 < count)
            def _():
                for copy in fetch(i + 1):
                    copy.start()

            for copy in fetch(i):
                copy.wait()
            g_hidden = dot(low_buf[slot], d_buf[:part_width, :units], 1, 0) + dot(
                high_buf[slot], d_buf[part_width:, :units], 1, 0
            )
            gg = g_hidden * slope_buf[slot].astype(F32)
            gu = g_hidden * silu_buf[slot].astype(F32)
            part = rows(i)
            g_ref[part, :main] = gg[:, :main].astype(BF16)
            g_ref[part, main : 2 * main] = gu[:, :main].astype(BF16)
            if main < units:
                g_ref[part, 2 * main :] = jnp.concatenate(
                    [gg[:, main:], gu[:, main:]], axis=1
                ).astype(BF16)
            g_given(i).start()

        last = width // tile

        @pl.loop(0, last)
        def _(n):
            @pl.when(n + 1 < last)
            def _():
                wanted(n + 1).start()

            wanted(n).wait()

            @pl.when(n >= 2)
            def _():
                given(n - 2).wait()

            slot = lax.rem(n, 2)
            out[slot] = dot(cols[slot], g_ref[...], 0, 0).astype(BF16)
            given(n).start()

        given(last - 2).wait()
        given(last - 1).wait()
        for i in range(count):
            g_given(i).wait()

    hbm = pl.BlockSpec(memory_space=pl.ANY)
    moved = 2 * tokens * (2 * width + 4 * units) + 6 * width * units
    return pl.pallas_call(
        kernel,
        in_specs=[hbm] * 6,
        out_specs=[hbm] * 2,
        out_shape=[
            jax.ShapeDtypeStruct((tokens, 2 * units), BF16),
            jax.ShapeDtypeStruct((width, 2 * units), BF16),
        ],
        scratch_shapes=[
            pltpu.VMEM((2, BLOCK, units), BF16),
            pltpu.VMEM((2, BLOCK, units), BF16),
            pltpu.VMEM((2, BLOCK, part_width), BF16),
            pltpu.VMEM((2, BLOCK, part_width), BF16),
            pltpu.VMEM(w_down.shape, BF16),
            pltpu.VMEM((tokens, 2 * units), BF16),
            pltpu.SemaphoreType.DMA((4, 2)),
            pltpu.SemaphoreType.DMA((count,)),
            pltpu.VMEM((2, tokens, tile), BF16),
            pltpu.VMEM((2, tile, 2 * units), BF16),
            pltpu.SemaphoreType.DMA((3,)),
            pltpu.SemaphoreType.DMA((2,)),
        ],
        compiler_params=pltpu.CompilerParams(vmem_limit_bytes=VMEM_MOST),
        cost_estimate=pl.CostEstimate(
            flops=6 * tokens * width * units, bytes_accessed=moved, transcendentals=0
        ),
        name="feed_forward",
    )(slope, silu, cot_low, cot_high, w_down, rows_two)


def to_branch(g_both, w_both, middle, cot, w_attn, wide, hidden, w_down):
    tokens, width = g_both.shape[0], middle.shape[1]
    own = tokens // 8
    units = hidden.shape[1]
    tile = width // 2

    def kernel(
        g_ref, w_ref, mid_ref, cot_ref, o_ref, hid_ref, d_ref, gm_ref, rows_out, mix_ref, term_ref,
        g_buf, w_buf, hid_buf, d_buf, term_buf, load, term_store, *rest,
    ):
        bufs, (s_send, s_receive, rows_ref, g_send, g_receive, store) = rest[:6], rest[6:]
        d, c, t = place_of()

        def fetch(i):
            part = pl.ds(pl.multiple_of(2 * scatter_order(i) * own, 2 * own), 2 * own)
            slot = lax.rem(i, 2)
            return pltpu.make_async_copy(g_ref.at[part], g_buf.at[slot], load.at[slot])

        weights = pltpu.make_async_copy(w_ref, w_buf, load.at[2])
        weights.start()
        fetch(0).start()
        say(around())
        weights.wait()
        down = pltpu.make_async_copy(d_ref, d_buf, load.at[3])
        down.start()
        pltpu.make_async_copy(
            hid_ref.at[pl.ds(0, BLOCK)], hid_buf, load.at[4]
        ).start()

        def terms(i, start):
            fetch(i).wait()

            @pl.when(i < 3)
            def _():
                fetch(i + 1).start()

            return [(g_buf[lax.rem(i, 2)], w_buf, slice(None))]

        total = scatter_rows(terms, bufs, s_send, s_receive, lambda: hear(3))
        scale, hat = norm_parts(mid_ref[...])
        g_middle = cot_ref[pl.ds(pl.multiple_of(t * own, own), own), :].astype(F32) + norm_back(
            total, hat, scale
        )
        gm_ref[...] = g_middle
        rows_ref[pl.ds(pl.multiple_of((2 * c + t) * own, own), own), :] = g_middle.astype(BF16)

        def mix(start):
            mix_ref[pl.ds(start, own), :] = dot(
                rows_ref[pl.ds(start, own), :], o_ref[:, wide : 2 * wide], 1, 0
            ).astype(BF16)

        def block(i):
            return pl.ds(pl.multiple_of(i * BLOCK, BLOCK), BLOCK)

        def hidden_of(i):
            return pltpu.make_async_copy(hid_ref.at[block(i)], hid_buf, load.at[4])

        def term_given(i):
            return pltpu.make_async_copy(term_buf, term_ref.at[block(i)], term_store.at[0])

        def out_terms(first, last):
            @pl.loop(first, last)
            def _(i):
                hidden_of(i).wait()

                @pl.when(i > 0)
                def _():
                    term_given(i - 1).wait()

                for n in (0, 1):
                    columns = slice(n * tile, (n + 1) * tile)
                    term_buf[:, columns] = dot(
                        hid_buf[...], d_buf[columns, :units], 1, 1
                    ).astype(BF16)
                term_given(i).start()

                @pl.when(i + 1 < tokens // BLOCK)
                def _():
                    hidden_of(i + 1).start()

        down.wait()
        blocks = tokens // BLOCK
        gather_rows(
            rows_ref, rows_out, g_send, g_receive, store, mix,
            lambda: out_terms(0, blocks // 2),
            lambda: out_terms(blocks // 2, blocks - 1),
            lambda: out_terms(blocks - 1, blocks),
        )
        term_given(blocks - 1).wait()

    vmem, hbm = pl.BlockSpec(memory_space=pltpu.VMEM), pl.BlockSpec(memory_space=pl.ANY)
    return call(
        kernel, "to_branch", 5, (g_both, w_both, middle, cot, w_attn, hidden, w_down),
        [
            jax.ShapeDtypeStruct((own, width), F32),
            jax.ShapeDtypeStruct((tokens, width), BF16),
            jax.ShapeDtypeStruct((tokens, wide), BF16),
            jax.ShapeDtypeStruct((tokens, width), BF16),
        ],
        [
            pltpu.VMEM((2, 2 * own, g_both.shape[1]), BF16),
            pltpu.VMEM(w_both.shape, BF16),
            pltpu.VMEM((BLOCK, units), BF16),
            pltpu.VMEM(w_down.shape, BF16),
            pltpu.VMEM((BLOCK, width), BF16),
            pltpu.SemaphoreType.DMA((5,)),
            pltpu.SemaphoreType.DMA((1,)),
        ]
        + scatter_scratch(own, width) + sems(SCATTER_COPIES) + gather_scratch(tokens, width),
        [hbm, hbm, vmem, vmem, vmem, hbm, hbm],
        [vmem, hbm, vmem, hbm],
        flops=4 * tokens * width * (g_both.shape[1] // 2 + wide),
    )


def as_row(column):
    return jnp.transpose(jnp.broadcast_to(column, (column.shape[0], 128)), (1, 0))[:8]


def to_input(g_qkv, w_attn, x, g_middle, rows_one, sum_both, weights, gains, heads):
    tokens, width = g_qkv.shape[0], x.shape[1]
    own = tokens // 8
    deep = lax.axis_size("dp")
    across = g_qkv.shape[1]
    group = width // deep
    held = group // 4
    wide, narrow = heads * DV, heads * F
    both = sum_both.shape[1]
    units = both // 2
    main = units // 128 * 128

    def kernel(
        g_ref, w_ref, x_ref, gm_ref, one_ref, both_ref,
        wq_ref, wk_ref, wv_ref, wg_ref, wu_ref, gain_ref, gain_two_ref,
        out_ref, gq_ref, gk_ref, gv_ref, gg_ref, gu_ref, row_ref, row_two_ref,
        *rest,
    ):
        bufs, (s_send, s_receive, t_send, t_receive) = rest[:6], rest[6:10]
        (
            came_deep, sums, parts_a, parts_b, scalar, back_ref, one_buf, load,
            d_send, d_receive, p_send, p_receive, local,
        ) = rest[10:]
        d, c, t = place_of()
        hand_on, landed = exchange(
            ((sums, parts_a), (both_ref, parts_b)), held, p_send, p_receive, local
        )

        def fetch(n):
            part = pl.ds(pl.multiple_of(depth(d, n + 1) * group, group), group)
            slot = lax.rem(n, 2)
            return pltpu.make_async_copy(one_ref.at[:, part], one_buf.at[slot], load.at[slot])

        fetch(0).start()
        met = (
            around()
            + [(d, beside(c, 3), t)]
            + [(depth(d, k), c, t) for k in range(1, deep)]
        )
        say(met)

        def deeper(n):
            rows = pl.ds(pl.multiple_of(depth(d, n + 1) * group, group), group)
            return remote(
                back_ref.at[rows], came_deep.at[n], d_send, d_receive, n, (depth(d, n + 1), c, t)
            )

        def plane(n, carry):
            rows = pl.ds(pl.multiple_of(depth(d, n + 1) * group, group), group)

            @pl.when(n < deep - 1)
            def _():
                fetch(n + 1).start()

            fetch(n).wait()
            back_ref[rows, :] = dot(one_buf[lax.rem(n, 2)], g_ref[...], 0, 0).astype(BF16)

            @pl.when(n < deep - 1)
            def _():
                deeper(n).start()

            return carry

        def terms(i, start):
            part = pl.ds(start, 2 * own)
            return [
                (g_ref[part, :wide], w_ref, slice(0, wide)),
                (g_ref[part, wide:], w_ref, slice(2 * wide, None)),
            ]

        def fill(n):
            if n == 0:
                hand_on(1)
                lax.fori_loop(0, deep, plane, 0)
                return
            landed(1)
            gain_two = gain_two_ref[...]
            for b in range(4):
                whole = parts_b[b].astype(F32)
                for ref, first, rest_of in (
                    (gg_ref, 0, 2 * main),
                    (gu_ref, main, main + units),
                ):
                    s = whole[:, first : first + main]
                    if main < units:
                        s = jnp.concatenate([s, whole[:, rest_of : rest_of + units - main]], axis=1)
                    ref[:, b * units : (b + 1) * units] = s * gain_two
            scalar[0, 1] = as_row(
                (
                    jnp.sum(gg_ref[...] * wg_ref[...].astype(F32), axis=1, keepdims=True)
                    + jnp.sum(gu_ref[...] * wu_ref[...].astype(F32), axis=1, keepdims=True)
                )
                / gain_two
            )
            for m in range(deep - 1):
                deeper(m).wait_recv()
            mine = pl.ds(pl.multiple_of(d * group, group), group)
            total = back_ref[mine, :].astype(F32)
            for m in range(deep - 1):
                total = total + came_deep[m].astype(F32)
            sums[...] = total.astype(BF16)
            hand_on(0)

        e_one = scatter_rows(terms, bufs, s_send, s_receive, lambda: hear(len(met)), fill)
        scale, hat = norm_parts(x_ref[pl.ds(pl.multiple_of(t * own, own), own), :].astype(F32))
        place = out_ref.at[pl.ds(pl.multiple_of(t * own, own), own)]
        place[...] = gm_ref[...] + norm_back(e_one, hat, scale)
        copy = remote(place, place, t_send, t_receive, 0, (d, c, 1 - t))
        copy.start()
        landed(0)
        gain_one = gain_ref[...]

        def owned(start, count):
            return jnp.concatenate(
                [parts_a[b][:, start : start + count].astype(F32) for b in range(4)], axis=1
            )

        term_one = jnp.zeros((held, 1), F32)
        for ref, weight, start, count in (
            (gv_ref, wv_ref, 0, wide),
            (gq_ref, wq_ref, wide, narrow),
            (gk_ref, wk_ref, wide + narrow, narrow),
        ):
            s = owned(start, count)
            term_one = term_one + jnp.sum(s * weight[...].astype(F32), axis=1, keepdims=True)
            ref[...] = s * gain_one
        scalar[0, 0] = as_row(term_one)
        swap = remote(scalar.at[0], scalar.at[1], t_send, t_receive, 1, (d, c, 1 - t))
        swap.start()
        swap.wait()
        row_ref[...] = (scalar[0, 0] + scalar[1, 0])[:1]
        row_two_ref[...] = (scalar[0, 1] + scalar[1, 1])[:1]
        copy.wait_send()
        there = out_ref.at[pl.ds(pl.multiple_of((1 - t) * own, own), own)]
        remote(there, there, t_send, t_receive, 0, (d, c, 1 - t)).wait_recv()
        for m in range(deep - 1):
            deeper(m).wait_send()

    w_q, w_k, w_v, w_gate, w_up = weights
    vmem, hbm = pl.BlockSpec(memory_space=pltpu.VMEM), pl.BlockSpec(memory_space=pl.ANY)
    return call(
        kernel, "to_input", 6,
        (g_qkv, w_attn, x, g_middle, rows_one, sum_both) + tuple(weights) + tuple(gains),
        [jax.ShapeDtypeStruct((2 * own, width), F32)]
        + [jax.ShapeDtypeStruct(w.shape, F32) for w in weights]
        + [jax.ShapeDtypeStruct((1, held), F32)] * 2,
        scatter_scratch(own, width) + sems(SCATTER_COPIES) + sems(2)
        + [
            pltpu.VMEM((deep - 1, group, across), BF16),
            pltpu.VMEM((group, across), BF16),
            pltpu.VMEM((4, held, across), BF16),
            pltpu.VMEM((4, held, both), BF16),
            pltpu.VMEM((2, 2, 8, held), F32),
            pltpu.VMEM((width, across), BF16),
            pltpu.VMEM((2, tokens, group), BF16),
            pltpu.SemaphoreType.DMA((2,)),
        ]
        + sems(deep - 1) + sems(6) + [pltpu.SemaphoreType.DMA((2,))],
        [vmem] * 4 + [hbm] * 2 + [vmem] * 7,
        flops=2 * tokens * width * g_qkv.shape[1],
    )


def plane_shards(
    activations,
    seg_ids,
    cotangent,
    q_weight,
    k_weight,
    v_weight,
    o_weight,
    gate_weight,
    up_weight,
    down_weight,
    attn_gain,
    mlp_gain,
):
    parts = lax.axis_size("ctx")
    heads = q_weight.shape[1] // F // parts
    tokens = activations.shape[1] * parts
    x, cot_block = activations[0], cotangent[0]
    gain_one = attn_gain.astype(F32)[:, None]
    gain_two = mlp_gain.astype(F32)[:, None]
    rows_one, segments, w_attn, cut_both = front(
        x,
        seg_ids,
        (q_weight, k_weight, v_weight, o_weight, gate_weight, up_weight),
        (gain_one, gain_two),
        tokens,
        heads,
    )
    w_attn = w_attn.reshape(-1, w_attn.shape[3])
    w_both = lax.all_gather(cut_both, "dp", axis=0, tiled=True).reshape(-1, cut_both.shape[2])
    seg_rows, seg_cols = segments.reshape(tokens, 1), segments.reshape(1, tokens)
    qkv, mixed, denom, heads_out, cot_low, cut_down = attend(
        rows_one, w_attn, seg_rows, seg_cols, cot_block, down_weight, heads
    )
    w_down = lax.all_gather(cut_down, "dp", axis=0, tiled=True).reshape(-1, cut_down.shape[2])
    middle, rows_two = to_middle(heads_out, w_attn, x)
    hidden, slope, silu, cot_high, back_down = gate_up(rows_two, w_both, cot_block, cot_low)
    sum_down = lax.psum_scatter(back_down, "dp", scatter_dimension=0, tiled=True)
    g_both, back_both = feed_forward(slope, silu, cot_low, cot_high, w_down, rows_two)
    sum_both = lax.psum_scatter(back_both, "dp", scatter_dimension=0, tiled=True)
    g_middle, branch, g_mixed, out_terms = to_branch(
        g_both, w_both, middle, cot_block, w_attn, heads * DV, hidden, w_down
    )
    g_qkv, out, s_o, s_down = attend_back(
        qkv,
        g_mixed,
        mixed,
        denom,
        seg_rows,
        seg_cols,
        branch,
        heads_out,
        out_terms,
        middle,
        sum_down,
        heads,
    )
    g_input, s_q, s_k, s_v, s_gate, s_up, attn_row, mlp_row = to_input(
        g_qkv,
        w_attn,
        x,
        g_middle,
        rows_one,
        sum_both,
        (q_weight, k_weight, v_weight, gate_weight, up_weight),
        (gain_one, gain_two),
        heads,
    )
    return (
        out[None],
        g_input[None],
        s_q,
        s_k,
        s_v,
        s_o,
        s_gate,
        s_up,
        s_down,
        attn_row[0],
        mlp_row[0],
    )


def layer(*arrays):
    heads = arrays[3].shape[1] // F
    plan = shards if heads % lax.axis_size("ctx") else plane_shards
    return plan(*arrays)


def solution(mesh):
    placed = (
        P("dp", "ctx", None),
        P("dp", "ctx"),
        P("dp", "ctx", None),
        P(("dp", "ctx"), "tp"),
        P(("dp", "ctx"), "tp"),
        P(("dp", "ctx"), "tp"),
        P(("dp", "ctx"), "tp"),
        P(("dp", "ctx"), "tp"),
        P(("dp", "ctx"), "tp"),
        P(("dp", "ctx"), "tp"),
        P(("dp", "ctx")),
        P(("dp", "ctx")),
    )
    return jax.shard_map(
        layer,
        mesh=mesh,
        in_specs=placed,
        out_specs=(
            P("dp", "ctx", None),
            P("dp", "ctx", None),
            P(("dp", "ctx"), "tp"),
            P(("dp", "ctx"), "tp"),
            P(("dp", "ctx"), "tp"),
            P(("dp", "ctx"), "tp"),
            P(("dp", "ctx"), "tp"),
            P(("dp", "ctx"), "tp"),
            P(("dp", "ctx"), "tp"),
            P(("dp", "ctx")),
            P(("dp", "ctx")),
        ),
        check_vma=False,
    )
```

```python
import functools

import jax
import jax.numpy as jnp
from jax import lax
from jax.experimental import pallas as pl
from jax.experimental.pallas import tpu as pltpu
from jax.sharding import PartitionSpec as P

F = 16
DV = 128


EPSILON = 1e-05
PRECISE = lax.Precision.HIGHEST
VMEM_MOST = 60 * 2**20


def prefix(x, axis, join, neutral, backward):
    count = lax.axis_size(axis)
    place = lax.axis_index(axis)
    ahead = count - 1 - place if backward else place
    gathered = jax.tree.map(
        lambda a, kind: lax.all_gather(a.astype(kind), axis),
        x,
        (jnp.bfloat16, jnp.bfloat16, jnp.bfloat16),
    )
    state = jax.tree.map(lambda a, e: jnp.zeros_like(a) + jnp.asarray(e, a.dtype), x, neutral)

    def one(lap, state):
        source = count - 1 - lap if backward else lap
        return join(
            state,
            jax.tree.map(
                lambda a, own: lax.dynamic_index_in_dim(a, source, 0, False).astype(own.dtype),
                gathered,
                x,
            ),
        )

    return lax.fori_loop(0, ahead, one, state)


def taylor(features_in):
    feature_count = features_in.shape[-1]
    products = (features_in[..., :, None] * features_in[..., None, :]).reshape(
        features_in.shape[:-1] + (feature_count * feature_count,)
    )
    constant = jnp.ones(features_in.shape[:-1] + (1,), jnp.float32)
    return jnp.concatenate(
        [
            constant,
            features_in * feature_count ** (-0.25),
            products * (2.0 * feature_count) ** (-0.5),
        ],
        axis=-1,
    )


def taylor_back(features_in, incoming_gradient):
    feature_count = features_in.shape[-1]
    linear = incoming_gradient[..., 1 : 1 + feature_count] * feature_count ** (-0.25)
    square = incoming_gradient[..., 1 + feature_count :].reshape(
        incoming_gradient.shape[:-1] + (feature_count, feature_count)
    )
    paired = jnp.einsum(
        "...ab,...b->...a", square + jnp.swapaxes(square, -1, -2), features_in, precision=PRECISE
    )
    return linear + paired * (2.0 * feature_count) ** (-0.5)


def norm_backward_step(incoming_gradient, unit_normalized_rows, multiplier_term, gain_vector_row):
    rescaled_rows = incoming_gradient * gain_vector_row
    return multiplier_term * (
        rescaled_rows
        - unit_normalized_rows
        * jnp.mean(rescaled_rows * unit_normalized_rows, axis=1, keepdims=True)
    )


def join_states(earlier, later_part):
    is_empty = later_part[2] < 0.0
    retain = jnp.where(is_empty | (earlier[2] == later_part[2]), 1.0, 0.0).astype(jnp.float32)
    return (
        later_part[0] + retain * earlier[0],
        later_part[1] + retain * earlier[1],
        jnp.where(is_empty, earlier[2], later_part[2]),
    )


def shards(
    activations,
    seg_ids,
    cotangent,
    q_weight,
    k_weight,
    v_weight,
    o_weight,
    gate_weight,
    up_weight,
    down_weight,
    attn_gain,
    mlp_gain,
):
    layer_input_rows = activations[0].astype(jnp.float32)
    segment = seg_ids[0].astype(jnp.float32)
    tokens = layer_input_rows.shape[0]
    head_count = q_weight.shape[1] // F
    w_query, w_key, w_value, w_out, first_norm_gain = (
        lax.all_gather(q_weight, ("dp", "ctx"), axis=0, tiled=True),
        lax.all_gather(k_weight, ("dp", "ctx"), axis=0, tiled=True),
        lax.all_gather(v_weight, ("dp", "ctx"), axis=0, tiled=True),
        lax.all_gather(o_weight, ("dp", "ctx"), axis=0, tiled=True),
        lax.all_gather(attn_gain, ("dp", "ctx"), axis=0, tiled=True),
    )
    first_inverse_scale = lax.rsqrt(
        jnp.mean(layer_input_rows * layer_input_rows, axis=1, keepdims=True) + EPSILON
    )
    first_unit_rows = layer_input_rows * first_inverse_scale
    first_normalized = (first_unit_rows * first_norm_gain.astype(jnp.float32)).astype(jnp.bfloat16)
    queries = (
        jnp.dot(first_normalized, w_query, preferred_element_type=jnp.float32)
        .astype(jnp.bfloat16)
        .reshape(tokens, head_count, F)
    )
    key_heads = (
        jnp.dot(first_normalized, w_key, preferred_element_type=jnp.float32)
        .astype(jnp.bfloat16)
        .reshape(tokens, head_count, F)
    )
    value_heads = (
        jnp.dot(first_normalized, w_value, preferred_element_type=jnp.float32)
        .astype(jnp.bfloat16)
        .reshape(tokens, head_count, DV)
    )
    w_gate, w_up, w_down, second_norm_gain = (
        lax.all_gather(gate_weight, ("dp", "ctx"), axis=0, tiled=True),
        lax.all_gather(up_weight, ("dp", "ctx"), axis=0, tiled=True),
        lax.all_gather(down_weight, ("dp", "ctx"), axis=0, tiled=True),
        lax.all_gather(mlp_gain, ("dp", "ctx"), axis=0, tiled=True),
    )
    scores = jnp.einsum(
        "thf,shf->hts", queries, key_heads, preferred_element_type=jnp.float32
    ) * F ** (-0.5)
    places = jnp.arange(tokens)
    visible = (
        (places[:, None] >= places[None, :]) & (segment[:, None] == segment[None, :])
    ).astype(jnp.float32)
    weights = (visible * (1.0 + scores + 0.5 * scores * scores)).astype(jnp.bfloat16)
    query_float = queries.astype(jnp.float32)
    key_float = key_heads.astype(jnp.float32)
    value_float = value_heads.astype(jnp.float32)
    feat_q = taylor(query_float)
    feat_k = taylor(key_float)
    ending = segment[-1]
    owned = (segment == ending).astype(jnp.float32)[:, None, None]
    local_state = jnp.einsum("thf,thd->hfd", feat_k * owned, value_float, precision=PRECISE)
    local_total = jnp.sum(feat_k * owned, axis=0)
    empty_state = (jnp.zeros_like(local_state), jnp.zeros_like(local_total), jnp.float32(-1.0))
    prior_state, prior_total, before = prefix(
        (local_state, local_total, ending), "ctx", join_states, empty_state, False
    )
    inherit = (segment == before).astype(jnp.float32)
    numerator = jnp.einsum(
        "hts,shd->thd", weights, value_heads, preferred_element_type=jnp.float32
    ) + inherit[:, None, None] * jnp.einsum("thf,hfd->thd", feat_q, prior_state, precision=PRECISE)
    denominator = jnp.sum(weights.astype(jnp.float32), axis=2).T + inherit[:, None] * jnp.einsum(
        "thf,hf->th", feat_q, prior_total, precision=PRECISE
    )
    mixed_heads = numerator / denominator[:, :, None]
    heads_out = mixed_heads.reshape(tokens, head_count * DV).astype(jnp.bfloat16)
    attn_out = lax.psum(
        jnp.einsum("tc,dc->td", heads_out, w_out, preferred_element_type=jnp.float32), "tp"
    )
    residual_midpoint = layer_input_rows + attn_out
    second_inverse_scale = lax.rsqrt(
        jnp.mean(residual_midpoint * residual_midpoint, axis=1, keepdims=True) + EPSILON
    )
    second_unit_rows = residual_midpoint * second_inverse_scale
    second_normalized = (second_unit_rows * second_norm_gain.astype(jnp.float32)).astype(
        jnp.bfloat16
    )
    gate_value = jnp.dot(second_normalized, w_gate, preferred_element_type=jnp.float32)
    up_value = jnp.dot(second_normalized, w_up, preferred_element_type=jnp.float32)
    sigmoid_gate = jax.nn.sigmoid(gate_value)
    hidden = (gate_value * sigmoid_gate * up_value).astype(jnp.bfloat16)
    mlp_out = lax.psum(
        jnp.einsum("tc,dc->td", hidden, w_down, preferred_element_type=jnp.float32).astype(
            jnp.bfloat16
        ),
        "tp",
    ).astype(jnp.float32)
    final_out = residual_midpoint + mlp_out
    grad_out = cotangent[0].astype(jnp.float32)
    grad_branch_two = cotangent[0]
    grad_w_down = jnp.einsum(
        "td,tc->dc", grad_branch_two, hidden, preferred_element_type=jnp.float32
    )
    grad_hidden = jnp.dot(grad_branch_two, w_down, preferred_element_type=jnp.float32)
    grad_gate = (
        grad_hidden * up_value * sigmoid_gate * (1.0 + gate_value * (1.0 - sigmoid_gate))
    ).astype(jnp.bfloat16)
    grad_up = (grad_hidden * gate_value * sigmoid_gate).astype(jnp.bfloat16)
    grad_w_gate = jnp.einsum(
        "td,tc->dc", second_normalized, grad_gate, preferred_element_type=jnp.float32
    )
    grad_w_up = jnp.einsum(
        "td,tc->dc", second_normalized, grad_up, preferred_element_type=jnp.float32
    )
    grad_normed_part = jnp.einsum(
        "tc,dc->td", grad_gate, w_gate, preferred_element_type=jnp.float32
    ) + jnp.einsum("tc,dc->td", grad_up, w_up, preferred_element_type=jnp.float32)
    second_normalized_gradient = lax.psum(grad_normed_part.astype(jnp.bfloat16), "tp").astype(
        jnp.float32
    )
    second_gain_gradient = jnp.sum(second_normalized_gradient * second_unit_rows, axis=0)
    grad_middle = grad_out + norm_backward_step(
        second_normalized_gradient,
        second_unit_rows,
        second_inverse_scale,
        second_norm_gain.astype(jnp.float32),
    )
    mlp_grads = (
        lax.psum_scatter(grad_w_gate, ("dp", "ctx"), scatter_dimension=0, tiled=True),
        lax.psum_scatter(grad_w_up, ("dp", "ctx"), scatter_dimension=0, tiled=True),
        lax.psum_scatter(grad_w_down, ("dp", "ctx"), scatter_dimension=0, tiled=True),
        lax.psum_scatter(second_gain_gradient, ("dp", "ctx"), scatter_dimension=0, tiled=True),
    )
    grad_branch_one = grad_middle.astype(jnp.bfloat16)
    grad_w_out = jnp.einsum(
        "td,tc->dc", grad_branch_one, heads_out, preferred_element_type=jnp.float32
    )
    grad_heads_low = jnp.dot(grad_branch_one, w_out, preferred_element_type=jnp.float32).astype(
        jnp.bfloat16
    )
    grad_mixed = (
        lax.optimization_barrier(grad_heads_low).astype(jnp.float32).reshape(tokens, head_count, DV)
    )
    numer_low = (grad_mixed / denominator[:, :, None]).astype(jnp.bfloat16)
    grad_numer = lax.optimization_barrier(numer_low).astype(jnp.float32)
    grad_denom = -jnp.sum(grad_mixed * mixed_heads, axis=2) / denominator
    grad_weights = (
        jnp.einsum("thd,shd->hts", numer_low, value_heads, preferred_element_type=jnp.float32)
        + grad_denom.T[:, :, None]
    )
    grad_scores = (grad_weights * visible * (1.0 + scores)).astype(jnp.bfloat16)
    grad_value = jnp.einsum("hts,thd->shd", weights, numer_low, preferred_element_type=jnp.float32)
    grad_query = jnp.einsum(
        "hts,shf->thf", grad_scores, key_heads, preferred_element_type=jnp.float32
    ) * F ** (-0.5)
    grad_key = jnp.einsum(
        "hts,thf->shf", grad_scores, queries, preferred_element_type=jnp.float32
    ) * F ** (-0.5)
    grad_feat_q = inherit[:, None, None] * (
        jnp.einsum("thd,hfd->thf", grad_numer, prior_state, precision=PRECISE)
        + grad_denom[:, :, None] * prior_total[None]
    )
    carried_state = jnp.einsum(
        "thf,thd->hfd", feat_q * inherit[:, None, None], grad_numer, precision=PRECISE
    )
    carried_total = jnp.sum(feat_q * (inherit[:, None] * grad_denom)[:, :, None], axis=0)
    starting = segment[0]
    later_state, later_total, after_seg = prefix(
        (carried_state, carried_total, starting), "ctx", join_states, empty_state, True
    )
    reached = (segment == after_seg).astype(jnp.float32)[:, None, None]
    grad_feat_k = reached * (
        jnp.einsum("hfd,thd->thf", later_state, value_float, precision=PRECISE) + later_total[None]
    )
    grad_value = grad_value + reached * jnp.einsum(
        "thf,hfd->thd", feat_k, later_state, precision=PRECISE
    )
    grad_query = grad_query + taylor_back(query_float, grad_feat_q)
    grad_key = grad_key + taylor_back(key_float, grad_feat_k)
    grad_query_low = grad_query.reshape(tokens, head_count * F).astype(jnp.bfloat16)
    grad_key_low = grad_key.reshape(tokens, head_count * F).astype(jnp.bfloat16)
    grad_value_low = grad_value.reshape(tokens, head_count * DV).astype(jnp.bfloat16)
    grad_w_query = jnp.einsum(
        "td,tc->dc", first_normalized, grad_query_low, preferred_element_type=jnp.float32
    )
    grad_w_key = jnp.einsum(
        "td,tc->dc", first_normalized, grad_key_low, preferred_element_type=jnp.float32
    )
    grad_w_value = jnp.einsum(
        "td,tc->dc", first_normalized, grad_value_low, preferred_element_type=jnp.float32
    )
    grad_normed_sum = (
        jnp.einsum("tc,dc->td", grad_query_low, w_query, preferred_element_type=jnp.float32)
        + jnp.einsum("tc,dc->td", grad_key_low, w_key, preferred_element_type=jnp.float32)
        + jnp.einsum("tc,dc->td", grad_value_low, w_value, preferred_element_type=jnp.float32)
    )
    first_normalized_gradient = lax.psum(grad_normed_sum.astype(jnp.bfloat16), "tp").astype(
        jnp.float32
    )
    first_gain_gradient = jnp.sum(first_normalized_gradient * first_unit_rows, axis=0)
    grad_inputs = grad_middle + norm_backward_step(
        first_normalized_gradient,
        first_unit_rows,
        first_inverse_scale,
        first_norm_gain.astype(jnp.float32),
    )
    attn_grads = (
        lax.psum_scatter(grad_w_query, ("dp", "ctx"), scatter_dimension=0, tiled=True),
        lax.psum_scatter(grad_w_key, ("dp", "ctx"), scatter_dimension=0, tiled=True),
        lax.psum_scatter(grad_w_value, ("dp", "ctx"), scatter_dimension=0, tiled=True),
        lax.psum_scatter(grad_w_out, ("dp", "ctx"), scatter_dimension=0, tiled=True),
        lax.psum_scatter(first_gain_gradient, ("dp", "ctx"), scatter_dimension=0, tiled=True),
    )
    return (
        final_out.astype(jnp.bfloat16)[None],
        grad_inputs[None],
        attn_grads[0],
        attn_grads[1],
        attn_grads[2],
        attn_grads[3],
        mlp_grads[0],
        mlp_grads[1],
        mlp_grads[2],
        attn_grads[4],
        mlp_grads[3],
    )


BLOCK = 512


MESH = pl.DeviceIdType.MESH
BF16, F32 = jnp.bfloat16, jnp.float32


def dot(a, b, ca, cb):
    return lax.dot_general(a, b, (((ca,), (cb,)), ((), ())), preferred_element_type=F32)


def place_of():
    return lax.axis_index("dp"), lax.axis_index("ctx"), lax.axis_index("tp")


def beside(c, across):
    x, y = lax.rem(c, 2), lax.div(c, 2)
    return lax.rem(x + across % 2, 2) + 2 * lax.rem(y + across // 2, 2)


def say(devices):
    barrier = pltpu.get_barrier_semaphore()
    for device in devices:
        pl.semaphore_signal(barrier, inc=1, device_id=device, device_id_type=MESH)


def hear(count):
    pl.semaphore_wait(pltpu.get_barrier_semaphore(), count)


def greet(devices):
    say(devices)
    hear(len(devices))


def around():
    d, c, t = place_of()
    return [(d, beside(c, 1), t), (d, beside(c, 2), t), (d, c, 1 - t)]


def remote(source, target, send, receive, k, device):
    return pltpu.make_async_remote_copy(
        src_ref=source,
        dst_ref=target,
        send_sem=send.at[k],
        recv_sem=receive.at[k],
        device_id=device,
        device_id_type=MESH,
    )


def gather_steps(buf, send, receive):
    d, c, t = place_of()
    own = buf.shape[0] // 8
    half = own // 2

    def part(across, core, h):
        block = c if across == 0 else beside(c, across)
        start = (2 * block + core) * own + h * half
        return buf.at[pl.ds(pl.multiple_of(start, half), half)]

    def put(k, across, h, device):
        ref = part(across, t, h)
        copy = remote(ref, ref, send, receive, k, device)
        copy.start()
        return copy

    return put, part


def gather_begin(buf, send, receive):
    put, _ = gather_steps(buf, send, receive)
    to_x, to_y, to_t = around()
    return [
        put(0, 0, 0, to_x),
        put(1, 0, 1, to_y),
        put(2, 0, 1, to_x),
        put(3, 0, 0, to_y),
        put(6, 0, 0, to_t),
        put(7, 0, 1, to_t),
    ]


def gather_rows(
    buf, out, send, receive, store, piece=None, early=None, middle=None, late=None, begun=None
):
    d, c, t = place_of()
    own = buf.shape[0] // 8
    to_x, to_y, to_t = around()
    put, part = gather_steps(buf, send, receive)
    started = gather_begin(buf, send, receive) if begun is None else begun

    def got(k, across, core, h):
        ref = part(across, core, h)
        remote(ref, ref, send, receive, k, to_t).wait_recv()

    stored = []

    def work(across, core):
        block = c if across == 0 else beside(c, across)
        start = pl.multiple_of((2 * block + core) * own, own)
        rows = pl.ds(start, own)
        copy = pltpu.make_async_copy(buf.at[rows], out.at[rows], store.at[len(stored)])
        copy.start()
        stored.append(copy)
        if piece is not None:
            piece(start)

    if early is not None:
        early()
    work(0, t)
    got(6, 0, 1 - t, 0)
    got(7, 0, 1 - t, 1)
    work(0, 1 - t)
    got(0, 1, t, 0)
    started.append(put(4, 1, 0, to_y))
    started.append(put(8, 1, 0, to_t))
    got(1, 2, t, 1)
    started.append(put(5, 2, 1, to_x))
    started.append(put(9, 2, 1, to_t))
    if middle is not None:
        middle()
    got(2, 1, t, 1)
    started.append(put(10, 1, 1, to_t))
    got(3, 2, t, 0)
    started.append(put(11, 2, 0, to_t))
    if late is not None:
        late()
    work(1, t)
    work(2, t)
    got(8, 1, 1 - t, 0)
    got(10, 1, 1 - t, 1)
    work(1, 1 - t)
    got(9, 2, 1 - t, 1)
    got(11, 2, 1 - t, 0)
    work(2, 1 - t)
    got(4, 3, t, 0)
    started.append(put(12, 3, 0, to_t))
    got(5, 3, t, 1)
    started.append(put(13, 3, 1, to_t))
    work(3, t)
    got(12, 3, 1 - t, 0)
    got(13, 3, 1 - t, 1)
    work(3, 1 - t)
    for copy in started:
        copy.wait_send()
    for copy in stored:
        copy.wait()


GATHER_COPIES = 14


def gather_scratch(tokens, width):
    return (
        [pltpu.VMEM((tokens, width), BF16)]
        + sems(GATHER_COPIES)
        + [pltpu.SemaphoreType.DMA((8,))]
    )


def exchange(jobs, held, send, receive, local):
    d, c, t = place_of()

    def rows_of(block):
        return pl.ds(pl.multiple_of(block * held, held), held)

    def to_block(n, k):
        source, target = jobs[n]
        return remote(
            source.at[rows_of(beside(c, k))], target.at[c], send, receive, 3 * n + k - 1,
            (d, beside(c, k), t),
        )

    def from_block(n, k):
        there = jobs[n][1].at[beside(c, k)]
        return remote(there, there, send, receive, 3 * n + k - 1, (d, beside(c, k), t))

    def at_home(n):
        source, target = jobs[n]
        return pltpu.make_async_copy(source.at[rows_of(c)], target.at[c], local.at[n])

    def hand_on(n):
        for k in (3, 1, 2):
            to_block(n, k).start()
        at_home(n).start()

    def landed(n):
        at_home(n).wait()
        for k in (1, 2, 3):
            from_block(n, k).wait_recv()
            to_block(n, k).wait_send()

    return hand_on, landed


def scatter_order(i):
    c = lax.axis_index("ctx")
    across = 3 - i
    x, y = lax.rem(c, 2), lax.div(c, 2)
    return lax.rem(x + lax.rem(across, 2), 2) + 2 * lax.rem(y + lax.div(across, 2), 2)


def scatter_rows(terms, bufs, send, receive, enter, fill=None):
    to_core, from_core, kept, over, came, stage = bufs
    d, c, t = place_of()
    own, tile = kept.shape[2:]
    half = own // 2
    to_x, to_y, to_t = (d, beside(c, 1), t), (d, beside(c, 2), t), (d, c, 1 - t)

    def link(k, n):
        return remote(
            over.at[k, n], came.at[k, n], send, receive, 8 + 2 * k + n, to_x if k % 2 == 0 else to_y
        )

    def core(i, n):
        return remote(to_core.at[lax.rem(i, 2), n], from_core.at[i, n], send, receive, 2 * i + n, to_t)

    def total(i, h, n, *extra):
        out = kept[i % 3, n, pl.ds(h * half, half), :]
        for k in extra:
            out = out + came[k, n].astype(F32)
        return out

    def go(k, i, h, n, *extra):
        over[k, n] = total(i, h, n, *extra).astype(BF16)
        link(k, n).start()

    def joined(i, n):
        core(i, n).wait_recv()
        kept[lax.rem(i, 3), n] = kept[lax.rem(i, 3), n] + from_core[i, n].astype(F32)

    def product(pairs, i, n):
        columns = pl.ds(n * tile, tile)
        theirs = pl.ds(pl.multiple_of((1 - t) * own, own), own)
        mine = pl.ds(pl.multiple_of(t * own, own), own)
        if not isinstance(pairs, list):
            to_core[lax.rem(i, 2), n] = pairs[theirs, columns]
            kept[lax.rem(i, 3), n] = pairs[mine, columns].astype(F32)
            return
        out = None
        for rows, matrix, part in pairs:
            term = dot(rows, matrix[columns, part], 1, 1)
            out = term if out is None else out + term
        stage[...] = out
        to_core[lax.rem(i, 2), n] = stage[theirs, :].astype(BF16)
        kept[lax.rem(i, 3), n] = stage[mine, :]

    def begin(i):
        return pl.multiple_of(2 * scatter_order(i) * own, 2 * own)

    pairs = terms(0, begin(0))
    product(pairs, 0, 0)
    enter()
    core(0, 0).start()
    product(pairs, 0, 1)
    core(0, 1).start()
    for n in (0, 1):
        joined(0, n)
        go(0, 0, 0, n)
        go(1, 0, 1, n)

    def step(i, carry):
        pairs = terms(i, begin(i))

        @pl.when(i >= 2)
        def _():
            for n in (0, 1):
                core(i - 2, n).wait_send()

        for n in (0, 1):
            product(pairs, i, n)
            core(i, n).start()

        @pl.when(i == 2)
        def _():
            for n in (0, 1):
                joined(1, n)
                go(3, 1, 1, n)

        return carry

    lax.fori_loop(1, 4, step, 0)
    for n in (0, 1):
        joined(2, n)
        go(2, 2, 0, n)
    if fill is not None:
        fill(0)
    for n in (0, 1):
        link(0, n).wait_recv()
        link(1, n).wait_recv()
        go(4, 2, 1, n, 1)
        go(5, 1, 0, n, 0)
    for n in (0, 1):
        joined(3, n)
    if fill is not None:
        fill(1)
    for n in (0, 1):
        for k in (2, 3, 4, 5):
            link(k, n).wait_recv()
        core(2, n).wait_send()
        core(3, n).wait_send()
        for k in range(6):
            link(k, n).wait_send()
    return jnp.concatenate(
        [
            jnp.concatenate([total(3, 0, n, 2, 5), total(3, 1, n, 3, 4)], axis=0)
            for n in (0, 1)
        ],
        axis=1,
    )


SCATTER_COPIES = 20


def scatter_scratch(own, width):
    tile = width // 2
    return [
        pltpu.VMEM((2, 2, own, tile), BF16),
        pltpu.VMEM((4, 2, own, tile), BF16),
        pltpu.VMEM((3, 2, own, tile), F32),
        pltpu.VMEM((6, 2, own // 2, tile), BF16),
        pltpu.VMEM((6, 2, own // 2, tile), BF16),
        pltpu.VMEM((2 * own, tile), F32),
    ]


def norm_parts(rows):
    scale = lax.rsqrt(jnp.mean(rows * rows, axis=1, keepdims=True) + EPSILON)
    return scale, rows * scale


def norm_back(e, hat, scale):
    return scale * (e - hat * jnp.mean(e * hat, axis=1, keepdims=True))


def call(kernel, name, collective, arrays, out_shape, scratch, spaces=None, out_spaces=None, flops=0):
    vmem = pl.BlockSpec(memory_space=pltpu.VMEM)
    moved = sum(a.size * a.dtype.itemsize for a in arrays)
    return pl.pallas_call(
        kernel,
        in_specs=spaces or [vmem] * len(arrays),
        out_specs=out_spaces or [vmem] * len(out_shape),
        out_shape=out_shape,
        scratch_shapes=scratch,
        compiler_params=pltpu.CompilerParams(
            collective_id=collective, has_side_effects=True, vmem_limit_bytes=VMEM_MOST
        ),
        cost_estimate=pl.CostEstimate(flops=flops, bytes_accessed=moved, transcendentals=0),
        name=name,
    )(*arrays)


def sems(count):
    return [pltpu.SemaphoreType.DMA((count,)), pltpu.SemaphoreType.DMA((count,))]


def depth(d, k):
    return lax.rem(d + k, lax.axis_size("dp"))


def columns(ref, gain, start, count):
    low = start // 128 * 128
    high = -(-(start + count) // 128) * 128
    value = ref[:, low:high].astype(F32)
    if gain is not None:
        value = value * gain
    return value[:, start - low : start - low + count]


def whole_tiles(count):
    return -(-count // 128) * 128


def front(x, seg, weights, gains, tokens, heads):
    width = x.shape[1]
    own = tokens // 8
    deep = lax.axis_size("dp")
    held, units = weights[4].shape[0], weights[4].shape[1] // 4
    wide, narrow = heads * DV, heads * F
    main = units // 128 * 128
    packed = 2 * wide + 2 * narrow
    part_width = width // 2
    filled = whole_tiles(units)
    line = {
        0: (((0, 2),), ((0, 1),), ()),
        1: (((1, 0),), ((1, 2), (1, 3)), ((3, 0),)),
        2: (((2, 3),), ((2, 1), (2, 0)), ((0, 3),)),
        3: (((3, 1),), ((3, 2),), ()),
    }
    if deep != 4:
        line = {
            p: (tuple((p, to) for to in range(deep) if to != p), (), ()) for p in range(deep)
        }

    def kernel(
        x_ref, seg_ref, q_ref, k_ref, v_ref, o_ref, g_ref, u_ref, d_ref, one_ref, two_ref,
        rows_out, own_ref, segs_ref, wa_out, wg_out, wd_out,
        cut_a, cut_g, cut_d, rows_ref, send, receive, store, small_send, small_receive, deep_send, deep_receive, here,
    ):
        d, c, t = place_of()
        jobs = (
            (lambda block: cut_a.at[block], lambda block: wa_out.at[d, block]),
            (lambda block: seg_ref.at[0], lambda block: segs_ref.at[block]),
            (lambda block: cut_g.at[block], lambda block: wg_out.at[block]),
            (lambda block: cut_d.at[block], lambda block: wd_out.at[block]),
        )

        def local(n):
            return pltpu.make_async_copy(jobs[n][0](c), jobs[n][1](c), here.at[n])

        def out(n, k):
            return remote(
                jobs[n][0](beside(c, k)), jobs[n][1](c), small_send, small_receive,
                3 * n + k - 1, (d, beside(c, k), t),
            )

        def arrival(n, k):
            block = beside(c, k)
            return remote(
                jobs[n][0](block), jobs[n][1](block), small_send, small_receive,
                3 * n + k - 1, (d, block, t),
            )

        def shard(slot, s, to):
            return pltpu.make_async_remote_copy(
                src_ref=wa_out.at[s], dst_ref=wa_out.at[s], send_sem=deep_send.at[slot],
                recv_sem=deep_receive.at[s], device_id=(to, c, t), device_id_type=MESH,
            )

        def in_plane(act):
            for p in range(deep):
                pl.when(d == p)(functools.partial(act, p, *line[p]))

        def first_shards(p, first, then, on):
            for slot, (s, to) in enumerate(first):
                shard(slot, s, to).start()

        def other_shards(p, first, then, on):
            for slot, (s, to) in enumerate(then):
                shard(len(first) + slot, s, to).start()
            for slot, (s, to) in enumerate(on):
                shard(len(first) + len(then) + slot, s, to).wait_recv()
                shard(len(first) + len(then) + slot, s, to).start()

        def end_shards(p, first, then, on):
            for s in range(deep):
                if s != p and s not in [handed for handed, _ in on]:
                    shard(0, s, (p + 1) % deep).wait_recv()
            for slot, (s, to) in enumerate(first + then + on):
                shard(slot, s, to).wait_send()

        one, two = one_ref[...], two_ref[...]
        met = (
            [(d, beside(c, k), t) for k in (1, 2, 3)]
            + [(d, c, 1 - t)]
            + [(depth(d, k), c, t) for k in range(1, deep)]
        )
        say(met)
        for b in range(4):
            cut_a[b, :, :wide] = columns(v_ref, one, b * wide, wide).astype(BF16)
            cut_a[b, :, wide : 2 * wide] = o_ref[:, b * wide : (b + 1) * wide]
            cut_a[b, :, 2 * wide :] = jnp.concatenate(
                [columns(ref, one, b * narrow, narrow) for ref in (q_ref, k_ref)], axis=1
            ).astype(BF16)
        hear(len(met))
        local(0).start()
        for k in (3, 1, 2):
            out(0, k).start()
        mine = pl.multiple_of((2 * c + t) * own, own)
        _, hat = norm_parts(x_ref[pl.ds(pl.multiple_of(t * own, own), own), :].astype(F32))
        rows_ref[pl.ds(mine, own), :] = hat[:, :part_width].astype(BF16)
        own_ref[...] = hat[:, part_width:].astype(BF16)
        local(0).wait()
        for k in (1, 2, 3):
            arrival(0, k).wait_recv()
        in_plane(first_shards)

        def early():
            for b in range(4):
                start = b * units
                cut_g[b, :, :main] = columns(g_ref, two, start, main).astype(BF16)
                cut_g[b, :, main : 2 * main] = columns(u_ref, two, start, main).astype(BF16)
                if main < units:
                    cut_g[b, :, 2 * main :] = jnp.concatenate(
                        [columns(r, two, start + main, units - main) for r in (g_ref, u_ref)],
                        axis=1,
                    ).astype(BF16)

            for n in (1, 2):
                local(n).start()
                for k in (3, 1, 2):
                    out(n, k).start()
            for b in range(4):
                part = columns(d_ref, None, b * units, units)
                if units < filled:
                    part = jnp.concatenate([part, jnp.zeros((held, filled - units), F32)], axis=1)
                cut_d[b] = part.astype(BF16)
            local(3).start()
            for k in (3, 1, 2):
                out(3, k).start()

        gather_rows(
            rows_ref, rows_out, send, receive, store, early=early,
            middle=lambda: in_plane(other_shards),
        )
        for n in (1, 2, 3):
            local(n).wait()
            for k in (1, 2, 3):
                arrival(n, k).wait_recv()
        in_plane(end_shards)
        for n in range(4):
            for k in (1, 2, 3):
                out(n, k).wait_send()

    vmem, hbm = pl.BlockSpec(memory_space=pltpu.VMEM), pl.BlockSpec(memory_space=pl.ANY)
    return call(
        kernel,
        "front",
        1,
        (x, seg[None]) + tuple(weights) + tuple(gains),
        [
            jax.ShapeDtypeStruct((tokens, part_width), BF16),
            jax.ShapeDtypeStruct((own, part_width), BF16),
            jax.ShapeDtypeStruct((4,) + seg.shape, seg.dtype),
            jax.ShapeDtypeStruct((deep, 4, held, packed), BF16),
            jax.ShapeDtypeStruct((4, held, 2 * units), BF16),
            jax.ShapeDtypeStruct((4, held, filled), BF16),
        ],
        [
            pltpu.VMEM((4, held, packed), BF16),
            pltpu.VMEM((4, held, 2 * units), BF16),
            pltpu.VMEM((4, held, filled), BF16),
        ]
        + gather_scratch(tokens, part_width) + sems(12) + sems(deep) + [pltpu.SemaphoreType.DMA((4,))],
        [vmem, hbm] + [vmem] * 9,
        [hbm, vmem, hbm, hbm, hbm, hbm],
    )


def apart(tokens):
    return (tokens // 2 - 2) // BLOCK + 2


def first_seen(i, tokens):
    return jnp.maximum(i - apart(tokens) + 1, 0)


def attend_back(
    qkv, g_mixed, mixed, denom, seg_rows, seg_cols, branch, heads_out, out_terms, middle, sum_down, heads
):
    tokens, width = branch.shape
    wide, narrow = heads * DV, heads * F
    blocks = tokens // BLOCK
    deep = lax.axis_size("dp")
    group = width // deep
    own = tokens // 8
    held, units = sum_down.shape[0] // 4, sum_down.shape[1]

    def kernel(
        x_ref, gm_ref, m_ref, d_ref, row_ref, col_ref, br_ref, h_ref, term_ref, mid_ref, down_ref,
        g_ref, out_ref, go_ref, gd_ref,
        gq_ref, numer_ref, gden_ref, key_ref, back_ref, came, br_buf, load, send, receive,
        term_buf, term_load, sums, parts_o, parts_d, p_send, p_receive, local, *rest,
    ):
        bufs, (s_send, s_receive, t_send, t_receive) = rest[:6], rest[6:]
        d, c, t = place_of()
        hand_on, landed = exchange(
            ((sums, parts_o), (down_ref, parts_d)), held, p_send, p_receive, local
        )

        def fetch_terms(i):
            part = pl.ds(pl.multiple_of(2 * scatter_order(i) * own, 2 * own), 2 * own)
            slot = lax.rem(i, 2)
            return pltpu.make_async_copy(term_ref.at[part], term_buf.at[slot], term_load.at[slot])

        fetch_terms(0).start()

        def fetch(n):
            part = pl.ds(pl.multiple_of(depth(d, n + 1) * group, group), group)
            slot = lax.rem(n, 2)
            return pltpu.make_async_copy(br_ref.at[:, part], br_buf.at[slot], load.at[slot])

        def deeper(n):
            return remote(
                back_ref.at[n], came.at[n], send, receive, n, (depth(d, n + 1), c, t)
            )

        fetch(0).start()
        met = (
            around()
            + [(d, beside(c, 3), t)]
            + [(depth(d, k), c, t) for k in range(1, deep)]
        )
        say(met)

        def plane(n, carry):
            @pl.when(n < deep - 1)
            def _():
                fetch(n + 1).start()

            fetch(n).wait()
            back_ref[n] = dot(br_buf[lax.rem(n, 2)], h_ref[...], 0, 0).astype(BF16)

            @pl.when(n < deep - 1)
            def _():
                deeper(n).start()

            return carry

        def prepare():
            gq_ref[...] = jnp.zeros_like(gq_ref)
            for h in range(heads):
                part = pl.ds(h * DV, DV)
                gm = gm_ref[:, part].astype(F32)
                inverse = 1.0 / d_ref[:, h : h + 1]
                numer_ref[:, part] = (gm * inverse).astype(BF16)
                down = -jnp.sum(gm * m_ref[:, part], axis=1, keepdims=True) * inverse
                gden_ref[h : h + 1, :] = jnp.transpose(
                    jnp.broadcast_to(down, (tokens, 128)), (1, 0)
                )[:1]
            key_ref[...] = jnp.transpose(
                x_ref[:, wide : wide + 2 * narrow].astype(F32), (1, 0)
            ).astype(BF16)

        place = lax.broadcasted_iota(jnp.int32, (BLOCK, BLOCK), 1) - lax.broadcasted_iota(
            jnp.int32, (BLOCK, BLOCK), 0
        )
        tempered = BF16(F**-0.5)

        def one_block(j):
            start = pl.multiple_of(j * BLOCK, BLOCK)
            ids = row_ref[pl.ds(start, BLOCK), :]
            values = [x_ref[pl.ds(start, BLOCK), h * DV : (h + 1) * DV] for h in range(heads)]
            keys = [
                x_ref[pl.ds(start, BLOCK), wide + (heads + h) * F : wide + (heads + h + 1) * F]
                * tempered
                for h in range(heads)
            ]
            across = [
                key_ref[(heads + h) * F : (heads + h + 1) * F, pl.ds(start, BLOCK)] * tempered
                for h in range(heads)
            ]

            def step(i, sums):
                base = pl.multiple_of(i * BLOCK, BLOCK)
                visible = (place >= start - base) & (ids == col_ref[:, pl.ds(base, BLOCK)])
                out = []
                for h in range(heads):
                    queries = x_ref[pl.ds(base, BLOCK), wide + h * F : wide + (h + 1) * F]
                    numer = numer_ref[pl.ds(base, BLOCK), h * DV : (h + 1) * DV]
                    s = dot(keys[h], queries, 1, 1)
                    a = jnp.where(visible, (0.5 * s + 1.0) * s + 1.0, 0.0).astype(BF16)
                    ga = dot(values[h], numer, 1, 1) + gden_ref[h : h + 1, pl.ds(base, BLOCK)]
                    gs = jnp.where(visible, ga * (1.0 + s), 0.0).astype(BF16)
                    gq_ref[h * F : (h + 1) * F, pl.ds(base, BLOCK)] += dot(across[h], gs, 1, 0)
                    out += [sums[2 * h] + dot(a, numer, 1, 0), sums[2 * h + 1] + dot(gs, queries, 1, 0)]
                return tuple(out)

            zeros = []
            for h in range(heads):
                zeros += [jnp.zeros((BLOCK, DV), F32), jnp.zeros((BLOCK, F), F32)]
            sums = lax.fori_loop(
                j, jnp.minimum(j + apart(tokens), blocks), step, tuple(zeros)
            )
            for h in range(heads):
                g_ref[pl.ds(start, BLOCK), h * DV : (h + 1) * DV] = sums[2 * h].astype(BF16)
                g_ref[
                    pl.ds(start, BLOCK), wide + (heads + h) * F : wide + (heads + h + 1) * F
                ] = (sums[2 * h + 1] * F**-0.5).astype(BF16)

        def terms(i, start):
            fetch_terms(i).wait()

            @pl.when(i < 3)
            def _():
                fetch_terms(i + 1).start()

            return term_buf.at[lax.rem(i, 2)]

        def fill(n):
            if n == 0:
                lax.fori_loop(0, deep, plane, 0)
                hand_on(1)
                prepare()
                pl.loop(0, 1)(one_block)
            else:
                pl.loop(1, blocks)(one_block)

        moved = scatter_rows(terms, bufs, s_send, s_receive, lambda: hear(len(met)), fill)
        here = out_ref.at[pl.ds(pl.multiple_of(t * own, own), own)]
        here[...] = (mid_ref[...] + moved).astype(BF16)
        copy = remote(here, here, t_send, t_receive, 0, (d, c, 1 - t))
        copy.start()
        g_ref[:, wide : wide + narrow] = jnp.transpose(gq_ref[...], (1, 0)).astype(BF16)
        total = back_ref[deep - 1].astype(F32)
        for n in range(deep - 1):
            deeper(n).wait_recv()
            total = total + came[n].astype(F32)
        sums[...] = total.astype(BF16)
        hand_on(0)
        landed(1)
        for b in range(4):
            gd_ref[:, b * units : (b + 1) * units] = parts_d[b].astype(F32)
        landed(0)
        for b in range(4):
            go_ref[:, b * wide : (b + 1) * wide] = parts_o[b].astype(F32)
        for n in range(deep - 1):
            deeper(n).wait_send()
        copy.wait_send()
        there = out_ref.at[pl.ds(pl.multiple_of((1 - t) * own, own), own)]
        remote(there, there, t_send, t_receive, 0, (d, c, 1 - t)).wait_recv()

    vmem, hbm = pl.BlockSpec(memory_space=pltpu.VMEM), pl.BlockSpec(memory_space=pl.ANY)
    return call(
        kernel, "attend_back", 7,
        (
            qkv, g_mixed, mixed, denom, seg_rows, seg_cols, branch, heads_out, out_terms, middle,
            sum_down,
        ),
        [
            jax.ShapeDtypeStruct(qkv.shape, BF16),
            jax.ShapeDtypeStruct((2 * own, width), BF16),
            jax.ShapeDtypeStruct((held, 4 * wide), F32),
            jax.ShapeDtypeStruct((held, 4 * units), F32),
        ],
        [
            pltpu.VMEM((narrow, tokens), F32),
            pltpu.VMEM((tokens, wide), BF16),
            pltpu.VMEM((8, tokens), F32),
            pltpu.VMEM((2 * narrow, tokens), BF16),
            pltpu.VMEM((deep, group, wide), BF16),
            pltpu.VMEM((deep - 1, group, wide), BF16),
            pltpu.VMEM((2, tokens, group), BF16),
            pltpu.SemaphoreType.DMA((2,)),
        ]
        + sems(deep - 1)
        + [pltpu.VMEM((2, 2 * own, width), BF16), pltpu.SemaphoreType.DMA((2,))]
        + [
            pltpu.VMEM((group, wide), BF16),
            pltpu.VMEM((4, held, wide), BF16),
            pltpu.VMEM((4, held, units), BF16),
        ]
        + sems(6) + [pltpu.SemaphoreType.DMA((2,))]
        + scatter_scratch(own, width) + sems(SCATTER_COPIES) + sems(1),
        [vmem] * 6 + [hbm, vmem, hbm, vmem, hbm],
    )


def attend_block(i, x_ref, ext_ref, row_ref, col_ref, mixed_ref, denom_ref, low_ref, heads):
    wide = heads * DV
    base = pl.multiple_of(i * BLOCK, BLOCK)
    own = row_ref[pl.ds(base, BLOCK), :]
    place = lax.broadcasted_iota(jnp.int32, (BLOCK, BLOCK), 0) - lax.broadcasted_iota(
        jnp.int32, (BLOCK, BLOCK), 1
    )
    queries = [
        x_ref[pl.ds(base, BLOCK), wide + h * F : wide + (h + 1) * F] * jnp.bfloat16(F**-0.5)
        for h in range(heads)
    ]

    def step(j, sums):
        start = pl.multiple_of(j * BLOCK, BLOCK)
        visible = (place >= start - base) & (own == col_ref[:, pl.ds(start, BLOCK)])
        out = []
        for h in range(heads):
            keys = x_ref[
                pl.ds(start, BLOCK), wide + (heads + h) * F : wide + (heads + h + 1) * F
            ]
            s = dot(queries[h], keys, 1, 1)
            a = jnp.where(visible, (0.5 * s + 1.0) * s + 1.0, 0.0).astype(BF16)
            out.append(
                sums[h] + dot(a, ext_ref[pl.ds(start, BLOCK), 2 * h * DV : (2 * h + 2) * DV], 1, 0)
            )
        return tuple(out)

    sums = lax.fori_loop(
        first_seen(i, x_ref.shape[0]),
        i + 1,
        step,
        tuple(jnp.zeros((BLOCK, 2 * DV), F32) for _ in range(heads)),
    )
    for h in range(heads):
        denom = sums[h][:, DV:]
        mixed = sums[h][:, :DV] / denom
        mixed_ref[pl.ds(base, BLOCK), h * DV : (h + 1) * DV] = mixed
        low_ref[pl.ds(base, BLOCK), h * DV : (h + 1) * DV] = mixed.astype(BF16)
        denom_ref[pl.ds(base, BLOCK), h : h + 1] = denom[:, :1]


def attend(rows_low, own_high, w_attn, seg_rows, seg_cols, cot, heads):
    tokens, part_width = rows_low.shape
    own = tokens // 8
    wide, narrow = heads * DV, heads * F

    def kernel(
        x_ref, own_ref, w_ref, row_ref, col_ref, cot_ref,
        qkv_ref, mixed_ref, denom_ref, low_ref, cot_out, rows_out,
        ext_ref, half_ref, here, x_buf, *rest,
    ):
        rows_ref, r_send, r_receive, r_store, cot_buf, c_send, c_receive, c_store = rest
        d, c, t = place_of()
        loaded = pltpu.make_async_copy(x_ref, x_buf, here.at[0])
        loaded.start()
        low_half = pltpu.make_async_copy(x_buf, rows_out.at[:, :part_width], here.at[1])

        met = around()
        say(met)
        mine = pl.ds(pl.multiple_of((2 * c + t) * own, own), own)
        rows_ref[mine, :] = own_ref[...]
        cot_buf[mine, :] = cot_ref[pl.ds(pl.multiple_of(t * own, own), own), :part_width]
        hear(len(met))

        def first_half():
            loaded.wait()

            @pl.loop(0, tokens // BLOCK)
            def _(n):
                rows = pl.ds(pl.multiple_of(n * BLOCK, BLOCK), BLOCK)
                half_ref[rows, :wide] = dot(x_buf[rows, :], w_ref[:part_width, :wide], 1, 0)
                half_ref[rows, wide:] = dot(x_buf[rows, :], w_ref[:part_width, 2 * wide :], 1, 0)

            low_half.start()

        def second_half(start):
            rows = pl.ds(start, own)
            values = (
                half_ref[rows, :wide] + dot(rows_ref[rows, :], w_ref[part_width:, :wide], 1, 0)
            ).astype(BF16)
            qkv_ref[rows, :wide] = values
            qkv_ref[rows, wide:] = (
                half_ref[rows, wide:] + dot(rows_ref[rows, :], w_ref[part_width:, 2 * wide :], 1, 0)
            ).astype(BF16)
            for h in range(heads):
                ext_ref[rows, 2 * h * DV : (2 * h + 1) * DV] = values[:, h * DV : (h + 1) * DV]
                ext_ref[rows, (2 * h + 1) * DV : (2 * h + 2) * DV] = jnp.ones((own, DV), BF16)

        begun = []

        def cot_begin():
            begun.extend(gather_begin(cot_buf, c_send, c_receive))

        gather_rows(
            rows_ref, rows_out.at[:, part_width:], r_send, r_receive, r_store, second_half, first_half,
            late=cot_begin,
        )

        def blocks(first, last):
            @pl.loop(first, last)
            def _(i):
                attend_block(
                    i, qkv_ref, ext_ref, row_ref, col_ref, mixed_ref, denom_ref, low_ref, heads
                )

        gather_rows(
            cot_buf, cot_out, c_send, c_receive, c_store, begun=begun,
            early=lambda: blocks(0, tokens // BLOCK // 2),
            middle=lambda: blocks(tokens // BLOCK // 2, tokens // BLOCK - 1),
            late=lambda: blocks(tokens // BLOCK - 1, tokens // BLOCK),
        )
        low_half.wait()

    vmem, hbm = pl.BlockSpec(memory_space=pltpu.VMEM), pl.BlockSpec(memory_space=pl.ANY)
    return call(
        kernel, "attend", 2, (rows_low, own_high, w_attn, seg_rows, seg_cols, cot),
        [
            jax.ShapeDtypeStruct((tokens, wide + 2 * narrow), BF16),
            jax.ShapeDtypeStruct((tokens, wide), F32),
            jax.ShapeDtypeStruct((tokens, heads), F32),
            jax.ShapeDtypeStruct((tokens, wide), BF16),
            jax.ShapeDtypeStruct((tokens, part_width), BF16),
            jax.ShapeDtypeStruct((tokens, 2 * part_width), BF16),
        ],
        [
            pltpu.VMEM((tokens, 2 * wide), BF16),
            pltpu.VMEM((tokens, wide + 2 * narrow), F32),
            pltpu.SemaphoreType.DMA((2,)),
            pltpu.VMEM((tokens, part_width), BF16),
        ]
        + gather_scratch(tokens, part_width) + gather_scratch(tokens, part_width),
        [hbm] + [vmem] * 5,
        [vmem] * 4 + [hbm] * 2,
    )


def to_middle(heads_out, w_attn, x):
    tokens, width = heads_out.shape[0], x.shape[1]
    own = tokens // 8
    wide = heads_out.shape[1]

    def kernel(h_ref, w_ref, x_ref, mid_ref, rows_out, *rest):
        bufs, (s_send, s_receive, rows_ref, g_send, g_receive, store) = rest[:6], rest[6:]
        d, c, t = place_of()
        say(around())

        def terms(i, start):
            return [(h_ref[pl.ds(start, 2 * own), :], w_ref, slice(wide, 2 * wide))]

        total = scatter_rows(terms, bufs, s_send, s_receive, lambda: hear(3))
        middle = total + x_ref[pl.ds(pl.multiple_of(t * own, own), own), :].astype(F32)
        mid_ref[...] = middle
        _, hat = norm_parts(middle)
        rows_ref[pl.ds(pl.multiple_of((2 * c + t) * own, own), own), :] = hat.astype(BF16)
        gather_rows(rows_ref, rows_out, g_send, g_receive, store)

    return call(
        kernel, "to_middle", 3, (heads_out, w_attn, x),
        [jax.ShapeDtypeStruct((own, width), F32), jax.ShapeDtypeStruct((tokens, width), BF16)],
        scatter_scratch(own, width) + sems(SCATTER_COPIES) + gather_scratch(tokens, width),
        None,
        [pl.BlockSpec(memory_space=pltpu.VMEM), pl.BlockSpec(memory_space=pl.ANY)],
        flops=2 * tokens * width * heads_out.shape[1],
    )


def gate_up(rows_two, w_both, cot, cot_low):
    tokens, width = rows_two.shape
    own = tokens // 8
    units = w_both.shape[1] // 2
    main = units // 128 * 128
    count = tokens // BLOCK
    tile = 256

    def kernel(
        x_ref, w_ref, cot_ref, low_ref, hid_out, slope_out, silu_out, rows_out, down_out,
        x_buf, w_buf, low_buf, hid_ref, slope_ref, silu_ref, down_buf, load, store, down_store,
        rows_ref, send, receive, row_store,
    ):
        d, c, t = place_of()

        def fetch(i):
            rows = pl.ds(pl.multiple_of(i * BLOCK, BLOCK), BLOCK)
            slot = lax.rem(i, 2)
            return pltpu.make_async_copy(x_ref.at[rows], x_buf.at[slot], load.at[slot])

        def given(i):
            rows = pl.ds(pl.multiple_of(i * BLOCK, BLOCK), BLOCK)
            slot = lax.rem(i, 2)
            return [
                pltpu.make_async_copy(source, target.at[rows], store.at[n, slot])
                for n, (source, target) in enumerate(
                    (
                        (hid_ref.at[rows], hid_out),
                        (slope_ref.at[slot], slope_out),
                        (silu_ref.at[slot], silu_out),
                    )
                )
            ]

        weights = pltpu.make_async_copy(w_ref, w_buf, load.at[2])
        weights.start()
        fetch(0).start()
        low_copy = pltpu.make_async_copy(low_ref, low_buf, load.at[3])
        low_copy.start()
        greet(around())
        mine = pl.multiple_of((2 * c + t) * own, own)
        rows_ref[pl.ds(mine, own), :] = cot_ref[
            pl.ds(pl.multiple_of(t * own, own), own), width // 2 :
        ]

        def blocks(first, last):
            @pl.loop(first, last)
            def _(i):
                slot = lax.rem(i, 2)

                @pl.when(i + 1 < count)
                def _():
                    fetch(i + 1).start()

                fetch(i).wait()
                both = dot(x_buf[slot], w_buf[...], 1, 0)

                @pl.when(i >= 2)
                def _():
                    for copy in given(i - 2):
                        copy.wait()

                def act(gate, up, part):
                    sig = jax.nn.sigmoid(gate)
                    silu = gate * sig
                    hid_ref[pl.ds(pl.multiple_of(i * BLOCK, BLOCK), BLOCK), part] = (
                        silu * up
                    ).astype(BF16)
                    slope_ref[slot, :, part] = (up * sig * (1.0 + gate * (1.0 - sig))).astype(BF16)
                    silu_ref[slot, :, part] = silu.astype(BF16)

                act(both[:, :main], both[:, main : 2 * main], slice(0, main))
                if main < units:
                    act(
                        both[:, 2 * main : main + units],
                        both[:, main + units :],
                        slice(main, units),
                    )
                for copy in given(i):
                    copy.start()

        per = width // 2 // tile

        def down_given(base, n):
            slot = lax.rem(n, 2)
            rows = pl.ds(pl.multiple_of(base + n * tile, tile), tile)
            return pltpu.make_async_copy(down_buf.at[slot], down_out.at[rows], down_store.at[slot])

        def down_tiles(source, base, end):
            @pl.loop(0, end)
            def _(n):
                @pl.when(n >= 2)
                def _():
                    down_given(base, n - 2).wait()

                part = pl.ds(pl.multiple_of(n * tile, tile), tile)
                down_buf[lax.rem(n, 2)] = dot(source[:, part], hid_ref[...], 0, 0).astype(BF16)
                down_given(base, n).start()

        def early():
            weights.wait()
            blocks(0, 1)

        def later():
            blocks(count // 2, count)
            low_copy.wait()
            down_tiles(low_buf, 0, per)
            for n in (per - 2, per - 1):
                down_given(0, n).wait()

        gather_rows(
            rows_ref, rows_out, send, receive, row_store, early=early,
            middle=lambda: blocks(1, count // 2), late=later,
        )
        down_tiles(rows_ref, width // 2, per)
        for n in (per - 2, per - 1):
            down_given(width // 2, n).wait()
        for i in (count - 2, count - 1):
            for copy in given(i):
                copy.wait()

    vmem, hbm = pl.BlockSpec(memory_space=pltpu.VMEM), pl.BlockSpec(memory_space=pl.ANY)
    return call(
        kernel, "gate_up", 8, (rows_two, w_both, cot, cot_low),
        [jax.ShapeDtypeStruct((tokens, units), BF16)] * 3
        + [
            jax.ShapeDtypeStruct((tokens, width // 2), BF16),
            jax.ShapeDtypeStruct((width, units), BF16),
        ],
        [
            pltpu.VMEM((2, BLOCK, width), BF16),
            pltpu.VMEM(w_both.shape, BF16),
            pltpu.VMEM(cot_low.shape, BF16),
            pltpu.VMEM((tokens, units), BF16),
            pltpu.VMEM((2, BLOCK, units), BF16),
            pltpu.VMEM((2, BLOCK, units), BF16),
            pltpu.VMEM((2, tile, units), BF16),
            pltpu.SemaphoreType.DMA((4,)),
            pltpu.SemaphoreType.DMA((3, 2)),
            pltpu.SemaphoreType.DMA((2,)),
        ]
        + gather_scratch(tokens, width // 2),
        [hbm, hbm, vmem, hbm],
        [hbm] * 5,
        flops=4 * tokens * width * units,
    )


def feed_forward(slope, silu, cot_low, cot_high, w_down, rows_two):
    tokens, width = rows_two.shape
    units = slope.shape[1]
    main = units // 128 * 128
    tile = 256
    part_width = width // 2
    count = tokens // BLOCK

    def kernel(
        slope_ref, silu_ref, low_ref, high_ref, d_ref, two_ref, g_out, grad_ref,
        slope_buf, silu_buf, low_buf, high_buf, d_buf, g_ref, here, g_store, cols, out, load, store,
    ):
        def rows(i):
            return pl.ds(pl.multiple_of(i * BLOCK, BLOCK), BLOCK)

        def fetch(i):
            slot = lax.rem(i, 2)
            return [
                pltpu.make_async_copy(source.at[rows(i)], target.at[slot], here.at[n, slot])
                for n, (source, target) in enumerate(
                    (
                        (low_ref, low_buf),
                        (high_ref, high_buf),
                        (slope_ref, slope_buf),
                        (silu_ref, silu_buf),
                    )
                )
            ]

        def g_given(i):
            return pltpu.make_async_copy(g_ref.at[rows(i)], g_out.at[rows(i)], g_store.at[i])

        def wanted(n):
            part = pl.ds(pl.multiple_of(n * tile, tile), tile)
            slot = lax.rem(n, 2)
            return pltpu.make_async_copy(two_ref.at[:, part], cols.at[slot], load.at[slot])

        def given(n):
            part = pl.ds(pl.multiple_of(n * tile, tile), tile)
            slot = lax.rem(n, 2)
            return pltpu.make_async_copy(out.at[slot], grad_ref.at[part], store.at[slot])

        weights = pltpu.make_async_copy(d_ref, d_buf, load.at[2])
        weights.start()
        for copy in fetch(0):
            copy.start()
        wanted(0).start()
        weights.wait()

        @pl.loop(0, count)
        def _(i):
            slot = lax.rem(i, 2)

            @pl.when(i + 1 < count)
            def _():
                for copy in fetch(i + 1):
                    copy.start()

            for copy in fetch(i):
                copy.wait()
            g_hidden = dot(low_buf[slot], d_buf[:part_width, :units], 1, 0) + dot(
                high_buf[slot], d_buf[part_width:, :units], 1, 0
            )
            gg = g_hidden * slope_buf[slot].astype(F32)
            gu = g_hidden * silu_buf[slot].astype(F32)
            part = rows(i)
            g_ref[part, :main] = gg[:, :main].astype(BF16)
            g_ref[part, main : 2 * main] = gu[:, :main].astype(BF16)
            if main < units:
                g_ref[part, 2 * main :] = jnp.concatenate(
                    [gg[:, main:], gu[:, main:]], axis=1
                ).astype(BF16)
            g_given(i).start()

        last = width // tile

        @pl.loop(0, last)
        def _(n):
            @pl.when(n + 1 < last)
            def _():
                wanted(n + 1).start()

            wanted(n).wait()

            @pl.when(n >= 2)
            def _():
                given(n - 2).wait()

            slot = lax.rem(n, 2)
            out[slot] = dot(cols[slot], g_ref[...], 0, 0).astype(BF16)
            given(n).start()

        given(last - 2).wait()
        given(last - 1).wait()
        for i in range(count):
            g_given(i).wait()

    hbm = pl.BlockSpec(memory_space=pl.ANY)
    moved = 2 * tokens * (2 * width + 4 * units) + 6 * width * units
    return pl.pallas_call(
        kernel,
        in_specs=[hbm] * 6,
        out_specs=[hbm] * 2,
        out_shape=[
            jax.ShapeDtypeStruct((tokens, 2 * units), BF16),
            jax.ShapeDtypeStruct((width, 2 * units), BF16),
        ],
        scratch_shapes=[
            pltpu.VMEM((2, BLOCK, units), BF16),
            pltpu.VMEM((2, BLOCK, units), BF16),
            pltpu.VMEM((2, BLOCK, part_width), BF16),
            pltpu.VMEM((2, BLOCK, part_width), BF16),
            pltpu.VMEM(w_down.shape, BF16),
            pltpu.VMEM((tokens, 2 * units), BF16),
            pltpu.SemaphoreType.DMA((4, 2)),
            pltpu.SemaphoreType.DMA((count,)),
            pltpu.VMEM((2, tokens, tile), BF16),
            pltpu.VMEM((2, tile, 2 * units), BF16),
            pltpu.SemaphoreType.DMA((3,)),
            pltpu.SemaphoreType.DMA((2,)),
        ],
        compiler_params=pltpu.CompilerParams(vmem_limit_bytes=VMEM_MOST),
        cost_estimate=pl.CostEstimate(
            flops=6 * tokens * width * units, bytes_accessed=moved, transcendentals=0
        ),
        name="feed_forward",
    )(slope, silu, cot_low, cot_high, w_down, rows_two)


def to_branch(g_both, w_both, middle, cot, w_attn, wide, hidden, w_down):
    tokens, width = g_both.shape[0], middle.shape[1]
    own = tokens // 8
    units = hidden.shape[1]
    tile = width // 2

    def kernel(
        g_ref, w_ref, mid_ref, cot_ref, o_ref, hid_ref, d_ref, gm_ref, rows_out, mix_ref, term_ref,
        g_buf, w_buf, hid_buf, d_buf, term_buf, load, term_store, *rest,
    ):
        bufs, (s_send, s_receive, rows_ref, g_send, g_receive, store) = rest[:6], rest[6:]
        d, c, t = place_of()

        def fetch(i):
            part = pl.ds(pl.multiple_of(2 * scatter_order(i) * own, 2 * own), 2 * own)
            slot = lax.rem(i, 2)
            return pltpu.make_async_copy(g_ref.at[part], g_buf.at[slot], load.at[slot])

        weights = pltpu.make_async_copy(w_ref, w_buf, load.at[2])
        weights.start()
        fetch(0).start()
        say(around())
        weights.wait()
        down = pltpu.make_async_copy(d_ref, d_buf, load.at[3])
        down.start()
        pltpu.make_async_copy(
            hid_ref.at[pl.ds(0, BLOCK)], hid_buf, load.at[4]
        ).start()

        def terms(i, start):
            fetch(i).wait()

            @pl.when(i < 3)
            def _():
                fetch(i + 1).start()

            return [(g_buf[lax.rem(i, 2)], w_buf, slice(None))]

        total = scatter_rows(terms, bufs, s_send, s_receive, lambda: hear(3))
        scale, hat = norm_parts(mid_ref[...])
        g_middle = cot_ref[pl.ds(pl.multiple_of(t * own, own), own), :].astype(F32) + norm_back(
            total, hat, scale
        )
        gm_ref[...] = g_middle
        rows_ref[pl.ds(pl.multiple_of((2 * c + t) * own, own), own), :] = g_middle.astype(BF16)

        def mix(start):
            mix_ref[pl.ds(start, own), :] = dot(
                rows_ref[pl.ds(start, own), :], o_ref[:, wide : 2 * wide], 1, 0
            ).astype(BF16)

        def block(i):
            return pl.ds(pl.multiple_of(i * BLOCK, BLOCK), BLOCK)

        def hidden_of(i):
            return pltpu.make_async_copy(hid_ref.at[block(i)], hid_buf, load.at[4])

        def term_given(i):
            return pltpu.make_async_copy(term_buf, term_ref.at[block(i)], term_store.at[0])

        def out_terms(first, last):
            @pl.loop(first, last)
            def _(i):
                hidden_of(i).wait()

                @pl.when(i > 0)
                def _():
                    term_given(i - 1).wait()

                for n in (0, 1):
                    columns = slice(n * tile, (n + 1) * tile)
                    term_buf[:, columns] = dot(
                        hid_buf[...], d_buf[columns, :units], 1, 1
                    ).astype(BF16)
                term_given(i).start()

                @pl.when(i + 1 < tokens // BLOCK)
                def _():
                    hidden_of(i + 1).start()

        down.wait()
        blocks = tokens // BLOCK
        gather_rows(
            rows_ref, rows_out, g_send, g_receive, store, mix,
            lambda: out_terms(0, blocks // 2),
            lambda: out_terms(blocks // 2, blocks - 1),
            lambda: out_terms(blocks - 1, blocks),
        )
        term_given(blocks - 1).wait()

    vmem, hbm = pl.BlockSpec(memory_space=pltpu.VMEM), pl.BlockSpec(memory_space=pl.ANY)
    return call(
        kernel, "to_branch", 5, (g_both, w_both, middle, cot, w_attn, hidden, w_down),
        [
            jax.ShapeDtypeStruct((own, width), F32),
            jax.ShapeDtypeStruct((tokens, width), BF16),
            jax.ShapeDtypeStruct((tokens, wide), BF16),
            jax.ShapeDtypeStruct((tokens, width), BF16),
        ],
        [
            pltpu.VMEM((2, 2 * own, g_both.shape[1]), BF16),
            pltpu.VMEM(w_both.shape, BF16),
            pltpu.VMEM((BLOCK, units), BF16),
            pltpu.VMEM(w_down.shape, BF16),
            pltpu.VMEM((BLOCK, width), BF16),
            pltpu.SemaphoreType.DMA((5,)),
            pltpu.SemaphoreType.DMA((1,)),
        ]
        + scatter_scratch(own, width) + sems(SCATTER_COPIES) + gather_scratch(tokens, width),
        [hbm, hbm, vmem, vmem, vmem, hbm, hbm],
        [vmem, hbm, vmem, hbm],
        flops=4 * tokens * width * (g_both.shape[1] // 2 + wide),
    )


def as_row(column):
    return jnp.transpose(jnp.broadcast_to(column, (column.shape[0], 128)), (1, 0))[:8]


def to_input(g_qkv, w_attn, x, g_middle, rows_one, sum_both, weights, gains, heads):
    tokens, width = g_qkv.shape[0], x.shape[1]
    own = tokens // 8
    deep = lax.axis_size("dp")
    across = g_qkv.shape[1]
    group = width // deep
    held = group // 4
    wide, narrow = heads * DV, heads * F
    both = sum_both.shape[1]
    units = both // 2
    main = units // 128 * 128

    def kernel(
        g_ref, w_ref, x_ref, gm_ref, one_ref, both_ref,
        wq_ref, wk_ref, wv_ref, wg_ref, wu_ref, gain_ref, gain_two_ref,
        out_ref, gq_ref, gk_ref, gv_ref, gg_ref, gu_ref, row_ref, row_two_ref,
        *rest,
    ):
        bufs, (s_send, s_receive, t_send, t_receive) = rest[:6], rest[6:10]
        (
            came_deep, sums, parts_a, parts_b, scalar, back_ref, one_buf, load,
            d_send, d_receive, p_send, p_receive, local, x_buf, gm_buf, gate_buf, up_buf, in_buf, large,
        ) = rest[10:]
        d, c, t = place_of()
        hand_on, landed = exchange(
            ((sums, parts_a), (both_ref, parts_b)), held, p_send, p_receive, local
        )

        def fetch(n):
            part = pl.ds(pl.multiple_of(depth(d, n + 1) * group, group), group)
            slot = lax.rem(n, 2)
            return pltpu.make_async_copy(one_ref.at[:, part], one_buf.at[slot], load.at[slot])

        fetch(0).start()
        mine = pl.ds(pl.multiple_of(t * own, own), own)
        loads = (
            pltpu.make_async_copy(x_ref.at[mine], x_buf, large.at[0]),
            pltpu.make_async_copy(gm_ref, gm_buf, large.at[1]),
        )
        stores = (
            pltpu.make_async_copy(gate_buf, gg_ref, large.at[2]),
            pltpu.make_async_copy(up_buf, gu_ref, large.at[3]),
            pltpu.make_async_copy(in_buf, out_ref.at[mine], large.at[4]),
        )
        for copy in loads:
            copy.start()
        met = (
            around()
            + [(d, beside(c, 3), t)]
            + [(depth(d, k), c, t) for k in range(1, deep)]
        )
        say(met)

        def deeper(n):
            rows = pl.ds(pl.multiple_of(depth(d, n + 1) * group, group), group)
            return remote(
                back_ref.at[rows], came_deep.at[n], d_send, d_receive, n, (depth(d, n + 1), c, t)
            )

        def plane(n, carry):
            rows = pl.ds(pl.multiple_of(depth(d, n + 1) * group, group), group)

            @pl.when(n < deep - 1)
            def _():
                fetch(n + 1).start()

            fetch(n).wait()
            back_ref[rows, :] = dot(one_buf[lax.rem(n, 2)], g_ref[...], 0, 0).astype(BF16)

            @pl.when(n < deep - 1)
            def _():
                deeper(n).start()

            return carry

        def terms(i, start):
            part = pl.ds(start, 2 * own)
            return [
                (g_ref[part, :wide], w_ref, slice(0, wide)),
                (g_ref[part, wide:], w_ref, slice(2 * wide, None)),
            ]

        def fill(n):
            if n == 0:
                hand_on(1)
                lax.fori_loop(0, deep, plane, 0)
                return
            landed(1)
            gain_two = gain_two_ref[...]
            for b in range(4):
                whole = parts_b[b].astype(F32)
                for ref, first, rest_of in (
                    (gate_buf, 0, 2 * main),
                    (up_buf, main, main + units),
                ):
                    s = whole[:, first : first + main]
                    if main < units:
                        s = jnp.concatenate([s, whole[:, rest_of : rest_of + units - main]], axis=1)
                    ref[:, b * units : (b + 1) * units] = s * gain_two
            scalar[0, 1] = as_row(
                (
                    jnp.sum(gate_buf[...] * wg_ref[...].astype(F32), axis=1, keepdims=True)
                    + jnp.sum(up_buf[...] * wu_ref[...].astype(F32), axis=1, keepdims=True)
                )
                / gain_two
            )
            stores[0].start()
            stores[1].start()
            for m in range(deep - 1):
                deeper(m).wait_recv()
            kept_rows = pl.ds(pl.multiple_of(d * group, group), group)
            total = back_ref[kept_rows, :].astype(F32)
            for m in range(deep - 1):
                total = total + came_deep[m].astype(F32)
            sums[...] = total.astype(BF16)
            hand_on(0)

        e_one = scatter_rows(terms, bufs, s_send, s_receive, lambda: hear(len(met)), fill)
        for copy in loads:
            copy.wait()
        scale, hat = norm_parts(x_buf[...].astype(F32))
        in_buf[...] = gm_buf[...] + norm_back(e_one, hat, scale)
        copy = remote(in_buf, out_ref.at[mine], t_send, t_receive, 0, (d, c, 1 - t))
        copy.start()
        stores[2].start()
        landed(0)
        gain_one = gain_ref[...]

        def owned(start, count):
            return jnp.concatenate(
                [parts_a[b][:, start : start + count].astype(F32) for b in range(4)], axis=1
            )

        term_one = jnp.zeros((held, 1), F32)
        for ref, weight, start, count in (
            (gv_ref, wv_ref, 0, wide),
            (gq_ref, wq_ref, wide, narrow),
            (gk_ref, wk_ref, wide + narrow, narrow),
        ):
            s = owned(start, count)
            term_one = term_one + jnp.sum(s * weight[...].astype(F32), axis=1, keepdims=True)
            ref[...] = s * gain_one
        scalar[0, 0] = as_row(term_one)
        swap = remote(scalar.at[0], scalar.at[1], t_send, t_receive, 1, (d, c, 1 - t))
        swap.start()
        swap.wait()
        row_ref[...] = (scalar[0, 0] + scalar[1, 0])[:1]
        row_two_ref[...] = (scalar[0, 1] + scalar[1, 1])[:1]
        copy.wait_send()
        there = out_ref.at[pl.ds(pl.multiple_of((1 - t) * own, own), own)]
        remote(there, there, t_send, t_receive, 0, (d, c, 1 - t)).wait_recv()
        for m in range(deep - 1):
            deeper(m).wait_send()
        for copy in stores:
            copy.wait()

    w_q, w_k, w_v, w_gate, w_up = weights
    vmem, hbm = pl.BlockSpec(memory_space=pltpu.VMEM), pl.BlockSpec(memory_space=pl.ANY)
    return call(
        kernel, "to_input", 6,
        (g_qkv, w_attn, x, g_middle, rows_one, sum_both) + tuple(weights) + tuple(gains),
        [jax.ShapeDtypeStruct((2 * own, width), F32)]
        + [jax.ShapeDtypeStruct(w.shape, F32) for w in weights]
        + [jax.ShapeDtypeStruct((1, held), F32)] * 2,
        scatter_scratch(own, width) + sems(SCATTER_COPIES) + sems(2)
        + [
            pltpu.VMEM((deep - 1, group, across), BF16),
            pltpu.VMEM((group, across), BF16),
            pltpu.VMEM((4, held, across), BF16),
            pltpu.VMEM((4, held, both), BF16),
            pltpu.VMEM((2, 2, 8, held), F32),
            pltpu.VMEM((width, across), BF16),
            pltpu.VMEM((2, tokens, group), BF16),
            pltpu.SemaphoreType.DMA((2,)),
        ]
        + sems(deep - 1) + sems(6)
        + [
            pltpu.SemaphoreType.DMA((2,)),
            pltpu.VMEM((own, width), BF16),
            pltpu.VMEM((own, width), F32),
            pltpu.VMEM(w_gate.shape, F32),
            pltpu.VMEM(w_up.shape, F32),
            pltpu.VMEM((own, width), F32),
            pltpu.SemaphoreType.DMA((5,)),
        ],
        [vmem] * 2 + [hbm] * 4 + [vmem] * 7,
        [hbm] + [vmem] * 3 + [hbm] * 2 + [vmem] * 2,
        flops=2 * tokens * width * g_qkv.shape[1],
    )


def plane_shards(
    activations,
    seg_ids,
    cotangent,
    q_weight,
    k_weight,
    v_weight,
    o_weight,
    gate_weight,
    up_weight,
    down_weight,
    attn_gain,
    mlp_gain,
):
    parts = lax.axis_size("ctx")
    heads = q_weight.shape[1] // F // parts
    tokens = activations.shape[1] * parts
    x, cot_block = activations[0], cotangent[0]
    gain_one = attn_gain.astype(F32)[:, None]
    gain_two = mlp_gain.astype(F32)[:, None]
    rows_low, own_high, segments, w_attn, cut_both, cut_down = front(
        x,
        seg_ids,
        (q_weight, k_weight, v_weight, o_weight, gate_weight, up_weight, down_weight),
        (gain_one, gain_two),
        tokens,
        heads,
    )
    w_attn = w_attn.reshape(-1, w_attn.shape[3])
    w_both = lax.all_gather(cut_both, "dp", axis=0, tiled=True).reshape(-1, cut_both.shape[2])
    seg_rows, seg_cols = segments.reshape(tokens, 1), segments.reshape(1, tokens)
    qkv, mixed, denom, heads_out, cot_low, rows_one = attend(
        rows_low, own_high, w_attn, seg_rows, seg_cols, cot_block, heads
    )
    cut_down, heads_out = lax.optimization_barrier((cut_down, heads_out))
    w_down = lax.all_gather(cut_down, "dp", axis=0, tiled=True).reshape(-1, cut_down.shape[2])
    middle, rows_two = to_middle(heads_out, w_attn, x)
    hidden, slope, silu, cot_high, back_down = gate_up(rows_two, w_both, cot_block, cot_low)
    sum_down = lax.psum_scatter(back_down, "dp", scatter_dimension=0, tiled=True)
    g_both, back_both = feed_forward(slope, silu, cot_low, cot_high, w_down, rows_two)
    sum_both = lax.psum_scatter(back_both, "dp", scatter_dimension=0, tiled=True)
    g_middle, branch, g_mixed, out_terms = to_branch(
        g_both, w_both, middle, cot_block, w_attn, heads * DV, hidden, w_down
    )
    g_qkv, out, s_o, s_down = attend_back(
        qkv,
        g_mixed,
        mixed,
        denom,
        seg_rows,
        seg_cols,
        branch,
        heads_out,
        out_terms,
        middle,
        sum_down,
        heads,
    )
    g_input, s_q, s_k, s_v, s_gate, s_up, attn_row, mlp_row = to_input(
        g_qkv,
        w_attn,
        x,
        g_middle,
        rows_one,
        sum_both,
        (q_weight, k_weight, v_weight, gate_weight, up_weight),
        (gain_one, gain_two),
        heads,
    )
    return (
        out[None],
        g_input[None],
        s_q,
        s_k,
        s_v,
        s_o,
        s_gate,
        s_up,
        s_down,
        attn_row[0],
        mlp_row[0],
    )


def layer(*arrays):
    heads = arrays[3].shape[1] // F
    plan = shards if heads % lax.axis_size("ctx") else plane_shards
    return plan(*arrays)


def solution(mesh):
    placed = (
        P("dp", "ctx", None),
        P("dp", "ctx"),
        P("dp", "ctx", None),
        P(("dp", "ctx"), "tp"),
        P(("dp", "ctx"), "tp"),
        P(("dp", "ctx"), "tp"),
        P(("dp", "ctx"), "tp"),
        P(("dp", "ctx"), "tp"),
        P(("dp", "ctx"), "tp"),
        P(("dp", "ctx"), "tp"),
        P(("dp", "ctx")),
        P(("dp", "ctx")),
    )
    return jax.shard_map(
        layer,
        mesh=mesh,
        in_specs=placed,
        out_specs=(
            P("dp", "ctx", None),
            P("dp", "ctx", None),
            P(("dp", "ctx"), "tp"),
            P(("dp", "ctx"), "tp"),
            P(("dp", "ctx"), "tp"),
            P(("dp", "ctx"), "tp"),
            P(("dp", "ctx"), "tp"),
            P(("dp", "ctx"), "tp"),
            P(("dp", "ctx"), "tp"),
            P(("dp", "ctx")),
            P(("dp", "ctx")),
        ),
        check_vma=False,
    )
```

```python
import functools

import jax
import jax.numpy as jnp
from jax import lax
from jax.experimental import pallas as pl
from jax.experimental.pallas import tpu as pltpu
from jax.sharding import PartitionSpec as P

F = 16
DV = 128


EPSILON = 1e-05
PRECISE = lax.Precision.HIGHEST
VMEM_MOST = 60 * 2**20


def prefix(x, axis, join, neutral, backward):
    count = lax.axis_size(axis)
    place = lax.axis_index(axis)
    ahead = count - 1 - place if backward else place
    gathered = jax.tree.map(
        lambda a, kind: lax.all_gather(a.astype(kind), axis),
        x,
        (jnp.bfloat16, jnp.bfloat16, jnp.bfloat16),
    )
    state = jax.tree.map(lambda a, e: jnp.zeros_like(a) + jnp.asarray(e, a.dtype), x, neutral)

    def one(lap, state):
        source = count - 1 - lap if backward else lap
        return join(
            state,
            jax.tree.map(
                lambda a, own: lax.dynamic_index_in_dim(a, source, 0, False).astype(own.dtype),
                gathered,
                x,
            ),
        )

    return lax.fori_loop(0, ahead, one, state)


def taylor(features_in):
    feature_count = features_in.shape[-1]
    products = (features_in[..., :, None] * features_in[..., None, :]).reshape(
        features_in.shape[:-1] + (feature_count * feature_count,)
    )
    constant = jnp.ones(features_in.shape[:-1] + (1,), jnp.float32)
    return jnp.concatenate(
        [
            constant,
            features_in * feature_count ** (-0.25),
            products * (2.0 * feature_count) ** (-0.5),
        ],
        axis=-1,
    )


def taylor_back(features_in, incoming_gradient):
    feature_count = features_in.shape[-1]
    linear = incoming_gradient[..., 1 : 1 + feature_count] * feature_count ** (-0.25)
    square = incoming_gradient[..., 1 + feature_count :].reshape(
        incoming_gradient.shape[:-1] + (feature_count, feature_count)
    )
    paired = jnp.einsum(
        "...ab,...b->...a", square + jnp.swapaxes(square, -1, -2), features_in, precision=PRECISE
    )
    return linear + paired * (2.0 * feature_count) ** (-0.5)


def norm_backward_step(incoming_gradient, unit_normalized_rows, multiplier_term, gain_vector_row):
    rescaled_rows = incoming_gradient * gain_vector_row
    return multiplier_term * (
        rescaled_rows
        - unit_normalized_rows
        * jnp.mean(rescaled_rows * unit_normalized_rows, axis=1, keepdims=True)
    )


def join_states(earlier, later_part):
    is_empty = later_part[2] < 0.0
    retain = jnp.where(is_empty | (earlier[2] == later_part[2]), 1.0, 0.0).astype(jnp.float32)
    return (
        later_part[0] + retain * earlier[0],
        later_part[1] + retain * earlier[1],
        jnp.where(is_empty, earlier[2], later_part[2]),
    )


def shards(
    activations,
    seg_ids,
    cotangent,
    q_weight,
    k_weight,
    v_weight,
    o_weight,
    gate_weight,
    up_weight,
    down_weight,
    attn_gain,
    mlp_gain,
):
    layer_input_rows = activations[0].astype(jnp.float32)
    segment = seg_ids[0].astype(jnp.float32)
    tokens = layer_input_rows.shape[0]
    head_count = q_weight.shape[1] // F
    w_query, w_key, w_value, w_out, first_norm_gain = (
        lax.all_gather(q_weight, ("dp", "ctx"), axis=0, tiled=True),
        lax.all_gather(k_weight, ("dp", "ctx"), axis=0, tiled=True),
        lax.all_gather(v_weight, ("dp", "ctx"), axis=0, tiled=True),
        lax.all_gather(o_weight, ("dp", "ctx"), axis=0, tiled=True),
        lax.all_gather(attn_gain, ("dp", "ctx"), axis=0, tiled=True),
    )
    first_inverse_scale = lax.rsqrt(
        jnp.mean(layer_input_rows * layer_input_rows, axis=1, keepdims=True) + EPSILON
    )
    first_unit_rows = layer_input_rows * first_inverse_scale
    first_normalized = (first_unit_rows * first_norm_gain.astype(jnp.float32)).astype(jnp.bfloat16)
    queries = (
        jnp.dot(first_normalized, w_query, preferred_element_type=jnp.float32)
        .astype(jnp.bfloat16)
        .reshape(tokens, head_count, F)
    )
    key_heads = (
        jnp.dot(first_normalized, w_key, preferred_element_type=jnp.float32)
        .astype(jnp.bfloat16)
        .reshape(tokens, head_count, F)
    )
    value_heads = (
        jnp.dot(first_normalized, w_value, preferred_element_type=jnp.float32)
        .astype(jnp.bfloat16)
        .reshape(tokens, head_count, DV)
    )
    w_gate, w_up, w_down, second_norm_gain = (
        lax.all_gather(gate_weight, ("dp", "ctx"), axis=0, tiled=True),
        lax.all_gather(up_weight, ("dp", "ctx"), axis=0, tiled=True),
        lax.all_gather(down_weight, ("dp", "ctx"), axis=0, tiled=True),
        lax.all_gather(mlp_gain, ("dp", "ctx"), axis=0, tiled=True),
    )
    scores = jnp.einsum(
        "thf,shf->hts", queries, key_heads, preferred_element_type=jnp.float32
    ) * F ** (-0.5)
    places = jnp.arange(tokens)
    visible = (
        (places[:, None] >= places[None, :]) & (segment[:, None] == segment[None, :])
    ).astype(jnp.float32)
    weights = (visible * (1.0 + scores + 0.5 * scores * scores)).astype(jnp.bfloat16)
    query_float = queries.astype(jnp.float32)
    key_float = key_heads.astype(jnp.float32)
    value_float = value_heads.astype(jnp.float32)
    feat_q = taylor(query_float)
    feat_k = taylor(key_float)
    ending = segment[-1]
    owned = (segment == ending).astype(jnp.float32)[:, None, None]
    local_state = jnp.einsum("thf,thd->hfd", feat_k * owned, value_float, precision=PRECISE)
    local_total = jnp.sum(feat_k * owned, axis=0)
    empty_state = (jnp.zeros_like(local_state), jnp.zeros_like(local_total), jnp.float32(-1.0))
    prior_state, prior_total, before = prefix(
        (local_state, local_total, ending), "ctx", join_states, empty_state, False
    )
    inherit = (segment == before).astype(jnp.float32)
    numerator = jnp.einsum(
        "hts,shd->thd", weights, value_heads, preferred_element_type=jnp.float32
    ) + inherit[:, None, None] * jnp.einsum("thf,hfd->thd", feat_q, prior_state, precision=PRECISE)
    denominator = jnp.sum(weights.astype(jnp.float32), axis=2).T + inherit[:, None] * jnp.einsum(
        "thf,hf->th", feat_q, prior_total, precision=PRECISE
    )
    mixed_heads = numerator / denominator[:, :, None]
    heads_out = mixed_heads.reshape(tokens, head_count * DV).astype(jnp.bfloat16)
    attn_out = lax.psum(
        jnp.einsum("tc,dc->td", heads_out, w_out, preferred_element_type=jnp.float32), "tp"
    )
    residual_midpoint = layer_input_rows + attn_out
    second_inverse_scale = lax.rsqrt(
        jnp.mean(residual_midpoint * residual_midpoint, axis=1, keepdims=True) + EPSILON
    )
    second_unit_rows = residual_midpoint * second_inverse_scale
    second_normalized = (second_unit_rows * second_norm_gain.astype(jnp.float32)).astype(
        jnp.bfloat16
    )
    gate_value = jnp.dot(second_normalized, w_gate, preferred_element_type=jnp.float32)
    up_value = jnp.dot(second_normalized, w_up, preferred_element_type=jnp.float32)
    sigmoid_gate = jax.nn.sigmoid(gate_value)
    hidden = (gate_value * sigmoid_gate * up_value).astype(jnp.bfloat16)
    mlp_out = lax.psum(
        jnp.einsum("tc,dc->td", hidden, w_down, preferred_element_type=jnp.float32).astype(
            jnp.bfloat16
        ),
        "tp",
    ).astype(jnp.float32)
    final_out = residual_midpoint + mlp_out
    grad_out = cotangent[0].astype(jnp.float32)
    grad_branch_two = cotangent[0]
    grad_w_down = jnp.einsum(
        "td,tc->dc", grad_branch_two, hidden, preferred_element_type=jnp.float32
    )
    grad_hidden = jnp.dot(grad_branch_two, w_down, preferred_element_type=jnp.float32)
    grad_gate = (
        grad_hidden * up_value * sigmoid_gate * (1.0 + gate_value * (1.0 - sigmoid_gate))
    ).astype(jnp.bfloat16)
    grad_up = (grad_hidden * gate_value * sigmoid_gate).astype(jnp.bfloat16)
    grad_w_gate = jnp.einsum(
        "td,tc->dc", second_normalized, grad_gate, preferred_element_type=jnp.float32
    )
    grad_w_up = jnp.einsum(
        "td,tc->dc", second_normalized, grad_up, preferred_element_type=jnp.float32
    )
    grad_normed_part = jnp.einsum(
        "tc,dc->td", grad_gate, w_gate, preferred_element_type=jnp.float32
    ) + jnp.einsum("tc,dc->td", grad_up, w_up, preferred_element_type=jnp.float32)
    second_normalized_gradient = lax.psum(grad_normed_part.astype(jnp.bfloat16), "tp").astype(
        jnp.float32
    )
    second_gain_gradient = jnp.sum(second_normalized_gradient * second_unit_rows, axis=0)
    grad_middle = grad_out + norm_backward_step(
        second_normalized_gradient,
        second_unit_rows,
        second_inverse_scale,
        second_norm_gain.astype(jnp.float32),
    )
    mlp_grads = (
        lax.psum_scatter(grad_w_gate, ("dp", "ctx"), scatter_dimension=0, tiled=True),
        lax.psum_scatter(grad_w_up, ("dp", "ctx"), scatter_dimension=0, tiled=True),
        lax.psum_scatter(grad_w_down, ("dp", "ctx"), scatter_dimension=0, tiled=True),
        lax.psum_scatter(second_gain_gradient, ("dp", "ctx"), scatter_dimension=0, tiled=True),
    )
    grad_branch_one = grad_middle.astype(jnp.bfloat16)
    grad_w_out = jnp.einsum(
        "td,tc->dc", grad_branch_one, heads_out, preferred_element_type=jnp.float32
    )
    grad_heads_low = jnp.dot(grad_branch_one, w_out, preferred_element_type=jnp.float32).astype(
        jnp.bfloat16
    )
    grad_mixed = (
        lax.optimization_barrier(grad_heads_low).astype(jnp.float32).reshape(tokens, head_count, DV)
    )
    numer_low = (grad_mixed / denominator[:, :, None]).astype(jnp.bfloat16)
    grad_numer = lax.optimization_barrier(numer_low).astype(jnp.float32)
    grad_denom = -jnp.sum(grad_mixed * mixed_heads, axis=2) / denominator
    grad_weights = (
        jnp.einsum("thd,shd->hts", numer_low, value_heads, preferred_element_type=jnp.float32)
        + grad_denom.T[:, :, None]
    )
    grad_scores = (grad_weights * visible * (1.0 + scores)).astype(jnp.bfloat16)
    grad_value = jnp.einsum("hts,thd->shd", weights, numer_low, preferred_element_type=jnp.float32)
    grad_query = jnp.einsum(
        "hts,shf->thf", grad_scores, key_heads, preferred_element_type=jnp.float32
    ) * F ** (-0.5)
    grad_key = jnp.einsum(
        "hts,thf->shf", grad_scores, queries, preferred_element_type=jnp.float32
    ) * F ** (-0.5)
    grad_feat_q = inherit[:, None, None] * (
        jnp.einsum("thd,hfd->thf", grad_numer, prior_state, precision=PRECISE)
        + grad_denom[:, :, None] * prior_total[None]
    )
    carried_state = jnp.einsum(
        "thf,thd->hfd", feat_q * inherit[:, None, None], grad_numer, precision=PRECISE
    )
    carried_total = jnp.sum(feat_q * (inherit[:, None] * grad_denom)[:, :, None], axis=0)
    starting = segment[0]
    later_state, later_total, after_seg = prefix(
        (carried_state, carried_total, starting), "ctx", join_states, empty_state, True
    )
    reached = (segment == after_seg).astype(jnp.float32)[:, None, None]
    grad_feat_k = reached * (
        jnp.einsum("hfd,thd->thf", later_state, value_float, precision=PRECISE) + later_total[None]
    )
    grad_value = grad_value + reached * jnp.einsum(
        "thf,hfd->thd", feat_k, later_state, precision=PRECISE
    )
    grad_query = grad_query + taylor_back(query_float, grad_feat_q)
    grad_key = grad_key + taylor_back(key_float, grad_feat_k)
    grad_query_low = grad_query.reshape(tokens, head_count * F).astype(jnp.bfloat16)
    grad_key_low = grad_key.reshape(tokens, head_count * F).astype(jnp.bfloat16)
    grad_value_low = grad_value.reshape(tokens, head_count * DV).astype(jnp.bfloat16)
    grad_w_query = jnp.einsum(
        "td,tc->dc", first_normalized, grad_query_low, preferred_element_type=jnp.float32
    )
    grad_w_key = jnp.einsum(
        "td,tc->dc", first_normalized, grad_key_low, preferred_element_type=jnp.float32
    )
    grad_w_value = jnp.einsum(
        "td,tc->dc", first_normalized, grad_value_low, preferred_element_type=jnp.float32
    )
    grad_normed_sum = (
        jnp.einsum("tc,dc->td", grad_query_low, w_query, preferred_element_type=jnp.float32)
        + jnp.einsum("tc,dc->td", grad_key_low, w_key, preferred_element_type=jnp.float32)
        + jnp.einsum("tc,dc->td", grad_value_low, w_value, preferred_element_type=jnp.float32)
    )
    first_normalized_gradient = lax.psum(grad_normed_sum.astype(jnp.bfloat16), "tp").astype(
        jnp.float32
    )
    first_gain_gradient = jnp.sum(first_normalized_gradient * first_unit_rows, axis=0)
    grad_inputs = grad_middle + norm_backward_step(
        first_normalized_gradient,
        first_unit_rows,
        first_inverse_scale,
        first_norm_gain.astype(jnp.float32),
    )
    attn_grads = (
        lax.psum_scatter(grad_w_query, ("dp", "ctx"), scatter_dimension=0, tiled=True),
        lax.psum_scatter(grad_w_key, ("dp", "ctx"), scatter_dimension=0, tiled=True),
        lax.psum_scatter(grad_w_value, ("dp", "ctx"), scatter_dimension=0, tiled=True),
        lax.psum_scatter(grad_w_out, ("dp", "ctx"), scatter_dimension=0, tiled=True),
        lax.psum_scatter(first_gain_gradient, ("dp", "ctx"), scatter_dimension=0, tiled=True),
    )
    return (
        final_out.astype(jnp.bfloat16)[None],
        grad_inputs[None],
        attn_grads[0],
        attn_grads[1],
        attn_grads[2],
        attn_grads[3],
        mlp_grads[0],
        mlp_grads[1],
        mlp_grads[2],
        attn_grads[4],
        mlp_grads[3],
    )


BLOCK = 512


MESH = pl.DeviceIdType.MESH
BF16, F32 = jnp.bfloat16, jnp.float32


def dot(a, b, ca, cb):
    return lax.dot_general(a, b, (((ca,), (cb,)), ((), ())), preferred_element_type=F32)


def place_of():
    return lax.axis_index("dp"), lax.axis_index("ctx"), lax.axis_index("tp")


def beside(c, across):
    x, y = lax.rem(c, 2), lax.div(c, 2)
    return lax.rem(x + across % 2, 2) + 2 * lax.rem(y + across // 2, 2)


def say(devices):
    barrier = pltpu.get_barrier_semaphore()
    for device in devices:
        pl.semaphore_signal(barrier, inc=1, device_id=device, device_id_type=MESH)


def hear(count):
    pl.semaphore_wait(pltpu.get_barrier_semaphore(), count)


def greet(devices):
    say(devices)
    hear(len(devices))


def around():
    d, c, t = place_of()
    return [(d, beside(c, 1), t), (d, beside(c, 2), t), (d, c, 1 - t)]


def remote(source, target, send, receive, k, device):
    return pltpu.make_async_remote_copy(
        src_ref=source,
        dst_ref=target,
        send_sem=send.at[k],
        recv_sem=receive.at[k],
        device_id=device,
        device_id_type=MESH,
    )


def gather_steps(buf, send, receive):
    d, c, t = place_of()
    own = buf.shape[0] // 8
    half = own // 2

    def part(across, core, h):
        block = c if across == 0 else beside(c, across)
        start = (2 * block + core) * own + h * half
        return buf.at[pl.ds(pl.multiple_of(start, half), half)]

    def put(k, across, h, device):
        ref = part(across, t, h)
        copy = remote(ref, ref, send, receive, k, device)
        copy.start()
        return copy

    return put, part


def gather_begin(buf, send, receive):
    put, _ = gather_steps(buf, send, receive)
    to_x, to_y, to_t = around()
    return [
        put(0, 0, 0, to_x),
        put(1, 0, 1, to_y),
        put(2, 0, 1, to_x),
        put(3, 0, 0, to_y),
        put(6, 0, 0, to_t),
        put(7, 0, 1, to_t),
    ]


def gather_rows(
    buf, out, send, receive, store, piece=None, early=None, middle=None, late=None, begun=None
):
    d, c, t = place_of()
    own = buf.shape[0] // 8
    to_x, to_y, to_t = around()
    put, part = gather_steps(buf, send, receive)
    started = gather_begin(buf, send, receive) if begun is None else begun

    def got(k, across, core, h):
        ref = part(across, core, h)
        remote(ref, ref, send, receive, k, to_t).wait_recv()

    stored = []

    def work(across, core):
        block = c if across == 0 else beside(c, across)
        start = pl.multiple_of((2 * block + core) * own, own)
        rows = pl.ds(start, own)
        copy = pltpu.make_async_copy(buf.at[rows], out.at[rows], store.at[len(stored)])
        copy.start()
        stored.append(copy)
        if piece is not None:
            piece(start)

    if early is not None:
        early()
    work(0, t)
    got(6, 0, 1 - t, 0)
    got(7, 0, 1 - t, 1)
    work(0, 1 - t)
    got(0, 1, t, 0)
    started.append(put(4, 1, 0, to_y))
    started.append(put(8, 1, 0, to_t))
    got(1, 2, t, 1)
    started.append(put(5, 2, 1, to_x))
    started.append(put(9, 2, 1, to_t))
    if middle is not None:
        middle()
    got(2, 1, t, 1)
    started.append(put(10, 1, 1, to_t))
    got(3, 2, t, 0)
    started.append(put(11, 2, 0, to_t))
    if late is not None:
        late()
    work(1, t)
    work(2, t)
    got(8, 1, 1 - t, 0)
    got(10, 1, 1 - t, 1)
    work(1, 1 - t)
    got(9, 2, 1 - t, 1)
    got(11, 2, 1 - t, 0)
    work(2, 1 - t)
    got(4, 3, t, 0)
    started.append(put(12, 3, 0, to_t))
    got(5, 3, t, 1)
    started.append(put(13, 3, 1, to_t))
    work(3, t)
    got(12, 3, 1 - t, 0)
    got(13, 3, 1 - t, 1)
    work(3, 1 - t)
    for copy in started:
        copy.wait_send()
    for copy in stored:
        copy.wait()


GATHER_COPIES = 14


def gather_scratch(tokens, width):
    return (
        [pltpu.VMEM((tokens, width), BF16)]
        + sems(GATHER_COPIES)
        + [pltpu.SemaphoreType.DMA((8,))]
    )


def exchange(jobs, held, send, receive, local):
    d, c, t = place_of()

    def rows_of(block):
        return pl.ds(pl.multiple_of(block * held, held), held)

    def to_block(n, k):
        source, target = jobs[n]
        return remote(
            source.at[rows_of(beside(c, k))], target.at[c], send, receive, 3 * n + k - 1,
            (d, beside(c, k), t),
        )

    def from_block(n, k):
        there = jobs[n][1].at[beside(c, k)]
        return remote(there, there, send, receive, 3 * n + k - 1, (d, beside(c, k), t))

    def at_home(n):
        source, target = jobs[n]
        return pltpu.make_async_copy(source.at[rows_of(c)], target.at[c], local.at[n])

    def hand_on(n):
        for k in (3, 1, 2):
            to_block(n, k).start()
        at_home(n).start()

    def landed(n):
        at_home(n).wait()
        for k in (1, 2, 3):
            from_block(n, k).wait_recv()
            to_block(n, k).wait_send()

    return hand_on, landed


def scatter_order(i):
    c = lax.axis_index("ctx")
    across = 3 - i
    x, y = lax.rem(c, 2), lax.div(c, 2)
    return lax.rem(x + lax.rem(across, 2), 2) + 2 * lax.rem(y + lax.div(across, 2), 2)


def scatter_rows(terms, bufs, send, receive, enter, fill=None):
    to_core, from_core, kept, over, came, stage = bufs
    d, c, t = place_of()
    own, tile = kept.shape[2:]
    half = own // 2
    to_x, to_y, to_t = (d, beside(c, 1), t), (d, beside(c, 2), t), (d, c, 1 - t)

    def link(k, n):
        return remote(
            over.at[k, n], came.at[k, n], send, receive, 8 + 2 * k + n, to_x if k % 2 == 0 else to_y
        )

    def core(i, n):
        return remote(to_core.at[lax.rem(i, 2), n], from_core.at[i, n], send, receive, 2 * i + n, to_t)

    def total(i, h, n, *extra):
        out = kept[i % 3, n, pl.ds(h * half, half), :]
        for k in extra:
            out = out + came[k, n].astype(F32)
        return out

    def go(k, i, h, n, *extra):
        over[k, n] = total(i, h, n, *extra).astype(BF16)
        link(k, n).start()

    def joined(i, n):
        core(i, n).wait_recv()
        kept[lax.rem(i, 3), n] = kept[lax.rem(i, 3), n] + from_core[i, n].astype(F32)

    def product(pairs, i, n):
        columns = pl.ds(n * tile, tile)
        theirs = pl.ds(pl.multiple_of((1 - t) * own, own), own)
        mine = pl.ds(pl.multiple_of(t * own, own), own)
        if not isinstance(pairs, list):
            to_core[lax.rem(i, 2), n] = pairs[theirs, columns]
            kept[lax.rem(i, 3), n] = pairs[mine, columns].astype(F32)
            return
        out = None
        for rows, matrix, part in pairs:
            term = dot(rows, matrix[columns, part], 1, 1)
            out = term if out is None else out + term
        stage[...] = out
        to_core[lax.rem(i, 2), n] = stage[theirs, :].astype(BF16)
        kept[lax.rem(i, 3), n] = stage[mine, :]

    def begin(i):
        return pl.multiple_of(2 * scatter_order(i) * own, 2 * own)

    pairs = terms(0, begin(0))
    product(pairs, 0, 0)
    enter()
    core(0, 0).start()
    product(pairs, 0, 1)
    core(0, 1).start()
    for n in (0, 1):
        joined(0, n)
        go(0, 0, 0, n)
        go(1, 0, 1, n)

    def step(i, carry):
        pairs = terms(i, begin(i))

        @pl.when(i >= 2)
        def _():
            for n in (0, 1):
                core(i - 2, n).wait_send()

        for n in (0, 1):
            product(pairs, i, n)
            core(i, n).start()

        @pl.when(i == 2)
        def _():
            for n in (0, 1):
                joined(1, n)
                go(3, 1, 1, n)

        return carry

    lax.fori_loop(1, 4, step, 0)
    for n in (0, 1):
        joined(2, n)
        go(2, 2, 0, n)
    if fill is not None:
        fill(0)
    for n in (0, 1):
        link(0, n).wait_recv()
        link(1, n).wait_recv()
        go(4, 2, 1, n, 1)
        go(5, 1, 0, n, 0)
    for n in (0, 1):
        joined(3, n)
    if fill is not None:
        fill(1)
    for n in (0, 1):
        for k in (2, 3, 4, 5):
            link(k, n).wait_recv()
        core(2, n).wait_send()
        core(3, n).wait_send()
        for k in range(6):
            link(k, n).wait_send()
    return jnp.concatenate(
        [
            jnp.concatenate([total(3, 0, n, 2, 5), total(3, 1, n, 3, 4)], axis=0)
            for n in (0, 1)
        ],
        axis=1,
    )


SCATTER_COPIES = 20


def scatter_scratch(own, width):
    tile = width // 2
    return [
        pltpu.VMEM((2, 2, own, tile), BF16),
        pltpu.VMEM((4, 2, own, tile), BF16),
        pltpu.VMEM((3, 2, own, tile), F32),
        pltpu.VMEM((6, 2, own // 2, tile), BF16),
        pltpu.VMEM((6, 2, own // 2, tile), BF16),
        pltpu.VMEM((2 * own, tile), F32),
    ]


def norm_parts(rows):
    scale = lax.rsqrt(jnp.mean(rows * rows, axis=1, keepdims=True) + EPSILON)
    return scale, rows * scale


def norm_back(e, hat, scale):
    return scale * (e - hat * jnp.mean(e * hat, axis=1, keepdims=True))


def call(kernel, name, collective, arrays, out_shape, scratch, spaces=None, out_spaces=None, flops=0):
    vmem = pl.BlockSpec(memory_space=pltpu.VMEM)
    moved = sum(a.size * a.dtype.itemsize for a in arrays)
    return pl.pallas_call(
        kernel,
        in_specs=spaces or [vmem] * len(arrays),
        out_specs=out_spaces or [vmem] * len(out_shape),
        out_shape=out_shape,
        scratch_shapes=scratch,
        compiler_params=pltpu.CompilerParams(
            collective_id=collective, has_side_effects=True, vmem_limit_bytes=VMEM_MOST
        ),
        cost_estimate=pl.CostEstimate(flops=flops, bytes_accessed=moved, transcendentals=0),
        name=name,
    )(*arrays)


def sems(count):
    return [pltpu.SemaphoreType.DMA((count,)), pltpu.SemaphoreType.DMA((count,))]


def depth(d, k):
    return lax.rem(d + k, lax.axis_size("dp"))


def columns(ref, gain, start, count):
    low = start // 128 * 128
    high = -(-(start + count) // 128) * 128
    value = ref[:, low:high].astype(F32)
    if gain is not None:
        value = value * gain
    return value[:, start - low : start - low + count]


def whole_tiles(count):
    return -(-count // 128) * 128


def front(x, seg, weights, gains, tokens, heads):
    width = x.shape[1]
    own = tokens // 8
    deep = lax.axis_size("dp")
    held, units = weights[4].shape[0], weights[4].shape[1] // 4
    wide, narrow = heads * DV, heads * F
    main = units // 128 * 128
    packed = 2 * wide + 2 * narrow
    part_width = width // 2
    filled = whole_tiles(units)
    line = {
        0: (((0, 2),), ((0, 1),), ()),
        1: (((1, 0),), ((1, 2), (1, 3)), ((3, 0),)),
        2: (((2, 3),), ((2, 1), (2, 0)), ((0, 3),)),
        3: (((3, 1),), ((3, 2),), ()),
    }
    if deep != 4:
        line = {
            p: (tuple((p, to) for to in range(deep) if to != p), (), ()) for p in range(deep)
        }

    def kernel(
        x_ref, seg_ref, q_ref, k_ref, v_ref, o_ref, g_ref, u_ref, d_ref, one_ref, two_ref,
        rows_out, own_ref, segs_ref, wa_out, wg_out, wd_out,
        cut_a, cut_g, cut_d, rows_ref, send, receive, store, small_send, small_receive, deep_send, deep_receive, here,
    ):
        d, c, t = place_of()
        jobs = (
            (lambda block: cut_a.at[block], lambda block: wa_out.at[d, block]),
            (lambda block: seg_ref.at[0], lambda block: segs_ref.at[block]),
            (lambda block: cut_g.at[block], lambda block: wg_out.at[block]),
            (lambda block: cut_d.at[block], lambda block: wd_out.at[block]),
        )

        def local(n):
            return pltpu.make_async_copy(jobs[n][0](c), jobs[n][1](c), here.at[n])

        def out(n, k):
            return remote(
                jobs[n][0](beside(c, k)), jobs[n][1](c), small_send, small_receive,
                3 * n + k - 1, (d, beside(c, k), t),
            )

        def arrival(n, k):
            block = beside(c, k)
            return remote(
                jobs[n][0](block), jobs[n][1](block), small_send, small_receive,
                3 * n + k - 1, (d, block, t),
            )

        def shard(slot, s, to):
            return pltpu.make_async_remote_copy(
                src_ref=wa_out.at[s], dst_ref=wa_out.at[s], send_sem=deep_send.at[slot],
                recv_sem=deep_receive.at[s], device_id=(to, c, t), device_id_type=MESH,
            )

        def in_plane(act):
            for p in range(deep):
                pl.when(d == p)(functools.partial(act, p, *line[p]))

        def first_shards(p, first, then, on):
            for slot, (s, to) in enumerate(first):
                shard(slot, s, to).start()

        def other_shards(p, first, then, on):
            for slot, (s, to) in enumerate(then):
                shard(len(first) + slot, s, to).start()
            for slot, (s, to) in enumerate(on):
                shard(len(first) + len(then) + slot, s, to).wait_recv()
                shard(len(first) + len(then) + slot, s, to).start()

        def end_shards(p, first, then, on):
            for s in range(deep):
                if s != p and s not in [handed for handed, _ in on]:
                    shard(0, s, (p + 1) % deep).wait_recv()
            for slot, (s, to) in enumerate(first + then + on):
                shard(slot, s, to).wait_send()

        one, two = one_ref[...], two_ref[...]
        met = (
            [(d, beside(c, k), t) for k in (1, 2, 3)]
            + [(d, c, 1 - t)]
            + [(depth(d, k), c, t) for k in range(1, deep)]
        )
        say(met)
        for b in range(4):
            cut_a[b, :, :wide] = columns(v_ref, one, b * wide, wide).astype(BF16)
            cut_a[b, :, wide : 2 * wide] = o_ref[:, b * wide : (b + 1) * wide]
            cut_a[b, :, 2 * wide :] = jnp.concatenate(
                [columns(ref, one, b * narrow, narrow) for ref in (q_ref, k_ref)], axis=1
            ).astype(BF16)
        hear(len(met))
        local(0).start()
        for k in (3, 1, 2):
            out(0, k).start()
        mine = pl.multiple_of((2 * c + t) * own, own)
        _, hat = norm_parts(x_ref[pl.ds(pl.multiple_of(t * own, own), own), :].astype(F32))
        rows_ref[pl.ds(mine, own), :] = hat[:, :part_width].astype(BF16)
        own_ref[...] = hat[:, part_width:].astype(BF16)
        local(0).wait()
        for k in (1, 2, 3):
            arrival(0, k).wait_recv()
        in_plane(first_shards)

        def early():
            for b in range(4):
                start = b * units
                cut_g[b, :, :main] = columns(g_ref, two, start, main).astype(BF16)
                cut_g[b, :, main : 2 * main] = columns(u_ref, two, start, main).astype(BF16)
                if main < units:
                    cut_g[b, :, 2 * main :] = jnp.concatenate(
                        [columns(r, two, start + main, units - main) for r in (g_ref, u_ref)],
                        axis=1,
                    ).astype(BF16)

            for n in (1, 2):
                local(n).start()
                for k in (3, 1, 2):
                    out(n, k).start()
            for b in range(4):
                part = columns(d_ref, None, b * units, units)
                if units < filled:
                    part = jnp.concatenate([part, jnp.zeros((held, filled - units), F32)], axis=1)
                cut_d[b] = part.astype(BF16)
            local(3).start()
            for k in (3, 1, 2):
                out(3, k).start()

        gather_rows(
            rows_ref, rows_out, send, receive, store, early=early,
            middle=lambda: in_plane(other_shards),
        )
        for n in (1, 2, 3):
            local(n).wait()
            for k in (1, 2, 3):
                arrival(n, k).wait_recv()
        in_plane(end_shards)
        for n in range(4):
            for k in (1, 2, 3):
                out(n, k).wait_send()

    vmem, hbm = pl.BlockSpec(memory_space=pltpu.VMEM), pl.BlockSpec(memory_space=pl.ANY)
    return call(
        kernel,
        "front",
        1,
        (x, seg[None]) + tuple(weights) + tuple(gains),
        [
            jax.ShapeDtypeStruct((tokens, part_width), BF16),
            jax.ShapeDtypeStruct((own, part_width), BF16),
            jax.ShapeDtypeStruct((4,) + seg.shape, seg.dtype),
            jax.ShapeDtypeStruct((deep, 4, held, packed), BF16),
            jax.ShapeDtypeStruct((4, held, 2 * units), BF16),
            jax.ShapeDtypeStruct((4, held, filled), BF16),
        ],
        [
            pltpu.VMEM((4, held, packed), BF16),
            pltpu.VMEM((4, held, 2 * units), BF16),
            pltpu.VMEM((4, held, filled), BF16),
        ]
        + gather_scratch(tokens, part_width) + sems(12) + sems(deep) + [pltpu.SemaphoreType.DMA((4,))],
        [vmem, hbm] + [vmem] * 9,
        [hbm, vmem, hbm, hbm, hbm, hbm],
    )


def apart(tokens):
    return (tokens // 2 - 2) // BLOCK + 2


def first_seen(i, tokens):
    return jnp.maximum(i - apart(tokens) + 1, 0)


def attend_back(
    qkv, g_mixed, mixed, denom, seg_rows, seg_cols, out_terms, middle, sum_down, heads
):
    tokens, width = out_terms.shape
    wide, narrow = heads * DV, heads * F
    blocks = tokens // BLOCK
    own = tokens // 8
    held, units = sum_down.shape[0] // 4, sum_down.shape[1]

    def kernel(
        x_ref, gm_ref, m_ref, d_ref, row_ref, col_ref, term_ref, mid_ref, down_ref,
        g_ref, out_ref, gd_ref,
        gq_ref, numer_ref, gden_ref, key_ref, gm_buf, m_buf, mid_buf, here_buf, large,
        term_buf, term_load, parts_d, p_send, p_receive, local, *rest,
    ):
        bufs, (s_send, s_receive, t_send, t_receive) = rest[:6], rest[6:]
        d, c, t = place_of()
        hand_on, landed = exchange(((down_ref, parts_d),), held, p_send, p_receive, local)
        mine = pl.ds(pl.multiple_of(t * own, own), own)
        loads = (
            pltpu.make_async_copy(gm_ref, gm_buf, large.at[0]),
            pltpu.make_async_copy(m_ref, m_buf, large.at[1]),
            pltpu.make_async_copy(mid_ref, mid_buf, large.at[2]),
        )
        stored = pltpu.make_async_copy(here_buf, out_ref.at[mine], large.at[3])

        def fetch_terms(i):
            part = pl.ds(pl.multiple_of(2 * scatter_order(i) * own, 2 * own), 2 * own)
            slot = lax.rem(i, 2)
            return pltpu.make_async_copy(term_ref.at[part], term_buf.at[slot], term_load.at[slot])

        fetch_terms(0).start()

        for copy in loads:
            copy.start()
        met = around() + [(d, beside(c, 3), t)]
        say(met)

        def prepare():
            loads[0].wait()
            loads[1].wait()
            gq_ref[...] = jnp.zeros_like(gq_ref)
            for h in range(heads):
                part = pl.ds(h * DV, DV)
                gm = gm_buf[:, part].astype(F32)
                inverse = 1.0 / d_ref[:, h : h + 1]
                numer_ref[:, part] = (gm * inverse).astype(BF16)
                down = -jnp.sum(gm * m_buf[:, part], axis=1, keepdims=True) * inverse
                gden_ref[h : h + 1, :] = jnp.transpose(
                    jnp.broadcast_to(down, (tokens, 128)), (1, 0)
                )[:1]
            key_ref[...] = jnp.transpose(
                x_ref[:, wide : wide + 2 * narrow].astype(F32), (1, 0)
            ).astype(BF16)

        place = lax.broadcasted_iota(jnp.int32, (BLOCK, BLOCK), 1) - lax.broadcasted_iota(
            jnp.int32, (BLOCK, BLOCK), 0
        )
        tempered = BF16(F**-0.5)

        def one_block(j):
            start = pl.multiple_of(j * BLOCK, BLOCK)
            ids = row_ref[pl.ds(start, BLOCK), :]
            values = [x_ref[pl.ds(start, BLOCK), h * DV : (h + 1) * DV] for h in range(heads)]
            keys = [
                x_ref[pl.ds(start, BLOCK), wide + (heads + h) * F : wide + (heads + h + 1) * F]
                * tempered
                for h in range(heads)
            ]
            across = [
                key_ref[(heads + h) * F : (heads + h + 1) * F, pl.ds(start, BLOCK)] * tempered
                for h in range(heads)
            ]

            def step(i, sums):
                base = pl.multiple_of(i * BLOCK, BLOCK)
                visible = (place >= start - base) & (ids == col_ref[:, pl.ds(base, BLOCK)])
                out = []
                for h in range(heads):
                    queries = x_ref[pl.ds(base, BLOCK), wide + h * F : wide + (h + 1) * F]
                    numer = numer_ref[pl.ds(base, BLOCK), h * DV : (h + 1) * DV]
                    s = dot(keys[h], queries, 1, 1)
                    a = jnp.where(visible, (0.5 * s + 1.0) * s + 1.0, 0.0).astype(BF16)
                    ga = dot(values[h], numer, 1, 1) + gden_ref[h : h + 1, pl.ds(base, BLOCK)]
                    gs = jnp.where(visible, ga * (1.0 + s), 0.0).astype(BF16)
                    gq_ref[h * F : (h + 1) * F, pl.ds(base, BLOCK)] += dot(across[h], gs, 1, 0)
                    out += [sums[2 * h] + dot(a, numer, 1, 0), sums[2 * h + 1] + dot(gs, queries, 1, 0)]
                return tuple(out)

            zeros = []
            for h in range(heads):
                zeros += [jnp.zeros((BLOCK, DV), F32), jnp.zeros((BLOCK, F), F32)]
            sums = lax.fori_loop(
                j, jnp.minimum(j + apart(tokens), blocks), step, tuple(zeros)
            )
            for h in range(heads):
                g_ref[pl.ds(start, BLOCK), h * DV : (h + 1) * DV] = sums[2 * h].astype(BF16)
                g_ref[
                    pl.ds(start, BLOCK), wide + (heads + h) * F : wide + (heads + h + 1) * F
                ] = (sums[2 * h + 1] * F**-0.5).astype(BF16)

        def terms(i, start):
            fetch_terms(i).wait()

            @pl.when(i < 3)
            def _():
                fetch_terms(i + 1).start()

            return term_buf.at[lax.rem(i, 2)]

        def fill(n):
            if n == 0:
                prepare()
                pl.loop(0, 1)(one_block)
            else:
                pl.loop(1, blocks)(one_block)
                hand_on(0)

        moved = scatter_rows(terms, bufs, s_send, s_receive, lambda: hear(len(met)), fill)
        loads[2].wait()
        here_buf[...] = (mid_buf[...] + moved).astype(BF16)
        copy = remote(here_buf, out_ref.at[mine], t_send, t_receive, 0, (d, c, 1 - t))
        copy.start()
        stored.start()
        g_ref[:, wide : wide + narrow] = jnp.transpose(gq_ref[...], (1, 0)).astype(BF16)
        landed(0)
        for b in range(4):
            gd_ref[:, b * units : (b + 1) * units] = parts_d[b].astype(F32)
        copy.wait_send()
        there = out_ref.at[pl.ds(pl.multiple_of((1 - t) * own, own), own)]
        remote(there, there, t_send, t_receive, 0, (d, c, 1 - t)).wait_recv()
        stored.wait()

    vmem, hbm = pl.BlockSpec(memory_space=pltpu.VMEM), pl.BlockSpec(memory_space=pl.ANY)
    return call(
        kernel, "attend_back", 7,
        (qkv, g_mixed, mixed, denom, seg_rows, seg_cols, out_terms, middle, sum_down),
        [
            jax.ShapeDtypeStruct(qkv.shape, BF16),
            jax.ShapeDtypeStruct((2 * own, width), BF16),
            jax.ShapeDtypeStruct((held, 4 * units), F32),
        ],
        [
            pltpu.VMEM((narrow, tokens), F32),
            pltpu.VMEM((tokens, wide), BF16),
            pltpu.VMEM((8, tokens), F32),
            pltpu.VMEM((2 * narrow, tokens), BF16),
            pltpu.VMEM(g_mixed.shape, BF16),
            pltpu.VMEM(mixed.shape, F32),
            pltpu.VMEM(middle.shape, F32),
            pltpu.VMEM((own, width), BF16),
            pltpu.SemaphoreType.DMA((4,)),
            pltpu.VMEM((2, 2 * own, width), BF16),
            pltpu.SemaphoreType.DMA((2,)),
            pltpu.VMEM((4, held, units), BF16),
        ]
        + sems(3) + [pltpu.SemaphoreType.DMA((1,))]
        + scatter_scratch(own, width) + sems(SCATTER_COPIES) + sems(1),
        [vmem, hbm, hbm, vmem, vmem, vmem, hbm, hbm, hbm],
        [vmem, hbm, vmem],
    )


def attend_block(i, x_ref, ext_ref, row_ref, col_ref, mixed_ref, denom_ref, low_ref, heads):
    wide = heads * DV
    base = pl.multiple_of(i * BLOCK, BLOCK)
    own = row_ref[pl.ds(base, BLOCK), :]
    place = lax.broadcasted_iota(jnp.int32, (BLOCK, BLOCK), 0) - lax.broadcasted_iota(
        jnp.int32, (BLOCK, BLOCK), 1
    )
    queries = [
        x_ref[pl.ds(base, BLOCK), wide + h * F : wide + (h + 1) * F] * jnp.bfloat16(F**-0.5)
        for h in range(heads)
    ]

    def step(j, sums):
        start = pl.multiple_of(j * BLOCK, BLOCK)
        visible = (place >= start - base) & (own == col_ref[:, pl.ds(start, BLOCK)])
        out = []
        for h in range(heads):
            keys = x_ref[
                pl.ds(start, BLOCK), wide + (heads + h) * F : wide + (heads + h + 1) * F
            ]
            s = dot(queries[h], keys, 1, 1)
            a = jnp.where(visible, (0.5 * s + 1.0) * s + 1.0, 0.0).astype(BF16)
            out.append(
                sums[h] + dot(a, ext_ref[pl.ds(start, BLOCK), 2 * h * DV : (2 * h + 2) * DV], 1, 0)
            )
        return tuple(out)

    sums = lax.fori_loop(
        first_seen(i, x_ref.shape[0]),
        i + 1,
        step,
        tuple(jnp.zeros((BLOCK, 2 * DV), F32) for _ in range(heads)),
    )
    for h in range(heads):
        denom = sums[h][:, DV:]
        mixed = sums[h][:, :DV] / denom
        mixed_ref[pl.ds(base, BLOCK), h * DV : (h + 1) * DV] = mixed
        low_ref[pl.ds(base, BLOCK), h * DV : (h + 1) * DV] = mixed.astype(BF16)
        denom_ref[pl.ds(base, BLOCK), h : h + 1] = denom[:, :1]


def attend(rows_low, own_high, w_attn, seg_rows, seg_cols, cot, heads):
    tokens, part_width = rows_low.shape
    own = tokens // 8
    wide, narrow = heads * DV, heads * F

    def kernel(
        x_ref, own_ref, w_ref, row_ref, col_ref, cot_ref,
        qkv_ref, mixed_ref, denom_ref, low_ref, cot_out, rows_out,
        ext_ref, half_ref, here, x_buf, *rest,
    ):
        rows_ref, r_send, r_receive, r_store, cot_buf, c_send, c_receive, c_store = rest
        d, c, t = place_of()
        loaded = pltpu.make_async_copy(x_ref, x_buf, here.at[0])
        loaded.start()
        low_half = pltpu.make_async_copy(x_buf, rows_out.at[:, :part_width], here.at[1])

        met = around()
        say(met)
        mine = pl.ds(pl.multiple_of((2 * c + t) * own, own), own)
        rows_ref[mine, :] = own_ref[...]
        cot_buf[mine, :] = cot_ref[pl.ds(pl.multiple_of(t * own, own), own), :part_width]
        hear(len(met))

        def first_half():
            loaded.wait()

            @pl.loop(0, tokens // BLOCK)
            def _(n):
                rows = pl.ds(pl.multiple_of(n * BLOCK, BLOCK), BLOCK)
                half_ref[rows, :wide] = dot(x_buf[rows, :], w_ref[:part_width, :wide], 1, 0)
                half_ref[rows, wide:] = dot(x_buf[rows, :], w_ref[:part_width, 2 * wide :], 1, 0)

            low_half.start()

        def second_half(start):
            rows = pl.ds(start, own)
            values = (
                half_ref[rows, :wide] + dot(rows_ref[rows, :], w_ref[part_width:, :wide], 1, 0)
            ).astype(BF16)
            qkv_ref[rows, :wide] = values
            qkv_ref[rows, wide:] = (
                half_ref[rows, wide:] + dot(rows_ref[rows, :], w_ref[part_width:, 2 * wide :], 1, 0)
            ).astype(BF16)
            for h in range(heads):
                ext_ref[rows, 2 * h * DV : (2 * h + 1) * DV] = values[:, h * DV : (h + 1) * DV]
                ext_ref[rows, (2 * h + 1) * DV : (2 * h + 2) * DV] = jnp.ones((own, DV), BF16)

        begun = []

        def cot_begin():
            begun.extend(gather_begin(cot_buf, c_send, c_receive))

        gather_rows(
            rows_ref, rows_out.at[:, part_width:], r_send, r_receive, r_store, second_half, first_half,
            late=cot_begin,
        )

        def blocks(first, last):
            @pl.loop(first, last)
            def _(i):
                attend_block(
                    i, qkv_ref, ext_ref, row_ref, col_ref, mixed_ref, denom_ref, low_ref, heads
                )

        gather_rows(
            cot_buf, cot_out, c_send, c_receive, c_store, begun=begun,
            early=lambda: blocks(0, tokens // BLOCK // 2),
            middle=lambda: blocks(tokens // BLOCK // 2, tokens // BLOCK - 1),
            late=lambda: blocks(tokens // BLOCK - 1, tokens // BLOCK),
        )
        low_half.wait()

    vmem, hbm = pl.BlockSpec(memory_space=pltpu.VMEM), pl.BlockSpec(memory_space=pl.ANY)
    return call(
        kernel, "attend", 2, (rows_low, own_high, w_attn, seg_rows, seg_cols, cot),
        [
            jax.ShapeDtypeStruct((tokens, wide + 2 * narrow), BF16),
            jax.ShapeDtypeStruct((tokens, wide), F32),
            jax.ShapeDtypeStruct((tokens, heads), F32),
            jax.ShapeDtypeStruct((tokens, wide), BF16),
            jax.ShapeDtypeStruct((tokens, part_width), BF16),
            jax.ShapeDtypeStruct((tokens, 2 * part_width), BF16),
        ],
        [
            pltpu.VMEM((tokens, 2 * wide), BF16),
            pltpu.VMEM((tokens, wide + 2 * narrow), F32),
            pltpu.SemaphoreType.DMA((2,)),
            pltpu.VMEM((tokens, part_width), BF16),
        ]
        + gather_scratch(tokens, part_width) + gather_scratch(tokens, part_width),
        [hbm] + [vmem] * 5,
        [vmem] * 4 + [hbm] * 2,
    )


def to_middle(heads_out, w_attn, x):
    tokens, width = heads_out.shape[0], x.shape[1]
    own = tokens // 8
    wide = heads_out.shape[1]

    def kernel(h_ref, w_ref, x_ref, mid_ref, rows_out, w_buf, x_buf, mid_buf, large, *rest):
        bufs, (s_send, s_receive, rows_ref, g_send, g_receive, store) = rest[:6], rest[6:]
        d, c, t = place_of()
        mine = pl.ds(pl.multiple_of(t * own, own), own)
        weights = pltpu.make_async_copy(w_ref.at[:, wide : 2 * wide], w_buf, large.at[0])
        loaded = pltpu.make_async_copy(x_ref.at[mine], x_buf, large.at[1])
        stored = pltpu.make_async_copy(mid_buf, mid_ref, large.at[2])
        weights.start()
        loaded.start()
        say(around())
        weights.wait()

        def terms(i, start):
            return [(h_ref[pl.ds(start, 2 * own), :], w_buf, slice(None))]

        total = scatter_rows(terms, bufs, s_send, s_receive, lambda: hear(3))
        loaded.wait()
        middle = total + x_buf[...].astype(F32)
        mid_buf[...] = middle
        stored.start()
        _, hat = norm_parts(middle)
        rows_ref[pl.ds(pl.multiple_of((2 * c + t) * own, own), own), :] = hat.astype(BF16)
        gather_rows(rows_ref, rows_out, g_send, g_receive, store)
        stored.wait()

    vmem, hbm = pl.BlockSpec(memory_space=pltpu.VMEM), pl.BlockSpec(memory_space=pl.ANY)
    return call(
        kernel, "to_middle", 3, (heads_out, w_attn, x),
        [jax.ShapeDtypeStruct((own, width), F32), jax.ShapeDtypeStruct((tokens, width), BF16)],
        [
            pltpu.VMEM((width, wide), BF16),
            pltpu.VMEM((own, width), BF16),
            pltpu.VMEM((own, width), F32),
            pltpu.SemaphoreType.DMA((3,)),
        ]
        + scatter_scratch(own, width) + sems(SCATTER_COPIES) + gather_scratch(tokens, width),
        [vmem, hbm, hbm],
        [hbm, hbm],
        flops=2 * tokens * width * heads_out.shape[1],
    )


def gate_up(rows_two, w_both, cot, cot_low):
    tokens, width = rows_two.shape
    own = tokens // 8
    units = w_both.shape[1] // 2
    main = units // 128 * 128
    count = tokens // BLOCK
    tile = 256

    def kernel(
        x_ref, w_ref, cot_ref, low_ref, hid_out, slope_out, silu_out, rows_out, down_out,
        x_buf, w_buf, low_buf, hid_ref, slope_ref, silu_ref, down_buf, load, store, down_store,
        rows_ref, send, receive, row_store,
    ):
        d, c, t = place_of()

        def fetch(i):
            rows = pl.ds(pl.multiple_of(i * BLOCK, BLOCK), BLOCK)
            slot = lax.rem(i, 2)
            return pltpu.make_async_copy(x_ref.at[rows], x_buf.at[slot], load.at[slot])

        def given(i):
            rows = pl.ds(pl.multiple_of(i * BLOCK, BLOCK), BLOCK)
            slot = lax.rem(i, 2)
            return [
                pltpu.make_async_copy(source, target.at[rows], store.at[n, slot])
                for n, (source, target) in enumerate(
                    (
                        (hid_ref.at[rows], hid_out),
                        (slope_ref.at[slot], slope_out),
                        (silu_ref.at[slot], silu_out),
                    )
                )
            ]

        weights = pltpu.make_async_copy(w_ref, w_buf, load.at[2])
        weights.start()
        fetch(0).start()
        low_copy = pltpu.make_async_copy(low_ref, low_buf, load.at[3])
        low_copy.start()
        greet(around())
        mine = pl.multiple_of((2 * c + t) * own, own)
        rows_ref[pl.ds(mine, own), :] = cot_ref[
            pl.ds(pl.multiple_of(t * own, own), own), width // 2 :
        ]

        def blocks(first, last):
            @pl.loop(first, last)
            def _(i):
                slot = lax.rem(i, 2)

                @pl.when(i + 1 < count)
                def _():
                    fetch(i + 1).start()

                fetch(i).wait()
                both = dot(x_buf[slot], w_buf[...], 1, 0)

                @pl.when(i >= 2)
                def _():
                    for copy in given(i - 2):
                        copy.wait()

                def act(gate, up, part):
                    sig = jax.nn.sigmoid(gate)
                    silu = gate * sig
                    hid_ref[pl.ds(pl.multiple_of(i * BLOCK, BLOCK), BLOCK), part] = (
                        silu * up
                    ).astype(BF16)
                    slope_ref[slot, :, part] = (up * sig * (1.0 + gate * (1.0 - sig))).astype(BF16)
                    silu_ref[slot, :, part] = silu.astype(BF16)

                act(both[:, :main], both[:, main : 2 * main], slice(0, main))
                if main < units:
                    act(
                        both[:, 2 * main : main + units],
                        both[:, main + units :],
                        slice(main, units),
                    )
                for copy in given(i):
                    copy.start()

        per = width // 2 // tile

        def down_given(base, n):
            slot = lax.rem(n, 2)
            rows = pl.ds(pl.multiple_of(base + n * tile, tile), tile)
            return pltpu.make_async_copy(down_buf.at[slot], down_out.at[rows], down_store.at[slot])

        def down_tiles(source, base, end):
            @pl.loop(0, end)
            def _(n):
                @pl.when(n >= 2)
                def _():
                    down_given(base, n - 2).wait()

                part = pl.ds(pl.multiple_of(n * tile, tile), tile)
                down_buf[lax.rem(n, 2)] = dot(source[:, part], hid_ref[...], 0, 0).astype(BF16)
                down_given(base, n).start()

        def early():
            weights.wait()
            blocks(0, 1)

        def later():
            blocks(count // 2, count)
            low_copy.wait()
            down_tiles(low_buf, 0, per)
            for n in (per - 2, per - 1):
                down_given(0, n).wait()

        gather_rows(
            rows_ref, rows_out, send, receive, row_store, early=early,
            middle=lambda: blocks(1, count // 2), late=later,
        )
        down_tiles(rows_ref, width // 2, per)
        for n in (per - 2, per - 1):
            down_given(width // 2, n).wait()
        for i in (count - 2, count - 1):
            for copy in given(i):
                copy.wait()

    vmem, hbm = pl.BlockSpec(memory_space=pltpu.VMEM), pl.BlockSpec(memory_space=pl.ANY)
    return call(
        kernel, "gate_up", 8, (rows_two, w_both, cot, cot_low),
        [jax.ShapeDtypeStruct((tokens, units), BF16)] * 3
        + [
            jax.ShapeDtypeStruct((tokens, width // 2), BF16),
            jax.ShapeDtypeStruct((width, units), BF16),
        ],
        [
            pltpu.VMEM((2, BLOCK, width), BF16),
            pltpu.VMEM(w_both.shape, BF16),
            pltpu.VMEM(cot_low.shape, BF16),
            pltpu.VMEM((tokens, units), BF16),
            pltpu.VMEM((2, BLOCK, units), BF16),
            pltpu.VMEM((2, BLOCK, units), BF16),
            pltpu.VMEM((2, tile, units), BF16),
            pltpu.SemaphoreType.DMA((4,)),
            pltpu.SemaphoreType.DMA((3, 2)),
            pltpu.SemaphoreType.DMA((2,)),
        ]
        + gather_scratch(tokens, width // 2),
        [hbm, hbm, vmem, hbm],
        [hbm] * 5,
        flops=4 * tokens * width * units,
    )


def feed_forward(slope, silu, cot_low, cot_high, w_down, rows_two):
    tokens, width = rows_two.shape
    units = slope.shape[1]
    main = units // 128 * 128
    tile = 256
    part_width = width // 2
    count = tokens // BLOCK

    def kernel(
        slope_ref, silu_ref, low_ref, high_ref, d_ref, two_ref, g_out, grad_ref,
        slope_buf, silu_buf, low_buf, high_buf, d_buf, g_ref, here, g_store, cols, out, load, store,
    ):
        def rows(i):
            return pl.ds(pl.multiple_of(i * BLOCK, BLOCK), BLOCK)

        def fetch(i):
            slot = lax.rem(i, 2)
            return [
                pltpu.make_async_copy(source.at[rows(i)], target.at[slot], here.at[n, slot])
                for n, (source, target) in enumerate(
                    (
                        (low_ref, low_buf),
                        (high_ref, high_buf),
                        (slope_ref, slope_buf),
                        (silu_ref, silu_buf),
                    )
                )
            ]

        def g_given(i):
            return pltpu.make_async_copy(g_ref.at[rows(i)], g_out.at[rows(i)], g_store.at[i])

        def wanted(n):
            part = pl.ds(pl.multiple_of(n * tile, tile), tile)
            slot = lax.rem(n, 2)
            return pltpu.make_async_copy(two_ref.at[:, part], cols.at[slot], load.at[slot])

        def given(n):
            part = pl.ds(pl.multiple_of(n * tile, tile), tile)
            slot = lax.rem(n, 2)
            return pltpu.make_async_copy(out.at[slot], grad_ref.at[part], store.at[slot])

        weights = pltpu.make_async_copy(d_ref, d_buf, load.at[2])
        weights.start()
        for copy in fetch(0):
            copy.start()
        wanted(0).start()
        weights.wait()

        @pl.loop(0, count)
        def _(i):
            slot = lax.rem(i, 2)

            @pl.when(i + 1 < count)
            def _():
                for copy in fetch(i + 1):
                    copy.start()

            for copy in fetch(i):
                copy.wait()
            g_hidden = dot(low_buf[slot], d_buf[:part_width, :units], 1, 0) + dot(
                high_buf[slot], d_buf[part_width:, :units], 1, 0
            )
            gg = g_hidden * slope_buf[slot].astype(F32)
            gu = g_hidden * silu_buf[slot].astype(F32)
            part = rows(i)
            g_ref[part, :main] = gg[:, :main].astype(BF16)
            g_ref[part, main : 2 * main] = gu[:, :main].astype(BF16)
            if main < units:
                g_ref[part, 2 * main :] = jnp.concatenate(
                    [gg[:, main:], gu[:, main:]], axis=1
                ).astype(BF16)
            g_given(i).start()

        last = width // tile

        @pl.loop(0, last)
        def _(n):
            @pl.when(n + 1 < last)
            def _():
                wanted(n + 1).start()

            wanted(n).wait()

            @pl.when(n >= 2)
            def _():
                given(n - 2).wait()

            slot = lax.rem(n, 2)
            out[slot] = dot(cols[slot], g_ref[...], 0, 0).astype(BF16)
            given(n).start()

        given(last - 2).wait()
        given(last - 1).wait()
        for i in range(count):
            g_given(i).wait()

    hbm = pl.BlockSpec(memory_space=pl.ANY)
    moved = 2 * tokens * (2 * width + 4 * units) + 6 * width * units
    return pl.pallas_call(
        kernel,
        in_specs=[hbm] * 6,
        out_specs=[hbm] * 2,
        out_shape=[
            jax.ShapeDtypeStruct((tokens, 2 * units), BF16),
            jax.ShapeDtypeStruct((width, 2 * units), BF16),
        ],
        scratch_shapes=[
            pltpu.VMEM((2, BLOCK, units), BF16),
            pltpu.VMEM((2, BLOCK, units), BF16),
            pltpu.VMEM((2, BLOCK, part_width), BF16),
            pltpu.VMEM((2, BLOCK, part_width), BF16),
            pltpu.VMEM(w_down.shape, BF16),
            pltpu.VMEM((tokens, 2 * units), BF16),
            pltpu.SemaphoreType.DMA((4, 2)),
            pltpu.SemaphoreType.DMA((count,)),
            pltpu.VMEM((2, tokens, tile), BF16),
            pltpu.VMEM((2, tile, 2 * units), BF16),
            pltpu.SemaphoreType.DMA((3,)),
            pltpu.SemaphoreType.DMA((2,)),
        ],
        compiler_params=pltpu.CompilerParams(vmem_limit_bytes=VMEM_MOST),
        cost_estimate=pl.CostEstimate(
            flops=6 * tokens * width * units, bytes_accessed=moved, transcendentals=0
        ),
        name="feed_forward",
    )(slope, silu, cot_low, cot_high, w_down, rows_two)


def to_branch(g_both, w_both, middle, cot, w_attn, wide, hidden, w_down):
    tokens, width = g_both.shape[0], middle.shape[1]
    own = tokens // 8
    units = hidden.shape[1]
    tile = width // 2

    def kernel(
        g_ref, w_ref, mid_ref, cot_ref, o_ref, hid_ref, d_ref, gm_ref, rows_out, mix_ref, term_ref,
        g_buf, w_buf, hid_buf, d_buf, term_buf, load, term_store,
        mid_buf, cot_buf, o_buf, gm_buf, large, *rest,
    ):
        bufs, (s_send, s_receive, rows_ref, g_send, g_receive, store) = rest[:6], rest[6:]
        d, c, t = place_of()
        mine = pl.ds(pl.multiple_of(t * own, own), own)
        loads = (
            pltpu.make_async_copy(mid_ref, mid_buf, large.at[0]),
            pltpu.make_async_copy(cot_ref.at[mine], cot_buf, large.at[1]),
            pltpu.make_async_copy(o_ref.at[:, wide : 2 * wide], o_buf, large.at[2]),
        )
        stored = pltpu.make_async_copy(gm_buf, gm_ref, large.at[3])

        def fetch(i):
            part = pl.ds(pl.multiple_of(2 * scatter_order(i) * own, 2 * own), 2 * own)
            slot = lax.rem(i, 2)
            return pltpu.make_async_copy(g_ref.at[part], g_buf.at[slot], load.at[slot])

        weights = pltpu.make_async_copy(w_ref, w_buf, load.at[2])
        weights.start()
        fetch(0).start()
        say(around())
        weights.wait()
        down = pltpu.make_async_copy(d_ref, d_buf, load.at[3])
        down.start()
        for copy in loads:
            copy.start()
        pltpu.make_async_copy(
            hid_ref.at[pl.ds(0, BLOCK)], hid_buf, load.at[4]
        ).start()

        def terms(i, start):
            fetch(i).wait()

            @pl.when(i < 3)
            def _():
                fetch(i + 1).start()

            return [(g_buf[lax.rem(i, 2)], w_buf, slice(None))]

        total = scatter_rows(terms, bufs, s_send, s_receive, lambda: hear(3))
        for copy in loads:
            copy.wait()
        scale, hat = norm_parts(mid_buf[...])
        g_middle = cot_buf[...].astype(F32) + norm_back(total, hat, scale)
        gm_buf[...] = g_middle
        stored.start()
        rows_ref[pl.ds(pl.multiple_of((2 * c + t) * own, own), own), :] = g_middle.astype(BF16)

        def mix(start):
            mix_ref[pl.ds(start, own), :] = dot(
                rows_ref[pl.ds(start, own), :], o_buf[...], 1, 0
            ).astype(BF16)

        def block(i):
            return pl.ds(pl.multiple_of(i * BLOCK, BLOCK), BLOCK)

        def hidden_of(i):
            return pltpu.make_async_copy(hid_ref.at[block(i)], hid_buf, load.at[4])

        def term_given(i):
            return pltpu.make_async_copy(term_buf, term_ref.at[block(i)], term_store.at[0])

        def out_terms(first, last):
            @pl.loop(first, last)
            def _(i):
                hidden_of(i).wait()

                @pl.when(i > 0)
                def _():
                    term_given(i - 1).wait()

                for n in (0, 1):
                    columns = slice(n * tile, (n + 1) * tile)
                    term_buf[:, columns] = dot(
                        hid_buf[...], d_buf[columns, :units], 1, 1
                    ).astype(BF16)
                term_given(i).start()

                @pl.when(i + 1 < tokens // BLOCK)
                def _():
                    hidden_of(i + 1).start()

        down.wait()
        blocks = tokens // BLOCK
        gather_rows(
            rows_ref, rows_out, g_send, g_receive, store, mix,
            lambda: out_terms(0, blocks // 2),
            lambda: out_terms(blocks // 2, blocks - 1),
            lambda: out_terms(blocks - 1, blocks),
        )
        term_given(blocks - 1).wait()
        stored.wait()

    vmem, hbm = pl.BlockSpec(memory_space=pltpu.VMEM), pl.BlockSpec(memory_space=pl.ANY)
    return call(
        kernel, "to_branch", 5, (g_both, w_both, middle, cot, w_attn, hidden, w_down),
        [
            jax.ShapeDtypeStruct((own, width), F32),
            jax.ShapeDtypeStruct((tokens, width), BF16),
            jax.ShapeDtypeStruct((tokens, wide), BF16),
            jax.ShapeDtypeStruct((tokens, width), BF16),
        ],
        [
            pltpu.VMEM((2, 2 * own, g_both.shape[1]), BF16),
            pltpu.VMEM(w_both.shape, BF16),
            pltpu.VMEM((BLOCK, units), BF16),
            pltpu.VMEM(w_down.shape, BF16),
            pltpu.VMEM((BLOCK, width), BF16),
            pltpu.SemaphoreType.DMA((5,)),
            pltpu.SemaphoreType.DMA((1,)),
            pltpu.VMEM((own, width), F32),
            pltpu.VMEM((own, width), BF16),
            pltpu.VMEM((width, wide), BF16),
            pltpu.VMEM((own, width), F32),
            pltpu.SemaphoreType.DMA((4,)),
        ]
        + scatter_scratch(own, width) + sems(SCATTER_COPIES) + gather_scratch(tokens, width),
        [hbm] * 7,
        [hbm, hbm, vmem, hbm],
        flops=4 * tokens * width * (g_both.shape[1] // 2 + wide),
    )


def as_row(column):
    return jnp.transpose(jnp.broadcast_to(column, (column.shape[0], 128)), (1, 0))[:8]


def to_input(
    g_qkv, w_attn, x, g_middle, rows_one, branch, heads_out, sum_both, weights, gains, heads
):
    tokens, width = g_qkv.shape[0], x.shape[1]
    own = tokens // 8
    deep = lax.axis_size("dp")
    across = g_qkv.shape[1]
    group = width // deep
    held = group // 4
    wide, narrow = heads * DV, heads * F
    both = sum_both.shape[1]
    units = both // 2
    main = units // 128 * 128

    def kernel(
        g_ref, w_ref, x_ref, gm_ref, one_ref, br_ref, h_ref, both_ref,
        wq_ref, wk_ref, wv_ref, wg_ref, wu_ref, gain_ref, gain_two_ref,
        out_ref, gq_ref, gk_ref, gv_ref, go_ref, gg_ref, gu_ref, row_ref, row_two_ref,
        *rest,
    ):
        bufs, (s_send, s_receive, t_send, t_receive) = rest[:6], rest[6:10]
        (
            came_deep, came_out, sums, sums_out, parts_a, parts_o, parts_b, scalar, back_ref, back_out,
            cols, load, d_send, d_receive, p_send, p_receive, local, x_buf, gm_buf, in_buf, gate_buf,
            up_buf, large,
        ) = rest[10:]
        d, c, t = place_of()
        hand_on, landed = exchange(
            ((sums, parts_a), (both_ref, parts_b), (sums_out, parts_o)), held, p_send, p_receive, local
        )

        def fetch(j):
            part = pl.ds(pl.multiple_of(depth(d, j % deep + 1) * group, group), group)
            source = br_ref if j < deep else one_ref
            return pltpu.make_async_copy(source.at[:, part], cols.at[j % 2], load.at[j % 2])

        def deeper(j):
            n = j % deep
            source, target = (back_out, came_out) if j < deep else (back_ref, came_deep)
            return remote(
                source.at[n], target.at[n], d_send, d_receive, j, (depth(d, n + 1), c, t)
            )

        def plane(j):
            n = j % deep
            if j + 1 < 2 * deep:
                fetch(j + 1).start()
            fetch(j).wait()
            if j < deep:
                back_out[n] = dot(cols[j % 2], h_ref[...], 0, 0).astype(BF16)
            else:
                back_ref[n] = dot(cols[j % 2], g_ref[...], 0, 0).astype(BF16)

        def sum_of(back, came, first):
            total = back[deep - 1].astype(F32)
            for n in range(deep - 1):
                deeper(first + n).wait_recv()
                total = total + came[n].astype(F32)
            return total.astype(BF16)

        fetch(0).start()
        mine = pl.ds(pl.multiple_of(t * own, own), own)
        loads = (
            pltpu.make_async_copy(x_ref.at[mine], x_buf, large.at[0]),
            pltpu.make_async_copy(gm_ref, gm_buf, large.at[1]),
        )
        stored = pltpu.make_async_copy(in_buf, out_ref.at[mine], large.at[2])
        wide_stores = (
            pltpu.make_async_copy(gate_buf, gg_ref, large.at[3]),
            pltpu.make_async_copy(up_buf, gu_ref, large.at[4]),
        )
        for copy in loads:
            copy.start()
        met = (
            around()
            + [(d, beside(c, 3), t)]
            + [(depth(d, k), c, t) for k in range(1, deep)]
        )
        say(met)

        early = deep // 2
        for j in range(early):
            plane(j)

        def enter():
            hear(len(met))
            for j in range(early):
                deeper(j).start()

        def terms(i, start):
            part = pl.ds(start, 2 * own)
            return [
                (g_ref[part, :wide], w_ref, slice(0, wide)),
                (g_ref[part, wide:], w_ref, slice(2 * wide, None)),
            ]

        def fill(n):
            if n == 0:
                hand_on(1)
                for j in range(early, 2 * deep):
                    plane(j)
                    if j % deep != deep - 1:
                        deeper(j).start()
                return
            landed(1)
            whole = [parts_b[b].astype(F32) for b in range(4)]
            term = jnp.zeros((held, 1), F32)
            for ref, weight, first, rest_of in (
                (gate_buf, wg_ref, 0, 2 * main),
                (up_buf, wu_ref, main, main + units),
            ):
                pieces = []
                for b in range(4):
                    pieces.append(whole[b][:, first : first + main])
                    if main < units:
                        pieces.append(whole[b][:, rest_of : rest_of + units - main])
                s = jnp.concatenate(pieces, axis=1)
                term = term + jnp.sum(s * weight[...].astype(F32), axis=1, keepdims=True)
                ref[...] = s * gain_two_ref[...]
            for copy in wide_stores:
                copy.start()
            scalar[0, 1] = as_row(term)

        e_one = scatter_rows(terms, bufs, s_send, s_receive, enter, fill)
        for copy in loads:
            copy.wait()
        scale, hat = norm_parts(x_buf[...].astype(F32))
        in_buf[...] = gm_buf[...] + norm_back(e_one, hat, scale)
        copy = remote(in_buf, out_ref.at[mine], t_send, t_receive, 0, (d, c, 1 - t))
        copy.start()
        stored.start()
        sums_out[...] = sum_of(back_out, came_out, 0)
        hand_on(2)
        sums[...] = sum_of(back_ref, came_deep, deep)
        hand_on(0)
        landed(2)
        for b in range(4):
            go_ref[:, b * wide : (b + 1) * wide] = parts_o[b].astype(F32)
        landed(0)

        term_one = jnp.zeros((held, 1), F32)
        for ref, weight, start, count in (
            (gv_ref, wv_ref, 0, wide),
            (gq_ref, wq_ref, wide, narrow),
            (gk_ref, wk_ref, wide + narrow, narrow),
        ):
            s = jnp.concatenate(
                [parts_a[b][:, start : start + count].astype(F32) for b in range(4)], axis=1
            )
            term_one = term_one + jnp.sum(s * weight[...].astype(F32), axis=1, keepdims=True)
            ref[...] = s * gain_ref[...]
        scalar[0, 0] = as_row(term_one)
        swap = remote(scalar.at[0], scalar.at[1], t_send, t_receive, 1, (d, c, 1 - t))
        swap.start()
        swap.wait()
        row_ref[...] = (scalar[0, 0] + scalar[1, 0])[:1]
        row_two_ref[...] = (scalar[0, 1] + scalar[1, 1])[:1]
        copy.wait_send()
        there = out_ref.at[pl.ds(pl.multiple_of((1 - t) * own, own), own)]
        remote(there, there, t_send, t_receive, 0, (d, c, 1 - t)).wait_recv()
        for n in range(deep - 1):
            deeper(n).wait_send()
            deeper(deep + n).wait_send()
        stored.wait()
        for copy in wide_stores:
            copy.wait()

    w_q, w_k, w_v, w_gate, w_up = weights
    vmem, hbm = pl.BlockSpec(memory_space=pltpu.VMEM), pl.BlockSpec(memory_space=pl.ANY)
    return call(
        kernel, "to_input", 6,
        (g_qkv, w_attn, x, g_middle, rows_one, branch, heads_out, sum_both) + tuple(weights)
        + tuple(gains),
        [jax.ShapeDtypeStruct((2 * own, width), F32)]
        + [jax.ShapeDtypeStruct(w.shape, F32) for w in (w_q, w_k, w_v, w_v, w_gate, w_up)]
        + [jax.ShapeDtypeStruct((1, held), F32)] * 2,
        scatter_scratch(own, width) + sems(SCATTER_COPIES) + sems(2)
        + [
            pltpu.VMEM((deep - 1, group, across), BF16),
            pltpu.VMEM((deep - 1, group, wide), BF16),
            pltpu.VMEM((group, across), BF16),
            pltpu.VMEM((group, wide), BF16),
            pltpu.VMEM((4, held, across), BF16),
            pltpu.VMEM((4, held, wide), BF16),
            pltpu.VMEM((4, held, both), BF16),
            pltpu.VMEM((2, 2, 8, held), F32),
            pltpu.VMEM((deep, group, across), BF16),
            pltpu.VMEM((deep, group, wide), BF16),
            pltpu.VMEM((2, tokens, group), BF16),
            pltpu.SemaphoreType.DMA((2,)),
        ]
        + sems(2 * deep) + sems(9)
        + [
            pltpu.SemaphoreType.DMA((3,)),
            pltpu.VMEM((own, width), BF16),
            pltpu.VMEM((own, width), F32),
            pltpu.VMEM((own, width), F32),
            pltpu.VMEM(w_gate.shape, F32),
            pltpu.VMEM(w_up.shape, F32),
            pltpu.SemaphoreType.DMA((5,)),
        ],
        [vmem] * 2 + [hbm] * 4 + [vmem, hbm] + [vmem] * 7,
        [hbm] + [vmem] * 4 + [hbm] * 2 + [vmem] * 2,
        flops=2 * tokens * width * g_qkv.shape[1],
    )


def plane_shards(
    activations,
    seg_ids,
    cotangent,
    q_weight,
    k_weight,
    v_weight,
    o_weight,
    gate_weight,
    up_weight,
    down_weight,
    attn_gain,
    mlp_gain,
):
    parts = lax.axis_size("ctx")
    heads = q_weight.shape[1] // F // parts
    tokens = activations.shape[1] * parts
    x, cot_block = activations[0], cotangent[0]
    gain_one = attn_gain.astype(F32)[:, None]
    gain_two = mlp_gain.astype(F32)[:, None]
    rows_low, own_high, segments, w_attn, cut_both, cut_down = front(
        x,
        seg_ids,
        (q_weight, k_weight, v_weight, o_weight, gate_weight, up_weight, down_weight),
        (gain_one, gain_two),
        tokens,
        heads,
    )
    w_attn = w_attn.reshape(-1, w_attn.shape[3])
    w_both = lax.all_gather(cut_both, "dp", axis=0, tiled=True).reshape(-1, cut_both.shape[2])
    seg_rows, seg_cols = segments.reshape(tokens, 1), segments.reshape(1, tokens)
    qkv, mixed, denom, heads_out, cot_low, rows_one = attend(
        rows_low, own_high, w_attn, seg_rows, seg_cols, cot_block, heads
    )
    cut_down, heads_out = lax.optimization_barrier((cut_down, heads_out))
    w_down = lax.all_gather(cut_down, "dp", axis=0, tiled=True).reshape(-1, cut_down.shape[2])
    middle, rows_two = to_middle(heads_out, w_attn, x)
    hidden, slope, silu, cot_high, back_down = gate_up(rows_two, w_both, cot_block, cot_low)
    sum_down = lax.psum_scatter(back_down, "dp", scatter_dimension=0, tiled=True)
    g_both, back_both = feed_forward(slope, silu, cot_low, cot_high, w_down, rows_two)
    sum_both = lax.psum_scatter(back_both, "dp", scatter_dimension=0, tiled=True)
    g_middle, branch, g_mixed, out_terms = to_branch(
        g_both, w_both, middle, cot_block, w_attn, heads * DV, hidden, w_down
    )
    g_qkv, out, s_down = attend_back(
        qkv, g_mixed, mixed, denom, seg_rows, seg_cols, out_terms, middle, sum_down, heads
    )
    g_input, s_q, s_k, s_v, s_o, s_gate, s_up, attn_row, mlp_row = to_input(
        g_qkv,
        w_attn,
        x,
        g_middle,
        rows_one,
        branch,
        heads_out,
        sum_both,
        (q_weight, k_weight, v_weight, gate_weight, up_weight),
        (gain_one, gain_two),
        heads,
    )
    return (
        out[None],
        g_input[None],
        s_q,
        s_k,
        s_v,
        s_o,
        s_gate,
        s_up,
        s_down,
        attn_row[0],
        mlp_row[0],
    )


def layer(*arrays):
    heads = arrays[3].shape[1] // F
    plan = shards if heads % lax.axis_size("ctx") else plane_shards
    return plan(*arrays)


def solution(mesh):
    placed = (
        P("dp", "ctx", None),
        P("dp", "ctx"),
        P("dp", "ctx", None),
        P(("dp", "ctx"), "tp"),
        P(("dp", "ctx"), "tp"),
        P(("dp", "ctx"), "tp"),
        P(("dp", "ctx"), "tp"),
        P(("dp", "ctx"), "tp"),
        P(("dp", "ctx"), "tp"),
        P(("dp", "ctx"), "tp"),
        P(("dp", "ctx")),
        P(("dp", "ctx")),
    )
    return jax.shard_map(
        layer,
        mesh=mesh,
        in_specs=placed,
        out_specs=(
            P("dp", "ctx", None),
            P("dp", "ctx", None),
            P(("dp", "ctx"), "tp"),
            P(("dp", "ctx"), "tp"),
            P(("dp", "ctx"), "tp"),
            P(("dp", "ctx"), "tp"),
            P(("dp", "ctx"), "tp"),
            P(("dp", "ctx"), "tp"),
            P(("dp", "ctx"), "tp"),
            P(("dp", "ctx")),
            P(("dp", "ctx")),
        ),
        check_vma=False,
    )
```

```python
import functools

import jax
import jax.numpy as jnp
from jax import lax
from jax.experimental import pallas as pl
from jax.experimental.pallas import tpu as pltpu
from jax.sharding import PartitionSpec as P

F = 16
DV = 128


EPSILON = 1e-05
PRECISE = lax.Precision.HIGHEST
VMEM_MOST = 60 * 2**20


def prefix(x, axis, join, neutral, backward):
    count = lax.axis_size(axis)
    place = lax.axis_index(axis)
    ahead = count - 1 - place if backward else place
    gathered = jax.tree.map(
        lambda a, kind: lax.all_gather(a.astype(kind), axis),
        x,
        (jnp.bfloat16, jnp.bfloat16, jnp.bfloat16),
    )
    state = jax.tree.map(lambda a, e: jnp.zeros_like(a) + jnp.asarray(e, a.dtype), x, neutral)

    def one(lap, state):
        source = count - 1 - lap if backward else lap
        return join(
            state,
            jax.tree.map(
                lambda a, own: lax.dynamic_index_in_dim(a, source, 0, False).astype(own.dtype),
                gathered,
                x,
            ),
        )

    return lax.fori_loop(0, ahead, one, state)


def taylor(features_in):
    feature_count = features_in.shape[-1]
    products = (features_in[..., :, None] * features_in[..., None, :]).reshape(
        features_in.shape[:-1] + (feature_count * feature_count,)
    )
    constant = jnp.ones(features_in.shape[:-1] + (1,), jnp.float32)
    return jnp.concatenate(
        [
            constant,
            features_in * feature_count ** (-0.25),
            products * (2.0 * feature_count) ** (-0.5),
        ],
        axis=-1,
    )


def taylor_back(features_in, incoming_gradient):
    feature_count = features_in.shape[-1]
    linear = incoming_gradient[..., 1 : 1 + feature_count] * feature_count ** (-0.25)
    square = incoming_gradient[..., 1 + feature_count :].reshape(
        incoming_gradient.shape[:-1] + (feature_count, feature_count)
    )
    paired = jnp.einsum(
        "...ab,...b->...a", square + jnp.swapaxes(square, -1, -2), features_in, precision=PRECISE
    )
    return linear + paired * (2.0 * feature_count) ** (-0.5)


def norm_backward_step(incoming_gradient, unit_normalized_rows, multiplier_term, gain_vector_row):
    rescaled_rows = incoming_gradient * gain_vector_row
    return multiplier_term * (
        rescaled_rows
        - unit_normalized_rows
        * jnp.mean(rescaled_rows * unit_normalized_rows, axis=1, keepdims=True)
    )


def join_states(earlier, later_part):
    is_empty = later_part[2] < 0.0
    retain = jnp.where(is_empty | (earlier[2] == later_part[2]), 1.0, 0.0).astype(jnp.float32)
    return (
        later_part[0] + retain * earlier[0],
        later_part[1] + retain * earlier[1],
        jnp.where(is_empty, earlier[2], later_part[2]),
    )


def shards(
    activations,
    seg_ids,
    cotangent,
    q_weight,
    k_weight,
    v_weight,
    o_weight,
    gate_weight,
    up_weight,
    down_weight,
    attn_gain,
    mlp_gain,
):
    layer_input_rows = activations[0].astype(jnp.float32)
    segment = seg_ids[0].astype(jnp.float32)
    tokens = layer_input_rows.shape[0]
    head_count = q_weight.shape[1] // F
    w_query, w_key, w_value, w_out, first_norm_gain = (
        lax.all_gather(q_weight, ("dp", "ctx"), axis=0, tiled=True),
        lax.all_gather(k_weight, ("dp", "ctx"), axis=0, tiled=True),
        lax.all_gather(v_weight, ("dp", "ctx"), axis=0, tiled=True),
        lax.all_gather(o_weight, ("dp", "ctx"), axis=0, tiled=True),
        lax.all_gather(attn_gain, ("dp", "ctx"), axis=0, tiled=True),
    )
    first_inverse_scale = lax.rsqrt(
        jnp.mean(layer_input_rows * layer_input_rows, axis=1, keepdims=True) + EPSILON
    )
    first_unit_rows = layer_input_rows * first_inverse_scale
    first_normalized = (first_unit_rows * first_norm_gain.astype(jnp.float32)).astype(jnp.bfloat16)
    queries = (
        jnp.dot(first_normalized, w_query, preferred_element_type=jnp.float32)
        .astype(jnp.bfloat16)
        .reshape(tokens, head_count, F)
    )
    key_heads = (
        jnp.dot(first_normalized, w_key, preferred_element_type=jnp.float32)
        .astype(jnp.bfloat16)
        .reshape(tokens, head_count, F)
    )
    value_heads = (
        jnp.dot(first_normalized, w_value, preferred_element_type=jnp.float32)
        .astype(jnp.bfloat16)
        .reshape(tokens, head_count, DV)
    )
    w_gate, w_up, w_down, second_norm_gain = (
        lax.all_gather(gate_weight, ("dp", "ctx"), axis=0, tiled=True),
        lax.all_gather(up_weight, ("dp", "ctx"), axis=0, tiled=True),
        lax.all_gather(down_weight, ("dp", "ctx"), axis=0, tiled=True),
        lax.all_gather(mlp_gain, ("dp", "ctx"), axis=0, tiled=True),
    )
    scores = jnp.einsum(
        "thf,shf->hts", queries, key_heads, preferred_element_type=jnp.float32
    ) * F ** (-0.5)
    places = jnp.arange(tokens)
    visible = (
        (places[:, None] >= places[None, :]) & (segment[:, None] == segment[None, :])
    ).astype(jnp.float32)
    weights = (visible * (1.0 + scores + 0.5 * scores * scores)).astype(jnp.bfloat16)
    query_float = queries.astype(jnp.float32)
    key_float = key_heads.astype(jnp.float32)
    value_float = value_heads.astype(jnp.float32)
    feat_q = taylor(query_float)
    feat_k = taylor(key_float)
    ending = segment[-1]
    owned = (segment == ending).astype(jnp.float32)[:, None, None]
    local_state = jnp.einsum("thf,thd->hfd", feat_k * owned, value_float, precision=PRECISE)
    local_total = jnp.sum(feat_k * owned, axis=0)
    empty_state = (jnp.zeros_like(local_state), jnp.zeros_like(local_total), jnp.float32(-1.0))
    prior_state, prior_total, before = prefix(
        (local_state, local_total, ending), "ctx", join_states, empty_state, False
    )
    inherit = (segment == before).astype(jnp.float32)
    numerator = jnp.einsum(
        "hts,shd->thd", weights, value_heads, preferred_element_type=jnp.float32
    ) + inherit[:, None, None] * jnp.einsum("thf,hfd->thd", feat_q, prior_state, precision=PRECISE)
    denominator = jnp.sum(weights.astype(jnp.float32), axis=2).T + inherit[:, None] * jnp.einsum(
        "thf,hf->th", feat_q, prior_total, precision=PRECISE
    )
    mixed_heads = numerator / denominator[:, :, None]
    heads_out = mixed_heads.reshape(tokens, head_count * DV).astype(jnp.bfloat16)
    attn_out = lax.psum(
        jnp.einsum("tc,dc->td", heads_out, w_out, preferred_element_type=jnp.float32), "tp"
    )
    residual_midpoint = layer_input_rows + attn_out
    second_inverse_scale = lax.rsqrt(
        jnp.mean(residual_midpoint * residual_midpoint, axis=1, keepdims=True) + EPSILON
    )
    second_unit_rows = residual_midpoint * second_inverse_scale
    second_normalized = (second_unit_rows * second_norm_gain.astype(jnp.float32)).astype(
        jnp.bfloat16
    )
    gate_value = jnp.dot(second_normalized, w_gate, preferred_element_type=jnp.float32)
    up_value = jnp.dot(second_normalized, w_up, preferred_element_type=jnp.float32)
    sigmoid_gate = jax.nn.sigmoid(gate_value)
    hidden = (gate_value * sigmoid_gate * up_value).astype(jnp.bfloat16)
    mlp_out = lax.psum(
        jnp.einsum("tc,dc->td", hidden, w_down, preferred_element_type=jnp.float32).astype(
            jnp.bfloat16
        ),
        "tp",
    ).astype(jnp.float32)
    final_out = residual_midpoint + mlp_out
    grad_out = cotangent[0].astype(jnp.float32)
    grad_branch_two = cotangent[0]
    grad_w_down = jnp.einsum(
        "td,tc->dc", grad_branch_two, hidden, preferred_element_type=jnp.float32
    )
    grad_hidden = jnp.dot(grad_branch_two, w_down, preferred_element_type=jnp.float32)
    grad_gate = (
        grad_hidden * up_value * sigmoid_gate * (1.0 + gate_value * (1.0 - sigmoid_gate))
    ).astype(jnp.bfloat16)
    grad_up = (grad_hidden * gate_value * sigmoid_gate).astype(jnp.bfloat16)
    grad_w_gate = jnp.einsum(
        "td,tc->dc", second_normalized, grad_gate, preferred_element_type=jnp.float32
    )
    grad_w_up = jnp.einsum(
        "td,tc->dc", second_normalized, grad_up, preferred_element_type=jnp.float32
    )
    grad_normed_part = jnp.einsum(
        "tc,dc->td", grad_gate, w_gate, preferred_element_type=jnp.float32
    ) + jnp.einsum("tc,dc->td", grad_up, w_up, preferred_element_type=jnp.float32)
    second_normalized_gradient = lax.psum(grad_normed_part.astype(jnp.bfloat16), "tp").astype(
        jnp.float32
    )
    second_gain_gradient = jnp.sum(second_normalized_gradient * second_unit_rows, axis=0)
    grad_middle = grad_out + norm_backward_step(
        second_normalized_gradient,
        second_unit_rows,
        second_inverse_scale,
        second_norm_gain.astype(jnp.float32),
    )
    mlp_grads = (
        lax.psum_scatter(grad_w_gate, ("dp", "ctx"), scatter_dimension=0, tiled=True),
        lax.psum_scatter(grad_w_up, ("dp", "ctx"), scatter_dimension=0, tiled=True),
        lax.psum_scatter(grad_w_down, ("dp", "ctx"), scatter_dimension=0, tiled=True),
        lax.psum_scatter(second_gain_gradient, ("dp", "ctx"), scatter_dimension=0, tiled=True),
    )
    grad_branch_one = grad_middle.astype(jnp.bfloat16)
    grad_w_out = jnp.einsum(
        "td,tc->dc", grad_branch_one, heads_out, preferred_element_type=jnp.float32
    )
    grad_heads_low = jnp.dot(grad_branch_one, w_out, preferred_element_type=jnp.float32).astype(
        jnp.bfloat16
    )
    grad_mixed = (
        lax.optimization_barrier(grad_heads_low).astype(jnp.float32).reshape(tokens, head_count, DV)
    )
    numer_low = (grad_mixed / denominator[:, :, None]).astype(jnp.bfloat16)
    grad_numer = lax.optimization_barrier(numer_low).astype(jnp.float32)
    grad_denom = -jnp.sum(grad_mixed * mixed_heads, axis=2) / denominator
    grad_weights = (
        jnp.einsum("thd,shd->hts", numer_low, value_heads, preferred_element_type=jnp.float32)
        + grad_denom.T[:, :, None]
    )
    grad_scores = (grad_weights * visible * (1.0 + scores)).astype(jnp.bfloat16)
    grad_value = jnp.einsum("hts,thd->shd", weights, numer_low, preferred_element_type=jnp.float32)
    grad_query = jnp.einsum(
        "hts,shf->thf", grad_scores, key_heads, preferred_element_type=jnp.float32
    ) * F ** (-0.5)
    grad_key = jnp.einsum(
        "hts,thf->shf", grad_scores, queries, preferred_element_type=jnp.float32
    ) * F ** (-0.5)
    grad_feat_q = inherit[:, None, None] * (
        jnp.einsum("thd,hfd->thf", grad_numer, prior_state, precision=PRECISE)
        + grad_denom[:, :, None] * prior_total[None]
    )
    carried_state = jnp.einsum(
        "thf,thd->hfd", feat_q * inherit[:, None, None], grad_numer, precision=PRECISE
    )
    carried_total = jnp.sum(feat_q * (inherit[:, None] * grad_denom)[:, :, None], axis=0)
    starting = segment[0]
    later_state, later_total, after_seg = prefix(
        (carried_state, carried_total, starting), "ctx", join_states, empty_state, True
    )
    reached = (segment == after_seg).astype(jnp.float32)[:, None, None]
    grad_feat_k = reached * (
        jnp.einsum("hfd,thd->thf", later_state, value_float, precision=PRECISE) + later_total[None]
    )
    grad_value = grad_value + reached * jnp.einsum(
        "thf,hfd->thd", feat_k, later_state, precision=PRECISE
    )
    grad_query = grad_query + taylor_back(query_float, grad_feat_q)
    grad_key = grad_key + taylor_back(key_float, grad_feat_k)
    grad_query_low = grad_query.reshape(tokens, head_count * F).astype(jnp.bfloat16)
    grad_key_low = grad_key.reshape(tokens, head_count * F).astype(jnp.bfloat16)
    grad_value_low = grad_value.reshape(tokens, head_count * DV).astype(jnp.bfloat16)
    grad_w_query = jnp.einsum(
        "td,tc->dc", first_normalized, grad_query_low, preferred_element_type=jnp.float32
    )
    grad_w_key = jnp.einsum(
        "td,tc->dc", first_normalized, grad_key_low, preferred_element_type=jnp.float32
    )
    grad_w_value = jnp.einsum(
        "td,tc->dc", first_normalized, grad_value_low, preferred_element_type=jnp.float32
    )
    grad_normed_sum = (
        jnp.einsum("tc,dc->td", grad_query_low, w_query, preferred_element_type=jnp.float32)
        + jnp.einsum("tc,dc->td", grad_key_low, w_key, preferred_element_type=jnp.float32)
        + jnp.einsum("tc,dc->td", grad_value_low, w_value, preferred_element_type=jnp.float32)
    )
    first_normalized_gradient = lax.psum(grad_normed_sum.astype(jnp.bfloat16), "tp").astype(
        jnp.float32
    )
    first_gain_gradient = jnp.sum(first_normalized_gradient * first_unit_rows, axis=0)
    grad_inputs = grad_middle + norm_backward_step(
        first_normalized_gradient,
        first_unit_rows,
        first_inverse_scale,
        first_norm_gain.astype(jnp.float32),
    )
    attn_grads = (
        lax.psum_scatter(grad_w_query, ("dp", "ctx"), scatter_dimension=0, tiled=True),
        lax.psum_scatter(grad_w_key, ("dp", "ctx"), scatter_dimension=0, tiled=True),
        lax.psum_scatter(grad_w_value, ("dp", "ctx"), scatter_dimension=0, tiled=True),
        lax.psum_scatter(grad_w_out, ("dp", "ctx"), scatter_dimension=0, tiled=True),
        lax.psum_scatter(first_gain_gradient, ("dp", "ctx"), scatter_dimension=0, tiled=True),
    )
    return (
        final_out.astype(jnp.bfloat16)[None],
        grad_inputs[None],
        attn_grads[0],
        attn_grads[1],
        attn_grads[2],
        attn_grads[3],
        mlp_grads[0],
        mlp_grads[1],
        mlp_grads[2],
        attn_grads[4],
        mlp_grads[3],
    )


BLOCK = 512


MESH = pl.DeviceIdType.MESH
BF16, F32 = jnp.bfloat16, jnp.float32


def dot(a, b, ca, cb):
    return lax.dot_general(a, b, (((ca,), (cb,)), ((), ())), preferred_element_type=F32)


def place_of():
    return lax.axis_index("dp"), lax.axis_index("ctx"), lax.axis_index("tp")


def beside(c, across):
    x, y = lax.rem(c, 2), lax.div(c, 2)
    return lax.rem(x + across % 2, 2) + 2 * lax.rem(y + across // 2, 2)


def say(devices):
    barrier = pltpu.get_barrier_semaphore()
    for device in devices:
        pl.semaphore_signal(barrier, inc=1, device_id=device, device_id_type=MESH)


def hear(count):
    pl.semaphore_wait(pltpu.get_barrier_semaphore(), count)


def greet(devices):
    say(devices)
    hear(len(devices))


def around():
    d, c, t = place_of()
    return [(d, beside(c, 1), t), (d, beside(c, 2), t), (d, c, 1 - t)]


def remote(source, target, send, receive, k, device):
    return pltpu.make_async_remote_copy(
        src_ref=source,
        dst_ref=target,
        send_sem=send.at[k],
        recv_sem=receive.at[k],
        device_id=device,
        device_id_type=MESH,
    )


def gather_steps(buf, send, receive):
    d, c, t = place_of()
    own = buf.shape[0] // 8
    half = own // 2

    def part(across, core, h):
        block = c if across == 0 else beside(c, across)
        start = (2 * block + core) * own + h * half
        return buf.at[pl.ds(pl.multiple_of(start, half), half)]

    def put(k, across, h, device):
        ref = part(across, t, h)
        copy = remote(ref, ref, send, receive, k, device)
        copy.start()
        return copy

    return put, part


def gather_begin(buf, send, receive):
    put, _ = gather_steps(buf, send, receive)
    to_x, to_y, to_t = around()
    return [
        put(0, 0, 0, to_x),
        put(1, 0, 1, to_y),
        put(2, 0, 1, to_x),
        put(3, 0, 0, to_y),
        put(6, 0, 0, to_t),
        put(7, 0, 1, to_t),
    ]


def gather_rows(
    buf, out, send, receive, store, piece=None, early=None, middle=None, late=None, begun=None
):
    d, c, t = place_of()
    own = buf.shape[0] // 8
    to_x, to_y, to_t = around()
    put, part = gather_steps(buf, send, receive)
    started = gather_begin(buf, send, receive) if begun is None else begun

    def got(k, across, core, h):
        ref = part(across, core, h)
        remote(ref, ref, send, receive, k, to_t).wait_recv()

    stored = []

    def work(across, core):
        block = c if across == 0 else beside(c, across)
        start = pl.multiple_of((2 * block + core) * own, own)
        rows = pl.ds(start, own)
        copy = pltpu.make_async_copy(buf.at[rows], out.at[rows], store.at[len(stored)])
        copy.start()
        stored.append(copy)
        if piece is not None:
            piece(start)

    if early is not None:
        early()
    work(0, t)
    got(6, 0, 1 - t, 0)
    got(7, 0, 1 - t, 1)
    work(0, 1 - t)
    got(0, 1, t, 0)
    started.append(put(4, 1, 0, to_y))
    started.append(put(8, 1, 0, to_t))
    got(1, 2, t, 1)
    started.append(put(5, 2, 1, to_x))
    started.append(put(9, 2, 1, to_t))
    if middle is not None:
        middle()
    got(2, 1, t, 1)
    started.append(put(10, 1, 1, to_t))
    got(3, 2, t, 0)
    started.append(put(11, 2, 0, to_t))
    if late is not None:
        late()
    work(1, t)
    work(2, t)
    got(8, 1, 1 - t, 0)
    got(10, 1, 1 - t, 1)
    work(1, 1 - t)
    got(9, 2, 1 - t, 1)
    got(11, 2, 1 - t, 0)
    work(2, 1 - t)
    got(4, 3, t, 0)
    started.append(put(12, 3, 0, to_t))
    got(5, 3, t, 1)
    started.append(put(13, 3, 1, to_t))
    work(3, t)
    got(12, 3, 1 - t, 0)
    got(13, 3, 1 - t, 1)
    work(3, 1 - t)
    for copy in started:
        copy.wait_send()
    for copy in stored:
        copy.wait()


GATHER_COPIES = 14


def gather_scratch(tokens, width):
    return (
        [pltpu.VMEM((tokens, width), BF16)]
        + sems(GATHER_COPIES)
        + [pltpu.SemaphoreType.DMA((8,))]
    )


def exchange(jobs, held, send, receive, local):
    d, c, t = place_of()

    def rows_of(block):
        return pl.ds(pl.multiple_of(block * held, held), held)

    def to_block(n, k):
        source, target = jobs[n]
        return remote(
            source.at[rows_of(beside(c, k))], target.at[c], send, receive, 3 * n + k - 1,
            (d, beside(c, k), t),
        )

    def from_block(n, k):
        there = jobs[n][1].at[beside(c, k)]
        return remote(there, there, send, receive, 3 * n + k - 1, (d, beside(c, k), t))

    def at_home(n):
        source, target = jobs[n]
        return pltpu.make_async_copy(source.at[rows_of(c)], target.at[c], local.at[n])

    def hand_on(n):
        for k in (3, 1, 2):
            to_block(n, k).start()
        at_home(n).start()

    def landed(n):
        at_home(n).wait()
        for k in (1, 2, 3):
            from_block(n, k).wait_recv()
            to_block(n, k).wait_send()

    return hand_on, landed


PARTS = 2


def scatter_order(i):
    c = lax.axis_index("ctx")
    across = 3 - i
    x, y = lax.rem(c, 2), lax.div(c, 2)
    return lax.rem(x + lax.rem(across, 2), 2) + 2 * lax.rem(y + lax.div(across, 2), 2)


def scatter_rows(terms, bufs, send, receive, enter, fill=None):
    to_core, from_core, kept, over, came, stage = bufs
    d, c, t = place_of()
    own, tile = kept.shape[2:]
    half = own // 2
    to_x, to_y, to_t = (d, beside(c, 1), t), (d, beside(c, 2), t), (d, c, 1 - t)

    def link(k, n):
        return remote(
            over.at[k, n], came.at[k, n], send, receive, PARTS * (4 + k) + n, to_x if k % 2 == 0 else to_y
        )

    def core(i, n):
        return remote(to_core.at[lax.rem(i, 2), n], from_core.at[i, n], send, receive, PARTS * i + n, to_t)

    def total(i, h, n, *extra):
        out = kept[i % 3, n, pl.ds(h * half, half), :]
        for k in extra:
            out = out + came[k, n].astype(F32)
        return out

    def go(k, i, h, n, *extra):
        over[k, n] = total(i, h, n, *extra).astype(BF16)
        link(k, n).start()

    def joined(i, n):
        core(i, n).wait_recv()
        kept[lax.rem(i, 3), n] = kept[lax.rem(i, 3), n] + from_core[i, n].astype(F32)

    def product(pairs, i, n):
        columns = pl.ds(n * tile, tile)
        theirs = pl.ds(pl.multiple_of((1 - t) * own, own), own)
        mine = pl.ds(pl.multiple_of(t * own, own), own)
        if not isinstance(pairs, list):
            to_core[lax.rem(i, 2), n] = pairs[theirs, columns]
            kept[lax.rem(i, 3), n] = pairs[mine, columns].astype(F32)
            return
        out = None
        for rows, matrix, part in pairs:
            term = dot(rows, matrix[columns, part], 1, 1)
            out = term if out is None else out + term
        stage[...] = out
        to_core[lax.rem(i, 2), n] = stage[theirs, :].astype(BF16)
        kept[lax.rem(i, 3), n] = stage[mine, :]

    def begin(i):
        return pl.multiple_of(2 * scatter_order(i) * own, 2 * own)

    pairs = terms(0, begin(0))
    for n in range(PARTS):
        product(pairs, 0, n)
        if n == 0:
            enter()
        core(0, n).start()
        if n > 0:
            joined(0, n - 1)
            go(0, 0, 0, n - 1)
            go(1, 0, 1, n - 1)
    joined(0, PARTS - 1)
    go(0, 0, 0, PARTS - 1)
    go(1, 0, 1, PARTS - 1)

    def step(i, carry):
        pairs = terms(i, begin(i))

        @pl.when(i >= 2)
        def _():
            for n in range(PARTS):
                core(i - 2, n).wait_send()

        product(pairs, i, 0)
        core(i, 0).start()

        @pl.when(i == 2)
        def _():
            for n in range(PARTS):
                joined(1, n)
                go(3, 1, 1, n)

        @pl.when(i == 3)
        def _():
            for n in range(PARTS):
                joined(2, n)
                go(2, 2, 0, n)

        for n in range(1, PARTS):
            product(pairs, i, n)
            core(i, n).start()

        return carry

    lax.fori_loop(1, 4, step, 0)
    if fill is not None:
        fill(0)
    for n in range(PARTS):
        link(0, n).wait_recv()
        link(1, n).wait_recv()
        go(4, 2, 1, n, 1)
        go(5, 1, 0, n, 0)
    for n in range(PARTS):
        joined(3, n)
    if fill is not None:
        fill(1)
    for n in range(PARTS):
        for k in (2, 3, 4, 5):
            link(k, n).wait_recv()
        core(2, n).wait_send()
        core(3, n).wait_send()
        for k in range(6):
            link(k, n).wait_send()
    return jnp.concatenate(
        [
            jnp.concatenate([total(3, 0, n, 2, 5), total(3, 1, n, 3, 4)], axis=0)
            for n in range(PARTS)
        ],
        axis=1,
    )


SCATTER_COPIES = 10 * PARTS


def scatter_scratch(own, width):
    tile = width // PARTS
    return [
        pltpu.VMEM((2, PARTS, own, tile), BF16),
        pltpu.VMEM((4, PARTS, own, tile), BF16),
        pltpu.VMEM((3, PARTS, own, tile), F32),
        pltpu.VMEM((6, PARTS, own // 2, tile), BF16),
        pltpu.VMEM((6, PARTS, own // 2, tile), BF16),
        pltpu.VMEM((2 * own, tile), F32),
    ]


def norm_parts(rows):
    scale = lax.rsqrt(jnp.mean(rows * rows, axis=1, keepdims=True) + EPSILON)
    return scale, rows * scale


def norm_back(e, hat, scale):
    return scale * (e - hat * jnp.mean(e * hat, axis=1, keepdims=True))


def call(kernel, name, collective, arrays, out_shape, scratch, spaces=None, out_spaces=None, flops=0):
    vmem = pl.BlockSpec(memory_space=pltpu.VMEM)
    moved = sum(a.size * a.dtype.itemsize for a in arrays)
    return pl.pallas_call(
        kernel,
        in_specs=spaces or [vmem] * len(arrays),
        out_specs=out_spaces or [vmem] * len(out_shape),
        out_shape=out_shape,
        scratch_shapes=scratch,
        compiler_params=pltpu.CompilerParams(
            collective_id=collective, has_side_effects=True, vmem_limit_bytes=VMEM_MOST
        ),
        cost_estimate=pl.CostEstimate(flops=flops, bytes_accessed=moved, transcendentals=0),
        name=name,
    )(*arrays)


def sems(count):
    return [pltpu.SemaphoreType.DMA((count,)), pltpu.SemaphoreType.DMA((count,))]


def depth(d, k):
    return lax.rem(d + k, lax.axis_size("dp"))


def as_column(row):
    return jnp.transpose(jnp.broadcast_to(row, (128, row.shape[1])), (1, 0))[:, :1]


def columns(ref, gain, start, count):
    low = start // 128 * 128
    high = -(-(start + count) // 128) * 128
    value = ref[:, low:high].astype(F32)
    if gain is not None:
        value = value * gain
    return value[:, start - low : start - low + count]


def packed_down(held, units):
    return units // 128 * held + (held // 2 if units % 128 else 0)


def down_scratch(w_down, units):
    return [
        pltpu.VMEM((w_down.shape[0], w_down.shape[1] * 128 // units, -(-units // 128) * 128), BF16),
        pltpu.VMEM((w_down.shape[0], w_down.shape[1] * 64 // units, 128), BF16),
        pltpu.SemaphoreType.DMA((-(-units // 128),)),
    ]


def load_down(w_ref, w_buf, rest_buf, load, units):
    held = w_buf.shape[1]
    tiles = units // 128
    copies = [
        pltpu.make_async_copy(
            w_ref.at[:, n * held : (n + 1) * held], w_buf.at[:, :, n * 128 : (n + 1) * 128], load.at[n]
        )
        for n in range(tiles)
    ]
    if units % 128:
        copies.append(pltpu.make_async_copy(w_ref.at[:, tiles * held :], rest_buf, load.at[tiles]))

    def finish():
        for copy in copies:
            copy.wait()
        if units % 128:
            w_buf[:, : held // 2, tiles * 128 : units] = rest_buf[:, :, :64]
            w_buf[:, held // 2 :, tiles * 128 : units] = rest_buf[:, :, 64:]

    for copy in copies:
        copy.start()
    return finish


def down_rows(w_buf, first, last, units):
    held = w_buf.shape[1]
    rows = w_buf[first // held : last // held, :, :units]
    return rows.reshape(last - first, units)


def front(x, seg, weights, gains, tokens, heads):
    width = x.shape[1]
    own = tokens // 8
    deep = lax.axis_size("dp")
    held, units = weights[4].shape[0], weights[4].shape[1] // 4
    wide, narrow = heads * DV, heads * F
    main = units // 128 * 128
    packed = 2 * wide + 2 * narrow
    part_width = width // 2
    down_shape = (4, packed_down(held, units), 128)
    line = {
        0: (((0, 2),), ((0, 1),), ()),
        1: (((1, 0),), ((1, 2), (1, 3)), ((3, 0),)),
        2: (((2, 3),), ((2, 1), (2, 0)), ((0, 3),)),
        3: (((3, 1),), ((3, 2),), ()),
    }
    if deep != 4:
        line = {
            p: (tuple((p, to) for to in range(deep) if to != p), (), ()) for p in range(deep)
        }

    def kernel(
        x_ref, seg_ref, q_ref, k_ref, v_ref, o_ref, g_ref, u_ref, d_ref, one_ref, two_ref,
        rows_out, own_ref, segs_ref, wa_out, wg_out, wd_out,
        cut_a, cut_g, cut_d, rows_ref, send, receive, store, small_send, small_receive, deep_send, deep_receive, here,
    ):
        d, c, t = place_of()
        jobs = (
            (lambda block: cut_a.at[block], lambda block: wa_out.at[d, block]),
            (lambda block: seg_ref.at[0], lambda block: segs_ref.at[block]),
            (lambda block: cut_g.at[block], lambda block: wg_out.at[block]),
            (lambda block: cut_d.at[block], lambda block: wd_out.at[block]),
        )

        def local(n):
            return pltpu.make_async_copy(jobs[n][0](c), jobs[n][1](c), here.at[n])

        def out(n, k):
            return remote(
                jobs[n][0](beside(c, k)), jobs[n][1](c), small_send, small_receive,
                3 * n + k - 1, (d, beside(c, k), t),
            )

        def arrival(n, k):
            block = beside(c, k)
            return remote(
                jobs[n][0](block), jobs[n][1](block), small_send, small_receive,
                3 * n + k - 1, (d, block, t),
            )

        def shard(slot, s, to):
            return pltpu.make_async_remote_copy(
                src_ref=wa_out.at[s], dst_ref=wa_out.at[s], send_sem=deep_send.at[slot],
                recv_sem=deep_receive.at[s], device_id=(to, c, t), device_id_type=MESH,
            )

        def in_plane(act):
            for p in range(deep):
                pl.when(d == p)(functools.partial(act, p, *line[p]))

        def first_shards(p, first, then, on):
            for slot, (s, to) in enumerate(first):
                shard(slot, s, to).start()

        def other_shards(p, first, then, on):
            for slot, (s, to) in enumerate(then):
                shard(len(first) + slot, s, to).start()
            for slot, (s, to) in enumerate(on):
                shard(len(first) + len(then) + slot, s, to).wait_recv()
                shard(len(first) + len(then) + slot, s, to).start()

        def end_shards(p, first, then, on):
            for s in range(deep):
                if s != p and s not in [handed for handed, _ in on]:
                    shard(0, s, (p + 1) % deep).wait_recv()
            for slot, (s, to) in enumerate(first + then + on):
                shard(slot, s, to).wait_send()

        one, two = as_column(one_ref[...].astype(F32)), as_column(two_ref[...].astype(F32))
        met = (
            [(d, beside(c, k), t) for k in (1, 2, 3)]
            + [(d, c, 1 - t)]
            + [(depth(d, k), c, t) for k in range(1, deep)]
        )
        say(met)
        for b in range(4):
            cut_a[b, :, :wide] = columns(v_ref, one, b * wide, wide).astype(BF16)
            cut_a[b, :, wide : 2 * wide] = o_ref[:, b * wide : (b + 1) * wide]
            cut_a[b, :, 2 * wide :] = jnp.concatenate(
                [columns(ref, one, b * narrow, narrow) for ref in (q_ref, k_ref)], axis=1
            ).astype(BF16)
        hear(len(met))
        local(0).start()
        for k in (3, 1, 2):
            out(0, k).start()
        mine = pl.multiple_of((2 * c + t) * own, own)
        _, hat = norm_parts(x_ref[pl.ds(pl.multiple_of(t * own, own), own), :].astype(F32))
        rows_ref[pl.ds(mine, own), :] = hat[:, :part_width].astype(BF16)
        own_ref[...] = hat[:, part_width:].astype(BF16)
        local(0).wait()
        for k in (1, 2, 3):
            arrival(0, k).wait_recv()
        in_plane(first_shards)

        def early():
            for b in range(4):
                start = b * units
                cut_g[b, :, :main] = columns(g_ref, two, start, main).astype(BF16)
                cut_g[b, :, main : 2 * main] = columns(u_ref, two, start, main).astype(BF16)
                if main < units:
                    cut_g[b, :, 2 * main :] = jnp.concatenate(
                        [columns(r, two, start + main, units - main) for r in (g_ref, u_ref)],
                        axis=1,
                    ).astype(BF16)

            for n in (1, 2):
                local(n).start()
                for k in (3, 1, 2):
                    out(n, k).start()
            for b in range(4):
                for n in range(units // 128):
                    cut_d[b, n * held : (n + 1) * held, :] = columns(
                        d_ref, None, b * units + n * 128, 128
                    ).astype(BF16)
                if main < units:
                    part = columns(d_ref, None, b * units + main, units - main)
                    cut_d[b, units // 128 * held :, :] = jnp.concatenate(
                        [part[: held // 2], part[held // 2 :]], axis=1
                    ).astype(BF16)
            local(3).start()
            for k in (3, 1, 2):
                out(3, k).start()

        gather_rows(
            rows_ref, rows_out, send, receive, store, early=early,
            middle=lambda: in_plane(other_shards),
        )
        for n in (1, 2, 3):
            local(n).wait()
            for k in (1, 2, 3):
                arrival(n, k).wait_recv()
        in_plane(end_shards)
        for n in range(4):
            for k in (1, 2, 3):
                out(n, k).wait_send()

    vmem, hbm = pl.BlockSpec(memory_space=pltpu.VMEM), pl.BlockSpec(memory_space=pl.ANY)
    return call(
        kernel,
        "front",
        1,
        (x, seg[None]) + tuple(weights) + tuple(gains),
        [
            jax.ShapeDtypeStruct((tokens, part_width), BF16),
            jax.ShapeDtypeStruct((own, part_width), BF16),
            jax.ShapeDtypeStruct((4,) + seg.shape, seg.dtype),
            jax.ShapeDtypeStruct((deep, 4, held, packed), BF16),
            jax.ShapeDtypeStruct((4, held, 2 * units), BF16),
            jax.ShapeDtypeStruct(down_shape, BF16),
        ],
        [
            pltpu.VMEM((4, held, packed), BF16),
            pltpu.VMEM((4, held, 2 * units), BF16),
            pltpu.VMEM(down_shape, BF16),
        ]
        + gather_scratch(tokens, part_width) + sems(12) + sems(deep) + [pltpu.SemaphoreType.DMA((4,))],
        [vmem, hbm] + [vmem] * 9,
        [hbm, vmem, hbm, hbm, hbm, hbm],
    )


def apart(tokens):
    return (tokens // 2 - 2) // BLOCK + 2


def first_seen(i, tokens):
    return jnp.maximum(i - apart(tokens) + 1, 0)


def attend_back(
    qkv, g_mixed, mixed, denom, seg_rows, seg_cols, out_terms, middle, sum_down, heads
):
    tokens, width = out_terms.shape
    wide, narrow = heads * DV, heads * F
    blocks = tokens // BLOCK
    own = tokens // 8
    held, units = sum_down.shape[0] // 4, sum_down.shape[1]

    def kernel(
        x_ref, gm_ref, m_ref, d_ref, row_ref, col_ref, term_ref, mid_ref, down_ref,
        g_ref, out_ref, gd_ref,
        gq_ref, numer_ref, gden_ref, key_ref, gm_buf, m_buf, mid_buf, here_buf, large,
        term_buf, term_load, parts_d, p_send, p_receive, local, *rest,
    ):
        bufs, (s_send, s_receive, t_send, t_receive) = rest[:6], rest[6:]
        d, c, t = place_of()
        hand_on, landed = exchange(((down_ref, parts_d),), held, p_send, p_receive, local)
        mine = pl.ds(pl.multiple_of(t * own, own), own)
        loads = (
            pltpu.make_async_copy(gm_ref, gm_buf, large.at[0]),
            pltpu.make_async_copy(m_ref, m_buf, large.at[1]),
            pltpu.make_async_copy(mid_ref, mid_buf, large.at[2]),
        )
        stored = pltpu.make_async_copy(here_buf, out_ref.at[mine], large.at[3])

        def fetch_terms(i):
            part = pl.ds(pl.multiple_of(2 * scatter_order(i) * own, 2 * own), 2 * own)
            slot = lax.rem(i, 2)
            return pltpu.make_async_copy(term_ref.at[part], term_buf.at[slot], term_load.at[slot])

        fetch_terms(0).start()

        for copy in loads:
            copy.start()
        met = around() + [(d, beside(c, 3), t)]
        say(met)

        def prepare():
            loads[0].wait()
            loads[1].wait()
            gq_ref[...] = jnp.zeros_like(gq_ref)
            for h in range(heads):
                part = pl.ds(h * DV, DV)
                gm = gm_buf[:, part].astype(F32)
                inverse = 1.0 / d_ref[:, h : h + 1]
                numer_ref[:, part] = (gm * inverse).astype(BF16)
                down = -jnp.sum(gm * m_buf[:, part], axis=1, keepdims=True) * inverse
                gden_ref[h : h + 1, :] = jnp.transpose(
                    jnp.broadcast_to(down, (tokens, 128)), (1, 0)
                )[:1]
            key_ref[...] = jnp.transpose(
                x_ref[:, wide : wide + 2 * narrow].astype(F32), (1, 0)
            ).astype(BF16)

        place = lax.broadcasted_iota(jnp.int32, (BLOCK, BLOCK), 1) - lax.broadcasted_iota(
            jnp.int32, (BLOCK, BLOCK), 0
        )
        tempered = BF16(F**-0.5)

        def one_block(j):
            start = pl.multiple_of(j * BLOCK, BLOCK)
            ids = row_ref[pl.ds(start, BLOCK), :]
            values = [x_ref[pl.ds(start, BLOCK), h * DV : (h + 1) * DV] for h in range(heads)]
            keys = [
                x_ref[pl.ds(start, BLOCK), wide + (heads + h) * F : wide + (heads + h + 1) * F]
                * tempered
                for h in range(heads)
            ]
            across = [
                key_ref[(heads + h) * F : (heads + h + 1) * F, pl.ds(start, BLOCK)] * tempered
                for h in range(heads)
            ]

            def step(i, sums):
                base = pl.multiple_of(i * BLOCK, BLOCK)
                visible = (place >= start - base) & (ids == col_ref[:, pl.ds(base, BLOCK)])
                out = []
                for h in range(heads):
                    queries = x_ref[pl.ds(base, BLOCK), wide + h * F : wide + (h + 1) * F]
                    numer = numer_ref[pl.ds(base, BLOCK), h * DV : (h + 1) * DV]
                    s = dot(keys[h], queries, 1, 1)
                    a = jnp.where(visible, (0.5 * s + 1.0) * s + 1.0, 0.0).astype(BF16)
                    ga = dot(values[h], numer, 1, 1) + gden_ref[h : h + 1, pl.ds(base, BLOCK)]
                    gs = jnp.where(visible, ga * (1.0 + s), 0.0).astype(BF16)
                    gq_ref[h * F : (h + 1) * F, pl.ds(base, BLOCK)] += dot(across[h], gs, 1, 0)
                    out += [sums[2 * h] + dot(a, numer, 1, 0), sums[2 * h + 1] + dot(gs, queries, 1, 0)]
                return tuple(out)

            zeros = []
            for h in range(heads):
                zeros += [jnp.zeros((BLOCK, DV), F32), jnp.zeros((BLOCK, F), F32)]
            sums = lax.fori_loop(
                j, jnp.minimum(j + apart(tokens), blocks), step, tuple(zeros)
            )
            for h in range(heads):
                g_ref[pl.ds(start, BLOCK), h * DV : (h + 1) * DV] = sums[2 * h].astype(BF16)
                g_ref[
                    pl.ds(start, BLOCK), wide + (heads + h) * F : wide + (heads + h + 1) * F
                ] = (sums[2 * h + 1] * F**-0.5).astype(BF16)

        def terms(i, start):
            fetch_terms(i).wait()

            @pl.when(i < 3)
            def _():
                fetch_terms(i + 1).start()

            return term_buf.at[lax.rem(i, 2)]

        def fill(n):
            if n == 0:
                prepare()
                pl.loop(0, 1)(one_block)
            else:
                pl.loop(1, blocks)(one_block)
                hand_on(0)

        moved = scatter_rows(terms, bufs, s_send, s_receive, lambda: hear(len(met)), fill)
        loads[2].wait()
        here_buf[...] = (mid_buf[...] + moved).astype(BF16)
        copy = remote(here_buf, out_ref.at[mine], t_send, t_receive, 0, (d, c, 1 - t))
        copy.start()
        stored.start()
        g_ref[:, wide : wide + narrow] = jnp.transpose(gq_ref[...], (1, 0)).astype(BF16)
        landed(0)
        for b in range(4):
            gd_ref[:, b * units : (b + 1) * units] = parts_d[b].astype(F32)
        copy.wait_send()
        there = out_ref.at[pl.ds(pl.multiple_of((1 - t) * own, own), own)]
        remote(there, there, t_send, t_receive, 0, (d, c, 1 - t)).wait_recv()
        stored.wait()

    vmem, hbm = pl.BlockSpec(memory_space=pltpu.VMEM), pl.BlockSpec(memory_space=pl.ANY)
    return call(
        kernel, "attend_back", 7,
        (qkv, g_mixed, mixed, denom, seg_rows, seg_cols, out_terms, middle, sum_down),
        [
            jax.ShapeDtypeStruct(qkv.shape, BF16),
            jax.ShapeDtypeStruct((2 * own, width), BF16),
            jax.ShapeDtypeStruct((held, 4 * units), F32),
        ],
        [
            pltpu.VMEM((narrow, tokens), F32),
            pltpu.VMEM((tokens, wide), BF16),
            pltpu.VMEM((8, tokens), F32),
            pltpu.VMEM((2 * narrow, tokens), BF16),
            pltpu.VMEM(g_mixed.shape, BF16),
            pltpu.VMEM(mixed.shape, F32),
            pltpu.VMEM(middle.shape, F32),
            pltpu.VMEM((own, width), BF16),
            pltpu.SemaphoreType.DMA((4,)),
            pltpu.VMEM((2, 2 * own, width), BF16),
            pltpu.SemaphoreType.DMA((2,)),
            pltpu.VMEM((4, held, units), BF16),
        ]
        + sems(3) + [pltpu.SemaphoreType.DMA((1,))]
        + scatter_scratch(own, width) + sems(SCATTER_COPIES) + sems(1),
        [vmem, hbm, hbm, vmem, vmem, vmem, hbm, hbm, hbm],
        [vmem, hbm, vmem],
    )


def attend_block(i, x_ref, ext_ref, row_ref, col_ref, mixed_ref, denom_ref, low_ref, heads):
    wide = heads * DV
    base = pl.multiple_of(i * BLOCK, BLOCK)
    own = row_ref[pl.ds(base, BLOCK), :]
    place = lax.broadcasted_iota(jnp.int32, (BLOCK, BLOCK), 0) - lax.broadcasted_iota(
        jnp.int32, (BLOCK, BLOCK), 1
    )
    queries = [
        x_ref[pl.ds(base, BLOCK), wide + h * F : wide + (h + 1) * F] * jnp.bfloat16(F**-0.5)
        for h in range(heads)
    ]

    def step(j, sums):
        start = pl.multiple_of(j * BLOCK, BLOCK)
        visible = (place >= start - base) & (own == col_ref[:, pl.ds(start, BLOCK)])
        out = []
        for h in range(heads):
            keys = x_ref[
                pl.ds(start, BLOCK), wide + (heads + h) * F : wide + (heads + h + 1) * F
            ]
            s = dot(queries[h], keys, 1, 1)
            a = jnp.where(visible, (0.5 * s + 1.0) * s + 1.0, 0.0).astype(BF16)
            out.append(
                sums[h] + dot(a, ext_ref[pl.ds(start, BLOCK), 2 * h * DV : (2 * h + 2) * DV], 1, 0)
            )
        return tuple(out)

    sums = lax.fori_loop(
        first_seen(i, x_ref.shape[0]),
        i + 1,
        step,
        tuple(jnp.zeros((BLOCK, 2 * DV), F32) for _ in range(heads)),
    )
    for h in range(heads):
        denom = sums[h][:, DV:]
        mixed = sums[h][:, :DV] / denom
        mixed_ref[pl.ds(base, BLOCK), h * DV : (h + 1) * DV] = mixed
        low_ref[pl.ds(base, BLOCK), h * DV : (h + 1) * DV] = mixed.astype(BF16)
        denom_ref[pl.ds(base, BLOCK), h : h + 1] = denom[:, :1]


def attend(rows_low, own_high, w_attn, seg_rows, seg_cols, cot, heads):
    tokens, part_width = rows_low.shape
    own = tokens // 8
    wide, narrow = heads * DV, heads * F

    def kernel(
        x_ref, own_ref, w_ref, row_ref, col_ref, cot_ref,
        qkv_ref, mixed_ref, denom_ref, low_ref, cot_out, rows_out,
        ext_ref, half_ref, here, x_buf, *rest,
    ):
        rows_ref, r_send, r_receive, r_store, cot_buf, c_send, c_receive, c_store = rest
        d, c, t = place_of()
        loaded = pltpu.make_async_copy(x_ref, x_buf, here.at[0])
        loaded.start()
        low_half = pltpu.make_async_copy(x_buf, rows_out.at[:, :part_width], here.at[1])

        met = around()
        say(met)
        mine = pl.ds(pl.multiple_of((2 * c + t) * own, own), own)
        rows_ref[mine, :] = own_ref[...]
        cot_buf[mine, :] = cot_ref[pl.ds(pl.multiple_of(t * own, own), own), :part_width]
        hear(len(met))

        def first_half():
            loaded.wait()

            @pl.loop(0, tokens // BLOCK)
            def _(n):
                rows = pl.ds(pl.multiple_of(n * BLOCK, BLOCK), BLOCK)
                half_ref[rows, :wide] = dot(x_buf[rows, :], w_ref[:part_width, :wide], 1, 0)
                half_ref[rows, wide:] = dot(x_buf[rows, :], w_ref[:part_width, 2 * wide :], 1, 0)

            low_half.start()

        def second_half(start):
            rows = pl.ds(start, own)
            values = (
                half_ref[rows, :wide] + dot(rows_ref[rows, :], w_ref[part_width:, :wide], 1, 0)
            ).astype(BF16)
            qkv_ref[rows, :wide] = values
            qkv_ref[rows, wide:] = (
                half_ref[rows, wide:] + dot(rows_ref[rows, :], w_ref[part_width:, 2 * wide :], 1, 0)
            ).astype(BF16)
            for h in range(heads):
                ext_ref[rows, 2 * h * DV : (2 * h + 1) * DV] = values[:, h * DV : (h + 1) * DV]
                ext_ref[rows, (2 * h + 1) * DV : (2 * h + 2) * DV] = jnp.ones((own, DV), BF16)

        begun = []

        def cot_begin():
            begun.extend(gather_begin(cot_buf, c_send, c_receive))

        gather_rows(
            rows_ref, rows_out.at[:, part_width:], r_send, r_receive, r_store, second_half, first_half,
            late=cot_begin,
        )

        def blocks(first, last):
            @pl.loop(first, last)
            def _(i):
                attend_block(
                    i, qkv_ref, ext_ref, row_ref, col_ref, mixed_ref, denom_ref, low_ref, heads
                )

        gather_rows(
            cot_buf, cot_out, c_send, c_receive, c_store, begun=begun,
            early=lambda: blocks(0, tokens // BLOCK // 2),
            middle=lambda: blocks(tokens // BLOCK // 2, tokens // BLOCK - 1),
            late=lambda: blocks(tokens // BLOCK - 1, tokens // BLOCK),
        )
        low_half.wait()

    vmem, hbm = pl.BlockSpec(memory_space=pltpu.VMEM), pl.BlockSpec(memory_space=pl.ANY)
    return call(
        kernel, "attend", 2, (rows_low, own_high, w_attn, seg_rows, seg_cols, cot),
        [
            jax.ShapeDtypeStruct((tokens, wide + 2 * narrow), BF16),
            jax.ShapeDtypeStruct((tokens, wide), F32),
            jax.ShapeDtypeStruct((tokens, heads), F32),
            jax.ShapeDtypeStruct((tokens, wide), BF16),
            jax.ShapeDtypeStruct((tokens, part_width), BF16),
            jax.ShapeDtypeStruct((tokens, 2 * part_width), BF16),
        ],
        [
            pltpu.VMEM((tokens, 2 * wide), BF16),
            pltpu.VMEM((tokens, wide + 2 * narrow), F32),
            pltpu.SemaphoreType.DMA((2,)),
            pltpu.VMEM((tokens, part_width), BF16),
        ]
        + gather_scratch(tokens, part_width) + gather_scratch(tokens, part_width),
        [hbm] + [vmem] * 5,
        [vmem] * 4 + [hbm] * 2,
    )


def to_middle(heads_out, w_attn, x):
    tokens, width = heads_out.shape[0], x.shape[1]
    own = tokens // 8
    wide = heads_out.shape[1]

    def kernel(h_ref, w_ref, x_ref, mid_ref, rows_out, w_buf, x_buf, mid_buf, large, *rest):
        bufs, (s_send, s_receive, rows_ref, g_send, g_receive, store) = rest[:6], rest[6:]
        d, c, t = place_of()
        mine = pl.ds(pl.multiple_of(t * own, own), own)
        weights = pltpu.make_async_copy(w_ref.at[:, wide : 2 * wide], w_buf, large.at[0])
        loaded = pltpu.make_async_copy(x_ref.at[mine], x_buf, large.at[1])
        stored = pltpu.make_async_copy(mid_buf, mid_ref, large.at[2])
        weights.start()
        loaded.start()
        say(around())
        weights.wait()

        def terms(i, start):
            return [(h_ref[pl.ds(start, 2 * own), :], w_buf, slice(None))]

        total = scatter_rows(terms, bufs, s_send, s_receive, lambda: hear(3))
        loaded.wait()
        middle = total + x_buf[...].astype(F32)
        mid_buf[...] = middle
        stored.start()
        _, hat = norm_parts(middle)
        rows_ref[pl.ds(pl.multiple_of((2 * c + t) * own, own), own), :] = hat.astype(BF16)
        gather_rows(rows_ref, rows_out, g_send, g_receive, store)
        stored.wait()

    vmem, hbm = pl.BlockSpec(memory_space=pltpu.VMEM), pl.BlockSpec(memory_space=pl.ANY)
    return call(
        kernel, "to_middle", 3, (heads_out, w_attn, x),
        [jax.ShapeDtypeStruct((own, width), F32), jax.ShapeDtypeStruct((tokens, width), BF16)],
        [
            pltpu.VMEM((width, wide), BF16),
            pltpu.VMEM((own, width), BF16),
            pltpu.VMEM((own, width), F32),
            pltpu.SemaphoreType.DMA((3,)),
        ]
        + scatter_scratch(own, width) + sems(SCATTER_COPIES) + gather_scratch(tokens, width),
        [vmem, hbm, hbm],
        [hbm, hbm],
        flops=2 * tokens * width * heads_out.shape[1],
    )


def gate_up(rows_two, w_both, cot, cot_low):
    tokens, width = rows_two.shape
    own = tokens // 8
    units = w_both.shape[1] // 2
    main = units // 128 * 128
    count = tokens // BLOCK
    tile = 256

    def kernel(
        x_ref, w_ref, cot_ref, low_ref, hid_out, slope_out, silu_out, rows_out, down_out,
        x_buf, w_buf, low_buf, hid_ref, slope_ref, silu_ref, down_buf, load, store, down_store,
        rows_ref, send, receive, row_store,
    ):
        d, c, t = place_of()

        def fetch(i):
            rows = pl.ds(pl.multiple_of(i * BLOCK, BLOCK), BLOCK)
            slot = lax.rem(i, 2)
            return pltpu.make_async_copy(x_ref.at[rows], x_buf.at[slot], load.at[slot])

        def given(i):
            rows = pl.ds(pl.multiple_of(i * BLOCK, BLOCK), BLOCK)
            slot = lax.rem(i, 2)
            return [
                pltpu.make_async_copy(source, target.at[rows], store.at[n, slot])
                for n, (source, target) in enumerate(
                    (
                        (hid_ref.at[rows], hid_out),
                        (slope_ref.at[slot], slope_out),
                        (silu_ref.at[slot], silu_out),
                    )
                )
            ]

        weights = pltpu.make_async_copy(w_ref, w_buf, load.at[2])
        weights.start()
        fetch(0).start()
        low_copy = pltpu.make_async_copy(low_ref, low_buf, load.at[3])
        low_copy.start()
        greet(around())
        mine = pl.multiple_of((2 * c + t) * own, own)
        rows_ref[pl.ds(mine, own), :] = cot_ref[
            pl.ds(pl.multiple_of(t * own, own), own), width // 2 :
        ]

        def blocks(first, last):
            @pl.loop(first, last)
            def _(i):
                slot = lax.rem(i, 2)

                @pl.when(i + 1 < count)
                def _():
                    fetch(i + 1).start()

                fetch(i).wait()
                both = dot(x_buf[slot], w_buf[...], 1, 0)

                @pl.when(i >= 2)
                def _():
                    for copy in given(i - 2):
                        copy.wait()

                def act(gate, up, part):
                    sig = jax.nn.sigmoid(gate)
                    silu = gate * sig
                    hid_ref[pl.ds(pl.multiple_of(i * BLOCK, BLOCK), BLOCK), part] = (
                        silu * up
                    ).astype(BF16)
                    slope_ref[slot, :, part] = (up * sig * (1.0 + gate * (1.0 - sig))).astype(BF16)
                    silu_ref[slot, :, part] = silu.astype(BF16)

                act(both[:, :main], both[:, main : 2 * main], slice(0, main))
                if main < units:
                    act(
                        both[:, 2 * main : main + units],
                        both[:, main + units :],
                        slice(main, units),
                    )
                for copy in given(i):
                    copy.start()

        per = width // 2 // tile

        def down_given(base, n):
            slot = lax.rem(n, 2)
            rows = pl.ds(pl.multiple_of(base + n * tile, tile), tile)
            return pltpu.make_async_copy(down_buf.at[slot], down_out.at[rows], down_store.at[slot])

        def down_tiles(source, base, end):
            @pl.loop(0, end)
            def _(n):
                @pl.when(n >= 2)
                def _():
                    down_given(base, n - 2).wait()

                part = pl.ds(pl.multiple_of(n * tile, tile), tile)
                down_buf[lax.rem(n, 2)] = dot(source[:, part], hid_ref[...], 0, 0).astype(BF16)
                down_given(base, n).start()

        def early():
            weights.wait()
            blocks(0, 1)

        def later():
            blocks(count // 2, count)
            low_copy.wait()
            down_tiles(low_buf, 0, per)
            for n in (per - 2, per - 1):
                down_given(0, n).wait()

        gather_rows(
            rows_ref, rows_out, send, receive, row_store, early=early,
            middle=lambda: blocks(1, count // 2), late=later,
        )
        down_tiles(rows_ref, width // 2, per)
        for n in (per - 2, per - 1):
            down_given(width // 2, n).wait()
        for i in (count - 2, count - 1):
            for copy in given(i):
                copy.wait()

    vmem, hbm = pl.BlockSpec(memory_space=pltpu.VMEM), pl.BlockSpec(memory_space=pl.ANY)
    return call(
        kernel, "gate_up", 8, (rows_two, w_both, cot, cot_low),
        [jax.ShapeDtypeStruct((tokens, units), BF16)] * 3
        + [
            jax.ShapeDtypeStruct((tokens, width // 2), BF16),
            jax.ShapeDtypeStruct((width, units), BF16),
        ],
        [
            pltpu.VMEM((2, BLOCK, width), BF16),
            pltpu.VMEM(w_both.shape, BF16),
            pltpu.VMEM(cot_low.shape, BF16),
            pltpu.VMEM((tokens, units), BF16),
            pltpu.VMEM((2, BLOCK, units), BF16),
            pltpu.VMEM((2, BLOCK, units), BF16),
            pltpu.VMEM((2, tile, units), BF16),
            pltpu.SemaphoreType.DMA((4,)),
            pltpu.SemaphoreType.DMA((3, 2)),
            pltpu.SemaphoreType.DMA((2,)),
        ]
        + gather_scratch(tokens, width // 2),
        [hbm, hbm, vmem, hbm],
        [hbm] * 5,
        flops=4 * tokens * width * units,
    )


def feed_forward(slope, silu, cot_low, cot_high, w_down, rows_two):
    tokens, width = rows_two.shape
    units = slope.shape[1]
    main = units // 128 * 128
    tile = 256
    part_width = width // 2
    count = tokens // BLOCK

    def kernel(
        slope_ref, silu_ref, low_ref, high_ref, d_ref, two_ref, g_out, grad_ref,
        slope_buf, silu_buf, low_buf, high_buf, d_buf, rest_buf, d_load, g_ref, here, g_store, cols,
        out, load, store,
    ):
        def rows(i):
            return pl.ds(pl.multiple_of(i * BLOCK, BLOCK), BLOCK)

        def fetch(i):
            slot = lax.rem(i, 2)
            return [
                pltpu.make_async_copy(source.at[rows(i)], target.at[slot], here.at[n, slot])
                for n, (source, target) in enumerate(
                    (
                        (low_ref, low_buf),
                        (high_ref, high_buf),
                        (slope_ref, slope_buf),
                        (silu_ref, silu_buf),
                    )
                )
            ]

        def g_given(i):
            return pltpu.make_async_copy(g_ref.at[rows(i)], g_out.at[rows(i)], g_store.at[i])

        def wanted(n):
            part = pl.ds(pl.multiple_of(n * tile, tile), tile)
            slot = lax.rem(n, 2)
            return pltpu.make_async_copy(two_ref.at[:, part], cols.at[slot], load.at[slot])

        def given(n):
            part = pl.ds(pl.multiple_of(n * tile, tile), tile)
            slot = lax.rem(n, 2)
            return pltpu.make_async_copy(out.at[slot], grad_ref.at[part], store.at[slot])

        weights_there = load_down(d_ref, d_buf, rest_buf, d_load, units)
        for copy in fetch(0):
            copy.start()
        wanted(0).start()
        weights_there()

        @pl.loop(0, count)
        def _(i):
            slot = lax.rem(i, 2)

            @pl.when(i + 1 < count)
            def _():
                for copy in fetch(i + 1):
                    copy.start()

            for copy in fetch(i):
                copy.wait()
            g_hidden = dot(low_buf[slot], down_rows(d_buf, 0, part_width, units), 1, 0) + dot(
                high_buf[slot], down_rows(d_buf, part_width, width, units), 1, 0
            )
            gg = g_hidden * slope_buf[slot].astype(F32)
            gu = g_hidden * silu_buf[slot].astype(F32)
            part = rows(i)
            g_ref[part, :main] = gg[:, :main].astype(BF16)
            g_ref[part, main : 2 * main] = gu[:, :main].astype(BF16)
            if main < units:
                g_ref[part, 2 * main :] = jnp.concatenate(
                    [gg[:, main:], gu[:, main:]], axis=1
                ).astype(BF16)
            g_given(i).start()

        last = width // tile

        @pl.loop(0, last)
        def _(n):
            @pl.when(n + 1 < last)
            def _():
                wanted(n + 1).start()

            wanted(n).wait()

            @pl.when(n >= 2)
            def _():
                given(n - 2).wait()

            slot = lax.rem(n, 2)
            out[slot] = dot(cols[slot], g_ref[...], 0, 0).astype(BF16)
            given(n).start()

        given(last - 2).wait()
        given(last - 1).wait()
        for i in range(count):
            g_given(i).wait()

    hbm = pl.BlockSpec(memory_space=pl.ANY)
    moved = 2 * tokens * (2 * width + 4 * units) + 6 * width * units
    return pl.pallas_call(
        kernel,
        in_specs=[hbm] * 6,
        out_specs=[hbm] * 2,
        out_shape=[
            jax.ShapeDtypeStruct((tokens, 2 * units), BF16),
            jax.ShapeDtypeStruct((width, 2 * units), BF16),
        ],
        scratch_shapes=[
            pltpu.VMEM((2, BLOCK, units), BF16),
            pltpu.VMEM((2, BLOCK, units), BF16),
            pltpu.VMEM((2, BLOCK, part_width), BF16),
            pltpu.VMEM((2, BLOCK, part_width), BF16),
            *down_scratch(w_down, units),
            pltpu.VMEM((tokens, 2 * units), BF16),
            pltpu.SemaphoreType.DMA((4, 2)),
            pltpu.SemaphoreType.DMA((count,)),
            pltpu.VMEM((2, tokens, tile), BF16),
            pltpu.VMEM((2, tile, 2 * units), BF16),
            pltpu.SemaphoreType.DMA((3,)),
            pltpu.SemaphoreType.DMA((2,)),
        ],
        compiler_params=pltpu.CompilerParams(vmem_limit_bytes=VMEM_MOST),
        cost_estimate=pl.CostEstimate(
            flops=6 * tokens * width * units, bytes_accessed=moved, transcendentals=0
        ),
        name="feed_forward",
    )(slope, silu, cot_low, cot_high, w_down, rows_two)


def to_branch(g_both, w_both, middle, cot, w_attn, wide, hidden, w_down):
    tokens, width = g_both.shape[0], middle.shape[1]
    own = tokens // 8
    units = hidden.shape[1]
    tile = width // 2

    def kernel(
        g_ref, w_ref, mid_ref, cot_ref, o_ref, hid_ref, d_ref, gm_ref, rows_out, mix_ref, term_ref,
        g_buf, w_buf, hid_buf, d_buf, rest_buf, d_load, term_buf, load, term_store,
        mid_buf, cot_buf, o_buf, gm_buf, large, *rest,
    ):
        bufs, (s_send, s_receive, rows_ref, g_send, g_receive, store) = rest[:6], rest[6:]
        d, c, t = place_of()
        mine = pl.ds(pl.multiple_of(t * own, own), own)
        loads = (
            pltpu.make_async_copy(mid_ref, mid_buf, large.at[0]),
            pltpu.make_async_copy(cot_ref.at[mine], cot_buf, large.at[1]),
            pltpu.make_async_copy(o_ref.at[:, wide : 2 * wide], o_buf, large.at[2]),
        )
        stored = pltpu.make_async_copy(gm_buf, gm_ref, large.at[3])

        def fetch(i):
            part = pl.ds(pl.multiple_of(2 * scatter_order(i) * own, 2 * own), 2 * own)
            slot = lax.rem(i, 2)
            return pltpu.make_async_copy(g_ref.at[part], g_buf.at[slot], load.at[slot])

        weights = pltpu.make_async_copy(w_ref, w_buf, load.at[2])
        weights.start()
        fetch(0).start()
        say(around())
        weights.wait()
        down_there = load_down(d_ref, d_buf, rest_buf, d_load, units)
        for copy in loads:
            copy.start()
        pltpu.make_async_copy(
            hid_ref.at[pl.ds(0, BLOCK)], hid_buf, load.at[4]
        ).start()

        def terms(i, start):
            fetch(i).wait()

            @pl.when(i < 3)
            def _():
                fetch(i + 1).start()

            return [(g_buf[lax.rem(i, 2)], w_buf, slice(None))]

        total = scatter_rows(terms, bufs, s_send, s_receive, lambda: hear(3))
        for copy in loads:
            copy.wait()
        scale, hat = norm_parts(mid_buf[...])
        g_middle = cot_buf[...].astype(F32) + norm_back(total, hat, scale)
        gm_buf[...] = g_middle
        stored.start()
        rows_ref[pl.ds(pl.multiple_of((2 * c + t) * own, own), own), :] = g_middle.astype(BF16)

        def mix(start):
            mix_ref[pl.ds(start, own), :] = dot(
                rows_ref[pl.ds(start, own), :], o_buf[...], 1, 0
            ).astype(BF16)

        def block(i):
            return pl.ds(pl.multiple_of(i * BLOCK, BLOCK), BLOCK)

        def hidden_of(i):
            return pltpu.make_async_copy(hid_ref.at[block(i)], hid_buf, load.at[4])

        def term_given(i):
            return pltpu.make_async_copy(term_buf, term_ref.at[block(i)], term_store.at[0])

        def out_terms(first, last):
            @pl.loop(first, last)
            def _(i):
                hidden_of(i).wait()

                @pl.when(i > 0)
                def _():
                    term_given(i - 1).wait()

                for n in (0, 1):
                    columns = slice(n * tile, (n + 1) * tile)
                    matrix = down_rows(d_buf, n * tile, (n + 1) * tile, units)
                    term_buf[:, columns] = dot(hid_buf[...], matrix, 1, 1).astype(BF16)
                term_given(i).start()

                @pl.when(i + 1 < tokens // BLOCK)
                def _():
                    hidden_of(i + 1).start()

        down_there()
        blocks = tokens // BLOCK
        gather_rows(
            rows_ref, rows_out, g_send, g_receive, store, mix,
            lambda: out_terms(0, blocks // 2),
            lambda: out_terms(blocks // 2, blocks - 1),
            lambda: out_terms(blocks - 1, blocks),
        )
        term_given(blocks - 1).wait()
        stored.wait()

    vmem, hbm = pl.BlockSpec(memory_space=pltpu.VMEM), pl.BlockSpec(memory_space=pl.ANY)
    return call(
        kernel, "to_branch", 5, (g_both, w_both, middle, cot, w_attn, hidden, w_down),
        [
            jax.ShapeDtypeStruct((own, width), F32),
            jax.ShapeDtypeStruct((tokens, width), BF16),
            jax.ShapeDtypeStruct((tokens, wide), BF16),
            jax.ShapeDtypeStruct((tokens, width), BF16),
        ],
        [
            pltpu.VMEM((2, 2 * own, g_both.shape[1]), BF16),
            pltpu.VMEM(w_both.shape, BF16),
            pltpu.VMEM((BLOCK, units), BF16),
            *down_scratch(w_down, units),
            pltpu.VMEM((BLOCK, width), BF16),
            pltpu.SemaphoreType.DMA((5,)),
            pltpu.SemaphoreType.DMA((1,)),
            pltpu.VMEM((own, width), F32),
            pltpu.VMEM((own, width), BF16),
            pltpu.VMEM((width, wide), BF16),
            pltpu.VMEM((own, width), F32),
            pltpu.SemaphoreType.DMA((4,)),
        ]
        + scatter_scratch(own, width) + sems(SCATTER_COPIES) + gather_scratch(tokens, width),
        [hbm] * 7,
        [hbm, hbm, vmem, hbm],
        flops=4 * tokens * width * (g_both.shape[1] // 2 + wide),
    )


def as_row(column):
    return jnp.transpose(jnp.broadcast_to(column, (column.shape[0], 128)), (1, 0))[:8]


def to_input(
    g_qkv, w_attn, x, g_middle, rows_one, branch, heads_out, sum_both, weights, gains, heads
):
    tokens, width = g_qkv.shape[0], x.shape[1]
    own = tokens // 8
    deep = lax.axis_size("dp")
    across = g_qkv.shape[1]
    group = width // deep
    held = group // 4
    wide, narrow = heads * DV, heads * F
    both = sum_both.shape[1]
    units = both // 2
    main = units // 128 * 128

    def kernel(
        g_ref, w_ref, x_ref, gm_ref, one_ref, br_ref, h_ref, both_ref,
        wq_ref, wk_ref, wv_ref, wg_ref, wu_ref, gain_ref, gain_two_ref,
        out_ref, gq_ref, gk_ref, gv_ref, go_ref, gg_ref, gu_ref, row_ref, row_two_ref,
        *rest,
    ):
        bufs, (s_send, s_receive, t_send, t_receive) = rest[:6], rest[6:10]
        (
            came_deep, came_out, sums, sums_out, parts_a, parts_o, parts_b, scalar, back_ref, back_out,
            cols, load, d_send, d_receive, p_send, p_receive, local, x_buf, gm_buf, in_buf, gate_buf,
            up_buf, large,
        ) = rest[10:]
        d, c, t = place_of()
        hand_on, landed = exchange(
            ((sums, parts_a), (both_ref, parts_b), (sums_out, parts_o)), held, p_send, p_receive, local
        )

        def fetch(j):
            part = pl.ds(pl.multiple_of(depth(d, j % deep + 1) * group, group), group)
            source = br_ref if j < deep else one_ref
            return pltpu.make_async_copy(source.at[:, part], cols.at[j % 2], load.at[j % 2])

        def deeper(j):
            n = j % deep
            source, target = (back_out, came_out) if j < deep else (back_ref, came_deep)
            return remote(
                source.at[n], target.at[n], d_send, d_receive, j, (depth(d, n + 1), c, t)
            )

        def plane(j):
            n = j % deep
            if j + 1 < 2 * deep:
                fetch(j + 1).start()
            fetch(j).wait()
            if j < deep:
                back_out[n] = dot(cols[j % 2], h_ref[...], 0, 0).astype(BF16)
            else:
                back_ref[n] = dot(cols[j % 2], g_ref[...], 0, 0).astype(BF16)

        def sum_of(back, came, first):
            total = back[deep - 1].astype(F32)
            for n in range(deep - 1):
                deeper(first + n).wait_recv()
                total = total + came[n].astype(F32)
            return total.astype(BF16)

        fetch(0).start()
        mine = pl.ds(pl.multiple_of(t * own, own), own)
        loads = (
            pltpu.make_async_copy(x_ref.at[mine], x_buf, large.at[0]),
            pltpu.make_async_copy(gm_ref, gm_buf, large.at[1]),
        )
        stored = pltpu.make_async_copy(in_buf, out_ref.at[mine], large.at[2])
        wide_stores = (
            pltpu.make_async_copy(gate_buf, gg_ref, large.at[3]),
            pltpu.make_async_copy(up_buf, gu_ref, large.at[4]),
        )
        for copy in loads:
            copy.start()
        met = (
            around()
            + [(d, beside(c, 3), t)]
            + [(depth(d, k), c, t) for k in range(1, deep)]
        )
        say(met)

        early = deep // 2
        for j in range(early):
            plane(j)

        def enter():
            hear(len(met))
            for j in range(early):
                deeper(j).start()

        def terms(i, start):
            part = pl.ds(start, 2 * own)
            return [
                (g_ref[part, :wide], w_ref, slice(0, wide)),
                (g_ref[part, wide:], w_ref, slice(2 * wide, None)),
            ]

        def fill(n):
            if n == 0:
                hand_on(1)
                for j in range(early, 2 * deep):
                    plane(j)
                    if j % deep != deep - 1:
                        deeper(j).start()
                return
            landed(1)
            whole = [parts_b[b].astype(F32) for b in range(4)]
            term = jnp.zeros((held, 1), F32)
            for ref, weight, first, rest_of in (
                (gate_buf, wg_ref, 0, 2 * main),
                (up_buf, wu_ref, main, main + units),
            ):
                pieces = []
                for b in range(4):
                    pieces.append(whole[b][:, first : first + main])
                    if main < units:
                        pieces.append(whole[b][:, rest_of : rest_of + units - main])
                s = jnp.concatenate(pieces, axis=1)
                term = term + jnp.sum(s * weight[...].astype(F32), axis=1, keepdims=True)
                ref[...] = s * as_column(gain_two_ref[...].astype(F32))
            for copy in wide_stores:
                copy.start()
            scalar[0, 1] = as_row(term)

        e_one = scatter_rows(terms, bufs, s_send, s_receive, enter, fill)
        for copy in loads:
            copy.wait()
        scale, hat = norm_parts(x_buf[...].astype(F32))
        in_buf[...] = gm_buf[...] + norm_back(e_one, hat, scale)
        copy = remote(in_buf, out_ref.at[mine], t_send, t_receive, 0, (d, c, 1 - t))
        copy.start()
        stored.start()
        sums_out[...] = sum_of(back_out, came_out, 0)
        hand_on(2)
        sums[...] = sum_of(back_ref, came_deep, deep)
        hand_on(0)
        landed(2)
        for b in range(4):
            go_ref[:, b * wide : (b + 1) * wide] = parts_o[b].astype(F32)
        landed(0)

        gain_one = as_column(gain_ref[...].astype(F32))
        term_one = jnp.zeros((held, 1), F32)
        for ref, weight, start, count in (
            (gv_ref, wv_ref, 0, wide),
            (gq_ref, wq_ref, wide, narrow),
            (gk_ref, wk_ref, wide + narrow, narrow),
        ):
            s = jnp.concatenate(
                [parts_a[b][:, start : start + count].astype(F32) for b in range(4)], axis=1
            )
            term_one = term_one + jnp.sum(s * weight[...].astype(F32), axis=1, keepdims=True)
            ref[...] = s * gain_one
        scalar[0, 0] = as_row(term_one)
        swap = remote(scalar.at[0], scalar.at[1], t_send, t_receive, 1, (d, c, 1 - t))
        swap.start()
        swap.wait()
        row_ref[...] = (scalar[0, 0] + scalar[1, 0])[:1]
        row_two_ref[...] = (scalar[0, 1] + scalar[1, 1])[:1]
        copy.wait_send()
        there = out_ref.at[pl.ds(pl.multiple_of((1 - t) * own, own), own)]
        remote(there, there, t_send, t_receive, 0, (d, c, 1 - t)).wait_recv()
        for n in range(deep - 1):
            deeper(n).wait_send()
            deeper(deep + n).wait_send()
        stored.wait()
        for copy in wide_stores:
            copy.wait()

    w_q, w_k, w_v, w_gate, w_up = weights
    vmem, hbm = pl.BlockSpec(memory_space=pltpu.VMEM), pl.BlockSpec(memory_space=pl.ANY)
    return call(
        kernel, "to_input", 6,
        (g_qkv, w_attn, x, g_middle, rows_one, branch, heads_out, sum_both) + tuple(weights)
        + tuple(gains),
        [jax.ShapeDtypeStruct((2 * own, width), F32)]
        + [jax.ShapeDtypeStruct(w.shape, F32) for w in (w_q, w_k, w_v, w_v, w_gate, w_up)]
        + [jax.ShapeDtypeStruct((1, held), F32)] * 2,
        scatter_scratch(own, width) + sems(SCATTER_COPIES) + sems(2)
        + [
            pltpu.VMEM((deep - 1, group, across), BF16),
            pltpu.VMEM((deep - 1, group, wide), BF16),
            pltpu.VMEM((group, across), BF16),
            pltpu.VMEM((group, wide), BF16),
            pltpu.VMEM((4, held, across), BF16),
            pltpu.VMEM((4, held, wide), BF16),
            pltpu.VMEM((4, held, both), BF16),
            pltpu.VMEM((2, 2, 8, held), F32),
            pltpu.VMEM((deep, group, across), BF16),
            pltpu.VMEM((deep, group, wide), BF16),
            pltpu.VMEM((2, tokens, group), BF16),
            pltpu.SemaphoreType.DMA((2,)),
        ]
        + sems(2 * deep) + sems(9)
        + [
            pltpu.SemaphoreType.DMA((3,)),
            pltpu.VMEM((own, width), BF16),
            pltpu.VMEM((own, width), F32),
            pltpu.VMEM((own, width), F32),
            pltpu.VMEM(w_gate.shape, F32),
            pltpu.VMEM(w_up.shape, F32),
            pltpu.SemaphoreType.DMA((5,)),
        ],
        [vmem] * 2 + [hbm] * 4 + [vmem, hbm] + [vmem] * 7,
        [hbm] + [vmem] * 4 + [hbm] * 2 + [vmem] * 2,
        flops=2 * tokens * width * g_qkv.shape[1],
    )


def plane_shards(
    activations,
    seg_ids,
    cotangent,
    q_weight,
    k_weight,
    v_weight,
    o_weight,
    gate_weight,
    up_weight,
    down_weight,
    attn_gain,
    mlp_gain,
):
    parts = lax.axis_size("ctx")
    heads = q_weight.shape[1] // F // parts
    tokens = activations.shape[1] * parts
    x, cot_block = activations[0], cotangent[0]
    gain_one, gain_two = attn_gain[None], mlp_gain[None]
    rows_low, own_high, segments, w_attn, cut_both, cut_down = front(
        x,
        seg_ids,
        (q_weight, k_weight, v_weight, o_weight, gate_weight, up_weight, down_weight),
        (gain_one, gain_two),
        tokens,
        heads,
    )
    w_attn = w_attn.reshape(-1, w_attn.shape[3])
    w_both = lax.all_gather(cut_both, "dp", axis=0, tiled=True).reshape(-1, cut_both.shape[2])
    seg_rows, seg_cols = segments.reshape(tokens, 1), segments.reshape(1, tokens)
    qkv, mixed, denom, heads_out, cot_low, rows_one = attend(
        rows_low, own_high, w_attn, seg_rows, seg_cols, cot_block, heads
    )
    cut_down, heads_out = lax.optimization_barrier((cut_down, heads_out))
    w_down = lax.all_gather(cut_down, "dp", axis=0, tiled=True)
    middle, rows_two = to_middle(heads_out, w_attn, x)
    hidden, slope, silu, cot_high, back_down = gate_up(rows_two, w_both, cot_block, cot_low)
    sum_down = lax.psum_scatter(back_down, "dp", scatter_dimension=0, tiled=True)
    g_both, back_both = feed_forward(slope, silu, cot_low, cot_high, w_down, rows_two)
    sum_both = lax.psum_scatter(back_both, "dp", scatter_dimension=0, tiled=True)
    g_middle, branch, g_mixed, out_terms = to_branch(
        g_both, w_both, middle, cot_block, w_attn, heads * DV, hidden, w_down
    )
    g_qkv, out, s_down = attend_back(
        qkv, g_mixed, mixed, denom, seg_rows, seg_cols, out_terms, middle, sum_down, heads
    )
    g_input, s_q, s_k, s_v, s_o, s_gate, s_up, attn_row, mlp_row = to_input(
        g_qkv,
        w_attn,
        x,
        g_middle,
        rows_one,
        branch,
        heads_out,
        sum_both,
        (q_weight, k_weight, v_weight, gate_weight, up_weight),
        (gain_one, gain_two),
        heads,
    )
    return (
        out[None],
        g_input[None],
        s_q,
        s_k,
        s_v,
        s_o,
        s_gate,
        s_up,
        s_down,
        attn_row[0],
        mlp_row[0],
    )


def layer(*arrays):
    heads, units = arrays[3].shape[1] // F, arrays[7].shape[1]
    fits = lax.axis_size("ctx") == 4 and lax.axis_size("tp") == 2
    fits = fits and heads % 4 == 0 and units % 256 == 0
    plan = plane_shards if fits else shards
    return plan(*arrays)


def solution(mesh):
    placed = (
        P("dp", "ctx", None),
        P("dp", "ctx"),
        P("dp", "ctx", None),
        P(("dp", "ctx"), "tp"),
        P(("dp", "ctx"), "tp"),
        P(("dp", "ctx"), "tp"),
        P(("dp", "ctx"), "tp"),
        P(("dp", "ctx"), "tp"),
        P(("dp", "ctx"), "tp"),
        P(("dp", "ctx"), "tp"),
        P(("dp", "ctx")),
        P(("dp", "ctx")),
    )
    return jax.shard_map(
        layer,
        mesh=mesh,
        in_specs=placed,
        out_specs=(
            P("dp", "ctx", None),
            P("dp", "ctx", None),
            P(("dp", "ctx"), "tp"),
            P(("dp", "ctx"), "tp"),
            P(("dp", "ctx"), "tp"),
            P(("dp", "ctx"), "tp"),
            P(("dp", "ctx"), "tp"),
            P(("dp", "ctx"), "tp"),
            P(("dp", "ctx"), "tp"),
            P(("dp", "ctx")),
            P(("dp", "ctx")),
        ),
        check_vma=False,
    )
```

```python
import functools

import jax
import jax.numpy as jnp
from jax import lax
from jax.experimental import pallas as pl
from jax.experimental.pallas import tpu as pltpu
from jax.sharding import PartitionSpec as P

F = 16
DV = 128


EPSILON = 1e-05
PRECISE = lax.Precision.HIGHEST
VMEM_MOST = 60 * 2**20


def prefix(x, axis, join, neutral, backward):
    count = lax.axis_size(axis)
    place = lax.axis_index(axis)
    ahead = count - 1 - place if backward else place
    gathered = jax.tree.map(
        lambda a, kind: lax.all_gather(a.astype(kind), axis),
        x,
        (jnp.bfloat16, jnp.bfloat16, jnp.bfloat16),
    )
    state = jax.tree.map(lambda a, e: jnp.zeros_like(a) + jnp.asarray(e, a.dtype), x, neutral)

    def one(lap, state):
        source = count - 1 - lap if backward else lap
        return join(
            state,
            jax.tree.map(
                lambda a, own: lax.dynamic_index_in_dim(a, source, 0, False).astype(own.dtype),
                gathered,
                x,
            ),
        )

    return lax.fori_loop(0, ahead, one, state)


def taylor(features_in):
    feature_count = features_in.shape[-1]
    products = (features_in[..., :, None] * features_in[..., None, :]).reshape(
        features_in.shape[:-1] + (feature_count * feature_count,)
    )
    constant = jnp.ones(features_in.shape[:-1] + (1,), jnp.float32)
    return jnp.concatenate(
        [
            constant,
            features_in * feature_count ** (-0.25),
            products * (2.0 * feature_count) ** (-0.5),
        ],
        axis=-1,
    )


def taylor_back(features_in, incoming_gradient):
    feature_count = features_in.shape[-1]
    linear = incoming_gradient[..., 1 : 1 + feature_count] * feature_count ** (-0.25)
    square = incoming_gradient[..., 1 + feature_count :].reshape(
        incoming_gradient.shape[:-1] + (feature_count, feature_count)
    )
    paired = jnp.einsum(
        "...ab,...b->...a", square + jnp.swapaxes(square, -1, -2), features_in, precision=PRECISE
    )
    return linear + paired * (2.0 * feature_count) ** (-0.5)


def norm_backward_step(incoming_gradient, unit_normalized_rows, multiplier_term, gain_vector_row):
    rescaled_rows = incoming_gradient * gain_vector_row
    return multiplier_term * (
        rescaled_rows
        - unit_normalized_rows
        * jnp.mean(rescaled_rows * unit_normalized_rows, axis=1, keepdims=True)
    )


def join_states(earlier, later_part):
    is_empty = later_part[2] < 0.0
    retain = jnp.where(is_empty | (earlier[2] == later_part[2]), 1.0, 0.0).astype(jnp.float32)
    return (
        later_part[0] + retain * earlier[0],
        later_part[1] + retain * earlier[1],
        jnp.where(is_empty, earlier[2], later_part[2]),
    )


def shards(
    activations,
    seg_ids,
    cotangent,
    q_weight,
    k_weight,
    v_weight,
    o_weight,
    gate_weight,
    up_weight,
    down_weight,
    attn_gain,
    mlp_gain,
):
    layer_input_rows = activations[0].astype(jnp.float32)
    segment = seg_ids[0].astype(jnp.float32)
    tokens = layer_input_rows.shape[0]
    head_count = q_weight.shape[1] // F
    w_query, w_key, w_value, w_out, first_norm_gain = (
        lax.all_gather(q_weight, ("dp", "ctx"), axis=0, tiled=True),
        lax.all_gather(k_weight, ("dp", "ctx"), axis=0, tiled=True),
        lax.all_gather(v_weight, ("dp", "ctx"), axis=0, tiled=True),
        lax.all_gather(o_weight, ("dp", "ctx"), axis=0, tiled=True),
        lax.all_gather(attn_gain, ("dp", "ctx"), axis=0, tiled=True),
    )
    first_inverse_scale = lax.rsqrt(
        jnp.mean(layer_input_rows * layer_input_rows, axis=1, keepdims=True) + EPSILON
    )
    first_unit_rows = layer_input_rows * first_inverse_scale
    first_normalized = (first_unit_rows * first_norm_gain.astype(jnp.float32)).astype(jnp.bfloat16)
    queries = (
        jnp.dot(first_normalized, w_query, preferred_element_type=jnp.float32)
        .astype(jnp.bfloat16)
        .reshape(tokens, head_count, F)
    )
    key_heads = (
        jnp.dot(first_normalized, w_key, preferred_element_type=jnp.float32)
        .astype(jnp.bfloat16)
        .reshape(tokens, head_count, F)
    )
    value_heads = (
        jnp.dot(first_normalized, w_value, preferred_element_type=jnp.float32)
        .astype(jnp.bfloat16)
        .reshape(tokens, head_count, DV)
    )
    w_gate, w_up, w_down, second_norm_gain = (
        lax.all_gather(gate_weight, ("dp", "ctx"), axis=0, tiled=True),
        lax.all_gather(up_weight, ("dp", "ctx"), axis=0, tiled=True),
        lax.all_gather(down_weight, ("dp", "ctx"), axis=0, tiled=True),
        lax.all_gather(mlp_gain, ("dp", "ctx"), axis=0, tiled=True),
    )
    scores = jnp.einsum(
        "thf,shf->hts", queries, key_heads, preferred_element_type=jnp.float32
    ) * F ** (-0.5)
    places = jnp.arange(tokens)
    visible = (
        (places[:, None] >= places[None, :]) & (segment[:, None] == segment[None, :])
    ).astype(jnp.float32)
    weights = (visible * (1.0 + scores + 0.5 * scores * scores)).astype(jnp.bfloat16)
    query_float = queries.astype(jnp.float32)
    key_float = key_heads.astype(jnp.float32)
    value_float = value_heads.astype(jnp.float32)
    feat_q = taylor(query_float)
    feat_k = taylor(key_float)
    ending = segment[-1]
    owned = (segment == ending).astype(jnp.float32)[:, None, None]
    local_state = jnp.einsum("thf,thd->hfd", feat_k * owned, value_float, precision=PRECISE)
    local_total = jnp.sum(feat_k * owned, axis=0)
    empty_state = (jnp.zeros_like(local_state), jnp.zeros_like(local_total), jnp.float32(-1.0))
    prior_state, prior_total, before = prefix(
        (local_state, local_total, ending), "ctx", join_states, empty_state, False
    )
    inherit = (segment == before).astype(jnp.float32)
    numerator = jnp.einsum(
        "hts,shd->thd", weights, value_heads, preferred_element_type=jnp.float32
    ) + inherit[:, None, None] * jnp.einsum("thf,hfd->thd", feat_q, prior_state, precision=PRECISE)
    denominator = jnp.sum(weights.astype(jnp.float32), axis=2).T + inherit[:, None] * jnp.einsum(
        "thf,hf->th", feat_q, prior_total, precision=PRECISE
    )
    mixed_heads = numerator / denominator[:, :, None]
    heads_out = mixed_heads.reshape(tokens, head_count * DV).astype(jnp.bfloat16)
    attn_out = lax.psum(
        jnp.einsum("tc,dc->td", heads_out, w_out, preferred_element_type=jnp.float32), "tp"
    )
    residual_midpoint = layer_input_rows + attn_out
    second_inverse_scale = lax.rsqrt(
        jnp.mean(residual_midpoint * residual_midpoint, axis=1, keepdims=True) + EPSILON
    )
    second_unit_rows = residual_midpoint * second_inverse_scale
    second_normalized = (second_unit_rows * second_norm_gain.astype(jnp.float32)).astype(
        jnp.bfloat16
    )
    gate_value = jnp.dot(second_normalized, w_gate, preferred_element_type=jnp.float32)
    up_value = jnp.dot(second_normalized, w_up, preferred_element_type=jnp.float32)
    sigmoid_gate = jax.nn.sigmoid(gate_value)
    hidden = (gate_value * sigmoid_gate * up_value).astype(jnp.bfloat16)
    mlp_out = lax.psum(
        jnp.einsum("tc,dc->td", hidden, w_down, preferred_element_type=jnp.float32).astype(
            jnp.bfloat16
        ),
        "tp",
    ).astype(jnp.float32)
    final_out = residual_midpoint + mlp_out
    grad_out = cotangent[0].astype(jnp.float32)
    grad_branch_two = cotangent[0]
    grad_w_down = jnp.einsum(
        "td,tc->dc", grad_branch_two, hidden, preferred_element_type=jnp.float32
    )
    grad_hidden = jnp.dot(grad_branch_two, w_down, preferred_element_type=jnp.float32)
    grad_gate = (
        grad_hidden * up_value * sigmoid_gate * (1.0 + gate_value * (1.0 - sigmoid_gate))
    ).astype(jnp.bfloat16)
    grad_up = (grad_hidden * gate_value * sigmoid_gate).astype(jnp.bfloat16)
    grad_w_gate = jnp.einsum(
        "td,tc->dc", second_normalized, grad_gate, preferred_element_type=jnp.float32
    )
    grad_w_up = jnp.einsum(
        "td,tc->dc", second_normalized, grad_up, preferred_element_type=jnp.float32
    )
    grad_normed_part = jnp.einsum(
        "tc,dc->td", grad_gate, w_gate, preferred_element_type=jnp.float32
    ) + jnp.einsum("tc,dc->td", grad_up, w_up, preferred_element_type=jnp.float32)
    second_normalized_gradient = lax.psum(grad_normed_part.astype(jnp.bfloat16), "tp").astype(
        jnp.float32
    )
    second_gain_gradient = jnp.sum(second_normalized_gradient * second_unit_rows, axis=0)
    grad_middle = grad_out + norm_backward_step(
        second_normalized_gradient,
        second_unit_rows,
        second_inverse_scale,
        second_norm_gain.astype(jnp.float32),
    )
    mlp_grads = (
        lax.psum_scatter(grad_w_gate, ("dp", "ctx"), scatter_dimension=0, tiled=True),
        lax.psum_scatter(grad_w_up, ("dp", "ctx"), scatter_dimension=0, tiled=True),
        lax.psum_scatter(grad_w_down, ("dp", "ctx"), scatter_dimension=0, tiled=True),
        lax.psum_scatter(second_gain_gradient, ("dp", "ctx"), scatter_dimension=0, tiled=True),
    )
    grad_branch_one = grad_middle.astype(jnp.bfloat16)
    grad_w_out = jnp.einsum(
        "td,tc->dc", grad_branch_one, heads_out, preferred_element_type=jnp.float32
    )
    grad_heads_low = jnp.dot(grad_branch_one, w_out, preferred_element_type=jnp.float32).astype(
        jnp.bfloat16
    )
    grad_mixed = (
        lax.optimization_barrier(grad_heads_low).astype(jnp.float32).reshape(tokens, head_count, DV)
    )
    numer_low = (grad_mixed / denominator[:, :, None]).astype(jnp.bfloat16)
    grad_numer = lax.optimization_barrier(numer_low).astype(jnp.float32)
    grad_denom = -jnp.sum(grad_mixed * mixed_heads, axis=2) / denominator
    grad_weights = (
        jnp.einsum("thd,shd->hts", numer_low, value_heads, preferred_element_type=jnp.float32)
        + grad_denom.T[:, :, None]
    )
    grad_scores = (grad_weights * visible * (1.0 + scores)).astype(jnp.bfloat16)
    grad_value = jnp.einsum("hts,thd->shd", weights, numer_low, preferred_element_type=jnp.float32)
    grad_query = jnp.einsum(
        "hts,shf->thf", grad_scores, key_heads, preferred_element_type=jnp.float32
    ) * F ** (-0.5)
    grad_key = jnp.einsum(
        "hts,thf->shf", grad_scores, queries, preferred_element_type=jnp.float32
    ) * F ** (-0.5)
    grad_feat_q = inherit[:, None, None] * (
        jnp.einsum("thd,hfd->thf", grad_numer, prior_state, precision=PRECISE)
        + grad_denom[:, :, None] * prior_total[None]
    )
    carried_state = jnp.einsum(
        "thf,thd->hfd", feat_q * inherit[:, None, None], grad_numer, precision=PRECISE
    )
    carried_total = jnp.sum(feat_q * (inherit[:, None] * grad_denom)[:, :, None], axis=0)
    starting = segment[0]
    later_state, later_total, after_seg = prefix(
        (carried_state, carried_total, starting), "ctx", join_states, empty_state, True
    )
    reached = (segment == after_seg).astype(jnp.float32)[:, None, None]
    grad_feat_k = reached * (
        jnp.einsum("hfd,thd->thf", later_state, value_float, precision=PRECISE) + later_total[None]
    )
    grad_value = grad_value + reached * jnp.einsum(
        "thf,hfd->thd", feat_k, later_state, precision=PRECISE
    )
    grad_query = grad_query + taylor_back(query_float, grad_feat_q)
    grad_key = grad_key + taylor_back(key_float, grad_feat_k)
    grad_query_low = grad_query.reshape(tokens, head_count * F).astype(jnp.bfloat16)
    grad_key_low = grad_key.reshape(tokens, head_count * F).astype(jnp.bfloat16)
    grad_value_low = grad_value.reshape(tokens, head_count * DV).astype(jnp.bfloat16)
    grad_w_query = jnp.einsum(
        "td,tc->dc", first_normalized, grad_query_low, preferred_element_type=jnp.float32
    )
    grad_w_key = jnp.einsum(
        "td,tc->dc", first_normalized, grad_key_low, preferred_element_type=jnp.float32
    )
    grad_w_value = jnp.einsum(
        "td,tc->dc", first_normalized, grad_value_low, preferred_element_type=jnp.float32
    )
    grad_normed_sum = (
        jnp.einsum("tc,dc->td", grad_query_low, w_query, preferred_element_type=jnp.float32)
        + jnp.einsum("tc,dc->td", grad_key_low, w_key, preferred_element_type=jnp.float32)
        + jnp.einsum("tc,dc->td", grad_value_low, w_value, preferred_element_type=jnp.float32)
    )
    first_normalized_gradient = lax.psum(grad_normed_sum.astype(jnp.bfloat16), "tp").astype(
        jnp.float32
    )
    first_gain_gradient = jnp.sum(first_normalized_gradient * first_unit_rows, axis=0)
    grad_inputs = grad_middle + norm_backward_step(
        first_normalized_gradient,
        first_unit_rows,
        first_inverse_scale,
        first_norm_gain.astype(jnp.float32),
    )
    attn_grads = (
        lax.psum_scatter(grad_w_query, ("dp", "ctx"), scatter_dimension=0, tiled=True),
        lax.psum_scatter(grad_w_key, ("dp", "ctx"), scatter_dimension=0, tiled=True),
        lax.psum_scatter(grad_w_value, ("dp", "ctx"), scatter_dimension=0, tiled=True),
        lax.psum_scatter(grad_w_out, ("dp", "ctx"), scatter_dimension=0, tiled=True),
        lax.psum_scatter(first_gain_gradient, ("dp", "ctx"), scatter_dimension=0, tiled=True),
    )
    return (
        final_out.astype(jnp.bfloat16)[None],
        grad_inputs[None],
        attn_grads[0],
        attn_grads[1],
        attn_grads[2],
        attn_grads[3],
        mlp_grads[0],
        mlp_grads[1],
        mlp_grads[2],
        attn_grads[4],
        mlp_grads[3],
    )


BLOCK = 512


MESH = pl.DeviceIdType.MESH
BF16, F32 = jnp.bfloat16, jnp.float32


def dot(a, b, ca, cb):
    return lax.dot_general(a, b, (((ca,), (cb,)), ((), ())), preferred_element_type=F32)


def place_of():
    return lax.axis_index("dp"), lax.axis_index("ctx"), lax.axis_index("tp")


def beside(c, across):
    x, y = lax.rem(c, 2), lax.div(c, 2)
    return lax.rem(x + across % 2, 2) + 2 * lax.rem(y + across // 2, 2)


def say(devices):
    barrier = pltpu.get_barrier_semaphore()
    for device in devices:
        pl.semaphore_signal(barrier, inc=1, device_id=device, device_id_type=MESH)


def hear(count):
    pl.semaphore_wait(pltpu.get_barrier_semaphore(), count)


def greet(devices):
    say(devices)
    hear(len(devices))


def around():
    d, c, t = place_of()
    return [(d, beside(c, 1), t), (d, beside(c, 2), t), (d, c, 1 - t)]


def remote(source, target, send, receive, k, device):
    return pltpu.make_async_remote_copy(
        src_ref=source,
        dst_ref=target,
        send_sem=send.at[k],
        recv_sem=receive.at[k],
        device_id=device,
        device_id_type=MESH,
    )


def gather_steps(buf, send, receive):
    d, c, t = place_of()
    own = buf.shape[0] // 8
    half = own // 2

    def part(across, core, h):
        block = c if across == 0 else beside(c, across)
        start = (2 * block + core) * own + h * half
        return buf.at[pl.ds(pl.multiple_of(start, half), half)]

    def put(k, across, h, device):
        ref = part(across, t, h)
        copy = remote(ref, ref, send, receive, k, device)
        copy.start()
        return copy

    return put, part


def gather_begin(buf, send, receive):
    put, _ = gather_steps(buf, send, receive)
    to_x, to_y, to_t = around()
    return [
        put(0, 0, 0, to_x),
        put(1, 0, 1, to_y),
        put(2, 0, 1, to_x),
        put(3, 0, 0, to_y),
        put(6, 0, 0, to_t),
        put(7, 0, 1, to_t),
    ]


def gather_rows(
    buf, out, send, receive, store, piece=None, early=None, middle=None, late=None, begun=None
):
    d, c, t = place_of()
    own = buf.shape[0] // 8
    to_x, to_y, to_t = around()
    put, part = gather_steps(buf, send, receive)
    started = gather_begin(buf, send, receive) if begun is None else begun

    def got(k, across, core, h):
        ref = part(across, core, h)
        remote(ref, ref, send, receive, k, to_t).wait_recv()

    stored = []

    def work(across, core):
        block = c if across == 0 else beside(c, across)
        start = pl.multiple_of((2 * block + core) * own, own)
        rows = pl.ds(start, own)
        copy = pltpu.make_async_copy(buf.at[rows], out.at[rows], store.at[len(stored)])
        copy.start()
        stored.append(copy)
        if piece is not None:
            piece(start)

    if early is not None:
        early()
    work(0, t)
    got(6, 0, 1 - t, 0)
    got(7, 0, 1 - t, 1)
    work(0, 1 - t)
    got(0, 1, t, 0)
    started.append(put(4, 1, 0, to_y))
    started.append(put(8, 1, 0, to_t))
    got(1, 2, t, 1)
    started.append(put(5, 2, 1, to_x))
    started.append(put(9, 2, 1, to_t))
    if middle is not None:
        middle()
    got(2, 1, t, 1)
    started.append(put(10, 1, 1, to_t))
    got(3, 2, t, 0)
    started.append(put(11, 2, 0, to_t))
    if late is not None:
        late()
    work(1, t)
    work(2, t)
    got(8, 1, 1 - t, 0)
    got(10, 1, 1 - t, 1)
    work(1, 1 - t)
    got(9, 2, 1 - t, 1)
    got(11, 2, 1 - t, 0)
    work(2, 1 - t)
    got(4, 3, t, 0)
    started.append(put(12, 3, 0, to_t))
    got(5, 3, t, 1)
    started.append(put(13, 3, 1, to_t))
    work(3, t)
    got(12, 3, 1 - t, 0)
    got(13, 3, 1 - t, 1)
    work(3, 1 - t)
    for copy in started:
        copy.wait_send()
    for copy in stored:
        copy.wait()


GATHER_COPIES = 14


def gather_scratch(tokens, width):
    return (
        [pltpu.VMEM((tokens, width), BF16)]
        + sems(GATHER_COPIES)
        + [pltpu.SemaphoreType.DMA((8,))]
    )


def exchange(jobs, held, send, receive, local):
    d, c, t = place_of()

    def rows_of(block):
        return pl.ds(pl.multiple_of(block * held, held), held)

    def to_block(n, k):
        source, target = jobs[n]
        return remote(
            source.at[rows_of(beside(c, k))], target.at[c], send, receive, 3 * n + k - 1,
            (d, beside(c, k), t),
        )

    def from_block(n, k):
        there = jobs[n][1].at[beside(c, k)]
        return remote(there, there, send, receive, 3 * n + k - 1, (d, beside(c, k), t))

    def at_home(n):
        source, target = jobs[n]
        return pltpu.make_async_copy(source.at[rows_of(c)], target.at[c], local.at[n])

    def hand_on(n):
        for k in (3, 1, 2):
            to_block(n, k).start()
        at_home(n).start()

    def landed(n):
        at_home(n).wait()
        for k in (1, 2, 3):
            from_block(n, k).wait_recv()
            to_block(n, k).wait_send()

    return hand_on, landed


PARTS = 2


def scatter_order(i):
    c = lax.axis_index("ctx")
    across = 3 - i
    x, y = lax.rem(c, 2), lax.div(c, 2)
    return lax.rem(x + lax.rem(across, 2), 2) + 2 * lax.rem(y + lax.div(across, 2), 2)


def scatter_rows(terms, bufs, send, receive, enter, fill=None):
    to_core, from_core, kept, over, came, stage = bufs
    d, c, t = place_of()
    own, tile = kept.shape[2:]
    half = own // 2
    to_x, to_y, to_t = (d, beside(c, 1), t), (d, beside(c, 2), t), (d, c, 1 - t)

    def link(k, n):
        return remote(
            over.at[k, n], came.at[k, n], send, receive, PARTS * (4 + k) + n, to_x if k % 2 == 0 else to_y
        )

    def core(i, n):
        return remote(to_core.at[lax.rem(i, 2), n], from_core.at[i, n], send, receive, PARTS * i + n, to_t)

    def total(i, h, n, *extra):
        out = kept[i % 3, n, pl.ds(h * half, half), :]
        for k in extra:
            out = out + came[k, n].astype(F32)
        return out

    def go(k, i, h, n, *extra):
        over[k, n] = total(i, h, n, *extra).astype(BF16)
        link(k, n).start()

    def joined(i, n):
        core(i, n).wait_recv()
        kept[lax.rem(i, 3), n] = kept[lax.rem(i, 3), n] + from_core[i, n].astype(F32)

    def product(pairs, i, n):
        columns = pl.ds(n * tile, tile)
        theirs = pl.ds(pl.multiple_of((1 - t) * own, own), own)
        mine = pl.ds(pl.multiple_of(t * own, own), own)
        if not isinstance(pairs, list):
            to_core[lax.rem(i, 2), n] = pairs[theirs, columns]
            kept[lax.rem(i, 3), n] = pairs[mine, columns].astype(F32)
            return
        out = None
        for rows, matrix, part in pairs:
            term = dot(rows, matrix[columns, part], 1, 1)
            out = term if out is None else out + term
        stage[...] = out
        to_core[lax.rem(i, 2), n] = stage[theirs, :].astype(BF16)
        kept[lax.rem(i, 3), n] = stage[mine, :]

    def begin(i):
        return pl.multiple_of(2 * scatter_order(i) * own, 2 * own)

    pairs = terms(0, begin(0))
    for n in range(PARTS):
        product(pairs, 0, n)
        if n == 0:
            enter()
        core(0, n).start()
        if n > 0:
            joined(0, n - 1)
            go(0, 0, 0, n - 1)
            go(1, 0, 1, n - 1)
    joined(0, PARTS - 1)
    go(0, 0, 0, PARTS - 1)
    go(1, 0, 1, PARTS - 1)

    def step(i, carry):
        pairs = terms(i, begin(i))

        @pl.when(i >= 2)
        def _():
            for n in range(PARTS):
                core(i - 2, n).wait_send()

        product(pairs, i, 0)
        core(i, 0).start()

        @pl.when(i == 2)
        def _():
            for n in range(PARTS):
                joined(1, n)
                go(3, 1, 1, n)

        @pl.when(i == 3)
        def _():
            for n in range(PARTS):
                joined(2, n)
                go(2, 2, 0, n)

        for n in range(1, PARTS):
            product(pairs, i, n)
            core(i, n).start()

        return carry

    lax.fori_loop(1, 4, step, 0)
    if fill is not None:
        fill(0)
    for n in range(PARTS):
        link(0, n).wait_recv()
        link(1, n).wait_recv()
        go(4, 2, 1, n, 1)
        go(5, 1, 0, n, 0)
    for n in range(PARTS):
        joined(3, n)
    if fill is not None:
        fill(1)
    for n in range(PARTS):
        for k in (2, 3, 4, 5):
            link(k, n).wait_recv()
        core(2, n).wait_send()
        core(3, n).wait_send()
        for k in range(6):
            link(k, n).wait_send()
    return jnp.concatenate(
        [
            jnp.concatenate([total(3, 0, n, 2, 5), total(3, 1, n, 3, 4)], axis=0)
            for n in range(PARTS)
        ],
        axis=1,
    )


SCATTER_COPIES = 10 * PARTS


def scatter_scratch(own, width):
    tile = width // PARTS
    return [
        pltpu.VMEM((2, PARTS, own, tile), BF16),
        pltpu.VMEM((4, PARTS, own, tile), BF16),
        pltpu.VMEM((3, PARTS, own, tile), F32),
        pltpu.VMEM((6, PARTS, own // 2, tile), BF16),
        pltpu.VMEM((6, PARTS, own // 2, tile), BF16),
        pltpu.VMEM((2 * own, tile), F32),
    ]


def norm_parts(rows):
    scale = lax.rsqrt(jnp.mean(rows * rows, axis=1, keepdims=True) + EPSILON)
    return scale, rows * scale


def norm_back(e, hat, scale):
    return scale * (e - hat * jnp.mean(e * hat, axis=1, keepdims=True))


def call(kernel, name, collective, arrays, out_shape, scratch, spaces=None, out_spaces=None, flops=0):
    vmem = pl.BlockSpec(memory_space=pltpu.VMEM)
    moved = sum(a.size * a.dtype.itemsize for a in arrays)
    return pl.pallas_call(
        kernel,
        in_specs=spaces or [vmem] * len(arrays),
        out_specs=out_spaces or [vmem] * len(out_shape),
        out_shape=out_shape,
        scratch_shapes=scratch,
        compiler_params=pltpu.CompilerParams(
            collective_id=collective, has_side_effects=True, vmem_limit_bytes=VMEM_MOST
        ),
        cost_estimate=pl.CostEstimate(flops=flops, bytes_accessed=moved, transcendentals=0),
        name=name,
    )(*arrays)


def sems(count):
    return [pltpu.SemaphoreType.DMA((count,)), pltpu.SemaphoreType.DMA((count,))]


def depth(d, k):
    return lax.rem(d + k, lax.axis_size("dp"))


def as_column(row):
    return jnp.transpose(jnp.broadcast_to(row, (128, row.shape[1])), (1, 0))[:, :1]


def columns(ref, gain, start, count):
    low = start // 128 * 128
    high = -(-(start + count) // 128) * 128
    value = ref[:, low:high].astype(F32)
    if gain is not None:
        value = value * gain
    return value[:, start - low : start - low + count]


def packed_down(held, units):
    return units // 128 * held + (held // 2 if units % 128 else 0)


def down_scratch(w_down, units):
    return [
        pltpu.VMEM((w_down.shape[0], w_down.shape[1] * 128 // units, -(-units // 128) * 128), BF16),
        pltpu.VMEM((w_down.shape[0], w_down.shape[1] * 64 // units, 128), BF16),
        pltpu.SemaphoreType.DMA((-(-units // 128),)),
    ]


def load_down(w_ref, w_buf, rest_buf, load, units):
    held = w_buf.shape[1]
    tiles = units // 128
    copies = [
        pltpu.make_async_copy(
            w_ref.at[:, n * held : (n + 1) * held], w_buf.at[:, :, n * 128 : (n + 1) * 128], load.at[n]
        )
        for n in range(tiles)
    ]
    if units % 128:
        copies.append(pltpu.make_async_copy(w_ref.at[:, tiles * held :], rest_buf, load.at[tiles]))

    def finish():
        for copy in copies:
            copy.wait()
        if units % 128:
            w_buf[:, : held // 2, tiles * 128 : units] = rest_buf[:, :, :64]
            w_buf[:, held // 2 :, tiles * 128 : units] = rest_buf[:, :, 64:]

    for copy in copies:
        copy.start()
    return finish


def down_rows(w_buf, first, last, units):
    held = w_buf.shape[1]
    rows = w_buf[first // held : last // held, :, :units]
    return rows.reshape(last - first, units)


def front(x, seg, weights, gains, tokens, heads):
    width = x.shape[1]
    own = tokens // 8
    deep = lax.axis_size("dp")
    held, units = weights[4].shape[0], weights[4].shape[1] // 4
    wide, narrow = heads * DV, heads * F
    main = units // 128 * 128
    packed = 2 * wide + 2 * narrow
    part_width = width // 2
    down_shape = (4, packed_down(held, units), 128)
    line = {
        0: (((0, 2),), ((0, 1),), ()),
        1: (((1, 0),), ((1, 2), (1, 3)), ((3, 0),)),
        2: (((2, 3),), ((2, 1), (2, 0)), ((0, 3),)),
        3: (((3, 1),), ((3, 2),), ()),
    }
    if deep != 4:
        line = {
            p: (tuple((p, to) for to in range(deep) if to != p), (), ()) for p in range(deep)
        }

    def kernel(
        x_ref, seg_ref, q_ref, k_ref, v_ref, o_ref, g_ref, u_ref, d_ref, one_ref, two_ref,
        rows_out, own_ref, segs_ref, wa_out, wg_out, wd_out,
        cut_a, cut_g, cut_d, rows_ref, send, receive, store, small_send, small_receive, deep_send, deep_receive, here,
    ):
        d, c, t = place_of()
        jobs = (
            (lambda block: cut_a.at[block], lambda block: wa_out.at[d, block]),
            (lambda block: seg_ref.at[0], lambda block: segs_ref.at[block]),
            (lambda block: cut_g.at[block], lambda block: wg_out.at[block]),
            (lambda block: cut_d.at[block], lambda block: wd_out.at[block]),
        )

        def local(n):
            return pltpu.make_async_copy(jobs[n][0](c), jobs[n][1](c), here.at[n])

        def out(n, k):
            return remote(
                jobs[n][0](beside(c, k)), jobs[n][1](c), small_send, small_receive,
                3 * n + k - 1, (d, beside(c, k), t),
            )

        def arrival(n, k):
            block = beside(c, k)
            return remote(
                jobs[n][0](block), jobs[n][1](block), small_send, small_receive,
                3 * n + k - 1, (d, block, t),
            )

        def shard(slot, s, to):
            return pltpu.make_async_remote_copy(
                src_ref=wa_out.at[s], dst_ref=wa_out.at[s], send_sem=deep_send.at[slot],
                recv_sem=deep_receive.at[s], device_id=(to, c, t), device_id_type=MESH,
            )

        def in_plane(act):
            for p in range(deep):
                pl.when(d == p)(functools.partial(act, p, *line[p]))

        def first_shards(p, first, then, on):
            for slot, (s, to) in enumerate(first):
                shard(slot, s, to).start()

        def other_shards(p, first, then, on):
            for slot, (s, to) in enumerate(then):
                shard(len(first) + slot, s, to).start()
            for slot, (s, to) in enumerate(on):
                shard(len(first) + len(then) + slot, s, to).wait_recv()
                shard(len(first) + len(then) + slot, s, to).start()

        def end_shards(p, first, then, on):
            for s in range(deep):
                if s != p and s not in [handed for handed, _ in on]:
                    shard(0, s, (p + 1) % deep).wait_recv()
            for slot, (s, to) in enumerate(first + then + on):
                shard(slot, s, to).wait_send()

        one, two = as_column(one_ref[...].astype(F32)), as_column(two_ref[...].astype(F32))
        met = (
            [(d, beside(c, k), t) for k in (1, 2, 3)]
            + [(d, c, 1 - t)]
            + [(depth(d, k), c, t) for k in range(1, deep)]
        )
        say(met)
        for b in range(4):
            cut_a[b, :, :wide] = columns(v_ref, one, b * wide, wide).astype(BF16)
            cut_a[b, :, wide : 2 * wide] = o_ref[:, b * wide : (b + 1) * wide]
            cut_a[b, :, 2 * wide :] = jnp.concatenate(
                [columns(ref, one, b * narrow, narrow) for ref in (q_ref, k_ref)], axis=1
            ).astype(BF16)
        hear(len(met))
        local(0).start()
        for k in (3, 1, 2):
            out(0, k).start()
        mine = pl.multiple_of((2 * c + t) * own, own)
        _, hat = norm_parts(x_ref[pl.ds(pl.multiple_of(t * own, own), own), :].astype(F32))
        rows_ref[pl.ds(mine, own), :] = hat[:, :part_width].astype(BF16)
        own_ref[...] = hat[:, part_width:].astype(BF16)
        local(0).wait()
        for k in (1, 2, 3):
            arrival(0, k).wait_recv()
        in_plane(first_shards)

        def early():
            for b in range(4):
                start = b * units
                cut_g[b, :, :main] = columns(g_ref, two, start, main).astype(BF16)
                cut_g[b, :, main : 2 * main] = columns(u_ref, two, start, main).astype(BF16)
                if main < units:
                    cut_g[b, :, 2 * main :] = jnp.concatenate(
                        [columns(r, two, start + main, units - main) for r in (g_ref, u_ref)],
                        axis=1,
                    ).astype(BF16)

            for n in (1, 2):
                local(n).start()
                for k in (3, 1, 2):
                    out(n, k).start()
            for b in range(4):
                for n in range(units // 128):
                    cut_d[b, n * held : (n + 1) * held, :] = columns(
                        d_ref, None, b * units + n * 128, 128
                    ).astype(BF16)
                if main < units:
                    part = columns(d_ref, None, b * units + main, units - main)
                    cut_d[b, units // 128 * held :, :] = jnp.concatenate(
                        [part[: held // 2], part[held // 2 :]], axis=1
                    ).astype(BF16)
            local(3).start()
            for k in (3, 1, 2):
                out(3, k).start()

        gather_rows(
            rows_ref, rows_out, send, receive, store, early=early,
            middle=lambda: in_plane(other_shards),
        )
        for n in (1, 2, 3):
            local(n).wait()
            for k in (1, 2, 3):
                arrival(n, k).wait_recv()
        in_plane(end_shards)
        for n in range(4):
            for k in (1, 2, 3):
                out(n, k).wait_send()

    vmem, hbm = pl.BlockSpec(memory_space=pltpu.VMEM), pl.BlockSpec(memory_space=pl.ANY)
    return call(
        kernel,
        "front",
        1,
        (x, seg[None]) + tuple(weights) + tuple(gains),
        [
            jax.ShapeDtypeStruct((tokens, part_width), BF16),
            jax.ShapeDtypeStruct((own, part_width), BF16),
            jax.ShapeDtypeStruct((4,) + seg.shape, seg.dtype),
            jax.ShapeDtypeStruct((deep, 4, held, packed), BF16),
            jax.ShapeDtypeStruct((4, held, 2 * units), BF16),
            jax.ShapeDtypeStruct(down_shape, BF16),
        ],
        [
            pltpu.VMEM((4, held, packed), BF16),
            pltpu.VMEM((4, held, 2 * units), BF16),
            pltpu.VMEM(down_shape, BF16),
        ]
        + gather_scratch(tokens, part_width) + sems(12) + sems(deep) + [pltpu.SemaphoreType.DMA((4,))],
        [vmem, hbm] + [vmem] * 9,
        [hbm, vmem, hbm, hbm, hbm, hbm],
    )


def apart(tokens):
    return (tokens // 2 - 2) // BLOCK + 2


def first_seen(i, tokens):
    return jnp.maximum(i - apart(tokens) + 1, 0)


def attend_back(
    qkv, g_mixed, mixed, denom, seg_rows, seg_cols, out_terms, middle, sum_down, heads
):
    tokens, width = out_terms.shape
    wide, narrow = heads * DV, heads * F
    blocks = tokens // BLOCK
    own = tokens // 8
    held, units = sum_down.shape[0] // 4, sum_down.shape[1]

    def kernel(
        x_ref, gm_ref, m_ref, d_ref, row_ref, col_ref, term_ref, mid_ref, down_ref,
        g_ref, out_ref, gd_ref,
        gq_ref, numer_ref, gden_ref, key_ref, gm_buf, m_buf, mid_buf, here_buf, large,
        term_buf, term_load, parts_d, p_send, p_receive, local, *rest,
    ):
        bufs, (s_send, s_receive, t_send, t_receive) = rest[:6], rest[6:]
        d, c, t = place_of()
        hand_on, landed = exchange(((down_ref, parts_d),), held, p_send, p_receive, local)
        mine = pl.ds(pl.multiple_of(t * own, own), own)
        loads = (
            pltpu.make_async_copy(gm_ref, gm_buf, large.at[0]),
            pltpu.make_async_copy(m_ref, m_buf, large.at[1]),
            pltpu.make_async_copy(mid_ref, mid_buf, large.at[2]),
        )
        stored = pltpu.make_async_copy(here_buf, out_ref.at[mine], large.at[3])

        def fetch_terms(i):
            part = pl.ds(pl.multiple_of(2 * scatter_order(i) * own, 2 * own), 2 * own)
            slot = lax.rem(i, 2)
            return pltpu.make_async_copy(term_ref.at[part], term_buf.at[slot], term_load.at[slot])

        fetch_terms(0).start()

        for copy in loads:
            copy.start()
        met = around() + [(d, beside(c, 3), t)]
        say(met)

        def prepare():
            loads[0].wait()
            loads[1].wait()
            gq_ref[...] = jnp.zeros_like(gq_ref)
            for h in range(heads):
                part = pl.ds(h * DV, DV)
                gm = gm_buf[:, part].astype(F32)
                inverse = 1.0 / d_ref[:, h : h + 1]
                numer_ref[:, part] = (gm * inverse).astype(BF16)
                down = -jnp.sum(gm * m_buf[:, part], axis=1, keepdims=True) * inverse
                gden_ref[h : h + 1, :] = jnp.transpose(
                    jnp.broadcast_to(down, (tokens, 128)), (1, 0)
                )[:1]
            key_ref[...] = jnp.transpose(
                x_ref[:, wide : wide + 2 * narrow].astype(F32), (1, 0)
            ).astype(BF16)

        place = lax.broadcasted_iota(jnp.int32, (BLOCK, BLOCK), 1) - lax.broadcasted_iota(
            jnp.int32, (BLOCK, BLOCK), 0
        )
        tempered = BF16(F**-0.5)

        def one_block(j):
            start = pl.multiple_of(j * BLOCK, BLOCK)
            ids = row_ref[pl.ds(start, BLOCK), :]
            values = [x_ref[pl.ds(start, BLOCK), h * DV : (h + 1) * DV] for h in range(heads)]
            keys = [
                x_ref[pl.ds(start, BLOCK), wide + (heads + h) * F : wide + (heads + h + 1) * F]
                * tempered
                for h in range(heads)
            ]
            across = [
                key_ref[(heads + h) * F : (heads + h + 1) * F, pl.ds(start, BLOCK)] * tempered
                for h in range(heads)
            ]

            def step(i, sums):
                base = pl.multiple_of(i * BLOCK, BLOCK)
                visible = (place >= start - base) & (ids == col_ref[:, pl.ds(base, BLOCK)])
                out = []
                for h in range(heads):
                    queries = x_ref[pl.ds(base, BLOCK), wide + h * F : wide + (h + 1) * F]
                    numer = numer_ref[pl.ds(base, BLOCK), h * DV : (h + 1) * DV]
                    s = dot(keys[h], queries, 1, 1)
                    a = jnp.where(visible, (0.5 * s + 1.0) * s + 1.0, 0.0).astype(BF16)
                    ga = dot(values[h], numer, 1, 1) + gden_ref[h : h + 1, pl.ds(base, BLOCK)]
                    gs = jnp.where(visible, ga * (1.0 + s), 0.0).astype(BF16)
                    gq_ref[h * F : (h + 1) * F, pl.ds(base, BLOCK)] += dot(across[h], gs, 1, 0)
                    out += [sums[2 * h] + dot(a, numer, 1, 0), sums[2 * h + 1] + dot(gs, queries, 1, 0)]
                return tuple(out)

            zeros = []
            for h in range(heads):
                zeros += [jnp.zeros((BLOCK, DV), F32), jnp.zeros((BLOCK, F), F32)]
            sums = lax.fori_loop(
                j, jnp.minimum(j + apart(tokens), blocks), step, tuple(zeros)
            )
            for h in range(heads):
                g_ref[pl.ds(start, BLOCK), h * DV : (h + 1) * DV] = sums[2 * h].astype(BF16)
                g_ref[
                    pl.ds(start, BLOCK), wide + (heads + h) * F : wide + (heads + h + 1) * F
                ] = (sums[2 * h + 1] * F**-0.5).astype(BF16)

        def terms(i, start):
            fetch_terms(i).wait()

            @pl.when(i < 3)
            def _():
                fetch_terms(i + 1).start()

            return term_buf.at[lax.rem(i, 2)]

        def fill(n):
            if n == 0:
                prepare()
                pl.loop(0, 1)(one_block)
            else:
                pl.loop(1, blocks)(one_block)
                hand_on(0)

        moved = scatter_rows(terms, bufs, s_send, s_receive, lambda: hear(len(met)), fill)
        loads[2].wait()
        here_buf[...] = (mid_buf[...] + moved).astype(BF16)
        copy = remote(here_buf, out_ref.at[mine], t_send, t_receive, 0, (d, c, 1 - t))
        copy.start()
        stored.start()
        g_ref[:, wide : wide + narrow] = jnp.transpose(gq_ref[...], (1, 0)).astype(BF16)
        landed(0)
        for b in range(4):
            gd_ref[:, b * units : (b + 1) * units] = parts_d[b].astype(F32)
        copy.wait_send()
        there = out_ref.at[pl.ds(pl.multiple_of((1 - t) * own, own), own)]
        remote(there, there, t_send, t_receive, 0, (d, c, 1 - t)).wait_recv()
        stored.wait()

    vmem, hbm = pl.BlockSpec(memory_space=pltpu.VMEM), pl.BlockSpec(memory_space=pl.ANY)
    return call(
        kernel, "attend_back", 7,
        (qkv, g_mixed, mixed, denom, seg_rows, seg_cols, out_terms, middle, sum_down),
        [
            jax.ShapeDtypeStruct(qkv.shape, BF16),
            jax.ShapeDtypeStruct((2 * own, width), BF16),
            jax.ShapeDtypeStruct((held, 4 * units), F32),
        ],
        [
            pltpu.VMEM((narrow, tokens), F32),
            pltpu.VMEM((tokens, wide), BF16),
            pltpu.VMEM((8, tokens), F32),
            pltpu.VMEM((2 * narrow, tokens), BF16),
            pltpu.VMEM(g_mixed.shape, BF16),
            pltpu.VMEM(mixed.shape, F32),
            pltpu.VMEM(middle.shape, F32),
            pltpu.VMEM((own, width), BF16),
            pltpu.SemaphoreType.DMA((4,)),
            pltpu.VMEM((2, 2 * own, width), BF16),
            pltpu.SemaphoreType.DMA((2,)),
            pltpu.VMEM((4, held, units), BF16),
        ]
        + sems(3) + [pltpu.SemaphoreType.DMA((1,))]
        + scatter_scratch(own, width) + sems(SCATTER_COPIES) + sems(1),
        [vmem, hbm, hbm, vmem, vmem, vmem, hbm, hbm, hbm],
        [vmem, hbm, vmem],
    )


def attend_block(i, x_ref, ext_ref, row_ref, col_ref, mixed_ref, denom_ref, low_ref, heads):
    wide = heads * DV
    base = pl.multiple_of(i * BLOCK, BLOCK)
    own = row_ref[pl.ds(base, BLOCK), :]
    place = lax.broadcasted_iota(jnp.int32, (BLOCK, BLOCK), 0) - lax.broadcasted_iota(
        jnp.int32, (BLOCK, BLOCK), 1
    )
    queries = [
        x_ref[pl.ds(base, BLOCK), wide + h * F : wide + (h + 1) * F] * jnp.bfloat16(F**-0.5)
        for h in range(heads)
    ]

    def step(j, sums):
        start = pl.multiple_of(j * BLOCK, BLOCK)
        visible = (place >= start - base) & (own == col_ref[:, pl.ds(start, BLOCK)])
        out = []
        for h in range(heads):
            keys = x_ref[
                pl.ds(start, BLOCK), wide + (heads + h) * F : wide + (heads + h + 1) * F
            ]
            s = dot(queries[h], keys, 1, 1)
            a = jnp.where(visible, (0.5 * s + 1.0) * s + 1.0, 0.0).astype(BF16)
            out.append(
                sums[h] + dot(a, ext_ref[pl.ds(start, BLOCK), 2 * h * DV : (2 * h + 2) * DV], 1, 0)
            )
        return tuple(out)

    sums = lax.fori_loop(
        first_seen(i, x_ref.shape[0]),
        i + 1,
        step,
        tuple(jnp.zeros((BLOCK, 2 * DV), F32) for _ in range(heads)),
    )
    for h in range(heads):
        denom = sums[h][:, DV:]
        mixed = sums[h][:, :DV] / denom
        mixed_ref[pl.ds(base, BLOCK), h * DV : (h + 1) * DV] = mixed
        low_ref[pl.ds(base, BLOCK), h * DV : (h + 1) * DV] = mixed.astype(BF16)
        denom_ref[pl.ds(base, BLOCK), h : h + 1] = denom[:, :1]


def attend(rows_low, own_high, w_attn, seg_rows, seg_cols, cot, heads):
    tokens, part_width = rows_low.shape
    own = tokens // 8
    wide, narrow = heads * DV, heads * F

    def kernel(
        x_ref, own_ref, w_ref, row_ref, col_ref, cot_ref,
        qkv_ref, mixed_ref, denom_ref, low_ref, cot_out, rows_out,
        ext_ref, half_ref, here, x_buf, *rest,
    ):
        rows_ref, r_send, r_receive, r_store, cot_buf, c_send, c_receive, c_store = rest
        d, c, t = place_of()
        loaded = pltpu.make_async_copy(x_ref, x_buf, here.at[0])
        loaded.start()
        low_half = pltpu.make_async_copy(x_buf, rows_out.at[:, :part_width], here.at[1])

        met = around()
        say(met)
        mine = pl.ds(pl.multiple_of((2 * c + t) * own, own), own)
        rows_ref[mine, :] = own_ref[...]
        cot_buf[mine, :] = cot_ref[pl.ds(pl.multiple_of(t * own, own), own), :part_width]
        hear(len(met))

        def first_half():
            loaded.wait()

            @pl.loop(0, tokens // BLOCK)
            def _(n):
                rows = pl.ds(pl.multiple_of(n * BLOCK, BLOCK), BLOCK)
                half_ref[rows, :wide] = dot(x_buf[rows, :], w_ref[:part_width, :wide], 1, 0)
                half_ref[rows, wide:] = dot(x_buf[rows, :], w_ref[:part_width, 2 * wide :], 1, 0)

            low_half.start()

        def second_half(start):
            rows = pl.ds(start, own)
            values = (
                half_ref[rows, :wide] + dot(rows_ref[rows, :], w_ref[part_width:, :wide], 1, 0)
            ).astype(BF16)
            qkv_ref[rows, :wide] = values
            qkv_ref[rows, wide:] = (
                half_ref[rows, wide:] + dot(rows_ref[rows, :], w_ref[part_width:, 2 * wide :], 1, 0)
            ).astype(BF16)
            for h in range(heads):
                ext_ref[rows, 2 * h * DV : (2 * h + 1) * DV] = values[:, h * DV : (h + 1) * DV]
                ext_ref[rows, (2 * h + 1) * DV : (2 * h + 2) * DV] = jnp.ones((own, DV), BF16)

        begun = []

        def cot_begin():
            begun.extend(gather_begin(cot_buf, c_send, c_receive))

        gather_rows(
            rows_ref, rows_out.at[:, part_width:], r_send, r_receive, r_store, second_half, first_half,
            late=cot_begin,
        )

        def blocks(first, last):
            @pl.loop(first, last)
            def _(i):
                attend_block(
                    i, qkv_ref, ext_ref, row_ref, col_ref, mixed_ref, denom_ref, low_ref, heads
                )

        gather_rows(
            cot_buf, cot_out, c_send, c_receive, c_store, begun=begun,
            early=lambda: blocks(0, tokens // BLOCK // 2),
            middle=lambda: blocks(tokens // BLOCK // 2, tokens // BLOCK - 1),
            late=lambda: blocks(tokens // BLOCK - 1, tokens // BLOCK),
        )
        low_half.wait()

    vmem, hbm = pl.BlockSpec(memory_space=pltpu.VMEM), pl.BlockSpec(memory_space=pl.ANY)
    return call(
        kernel, "attend", 2, (rows_low, own_high, w_attn, seg_rows, seg_cols, cot),
        [
            jax.ShapeDtypeStruct((tokens, wide + 2 * narrow), BF16),
            jax.ShapeDtypeStruct((tokens, wide), F32),
            jax.ShapeDtypeStruct((tokens, heads), F32),
            jax.ShapeDtypeStruct((tokens, wide), BF16),
            jax.ShapeDtypeStruct((tokens, part_width), BF16),
            jax.ShapeDtypeStruct((tokens, 2 * part_width), BF16),
        ],
        [
            pltpu.VMEM((tokens, 2 * wide), BF16),
            pltpu.VMEM((tokens, wide + 2 * narrow), F32),
            pltpu.SemaphoreType.DMA((2,)),
            pltpu.VMEM((tokens, part_width), BF16),
        ]
        + gather_scratch(tokens, part_width) + gather_scratch(tokens, part_width),
        [hbm] + [vmem] * 5,
        [vmem] * 4 + [hbm] * 2,
    )


def to_middle(heads_out, w_attn, x):
    tokens, width = heads_out.shape[0], x.shape[1]
    own = tokens // 8
    wide = heads_out.shape[1]

    def kernel(h_ref, w_ref, x_ref, mid_ref, rows_out, w_buf, x_buf, mid_buf, large, *rest):
        bufs, (s_send, s_receive, rows_ref, g_send, g_receive, store) = rest[:6], rest[6:]
        d, c, t = place_of()
        mine = pl.ds(pl.multiple_of(t * own, own), own)
        weights = pltpu.make_async_copy(w_ref.at[:, wide : 2 * wide], w_buf, large.at[0])
        loaded = pltpu.make_async_copy(x_ref.at[mine], x_buf, large.at[1])
        stored = pltpu.make_async_copy(mid_buf, mid_ref, large.at[2])
        weights.start()
        loaded.start()
        say(around())
        weights.wait()

        def terms(i, start):
            return [(h_ref[pl.ds(start, 2 * own), :], w_buf, slice(None))]

        total = scatter_rows(terms, bufs, s_send, s_receive, lambda: hear(3))
        loaded.wait()
        middle = total + x_buf[...].astype(F32)
        mid_buf[...] = middle
        stored.start()
        _, hat = norm_parts(middle)
        rows_ref[pl.ds(pl.multiple_of((2 * c + t) * own, own), own), :] = hat.astype(BF16)
        gather_rows(rows_ref, rows_out, g_send, g_receive, store)
        stored.wait()

    vmem, hbm = pl.BlockSpec(memory_space=pltpu.VMEM), pl.BlockSpec(memory_space=pl.ANY)
    return call(
        kernel, "to_middle", 3, (heads_out, w_attn, x),
        [jax.ShapeDtypeStruct((own, width), F32), jax.ShapeDtypeStruct((tokens, width), BF16)],
        [
            pltpu.VMEM((width, wide), BF16),
            pltpu.VMEM((own, width), BF16),
            pltpu.VMEM((own, width), F32),
            pltpu.SemaphoreType.DMA((3,)),
        ]
        + scatter_scratch(own, width) + sems(SCATTER_COPIES) + gather_scratch(tokens, width),
        [vmem, hbm, hbm],
        [hbm, hbm],
        flops=2 * tokens * width * heads_out.shape[1],
    )


def gate_up(rows_two, w_both, cot, cot_low):
    tokens, width = rows_two.shape
    own = tokens // 8
    units = w_both.shape[1] // 2
    main = units // 128 * 128
    count = tokens // BLOCK
    tile = 256

    def kernel(
        x_ref, w_ref, cot_ref, low_ref, hid_out, slope_out, silu_out, rows_out, down_out,
        x_buf, w_buf, low_buf, hid_ref, slope_ref, silu_ref, down_buf, load, store, down_store,
        rows_ref, send, receive, row_store,
    ):
        d, c, t = place_of()

        def fetch(i):
            rows = pl.ds(pl.multiple_of(i * BLOCK, BLOCK), BLOCK)
            slot = lax.rem(i, 2)
            return pltpu.make_async_copy(x_ref.at[rows], x_buf.at[slot], load.at[slot])

        def given(i):
            rows = pl.ds(pl.multiple_of(i * BLOCK, BLOCK), BLOCK)
            slot = lax.rem(i, 2)
            return [
                pltpu.make_async_copy(source, target.at[rows], store.at[n, slot])
                for n, (source, target) in enumerate(
                    (
                        (hid_ref.at[rows], hid_out),
                        (slope_ref.at[slot], slope_out),
                        (silu_ref.at[slot], silu_out),
                    )
                )
            ]

        weights = pltpu.make_async_copy(w_ref, w_buf, load.at[2])
        weights.start()
        fetch(0).start()
        low_copy = pltpu.make_async_copy(low_ref, low_buf, load.at[3])
        low_copy.start()
        greet(around())
        mine = pl.multiple_of((2 * c + t) * own, own)
        rows_ref[pl.ds(mine, own), :] = cot_ref[
            pl.ds(pl.multiple_of(t * own, own), own), width // 2 :
        ]

        def blocks(first, last):
            @pl.loop(first, last)
            def _(i):
                slot = lax.rem(i, 2)

                @pl.when(i + 1 < count)
                def _():
                    fetch(i + 1).start()

                fetch(i).wait()
                both = dot(x_buf[slot], w_buf[...], 1, 0)

                @pl.when(i >= 2)
                def _():
                    for copy in given(i - 2):
                        copy.wait()

                def act(gate, up, part):
                    sig = jax.nn.sigmoid(gate)
                    silu = gate * sig
                    hid_ref[pl.ds(pl.multiple_of(i * BLOCK, BLOCK), BLOCK), part] = (
                        silu * up
                    ).astype(BF16)
                    slope_ref[slot, :, part] = (up * sig * (1.0 + gate * (1.0 - sig))).astype(BF16)
                    silu_ref[slot, :, part] = silu.astype(BF16)

                act(both[:, :main], both[:, main : 2 * main], slice(0, main))
                if main < units:
                    act(
                        both[:, 2 * main : main + units],
                        both[:, main + units :],
                        slice(main, units),
                    )
                for copy in given(i):
                    copy.start()

        per = width // 2 // tile

        def down_given(base, n):
            slot = lax.rem(n, 2)
            rows = pl.ds(pl.multiple_of(base + n * tile, tile), tile)
            return pltpu.make_async_copy(down_buf.at[slot], down_out.at[rows], down_store.at[slot])

        def down_tiles(source, base, end):
            @pl.loop(0, end)
            def _(n):
                @pl.when(n >= 2)
                def _():
                    down_given(base, n - 2).wait()

                part = pl.ds(pl.multiple_of(n * tile, tile), tile)
                down_buf[lax.rem(n, 2)] = dot(source[:, part], hid_ref[...], 0, 0).astype(BF16)
                down_given(base, n).start()

        def early():
            weights.wait()
            blocks(0, 1)

        def later():
            blocks(count // 2, count)
            low_copy.wait()
            down_tiles(low_buf, 0, per)
            for n in (per - 2, per - 1):
                down_given(0, n).wait()

        gather_rows(
            rows_ref, rows_out, send, receive, row_store, early=early,
            middle=lambda: blocks(1, count // 2), late=later,
        )
        down_tiles(rows_ref, width // 2, per)
        for n in (per - 2, per - 1):
            down_given(width // 2, n).wait()
        for i in (count - 2, count - 1):
            for copy in given(i):
                copy.wait()

    vmem, hbm = pl.BlockSpec(memory_space=pltpu.VMEM), pl.BlockSpec(memory_space=pl.ANY)
    return call(
        kernel, "gate_up", 8, (rows_two, w_both, cot, cot_low),
        [jax.ShapeDtypeStruct((tokens, units), BF16)] * 3
        + [
            jax.ShapeDtypeStruct((tokens, width // 2), BF16),
            jax.ShapeDtypeStruct((width, units), BF16),
        ],
        [
            pltpu.VMEM((2, BLOCK, width), BF16),
            pltpu.VMEM(w_both.shape, BF16),
            pltpu.VMEM(cot_low.shape, BF16),
            pltpu.VMEM((tokens, units), BF16),
            pltpu.VMEM((2, BLOCK, units), BF16),
            pltpu.VMEM((2, BLOCK, units), BF16),
            pltpu.VMEM((2, tile, units), BF16),
            pltpu.SemaphoreType.DMA((4,)),
            pltpu.SemaphoreType.DMA((3, 2)),
            pltpu.SemaphoreType.DMA((2,)),
        ]
        + gather_scratch(tokens, width // 2),
        [hbm, hbm, vmem, hbm],
        [hbm] * 5,
        flops=4 * tokens * width * units,
    )


def feed_forward(slope, silu, cot_low, cot_high, w_down, rows_two):
    tokens, width = rows_two.shape
    units = slope.shape[1]
    main = units // 128 * 128
    tile = 256
    part_width = width // 2
    count = tokens // BLOCK

    def kernel(
        slope_ref, silu_ref, low_ref, high_ref, d_ref, two_ref, g_out, grad_ref,
        slope_buf, silu_buf, low_buf, high_buf, d_buf, rest_buf, d_load, g_ref, here, g_store, cols,
        out, load, store,
    ):
        def rows(i):
            return pl.ds(pl.multiple_of(i * BLOCK, BLOCK), BLOCK)

        def fetch(i):
            slot = lax.rem(i, 2)
            return [
                pltpu.make_async_copy(source.at[rows(i)], target.at[slot], here.at[n, slot])
                for n, (source, target) in enumerate(
                    (
                        (low_ref, low_buf),
                        (high_ref, high_buf),
                        (slope_ref, slope_buf),
                        (silu_ref, silu_buf),
                    )
                )
            ]

        def g_given(i):
            return pltpu.make_async_copy(g_ref.at[rows(i)], g_out.at[rows(i)], g_store.at[i])

        def wanted(n):
            part = pl.ds(pl.multiple_of(n * tile, tile), tile)
            slot = lax.rem(n, 2)
            return pltpu.make_async_copy(two_ref.at[:, part], cols.at[slot], load.at[slot])

        def given(n):
            part = pl.ds(pl.multiple_of(n * tile, tile), tile)
            slot = lax.rem(n, 2)
            return pltpu.make_async_copy(out.at[slot], grad_ref.at[part], store.at[slot])

        weights_there = load_down(d_ref, d_buf, rest_buf, d_load, units)
        for copy in fetch(0):
            copy.start()
        wanted(0).start()
        weights_there()

        @pl.loop(0, count)
        def _(i):
            slot = lax.rem(i, 2)

            @pl.when(i + 1 < count)
            def _():
                for copy in fetch(i + 1):
                    copy.start()

            for copy in fetch(i):
                copy.wait()
            g_hidden = dot(low_buf[slot], down_rows(d_buf, 0, part_width, units), 1, 0) + dot(
                high_buf[slot], down_rows(d_buf, part_width, width, units), 1, 0
            )
            gg = g_hidden * slope_buf[slot].astype(F32)
            gu = g_hidden * silu_buf[slot].astype(F32)
            part = rows(i)
            g_ref[part, :main] = gg[:, :main].astype(BF16)
            g_ref[part, main : 2 * main] = gu[:, :main].astype(BF16)
            if main < units:
                g_ref[part, 2 * main :] = jnp.concatenate(
                    [gg[:, main:], gu[:, main:]], axis=1
                ).astype(BF16)
            g_given(i).start()

        last = width // tile

        @pl.loop(0, last)
        def _(n):
            @pl.when(n + 1 < last)
            def _():
                wanted(n + 1).start()

            wanted(n).wait()

            @pl.when(n >= 2)
            def _():
                given(n - 2).wait()

            slot = lax.rem(n, 2)
            out[slot] = dot(cols[slot], g_ref[...], 0, 0).astype(BF16)
            given(n).start()

        given(last - 2).wait()
        given(last - 1).wait()
        for i in range(count):
            g_given(i).wait()

    hbm = pl.BlockSpec(memory_space=pl.ANY)
    moved = 2 * tokens * (2 * width + 4 * units) + 6 * width * units
    return pl.pallas_call(
        kernel,
        in_specs=[hbm] * 6,
        out_specs=[hbm] * 2,
        out_shape=[
            jax.ShapeDtypeStruct((tokens, 2 * units), BF16),
            jax.ShapeDtypeStruct((width, 2 * units), BF16),
        ],
        scratch_shapes=[
            pltpu.VMEM((2, BLOCK, units), BF16),
            pltpu.VMEM((2, BLOCK, units), BF16),
            pltpu.VMEM((2, BLOCK, part_width), BF16),
            pltpu.VMEM((2, BLOCK, part_width), BF16),
            *down_scratch(w_down, units),
            pltpu.VMEM((tokens, 2 * units), BF16),
            pltpu.SemaphoreType.DMA((4, 2)),
            pltpu.SemaphoreType.DMA((count,)),
            pltpu.VMEM((2, tokens, tile), BF16),
            pltpu.VMEM((2, tile, 2 * units), BF16),
            pltpu.SemaphoreType.DMA((3,)),
            pltpu.SemaphoreType.DMA((2,)),
        ],
        compiler_params=pltpu.CompilerParams(vmem_limit_bytes=VMEM_MOST),
        cost_estimate=pl.CostEstimate(
            flops=6 * tokens * width * units, bytes_accessed=moved, transcendentals=0
        ),
        name="feed_forward",
    )(slope, silu, cot_low, cot_high, w_down, rows_two)


def to_branch(g_both, w_both, middle, cot, w_attn, wide, hidden, w_down):
    tokens, width = g_both.shape[0], middle.shape[1]
    own = tokens // 8
    units = hidden.shape[1]
    tile = width // 2

    def kernel(
        g_ref, w_ref, mid_ref, cot_ref, o_ref, hid_ref, d_ref, gm_ref, rows_out, mix_ref, term_ref,
        g_buf, w_buf, hid_buf, d_buf, rest_buf, d_load, term_buf, load, term_store,
        mid_buf, cot_buf, o_buf, gm_buf, large, *rest,
    ):
        bufs, (s_send, s_receive, rows_ref, g_send, g_receive, store) = rest[:6], rest[6:]
        d, c, t = place_of()
        mine = pl.ds(pl.multiple_of(t * own, own), own)
        loads = (
            pltpu.make_async_copy(mid_ref, mid_buf, large.at[0]),
            pltpu.make_async_copy(cot_ref.at[mine], cot_buf, large.at[1]),
            pltpu.make_async_copy(o_ref.at[:, wide : 2 * wide], o_buf, large.at[2]),
        )
        stored = pltpu.make_async_copy(gm_buf, gm_ref, large.at[3])

        def fetch(i):
            part = pl.ds(pl.multiple_of(2 * scatter_order(i) * own, 2 * own), 2 * own)
            slot = lax.rem(i, 2)
            return pltpu.make_async_copy(g_ref.at[part], g_buf.at[slot], load.at[slot])

        weights = pltpu.make_async_copy(w_ref, w_buf, load.at[2])
        weights.start()
        fetch(0).start()
        say(around())
        weights.wait()
        down_there = load_down(d_ref, d_buf, rest_buf, d_load, units)
        for copy in loads:
            copy.start()
        pltpu.make_async_copy(
            hid_ref.at[pl.ds(0, BLOCK)], hid_buf, load.at[4]
        ).start()

        def terms(i, start):
            fetch(i).wait()

            @pl.when(i < 3)
            def _():
                fetch(i + 1).start()

            return [(g_buf[lax.rem(i, 2)], w_buf, slice(None))]

        total = scatter_rows(terms, bufs, s_send, s_receive, lambda: hear(3))
        for copy in loads:
            copy.wait()
        scale, hat = norm_parts(mid_buf[...])
        g_middle = cot_buf[...].astype(F32) + norm_back(total, hat, scale)
        gm_buf[...] = g_middle
        stored.start()
        rows_ref[pl.ds(pl.multiple_of((2 * c + t) * own, own), own), :] = g_middle.astype(BF16)

        def mix(start):
            mix_ref[pl.ds(start, own), :] = dot(
                rows_ref[pl.ds(start, own), :], o_buf[...], 1, 0
            ).astype(BF16)

        def block(i):
            return pl.ds(pl.multiple_of(i * BLOCK, BLOCK), BLOCK)

        def hidden_of(i):
            return pltpu.make_async_copy(hid_ref.at[block(i)], hid_buf, load.at[4])

        def term_given(i):
            return pltpu.make_async_copy(term_buf, term_ref.at[block(i)], term_store.at[0])

        def out_terms(first, last):
            @pl.loop(first, last)
            def _(i):
                hidden_of(i).wait()

                @pl.when(i > 0)
                def _():
                    term_given(i - 1).wait()

                for n in (0, 1):
                    columns = slice(n * tile, (n + 1) * tile)
                    matrix = down_rows(d_buf, n * tile, (n + 1) * tile, units)
                    term_buf[:, columns] = dot(hid_buf[...], matrix, 1, 1).astype(BF16)
                term_given(i).start()

                @pl.when(i + 1 < tokens // BLOCK)
                def _():
                    hidden_of(i + 1).start()

        down_there()
        blocks = tokens // BLOCK
        gather_rows(
            rows_ref, rows_out, g_send, g_receive, store, mix,
            lambda: out_terms(0, blocks // 2),
            lambda: out_terms(blocks // 2, blocks - 1),
            lambda: out_terms(blocks - 1, blocks),
        )
        term_given(blocks - 1).wait()
        stored.wait()

    vmem, hbm = pl.BlockSpec(memory_space=pltpu.VMEM), pl.BlockSpec(memory_space=pl.ANY)
    return call(
        kernel, "to_branch", 5, (g_both, w_both, middle, cot, w_attn, hidden, w_down),
        [
            jax.ShapeDtypeStruct((own, width), F32),
            jax.ShapeDtypeStruct((tokens, width), BF16),
            jax.ShapeDtypeStruct((tokens, wide), BF16),
            jax.ShapeDtypeStruct((tokens, width), BF16),
        ],
        [
            pltpu.VMEM((2, 2 * own, g_both.shape[1]), BF16),
            pltpu.VMEM(w_both.shape, BF16),
            pltpu.VMEM((BLOCK, units), BF16),
            *down_scratch(w_down, units),
            pltpu.VMEM((BLOCK, width), BF16),
            pltpu.SemaphoreType.DMA((5,)),
            pltpu.SemaphoreType.DMA((1,)),
            pltpu.VMEM((own, width), F32),
            pltpu.VMEM((own, width), BF16),
            pltpu.VMEM((width, wide), BF16),
            pltpu.VMEM((own, width), F32),
            pltpu.SemaphoreType.DMA((4,)),
        ]
        + scatter_scratch(own, width) + sems(SCATTER_COPIES) + gather_scratch(tokens, width),
        [hbm] * 7,
        [hbm, hbm, vmem, hbm],
        flops=4 * tokens * width * (g_both.shape[1] // 2 + wide),
    )


def as_row(column):
    return jnp.transpose(jnp.broadcast_to(column, (column.shape[0], 128)), (1, 0))[:8]


def to_input(
    g_qkv, w_attn, x, g_middle, rows_one, branch, heads_out, sum_both, weights, gains, heads
):
    tokens, width = g_qkv.shape[0], x.shape[1]
    own = tokens // 8
    deep = lax.axis_size("dp")
    across = g_qkv.shape[1]
    group = width // deep
    held = group // 4
    wide, narrow = heads * DV, heads * F
    both = sum_both.shape[1]
    units = both // 2
    main = units // 128 * 128

    def kernel(
        g_ref, w_ref, x_ref, gm_ref, one_ref, br_ref, h_ref, both_ref,
        wq_ref, wk_ref, wv_ref, wg_ref, wu_ref, gain_ref, gain_two_ref,
        out_ref, gq_ref, gk_ref, gv_ref, go_ref, gg_ref, gu_ref, row_ref, row_two_ref,
        *rest,
    ):
        bufs, (s_send, s_receive, t_send, t_receive) = rest[:6], rest[6:10]
        (
            came_deep, came_out, sums, sums_out, parts_a, parts_o, parts_b, scalar, back_ref, back_out,
            cols, load, d_send, d_receive, p_send, p_receive, local, x_buf, gm_buf, in_buf, gate_buf,
            up_buf, large,
        ) = rest[10:]
        d, c, t = place_of()
        hand_on, landed = exchange(
            ((sums, parts_a), (both_ref, parts_b), (sums_out, parts_o)), held, p_send, p_receive, local
        )

        def fetch(j):
            part = pl.ds(pl.multiple_of(depth(d, j % deep + 1) * group, group), group)
            source = br_ref if j < deep else one_ref
            return pltpu.make_async_copy(source.at[:, part], cols.at[j % 2], load.at[j % 2])

        def deeper(j):
            n = j % deep
            source, target = (back_out, came_out) if j < deep else (back_ref, came_deep)
            return remote(
                source.at[n], target.at[n], d_send, d_receive, j, (depth(d, n + 1), c, t)
            )

        def plane(j):
            n = j % deep
            if j + 1 < 2 * deep:
                fetch(j + 1).start()
            fetch(j).wait()
            if j < deep:
                back_out[n] = dot(cols[j % 2], h_ref[...], 0, 0).astype(BF16)
            else:
                back_ref[n] = dot(cols[j % 2], g_ref[...], 0, 0).astype(BF16)

        def sum_of(back, came, first):
            total = back[deep - 1].astype(F32)
            for n in range(deep - 1):
                deeper(first + n).wait_recv()
                total = total + came[n].astype(F32)
            return total.astype(BF16)

        fetch(0).start()
        mine = pl.ds(pl.multiple_of(t * own, own), own)
        loads = (
            pltpu.make_async_copy(x_ref.at[mine], x_buf, large.at[0]),
            pltpu.make_async_copy(gm_ref, gm_buf, large.at[1]),
        )
        stored = pltpu.make_async_copy(in_buf, out_ref.at[mine], large.at[2])
        wide_stores = (
            pltpu.make_async_copy(gate_buf, gg_ref, large.at[3]),
            pltpu.make_async_copy(up_buf, gu_ref, large.at[4]),
        )
        for copy in loads:
            copy.start()
        met = (
            around()
            + [(d, beside(c, 3), t)]
            + [(depth(d, k), c, t) for k in range(1, deep)]
        )
        say(met)

        early = deep // 2
        for j in range(early):
            plane(j)

        def enter():
            hear(len(met))
            hand_on(1)
            for j in range(early):
                deeper(j).start()

        def terms(i, start):
            part = pl.ds(start, 2 * own)
            return [
                (g_ref[part, :wide], w_ref, slice(0, wide)),
                (g_ref[part, wide:], w_ref, slice(2 * wide, None)),
            ]

        def fill(n):
            if n == 0:
                for j in range(early, 2 * deep):
                    plane(j)
                    if j % deep != deep - 1:
                        deeper(j).start()
                return
            landed(1)
            whole = [parts_b[b].astype(F32) for b in range(4)]
            term = jnp.zeros((held, 1), F32)
            for ref, weight, first, rest_of in (
                (gate_buf, wg_ref, 0, 2 * main),
                (up_buf, wu_ref, main, main + units),
            ):
                pieces = []
                for b in range(4):
                    pieces.append(whole[b][:, first : first + main])
                    if main < units:
                        pieces.append(whole[b][:, rest_of : rest_of + units - main])
                s = jnp.concatenate(pieces, axis=1)
                term = term + jnp.sum(s * weight[...].astype(F32), axis=1, keepdims=True)
                ref[...] = s * as_column(gain_two_ref[...].astype(F32))
            for copy in wide_stores:
                copy.start()
            scalar[0, 1] = as_row(term)

        e_one = scatter_rows(terms, bufs, s_send, s_receive, enter, fill)
        for copy in loads:
            copy.wait()
        scale, hat = norm_parts(x_buf[...].astype(F32))
        in_buf[...] = gm_buf[...] + norm_back(e_one, hat, scale)
        copy = remote(in_buf, out_ref.at[mine], t_send, t_receive, 0, (d, c, 1 - t))
        copy.start()
        stored.start()
        sums_out[...] = sum_of(back_out, came_out, 0)
        hand_on(2)
        sums[...] = sum_of(back_ref, came_deep, deep)
        hand_on(0)
        landed(2)
        for b in range(4):
            go_ref[:, b * wide : (b + 1) * wide] = parts_o[b].astype(F32)
        landed(0)

        gain_one = as_column(gain_ref[...].astype(F32))
        term_one = jnp.zeros((held, 1), F32)
        for ref, weight, start, count in (
            (gv_ref, wv_ref, 0, wide),
            (gq_ref, wq_ref, wide, narrow),
            (gk_ref, wk_ref, wide + narrow, narrow),
        ):
            s = jnp.concatenate(
                [parts_a[b][:, start : start + count].astype(F32) for b in range(4)], axis=1
            )
            term_one = term_one + jnp.sum(s * weight[...].astype(F32), axis=1, keepdims=True)
            ref[...] = s * gain_one
        scalar[0, 0] = as_row(term_one)
        swap = remote(scalar.at[0], scalar.at[1], t_send, t_receive, 1, (d, c, 1 - t))
        swap.start()
        swap.wait()
        row_ref[...] = (scalar[0, 0] + scalar[1, 0])[:1]
        row_two_ref[...] = (scalar[0, 1] + scalar[1, 1])[:1]
        copy.wait_send()
        there = out_ref.at[pl.ds(pl.multiple_of((1 - t) * own, own), own)]
        remote(there, there, t_send, t_receive, 0, (d, c, 1 - t)).wait_recv()
        for n in range(deep - 1):
            deeper(n).wait_send()
            deeper(deep + n).wait_send()
        stored.wait()
        for copy in wide_stores:
            copy.wait()

    w_q, w_k, w_v, w_gate, w_up = weights
    vmem, hbm = pl.BlockSpec(memory_space=pltpu.VMEM), pl.BlockSpec(memory_space=pl.ANY)
    return call(
        kernel, "to_input", 6,
        (g_qkv, w_attn, x, g_middle, rows_one, branch, heads_out, sum_both) + tuple(weights)
        + tuple(gains),
        [jax.ShapeDtypeStruct((2 * own, width), F32)]
        + [jax.ShapeDtypeStruct(w.shape, F32) for w in (w_q, w_k, w_v, w_v, w_gate, w_up)]
        + [jax.ShapeDtypeStruct((1, held), F32)] * 2,
        scatter_scratch(own, width) + sems(SCATTER_COPIES) + sems(2)
        + [
            pltpu.VMEM((deep - 1, group, across), BF16),
            pltpu.VMEM((deep - 1, group, wide), BF16),
            pltpu.VMEM((group, across), BF16),
            pltpu.VMEM((group, wide), BF16),
            pltpu.VMEM((4, held, across), BF16),
            pltpu.VMEM((4, held, wide), BF16),
            pltpu.VMEM((4, held, both), BF16),
            pltpu.VMEM((2, 2, 8, held), F32),
            pltpu.VMEM((deep, group, across), BF16),
            pltpu.VMEM((deep, group, wide), BF16),
            pltpu.VMEM((2, tokens, group), BF16),
            pltpu.SemaphoreType.DMA((2,)),
        ]
        + sems(2 * deep) + sems(9)
        + [
            pltpu.SemaphoreType.DMA((3,)),
            pltpu.VMEM((own, width), BF16),
            pltpu.VMEM((own, width), F32),
            pltpu.VMEM((own, width), F32),
            pltpu.VMEM(w_gate.shape, F32),
            pltpu.VMEM(w_up.shape, F32),
            pltpu.SemaphoreType.DMA((5,)),
        ],
        [vmem] * 2 + [hbm] * 4 + [vmem, hbm] + [vmem] * 7,
        [hbm] + [vmem] * 4 + [hbm] * 2 + [vmem] * 2,
        flops=2 * tokens * width * g_qkv.shape[1],
    )


def plane_shards(
    activations,
    seg_ids,
    cotangent,
    q_weight,
    k_weight,
    v_weight,
    o_weight,
    gate_weight,
    up_weight,
    down_weight,
    attn_gain,
    mlp_gain,
):
    parts = lax.axis_size("ctx")
    heads = q_weight.shape[1] // F // parts
    tokens = activations.shape[1] * parts
    x, cot_block = activations[0], cotangent[0]
    gain_one, gain_two = attn_gain[None], mlp_gain[None]
    rows_low, own_high, segments, w_attn, cut_both, cut_down = front(
        x,
        seg_ids,
        (q_weight, k_weight, v_weight, o_weight, gate_weight, up_weight, down_weight),
        (gain_one, gain_two),
        tokens,
        heads,
    )
    w_attn = w_attn.reshape(-1, w_attn.shape[3])
    w_both = lax.all_gather(cut_both, "dp", axis=0, tiled=True).reshape(-1, cut_both.shape[2])
    seg_rows, seg_cols = segments.reshape(tokens, 1), segments.reshape(1, tokens)
    qkv, mixed, denom, heads_out, cot_low, rows_one = attend(
        rows_low, own_high, w_attn, seg_rows, seg_cols, cot_block, heads
    )
    cut_down, heads_out = lax.optimization_barrier((cut_down, heads_out))
    w_down = lax.all_gather(cut_down, "dp", axis=0, tiled=True)
    middle, rows_two = to_middle(heads_out, w_attn, x)
    hidden, slope, silu, cot_high, back_down = gate_up(rows_two, w_both, cot_block, cot_low)
    sum_down = lax.psum_scatter(back_down, "dp", scatter_dimension=0, tiled=True)
    g_both, back_both = feed_forward(slope, silu, cot_low, cot_high, w_down, rows_two)
    sum_both = lax.psum_scatter(back_both, "dp", scatter_dimension=0, tiled=True)
    g_middle, branch, g_mixed, out_terms = to_branch(
        g_both, w_both, middle, cot_block, w_attn, heads * DV, hidden, w_down
    )
    g_qkv, out, s_down = attend_back(
        qkv, g_mixed, mixed, denom, seg_rows, seg_cols, out_terms, middle, sum_down, heads
    )
    g_input, s_q, s_k, s_v, s_o, s_gate, s_up, attn_row, mlp_row = to_input(
        g_qkv,
        w_attn,
        x,
        g_middle,
        rows_one,
        branch,
        heads_out,
        sum_both,
        (q_weight, k_weight, v_weight, gate_weight, up_weight),
        (gain_one, gain_two),
        heads,
    )
    return (
        out[None],
        g_input[None],
        s_q,
        s_k,
        s_v,
        s_o,
        s_gate,
        s_up,
        s_down,
        attn_row[0],
        mlp_row[0],
    )


def layer(*arrays):
    heads, units = arrays[3].shape[1] // F, arrays[7].shape[1]
    fits = lax.axis_size("ctx") == 4 and lax.axis_size("tp") == 2
    fits = fits and heads % 4 == 0 and units % 256 == 0
    plan = plane_shards if fits else shards
    return plan(*arrays)


def solution(mesh):
    placed = (
        P("dp", "ctx", None),
        P("dp", "ctx"),
        P("dp", "ctx", None),
        P(("dp", "ctx"), "tp"),
        P(("dp", "ctx"), "tp"),
        P(("dp", "ctx"), "tp"),
        P(("dp", "ctx"), "tp"),
        P(("dp", "ctx"), "tp"),
        P(("dp", "ctx"), "tp"),
        P(("dp", "ctx"), "tp"),
        P(("dp", "ctx")),
        P(("dp", "ctx")),
    )
    return jax.shard_map(
        layer,
        mesh=mesh,
        in_specs=placed,
        out_specs=(
            P("dp", "ctx", None),
            P("dp", "ctx", None),
            P(("dp", "ctx"), "tp"),
            P(("dp", "ctx"), "tp"),
            P(("dp", "ctx"), "tp"),
            P(("dp", "ctx"), "tp"),
            P(("dp", "ctx"), "tp"),
            P(("dp", "ctx"), "tp"),
            P(("dp", "ctx"), "tp"),
            P(("dp", "ctx")),
            P(("dp", "ctx")),
        ),
        check_vma=False,
    )
```

```python
import functools

import jax
import jax.numpy as jnp
from jax import lax
from jax.experimental import pallas as pl
from jax.experimental.pallas import tpu as pltpu
from jax.sharding import PartitionSpec as P

F = 16
DV = 128


EPSILON = 1e-05
PRECISE = lax.Precision.HIGHEST
VMEM_MOST = 60 * 2**20


def prefix(x, axis, join, neutral, backward):
    count = lax.axis_size(axis)
    place = lax.axis_index(axis)
    ahead = count - 1 - place if backward else place
    gathered = jax.tree.map(
        lambda a, kind: lax.all_gather(a.astype(kind), axis),
        x,
        (jnp.bfloat16, jnp.bfloat16, jnp.bfloat16),
    )
    state = jax.tree.map(lambda a, e: jnp.zeros_like(a) + jnp.asarray(e, a.dtype), x, neutral)

    def one(lap, state):
        source = count - 1 - lap if backward else lap
        return join(
            state,
            jax.tree.map(
                lambda a, own: lax.dynamic_index_in_dim(a, source, 0, False).astype(own.dtype),
                gathered,
                x,
            ),
        )

    return lax.fori_loop(0, ahead, one, state)


def taylor(features_in):
    feature_count = features_in.shape[-1]
    products = (features_in[..., :, None] * features_in[..., None, :]).reshape(
        features_in.shape[:-1] + (feature_count * feature_count,)
    )
    constant = jnp.ones(features_in.shape[:-1] + (1,), jnp.float32)
    return jnp.concatenate(
        [
            constant,
            features_in * feature_count ** (-0.25),
            products * (2.0 * feature_count) ** (-0.5),
        ],
        axis=-1,
    )


def taylor_back(features_in, incoming_gradient):
    feature_count = features_in.shape[-1]
    linear = incoming_gradient[..., 1 : 1 + feature_count] * feature_count ** (-0.25)
    square = incoming_gradient[..., 1 + feature_count :].reshape(
        incoming_gradient.shape[:-1] + (feature_count, feature_count)
    )
    paired = jnp.einsum(
        "...ab,...b->...a", square + jnp.swapaxes(square, -1, -2), features_in, precision=PRECISE
    )
    return linear + paired * (2.0 * feature_count) ** (-0.5)


def norm_backward_step(incoming_gradient, unit_normalized_rows, multiplier_term, gain_vector_row):
    rescaled_rows = incoming_gradient * gain_vector_row
    return multiplier_term * (
        rescaled_rows
        - unit_normalized_rows
        * jnp.mean(rescaled_rows * unit_normalized_rows, axis=1, keepdims=True)
    )


def join_states(earlier, later_part):
    is_empty = later_part[2] < 0.0
    retain = jnp.where(is_empty | (earlier[2] == later_part[2]), 1.0, 0.0).astype(jnp.float32)
    return (
        later_part[0] + retain * earlier[0],
        later_part[1] + retain * earlier[1],
        jnp.where(is_empty, earlier[2], later_part[2]),
    )


def shards(
    activations,
    seg_ids,
    cotangent,
    q_weight,
    k_weight,
    v_weight,
    o_weight,
    gate_weight,
    up_weight,
    down_weight,
    attn_gain,
    mlp_gain,
):
    layer_input_rows = activations[0].astype(jnp.float32)
    segment = seg_ids[0].astype(jnp.float32)
    tokens = layer_input_rows.shape[0]
    head_count = q_weight.shape[1] // F
    w_query, w_key, w_value, w_out, first_norm_gain = (
        lax.all_gather(q_weight, ("dp", "ctx"), axis=0, tiled=True),
        lax.all_gather(k_weight, ("dp", "ctx"), axis=0, tiled=True),
        lax.all_gather(v_weight, ("dp", "ctx"), axis=0, tiled=True),
        lax.all_gather(o_weight, ("dp", "ctx"), axis=0, tiled=True),
        lax.all_gather(attn_gain, ("dp", "ctx"), axis=0, tiled=True),
    )
    first_inverse_scale = lax.rsqrt(
        jnp.mean(layer_input_rows * layer_input_rows, axis=1, keepdims=True) + EPSILON
    )
    first_unit_rows = layer_input_rows * first_inverse_scale
    first_normalized = (first_unit_rows * first_norm_gain.astype(jnp.float32)).astype(jnp.bfloat16)
    queries = (
        jnp.dot(first_normalized, w_query, preferred_element_type=jnp.float32)
        .astype(jnp.bfloat16)
        .reshape(tokens, head_count, F)
    )
    key_heads = (
        jnp.dot(first_normalized, w_key, preferred_element_type=jnp.float32)
        .astype(jnp.bfloat16)
        .reshape(tokens, head_count, F)
    )
    value_heads = (
        jnp.dot(first_normalized, w_value, preferred_element_type=jnp.float32)
        .astype(jnp.bfloat16)
        .reshape(tokens, head_count, DV)
    )
    w_gate, w_up, w_down, second_norm_gain = (
        lax.all_gather(gate_weight, ("dp", "ctx"), axis=0, tiled=True),
        lax.all_gather(up_weight, ("dp", "ctx"), axis=0, tiled=True),
        lax.all_gather(down_weight, ("dp", "ctx"), axis=0, tiled=True),
        lax.all_gather(mlp_gain, ("dp", "ctx"), axis=0, tiled=True),
    )
    scores = jnp.einsum(
        "thf,shf->hts", queries, key_heads, preferred_element_type=jnp.float32
    ) * F ** (-0.5)
    places = jnp.arange(tokens)
    visible = (
        (places[:, None] >= places[None, :]) & (segment[:, None] == segment[None, :])
    ).astype(jnp.float32)
    weights = (visible * (1.0 + scores + 0.5 * scores * scores)).astype(jnp.bfloat16)
    query_float = queries.astype(jnp.float32)
    key_float = key_heads.astype(jnp.float32)
    value_float = value_heads.astype(jnp.float32)
    feat_q = taylor(query_float)
    feat_k = taylor(key_float)
    ending = segment[-1]
    owned = (segment == ending).astype(jnp.float32)[:, None, None]
    local_state = jnp.einsum("thf,thd->hfd", feat_k * owned, value_float, precision=PRECISE)
    local_total = jnp.sum(feat_k * owned, axis=0)
    empty_state = (jnp.zeros_like(local_state), jnp.zeros_like(local_total), jnp.float32(-1.0))
    prior_state, prior_total, before = prefix(
        (local_state, local_total, ending), "ctx", join_states, empty_state, False
    )
    inherit = (segment == before).astype(jnp.float32)
    numerator = jnp.einsum(
        "hts,shd->thd", weights, value_heads, preferred_element_type=jnp.float32
    ) + inherit[:, None, None] * jnp.einsum("thf,hfd->thd", feat_q, prior_state, precision=PRECISE)
    denominator = jnp.sum(weights.astype(jnp.float32), axis=2).T + inherit[:, None] * jnp.einsum(
        "thf,hf->th", feat_q, prior_total, precision=PRECISE
    )
    mixed_heads = numerator / denominator[:, :, None]
    heads_out = mixed_heads.reshape(tokens, head_count * DV).astype(jnp.bfloat16)
    attn_out = lax.psum(
        jnp.einsum("tc,dc->td", heads_out, w_out, preferred_element_type=jnp.float32), "tp"
    )
    residual_midpoint = layer_input_rows + attn_out
    second_inverse_scale = lax.rsqrt(
        jnp.mean(residual_midpoint * residual_midpoint, axis=1, keepdims=True) + EPSILON
    )
    second_unit_rows = residual_midpoint * second_inverse_scale
    second_normalized = (second_unit_rows * second_norm_gain.astype(jnp.float32)).astype(
        jnp.bfloat16
    )
    gate_value = jnp.dot(second_normalized, w_gate, preferred_element_type=jnp.float32)
    up_value = jnp.dot(second_normalized, w_up, preferred_element_type=jnp.float32)
    sigmoid_gate = jax.nn.sigmoid(gate_value)
    hidden = (gate_value * sigmoid_gate * up_value).astype(jnp.bfloat16)
    mlp_out = lax.psum(
        jnp.einsum("tc,dc->td", hidden, w_down, preferred_element_type=jnp.float32).astype(
            jnp.bfloat16
        ),
        "tp",
    ).astype(jnp.float32)
    final_out = residual_midpoint + mlp_out
    grad_out = cotangent[0].astype(jnp.float32)
    grad_branch_two = cotangent[0]
    grad_w_down = jnp.einsum(
        "td,tc->dc", grad_branch_two, hidden, preferred_element_type=jnp.float32
    )
    grad_hidden = jnp.dot(grad_branch_two, w_down, preferred_element_type=jnp.float32)
    grad_gate = (
        grad_hidden * up_value * sigmoid_gate * (1.0 + gate_value * (1.0 - sigmoid_gate))
    ).astype(jnp.bfloat16)
    grad_up = (grad_hidden * gate_value * sigmoid_gate).astype(jnp.bfloat16)
    grad_w_gate = jnp.einsum(
        "td,tc->dc", second_normalized, grad_gate, preferred_element_type=jnp.float32
    )
    grad_w_up = jnp.einsum(
        "td,tc->dc", second_normalized, grad_up, preferred_element_type=jnp.float32
    )
    grad_normed_part = jnp.einsum(
        "tc,dc->td", grad_gate, w_gate, preferred_element_type=jnp.float32
    ) + jnp.einsum("tc,dc->td", grad_up, w_up, preferred_element_type=jnp.float32)
    second_normalized_gradient = lax.psum(grad_normed_part.astype(jnp.bfloat16), "tp").astype(
        jnp.float32
    )
    second_gain_gradient = jnp.sum(second_normalized_gradient * second_unit_rows, axis=0)
    grad_middle = grad_out + norm_backward_step(
        second_normalized_gradient,
        second_unit_rows,
        second_inverse_scale,
        second_norm_gain.astype(jnp.float32),
    )
    mlp_grads = (
        lax.psum_scatter(grad_w_gate, ("dp", "ctx"), scatter_dimension=0, tiled=True),
        lax.psum_scatter(grad_w_up, ("dp", "ctx"), scatter_dimension=0, tiled=True),
        lax.psum_scatter(grad_w_down, ("dp", "ctx"), scatter_dimension=0, tiled=True),
        lax.psum_scatter(second_gain_gradient, ("dp", "ctx"), scatter_dimension=0, tiled=True),
    )
    grad_branch_one = grad_middle.astype(jnp.bfloat16)
    grad_w_out = jnp.einsum(
        "td,tc->dc", grad_branch_one, heads_out, preferred_element_type=jnp.float32
    )
    grad_heads_low = jnp.dot(grad_branch_one, w_out, preferred_element_type=jnp.float32).astype(
        jnp.bfloat16
    )
    grad_mixed = (
        lax.optimization_barrier(grad_heads_low).astype(jnp.float32).reshape(tokens, head_count, DV)
    )
    numer_low = (grad_mixed / denominator[:, :, None]).astype(jnp.bfloat16)
    grad_numer = lax.optimization_barrier(numer_low).astype(jnp.float32)
    grad_denom = -jnp.sum(grad_mixed * mixed_heads, axis=2) / denominator
    grad_weights = (
        jnp.einsum("thd,shd->hts", numer_low, value_heads, preferred_element_type=jnp.float32)
        + grad_denom.T[:, :, None]
    )
    grad_scores = (grad_weights * visible * (1.0 + scores)).astype(jnp.bfloat16)
    grad_value = jnp.einsum("hts,thd->shd", weights, numer_low, preferred_element_type=jnp.float32)
    grad_query = jnp.einsum(
        "hts,shf->thf", grad_scores, key_heads, preferred_element_type=jnp.float32
    ) * F ** (-0.5)
    grad_key = jnp.einsum(
        "hts,thf->shf", grad_scores, queries, preferred_element_type=jnp.float32
    ) * F ** (-0.5)
    grad_feat_q = inherit[:, None, None] * (
        jnp.einsum("thd,hfd->thf", grad_numer, prior_state, precision=PRECISE)
        + grad_denom[:, :, None] * prior_total[None]
    )
    carried_state = jnp.einsum(
        "thf,thd->hfd", feat_q * inherit[:, None, None], grad_numer, precision=PRECISE
    )
    carried_total = jnp.sum(feat_q * (inherit[:, None] * grad_denom)[:, :, None], axis=0)
    starting = segment[0]
    later_state, later_total, after_seg = prefix(
        (carried_state, carried_total, starting), "ctx", join_states, empty_state, True
    )
    reached = (segment == after_seg).astype(jnp.float32)[:, None, None]
    grad_feat_k = reached * (
        jnp.einsum("hfd,thd->thf", later_state, value_float, precision=PRECISE) + later_total[None]
    )
    grad_value = grad_value + reached * jnp.einsum(
        "thf,hfd->thd", feat_k, later_state, precision=PRECISE
    )
    grad_query = grad_query + taylor_back(query_float, grad_feat_q)
    grad_key = grad_key + taylor_back(key_float, grad_feat_k)
    grad_query_low = grad_query.reshape(tokens, head_count * F).astype(jnp.bfloat16)
    grad_key_low = grad_key.reshape(tokens, head_count * F).astype(jnp.bfloat16)
    grad_value_low = grad_value.reshape(tokens, head_count * DV).astype(jnp.bfloat16)
    grad_w_query = jnp.einsum(
        "td,tc->dc", first_normalized, grad_query_low, preferred_element_type=jnp.float32
    )
    grad_w_key = jnp.einsum(
        "td,tc->dc", first_normalized, grad_key_low, preferred_element_type=jnp.float32
    )
    grad_w_value = jnp.einsum(
        "td,tc->dc", first_normalized, grad_value_low, preferred_element_type=jnp.float32
    )
    grad_normed_sum = (
        jnp.einsum("tc,dc->td", grad_query_low, w_query, preferred_element_type=jnp.float32)
        + jnp.einsum("tc,dc->td", grad_key_low, w_key, preferred_element_type=jnp.float32)
        + jnp.einsum("tc,dc->td", grad_value_low, w_value, preferred_element_type=jnp.float32)
    )
    first_normalized_gradient = lax.psum(grad_normed_sum.astype(jnp.bfloat16), "tp").astype(
        jnp.float32
    )
    first_gain_gradient = jnp.sum(first_normalized_gradient * first_unit_rows, axis=0)
    grad_inputs = grad_middle + norm_backward_step(
        first_normalized_gradient,
        first_unit_rows,
        first_inverse_scale,
        first_norm_gain.astype(jnp.float32),
    )
    attn_grads = (
        lax.psum_scatter(grad_w_query, ("dp", "ctx"), scatter_dimension=0, tiled=True),
        lax.psum_scatter(grad_w_key, ("dp", "ctx"), scatter_dimension=0, tiled=True),
        lax.psum_scatter(grad_w_value, ("dp", "ctx"), scatter_dimension=0, tiled=True),
        lax.psum_scatter(grad_w_out, ("dp", "ctx"), scatter_dimension=0, tiled=True),
        lax.psum_scatter(first_gain_gradient, ("dp", "ctx"), scatter_dimension=0, tiled=True),
    )
    return (
        final_out.astype(jnp.bfloat16)[None],
        grad_inputs[None],
        attn_grads[0],
        attn_grads[1],
        attn_grads[2],
        attn_grads[3],
        mlp_grads[0],
        mlp_grads[1],
        mlp_grads[2],
        attn_grads[4],
        mlp_grads[3],
    )


BLOCK = 512


MESH = pl.DeviceIdType.MESH
BF16, F32 = jnp.bfloat16, jnp.float32


def dot(a, b, ca, cb):
    return lax.dot_general(a, b, (((ca,), (cb,)), ((), ())), preferred_element_type=F32)


def place_of():
    return lax.axis_index("dp"), lax.axis_index("ctx"), lax.axis_index("tp")


def beside(c, across):
    x, y = lax.rem(c, 2), lax.div(c, 2)
    return lax.rem(x + across % 2, 2) + 2 * lax.rem(y + across // 2, 2)


def say(devices):
    barrier = pltpu.get_barrier_semaphore()
    for device in devices:
        pl.semaphore_signal(barrier, inc=1, device_id=device, device_id_type=MESH)


def hear(count):
    pl.semaphore_wait(pltpu.get_barrier_semaphore(), count)


def greet(devices):
    say(devices)
    hear(len(devices))


def around():
    d, c, t = place_of()
    return [(d, beside(c, 1), t), (d, beside(c, 2), t), (d, c, 1 - t)]


def remote(source, target, send, receive, k, device):
    return pltpu.make_async_remote_copy(
        src_ref=source,
        dst_ref=target,
        send_sem=send.at[k],
        recv_sem=receive.at[k],
        device_id=device,
        device_id_type=MESH,
    )


def gather_steps(buf, send, receive):
    d, c, t = place_of()
    own = buf.shape[0] // 8
    half = own // 2

    def part(across, core, h):
        block = c if across == 0 else beside(c, across)
        start = (2 * block + core) * own + h * half
        return buf.at[pl.ds(pl.multiple_of(start, half), half)]

    def put(k, across, h, device):
        ref = part(across, t, h)
        copy = remote(ref, ref, send, receive, k, device)
        copy.start()
        return copy

    return put, part


def gather_begin(buf, send, receive):
    put, _ = gather_steps(buf, send, receive)
    to_x, to_y, to_t = around()
    return [
        put(0, 0, 0, to_x),
        put(1, 0, 1, to_y),
        put(2, 0, 1, to_x),
        put(3, 0, 0, to_y),
        put(6, 0, 0, to_t),
        put(7, 0, 1, to_t),
    ]


def gather_rows(
    buf, out, send, receive, store, piece=None, early=None, middle=None, late=None, begun=None
):
    d, c, t = place_of()
    own = buf.shape[0] // 8
    to_x, to_y, to_t = around()
    put, part = gather_steps(buf, send, receive)
    started = gather_begin(buf, send, receive) if begun is None else begun

    def got(k, across, core, h):
        ref = part(across, core, h)
        remote(ref, ref, send, receive, k, to_t).wait_recv()

    stored = []

    def work(across, core):
        block = c if across == 0 else beside(c, across)
        start = pl.multiple_of((2 * block + core) * own, own)
        rows = pl.ds(start, own)
        copy = pltpu.make_async_copy(buf.at[rows], out.at[rows], store.at[len(stored)])
        copy.start()
        stored.append(copy)
        if piece is not None:
            piece(start)

    if early is not None:
        early()
    work(0, t)
    got(6, 0, 1 - t, 0)
    got(7, 0, 1 - t, 1)
    work(0, 1 - t)
    got(0, 1, t, 0)
    started.append(put(4, 1, 0, to_y))
    started.append(put(8, 1, 0, to_t))
    got(1, 2, t, 1)
    started.append(put(5, 2, 1, to_x))
    started.append(put(9, 2, 1, to_t))
    if middle is not None:
        middle()
    got(2, 1, t, 1)
    started.append(put(10, 1, 1, to_t))
    got(3, 2, t, 0)
    started.append(put(11, 2, 0, to_t))
    if late is not None:
        late()
    work(1, t)
    work(2, t)
    got(8, 1, 1 - t, 0)
    got(10, 1, 1 - t, 1)
    work(1, 1 - t)
    got(9, 2, 1 - t, 1)
    got(11, 2, 1 - t, 0)
    work(2, 1 - t)
    got(4, 3, t, 0)
    started.append(put(12, 3, 0, to_t))
    got(5, 3, t, 1)
    started.append(put(13, 3, 1, to_t))
    work(3, t)
    got(12, 3, 1 - t, 0)
    got(13, 3, 1 - t, 1)
    work(3, 1 - t)
    for copy in started:
        copy.wait_send()
    for copy in stored:
        copy.wait()


GATHER_COPIES = 14


def gather_scratch(tokens, width):
    return (
        [pltpu.VMEM((tokens, width), BF16)]
        + sems(GATHER_COPIES)
        + [pltpu.SemaphoreType.DMA((8,))]
    )


def exchange(jobs, held, send, receive, local):
    d, c, t = place_of()

    def rows_of(block):
        return pl.ds(pl.multiple_of(block * held, held), held)

    def to_block(n, k):
        source, target = jobs[n]
        return remote(
            source.at[rows_of(beside(c, k))], target.at[c], send, receive, 3 * n + k - 1,
            (d, beside(c, k), t),
        )

    def from_block(n, k):
        there = jobs[n][1].at[beside(c, k)]
        return remote(there, there, send, receive, 3 * n + k - 1, (d, beside(c, k), t))

    def at_home(n):
        source, target = jobs[n]
        return pltpu.make_async_copy(source.at[rows_of(c)], target.at[c], local.at[n])

    def hand_on(n):
        for k in (3, 1, 2):
            to_block(n, k).start()
        at_home(n).start()

    def landed(n):
        at_home(n).wait()
        for k in (1, 2, 3):
            from_block(n, k).wait_recv()
            to_block(n, k).wait_send()

    return hand_on, landed


PARTS = 2


def scatter_order(i):
    c = lax.axis_index("ctx")
    across = 3 - i
    x, y = lax.rem(c, 2), lax.div(c, 2)
    return lax.rem(x + lax.rem(across, 2), 2) + 2 * lax.rem(y + lax.div(across, 2), 2)


def scatter_rows(terms, bufs, send, receive, enter, fill=None):
    to_core, from_core, kept, over, came, stage = bufs
    d, c, t = place_of()
    own, tile = kept.shape[2:]
    half = own // 2
    to_x, to_y, to_t = (d, beside(c, 1), t), (d, beside(c, 2), t), (d, c, 1 - t)

    def link(k, n):
        return remote(
            over.at[k, n], came.at[k, n], send, receive, PARTS * (4 + k) + n, to_x if k % 2 == 0 else to_y
        )

    def core(i, n):
        return remote(to_core.at[lax.rem(i, 2), n], from_core.at[i, n], send, receive, PARTS * i + n, to_t)

    def total(i, h, n, *extra):
        out = kept[i % 3, n, pl.ds(h * half, half), :]
        for k in extra:
            out = out + came[k, n].astype(F32)
        return out

    def go(k, i, h, n, *extra):
        over[k, n] = total(i, h, n, *extra).astype(BF16)
        link(k, n).start()

    def joined(i, n):
        core(i, n).wait_recv()
        kept[lax.rem(i, 3), n] = kept[lax.rem(i, 3), n] + from_core[i, n].astype(F32)

    def product(pairs, i, n):
        columns = pl.ds(n * tile, tile)
        theirs = pl.ds(pl.multiple_of((1 - t) * own, own), own)
        mine = pl.ds(pl.multiple_of(t * own, own), own)
        if not isinstance(pairs, list):
            to_core[lax.rem(i, 2), n] = pairs[theirs, columns]
            kept[lax.rem(i, 3), n] = pairs[mine, columns].astype(F32)
            return
        out = None
        for rows, matrix, part in pairs:
            term = dot(rows, matrix[columns, part], 1, 1)
            out = term if out is None else out + term
        stage[...] = out
        to_core[lax.rem(i, 2), n] = stage[theirs, :].astype(BF16)
        kept[lax.rem(i, 3), n] = stage[mine, :]

    def begin(i):
        return pl.multiple_of(2 * scatter_order(i) * own, 2 * own)

    pairs = terms(0, begin(0))
    for n in range(PARTS):
        product(pairs, 0, n)
        if n == 0:
            enter()
        core(0, n).start()
        if n > 0:
            joined(0, n - 1)
            go(0, 0, 0, n - 1)
            go(1, 0, 1, n - 1)
    joined(0, PARTS - 1)
    go(0, 0, 0, PARTS - 1)
    go(1, 0, 1, PARTS - 1)

    def step(i, carry):
        pairs = terms(i, begin(i))

        @pl.when(i >= 2)
        def _():
            for n in range(PARTS):
                core(i - 2, n).wait_send()

        product(pairs, i, 0)
        core(i, 0).start()

        @pl.when(i == 2)
        def _():
            for n in range(PARTS):
                joined(1, n)
                go(3, 1, 1, n)

        @pl.when(i == 3)
        def _():
            for n in range(PARTS):
                joined(2, n)
                go(2, 2, 0, n)

        for n in range(1, PARTS):
            product(pairs, i, n)
            core(i, n).start()

        return carry

    lax.fori_loop(1, 4, step, 0)
    if fill is not None:
        fill(0)
    for n in range(PARTS):
        link(0, n).wait_recv()
        link(1, n).wait_recv()
        go(4, 2, 1, n, 1)
        go(5, 1, 0, n, 0)
    for n in range(PARTS):
        joined(3, n)
    if fill is not None:
        fill(1)
    for n in range(PARTS):
        for k in (2, 3, 4, 5):
            link(k, n).wait_recv()
        core(2, n).wait_send()
        core(3, n).wait_send()
        for k in range(6):
            link(k, n).wait_send()
    return jnp.concatenate(
        [
            jnp.concatenate([total(3, 0, n, 2, 5), total(3, 1, n, 3, 4)], axis=0)
            for n in range(PARTS)
        ],
        axis=1,
    )


SCATTER_COPIES = 10 * PARTS


def scatter_scratch(own, width):
    tile = width // PARTS
    return [
        pltpu.VMEM((2, PARTS, own, tile), BF16),
        pltpu.VMEM((4, PARTS, own, tile), BF16),
        pltpu.VMEM((3, PARTS, own, tile), F32),
        pltpu.VMEM((6, PARTS, own // 2, tile), BF16),
        pltpu.VMEM((6, PARTS, own // 2, tile), BF16),
        pltpu.VMEM((2 * own, tile), F32),
    ]


def norm_parts(rows):
    scale = lax.rsqrt(jnp.mean(rows * rows, axis=1, keepdims=True) + EPSILON)
    return scale, rows * scale


def norm_back(e, hat, scale):
    return scale * (e - hat * jnp.mean(e * hat, axis=1, keepdims=True))


def call(kernel, name, collective, arrays, out_shape, scratch, spaces=None, out_spaces=None, flops=0):
    vmem = pl.BlockSpec(memory_space=pltpu.VMEM)
    moved = sum(a.size * a.dtype.itemsize for a in arrays)
    return pl.pallas_call(
        kernel,
        in_specs=spaces or [vmem] * len(arrays),
        out_specs=out_spaces or [vmem] * len(out_shape),
        out_shape=out_shape,
        scratch_shapes=scratch,
        compiler_params=pltpu.CompilerParams(
            collective_id=collective, has_side_effects=True, vmem_limit_bytes=VMEM_MOST
        ),
        cost_estimate=pl.CostEstimate(flops=flops, bytes_accessed=moved, transcendentals=0),
        name=name,
    )(*arrays)


def sems(count):
    return [pltpu.SemaphoreType.DMA((count,)), pltpu.SemaphoreType.DMA((count,))]


def depth(d, k):
    return lax.rem(d + k, lax.axis_size("dp"))


def as_column(row):
    return jnp.transpose(jnp.broadcast_to(row, (128, row.shape[1])), (1, 0))[:, :1]


def columns(ref, gain, start, count):
    low = start // 128 * 128
    high = -(-(start + count) // 128) * 128
    value = ref[:, low:high].astype(F32)
    if gain is not None:
        value = value * gain
    return value[:, start - low : start - low + count]


def packed_down(held, units):
    return units // 128 * held + (held // 2 if units % 128 else 0)


def down_scratch(w_down, units):
    return [
        pltpu.VMEM((w_down.shape[0], w_down.shape[1] * 128 // units, -(-units // 128) * 128), BF16),
        pltpu.VMEM((w_down.shape[0], w_down.shape[1] * 64 // units, 128), BF16),
        pltpu.SemaphoreType.DMA((-(-units // 128),)),
    ]


def load_down(w_ref, w_buf, rest_buf, load, units):
    held = w_buf.shape[1]
    tiles = units // 128
    copies = [
        pltpu.make_async_copy(
            w_ref.at[:, n * held : (n + 1) * held], w_buf.at[:, :, n * 128 : (n + 1) * 128], load.at[n]
        )
        for n in range(tiles)
    ]
    if units % 128:
        copies.append(pltpu.make_async_copy(w_ref.at[:, tiles * held :], rest_buf, load.at[tiles]))

    def finish():
        for copy in copies:
            copy.wait()
        if units % 128:
            w_buf[:, : held // 2, tiles * 128 : units] = rest_buf[:, :, :64]
            w_buf[:, held // 2 :, tiles * 128 : units] = rest_buf[:, :, 64:]

    for copy in copies:
        copy.start()
    return finish


def down_rows(w_buf, first, last, units):
    held = w_buf.shape[1]
    rows = w_buf[first // held : last // held, :, :units]
    return rows.reshape(last - first, units)


def front(x, seg, weights, gains, tokens, heads):
    width = x.shape[1]
    own = tokens // 8
    deep = lax.axis_size("dp")
    held, units = weights[4].shape[0], weights[4].shape[1] // 4
    wide, narrow = heads * DV, heads * F
    main = units // 128 * 128
    packed = 2 * wide + 2 * narrow
    part_width = width // 2
    down_shape = (4, packed_down(held, units), 128)
    line = {
        0: (((0, 2),), ((0, 1),), ()),
        1: (((1, 0),), ((1, 2), (1, 3)), ((3, 0),)),
        2: (((2, 3),), ((2, 1), (2, 0)), ((0, 3),)),
        3: (((3, 1),), ((3, 2),), ()),
    }
    if deep != 4:
        line = {
            p: (tuple((p, to) for to in range(deep) if to != p), (), ()) for p in range(deep)
        }

    def kernel(
        x_ref, seg_ref, q_ref, k_ref, v_ref, o_ref, g_ref, u_ref, d_ref, one_ref, two_ref,
        rows_out, own_ref, segs_ref, wa_out, wg_out, wd_out,
        cut_a, cut_g, cut_d, rows_ref, send, receive, store, small_send, small_receive, deep_send, deep_receive, here,
    ):
        d, c, t = place_of()
        jobs = (
            (lambda block: cut_a.at[block], lambda block: wa_out.at[d, block]),
            (lambda block: seg_ref.at[0], lambda block: segs_ref.at[block]),
            (lambda block: cut_g.at[block], lambda block: wg_out.at[block]),
            (lambda block: cut_d.at[block], lambda block: wd_out.at[block]),
        )

        def local(n):
            return pltpu.make_async_copy(jobs[n][0](c), jobs[n][1](c), here.at[n])

        def out(n, k):
            return remote(
                jobs[n][0](beside(c, k)), jobs[n][1](c), small_send, small_receive,
                3 * n + k - 1, (d, beside(c, k), t),
            )

        def arrival(n, k):
            block = beside(c, k)
            return remote(
                jobs[n][0](block), jobs[n][1](block), small_send, small_receive,
                3 * n + k - 1, (d, block, t),
            )

        def shard(slot, s, to):
            return pltpu.make_async_remote_copy(
                src_ref=wa_out.at[s], dst_ref=wa_out.at[s], send_sem=deep_send.at[slot],
                recv_sem=deep_receive.at[s], device_id=(to, c, t), device_id_type=MESH,
            )

        def in_plane(act):
            for p in range(deep):
                pl.when(d == p)(functools.partial(act, p, *line[p]))

        def first_shards(p, first, then, on):
            for slot, (s, to) in enumerate(first):
                shard(slot, s, to).start()

        def other_shards(p, first, then, on):
            for slot, (s, to) in enumerate(then):
                shard(len(first) + slot, s, to).start()
            for slot, (s, to) in enumerate(on):
                shard(len(first) + len(then) + slot, s, to).wait_recv()
                shard(len(first) + len(then) + slot, s, to).start()

        def end_shards(p, first, then, on):
            for s in range(deep):
                if s != p and s not in [handed for handed, _ in on]:
                    shard(0, s, (p + 1) % deep).wait_recv()
            for slot, (s, to) in enumerate(first + then + on):
                shard(slot, s, to).wait_send()

        one, two = as_column(one_ref[...].astype(F32)), as_column(two_ref[...].astype(F32))
        met = (
            [(d, beside(c, k), t) for k in (1, 2, 3)]
            + [(d, c, 1 - t)]
            + [(depth(d, k), c, t) for k in range(1, deep)]
        )
        say(met)
        for b in range(4):
            cut_a[b, :, :wide] = columns(v_ref, one, b * wide, wide).astype(BF16)
            cut_a[b, :, wide : 2 * wide] = o_ref[:, b * wide : (b + 1) * wide]
            cut_a[b, :, 2 * wide :] = jnp.concatenate(
                [columns(ref, one, b * narrow, narrow) for ref in (q_ref, k_ref)], axis=1
            ).astype(BF16)
        hear(len(met))
        local(0).start()
        for k in (3, 1, 2):
            out(0, k).start()
        mine = pl.multiple_of((2 * c + t) * own, own)
        _, hat = norm_parts(x_ref[pl.ds(pl.multiple_of(t * own, own), own), :].astype(F32))
        rows_ref[pl.ds(mine, own), :] = hat[:, :part_width].astype(BF16)
        own_ref[...] = hat[:, part_width:].astype(BF16)
        local(0).wait()
        for k in (1, 2, 3):
            arrival(0, k).wait_recv()
        in_plane(first_shards)

        def early():
            for b in range(4):
                start = b * units
                cut_g[b, :, :main] = columns(g_ref, two, start, main).astype(BF16)
                cut_g[b, :, main : 2 * main] = columns(u_ref, two, start, main).astype(BF16)
                if main < units:
                    cut_g[b, :, 2 * main :] = jnp.concatenate(
                        [columns(r, two, start + main, units - main) for r in (g_ref, u_ref)],
                        axis=1,
                    ).astype(BF16)

            for n in (1, 2):
                local(n).start()
                for k in (3, 1, 2):
                    out(n, k).start()
            for b in range(4):
                for n in range(units // 128):
                    cut_d[b, n * held : (n + 1) * held, :] = columns(
                        d_ref, None, b * units + n * 128, 128
                    ).astype(BF16)
                if main < units:
                    part = columns(d_ref, None, b * units + main, units - main)
                    cut_d[b, units // 128 * held :, :] = jnp.concatenate(
                        [part[: held // 2], part[held // 2 :]], axis=1
                    ).astype(BF16)
            local(3).start()
            for k in (3, 1, 2):
                out(3, k).start()

        gather_rows(
            rows_ref, rows_out, send, receive, store, early=early,
            middle=lambda: in_plane(other_shards),
        )
        for n in (1, 2, 3):
            local(n).wait()
            for k in (1, 2, 3):
                arrival(n, k).wait_recv()
        in_plane(end_shards)
        for n in range(4):
            for k in (1, 2, 3):
                out(n, k).wait_send()

    vmem, hbm = pl.BlockSpec(memory_space=pltpu.VMEM), pl.BlockSpec(memory_space=pl.ANY)
    return call(
        kernel,
        "front",
        1,
        (x, seg[None]) + tuple(weights) + tuple(gains),
        [
            jax.ShapeDtypeStruct((tokens, part_width), BF16),
            jax.ShapeDtypeStruct((own, part_width), BF16),
            jax.ShapeDtypeStruct((4,) + seg.shape, seg.dtype),
            jax.ShapeDtypeStruct((deep, 4, held, packed), BF16),
            jax.ShapeDtypeStruct((4, held, 2 * units), BF16),
            jax.ShapeDtypeStruct(down_shape, BF16),
        ],
        [
            pltpu.VMEM((4, held, packed), BF16),
            pltpu.VMEM((4, held, 2 * units), BF16),
            pltpu.VMEM(down_shape, BF16),
        ]
        + gather_scratch(tokens, part_width) + sems(12) + sems(deep) + [pltpu.SemaphoreType.DMA((4,))],
        [vmem, hbm] + [vmem] * 9,
        [hbm, vmem, hbm, hbm, hbm, hbm],
    )


def apart(tokens):
    return (tokens // 2 - 2) // BLOCK + 2


def first_seen(i, tokens):
    return jnp.maximum(i - apart(tokens) + 1, 0)


def attend_back(
    qkv, g_mixed, mixed, denom, seg_rows, seg_cols, out_terms, middle, sum_down, heads
):
    tokens, width = out_terms.shape
    wide, narrow = heads * DV, heads * F
    blocks = tokens // BLOCK
    own = tokens // 8
    held, units = sum_down.shape[0] // 4, sum_down.shape[1]

    def kernel(
        x_ref, gm_ref, m_ref, d_ref, row_ref, col_ref, term_ref, mid_ref, down_ref,
        g_ref, out_ref, gd_ref,
        gq_ref, numer_ref, gden_ref, key_ref, gm_buf, m_buf, mid_buf, here_buf, large,
        term_buf, term_load, parts_d, p_send, p_receive, local, *rest,
    ):
        bufs, (s_send, s_receive, t_send, t_receive) = rest[:6], rest[6:]
        d, c, t = place_of()
        hand_on, landed = exchange(((down_ref, parts_d),), held, p_send, p_receive, local)
        mine = pl.ds(pl.multiple_of(t * own, own), own)
        loads = (
            pltpu.make_async_copy(gm_ref, gm_buf, large.at[0]),
            pltpu.make_async_copy(m_ref, m_buf, large.at[1]),
            pltpu.make_async_copy(mid_ref, mid_buf, large.at[2]),
        )
        stored = pltpu.make_async_copy(here_buf, out_ref.at[mine], large.at[3])

        def fetch_terms(i):
            part = pl.ds(pl.multiple_of(2 * scatter_order(i) * own, 2 * own), 2 * own)
            slot = lax.rem(i, 2)
            return pltpu.make_async_copy(term_ref.at[part], term_buf.at[slot], term_load.at[slot])

        fetch_terms(0).start()

        for copy in loads:
            copy.start()
        met = around() + [(d, beside(c, 3), t)]
        say(met)

        def prepare():
            loads[0].wait()
            loads[1].wait()
            gq_ref[...] = jnp.zeros_like(gq_ref)
            for h in range(heads):
                part = pl.ds(h * DV, DV)
                gm = gm_buf[:, part].astype(F32)
                inverse = 1.0 / d_ref[:, h : h + 1]
                numer_ref[:, part] = (gm * inverse).astype(BF16)
                down = -jnp.sum(gm * m_buf[:, part], axis=1, keepdims=True) * inverse
                gden_ref[h : h + 1, :] = jnp.transpose(
                    jnp.broadcast_to(down, (tokens, 128)), (1, 0)
                )[:1]
            key_ref[...] = jnp.transpose(
                x_ref[:, wide : wide + 2 * narrow].astype(F32), (1, 0)
            ).astype(BF16)

        place = lax.broadcasted_iota(jnp.int32, (BLOCK, BLOCK), 1) - lax.broadcasted_iota(
            jnp.int32, (BLOCK, BLOCK), 0
        )
        tempered = BF16(F**-0.5)

        def one_block(j):
            start = pl.multiple_of(j * BLOCK, BLOCK)
            ids = row_ref[pl.ds(start, BLOCK), :]
            values = [x_ref[pl.ds(start, BLOCK), h * DV : (h + 1) * DV] for h in range(heads)]
            keys = [
                x_ref[pl.ds(start, BLOCK), wide + (heads + h) * F : wide + (heads + h + 1) * F]
                * tempered
                for h in range(heads)
            ]
            across = [
                key_ref[(heads + h) * F : (heads + h + 1) * F, pl.ds(start, BLOCK)] * tempered
                for h in range(heads)
            ]

            def step(i, sums):
                base = pl.multiple_of(i * BLOCK, BLOCK)
                visible = (place >= start - base) & (ids == col_ref[:, pl.ds(base, BLOCK)])
                out = []
                for h in range(heads):
                    queries = x_ref[pl.ds(base, BLOCK), wide + h * F : wide + (h + 1) * F]
                    numer = numer_ref[pl.ds(base, BLOCK), h * DV : (h + 1) * DV]
                    s = dot(keys[h], queries, 1, 1)
                    a = jnp.where(visible, (0.5 * s + 1.0) * s + 1.0, 0.0).astype(BF16)
                    ga = dot(values[h], numer, 1, 1) + gden_ref[h : h + 1, pl.ds(base, BLOCK)]
                    gs = jnp.where(visible, ga * (1.0 + s), 0.0).astype(BF16)
                    gq_ref[h * F : (h + 1) * F, pl.ds(base, BLOCK)] += dot(across[h], gs, 1, 0)
                    out += [sums[2 * h] + dot(a, numer, 1, 0), sums[2 * h + 1] + dot(gs, queries, 1, 0)]
                return tuple(out)

            zeros = []
            for h in range(heads):
                zeros += [jnp.zeros((BLOCK, DV), F32), jnp.zeros((BLOCK, F), F32)]
            sums = lax.fori_loop(
                j, jnp.minimum(j + apart(tokens), blocks), step, tuple(zeros)
            )
            for h in range(heads):
                g_ref[pl.ds(start, BLOCK), h * DV : (h + 1) * DV] = sums[2 * h].astype(BF16)
                g_ref[
                    pl.ds(start, BLOCK), wide + (heads + h) * F : wide + (heads + h + 1) * F
                ] = (sums[2 * h + 1] * F**-0.5).astype(BF16)

        def terms(i, start):
            fetch_terms(i).wait()

            @pl.when(i < 3)
            def _():
                fetch_terms(i + 1).start()

            return term_buf.at[lax.rem(i, 2)]

        def fill(n):
            if n == 0:
                prepare()
                pl.loop(0, 1)(one_block)
            else:
                pl.loop(1, blocks - 1)(one_block)
                hand_on(0)
                one_block(blocks - 1)

        moved = scatter_rows(terms, bufs, s_send, s_receive, lambda: hear(len(met)), fill)
        loads[2].wait()
        here_buf[...] = (mid_buf[...] + moved).astype(BF16)
        copy = remote(here_buf, out_ref.at[mine], t_send, t_receive, 0, (d, c, 1 - t))
        copy.start()
        stored.start()
        g_ref[:, wide : wide + narrow] = jnp.transpose(gq_ref[...], (1, 0)).astype(BF16)
        landed(0)
        for b in range(4):
            gd_ref[:, b * units : (b + 1) * units] = parts_d[b].astype(F32)
        copy.wait_send()
        there = out_ref.at[pl.ds(pl.multiple_of((1 - t) * own, own), own)]
        remote(there, there, t_send, t_receive, 0, (d, c, 1 - t)).wait_recv()
        stored.wait()

    vmem, hbm = pl.BlockSpec(memory_space=pltpu.VMEM), pl.BlockSpec(memory_space=pl.ANY)
    return call(
        kernel, "attend_back", 7,
        (qkv, g_mixed, mixed, denom, seg_rows, seg_cols, out_terms, middle, sum_down),
        [
            jax.ShapeDtypeStruct(qkv.shape, BF16),
            jax.ShapeDtypeStruct((2 * own, width), BF16),
            jax.ShapeDtypeStruct((held, 4 * units), F32),
        ],
        [
            pltpu.VMEM((narrow, tokens), F32),
            pltpu.VMEM((tokens, wide), BF16),
            pltpu.VMEM((8, tokens), F32),
            pltpu.VMEM((2 * narrow, tokens), BF16),
            pltpu.VMEM(g_mixed.shape, BF16),
            pltpu.VMEM(mixed.shape, F32),
            pltpu.VMEM(middle.shape, F32),
            pltpu.VMEM((own, width), BF16),
            pltpu.SemaphoreType.DMA((4,)),
            pltpu.VMEM((2, 2 * own, width), BF16),
            pltpu.SemaphoreType.DMA((2,)),
            pltpu.VMEM((4, held, units), BF16),
        ]
        + sems(3) + [pltpu.SemaphoreType.DMA((1,))]
        + scatter_scratch(own, width) + sems(SCATTER_COPIES) + sems(1),
        [vmem, hbm, hbm, vmem, vmem, vmem, hbm, hbm, hbm],
        [vmem, hbm, vmem],
    )


def attend_block(i, x_ref, ext_ref, row_ref, col_ref, mixed_ref, denom_ref, low_ref, heads):
    wide = heads * DV
    base = pl.multiple_of(i * BLOCK, BLOCK)
    own = row_ref[pl.ds(base, BLOCK), :]
    place = lax.broadcasted_iota(jnp.int32, (BLOCK, BLOCK), 0) - lax.broadcasted_iota(
        jnp.int32, (BLOCK, BLOCK), 1
    )
    queries = [
        x_ref[pl.ds(base, BLOCK), wide + h * F : wide + (h + 1) * F] * jnp.bfloat16(F**-0.5)
        for h in range(heads)
    ]

    def step(j, sums):
        start = pl.multiple_of(j * BLOCK, BLOCK)
        visible = (place >= start - base) & (own == col_ref[:, pl.ds(start, BLOCK)])
        out = []
        for h in range(heads):
            keys = x_ref[
                pl.ds(start, BLOCK), wide + (heads + h) * F : wide + (heads + h + 1) * F
            ]
            s = dot(queries[h], keys, 1, 1)
            a = jnp.where(visible, (0.5 * s + 1.0) * s + 1.0, 0.0).astype(BF16)
            out.append(
                sums[h] + dot(a, ext_ref[pl.ds(start, BLOCK), 2 * h * DV : (2 * h + 2) * DV], 1, 0)
            )
        return tuple(out)

    sums = lax.fori_loop(
        first_seen(i, x_ref.shape[0]),
        i + 1,
        step,
        tuple(jnp.zeros((BLOCK, 2 * DV), F32) for _ in range(heads)),
    )
    for h in range(heads):
        denom = sums[h][:, DV:]
        mixed = sums[h][:, :DV] / denom
        mixed_ref[pl.ds(base, BLOCK), h * DV : (h + 1) * DV] = mixed
        low_ref[pl.ds(base, BLOCK), h * DV : (h + 1) * DV] = mixed.astype(BF16)
        denom_ref[pl.ds(base, BLOCK), h : h + 1] = denom[:, :1]


def attend(rows_low, own_high, w_attn, seg_rows, seg_cols, cot, heads):
    tokens, part_width = rows_low.shape
    own = tokens // 8
    wide, narrow = heads * DV, heads * F

    def kernel(
        x_ref, own_ref, w_ref, row_ref, col_ref, cot_ref,
        qkv_ref, mixed_ref, denom_ref, low_ref, cot_out, rows_out,
        ext_ref, half_ref, here, x_buf, *rest,
    ):
        rows_ref, r_send, r_receive, r_store, cot_buf, c_send, c_receive, c_store = rest
        d, c, t = place_of()
        loaded = pltpu.make_async_copy(x_ref, x_buf, here.at[0])
        loaded.start()
        low_half = pltpu.make_async_copy(x_buf, rows_out.at[:, :part_width], here.at[1])

        met = around()
        say(met)
        mine = pl.ds(pl.multiple_of((2 * c + t) * own, own), own)
        rows_ref[mine, :] = own_ref[...]
        cot_buf[mine, :] = cot_ref[pl.ds(pl.multiple_of(t * own, own), own), :part_width]
        hear(len(met))

        def first_half():
            loaded.wait()

            @pl.loop(0, tokens // BLOCK)
            def _(n):
                rows = pl.ds(pl.multiple_of(n * BLOCK, BLOCK), BLOCK)
                half_ref[rows, :wide] = dot(x_buf[rows, :], w_ref[:part_width, :wide], 1, 0)
                half_ref[rows, wide:] = dot(x_buf[rows, :], w_ref[:part_width, 2 * wide :], 1, 0)

            low_half.start()

        def second_half(start):
            rows = pl.ds(start, own)
            values = (
                half_ref[rows, :wide] + dot(rows_ref[rows, :], w_ref[part_width:, :wide], 1, 0)
            ).astype(BF16)
            qkv_ref[rows, :wide] = values
            qkv_ref[rows, wide:] = (
                half_ref[rows, wide:] + dot(rows_ref[rows, :], w_ref[part_width:, 2 * wide :], 1, 0)
            ).astype(BF16)
            for h in range(heads):
                ext_ref[rows, 2 * h * DV : (2 * h + 1) * DV] = values[:, h * DV : (h + 1) * DV]
                ext_ref[rows, (2 * h + 1) * DV : (2 * h + 2) * DV] = jnp.ones((own, DV), BF16)

        begun = []

        def cot_begin():
            begun.extend(gather_begin(cot_buf, c_send, c_receive))

        gather_rows(
            rows_ref, rows_out.at[:, part_width:], r_send, r_receive, r_store, second_half, first_half,
            late=cot_begin,
        )

        def blocks(first, last):
            @pl.loop(first, last)
            def _(i):
                attend_block(
                    i, qkv_ref, ext_ref, row_ref, col_ref, mixed_ref, denom_ref, low_ref, heads
                )

        gather_rows(
            cot_buf, cot_out, c_send, c_receive, c_store, begun=begun,
            early=lambda: blocks(0, tokens // BLOCK // 2),
            middle=lambda: blocks(tokens // BLOCK // 2, tokens // BLOCK - 1),
            late=lambda: blocks(tokens // BLOCK - 1, tokens // BLOCK),
        )
        low_half.wait()

    vmem, hbm = pl.BlockSpec(memory_space=pltpu.VMEM), pl.BlockSpec(memory_space=pl.ANY)
    return call(
        kernel, "attend", 2, (rows_low, own_high, w_attn, seg_rows, seg_cols, cot),
        [
            jax.ShapeDtypeStruct((tokens, wide + 2 * narrow), BF16),
            jax.ShapeDtypeStruct((tokens, wide), F32),
            jax.ShapeDtypeStruct((tokens, heads), F32),
            jax.ShapeDtypeStruct((tokens, wide), BF16),
            jax.ShapeDtypeStruct((tokens, part_width), BF16),
            jax.ShapeDtypeStruct((tokens, 2 * part_width), BF16),
        ],
        [
            pltpu.VMEM((tokens, 2 * wide), BF16),
            pltpu.VMEM((tokens, wide + 2 * narrow), F32),
            pltpu.SemaphoreType.DMA((2,)),
            pltpu.VMEM((tokens, part_width), BF16),
        ]
        + gather_scratch(tokens, part_width) + gather_scratch(tokens, part_width),
        [hbm] + [vmem] * 5,
        [vmem] * 4 + [hbm] * 2,
    )


def to_middle(heads_out, w_attn, x):
    tokens, width = heads_out.shape[0], x.shape[1]
    own = tokens // 8
    wide = heads_out.shape[1]

    def kernel(h_ref, w_ref, x_ref, mid_ref, rows_out, w_buf, x_buf, mid_buf, large, *rest):
        bufs, (s_send, s_receive, rows_ref, g_send, g_receive, store) = rest[:6], rest[6:]
        d, c, t = place_of()
        mine = pl.ds(pl.multiple_of(t * own, own), own)
        weights = pltpu.make_async_copy(w_ref.at[:, wide : 2 * wide], w_buf, large.at[0])
        loaded = pltpu.make_async_copy(x_ref.at[mine], x_buf, large.at[1])
        stored = pltpu.make_async_copy(mid_buf, mid_ref, large.at[2])
        weights.start()
        loaded.start()
        say(around())
        weights.wait()

        def terms(i, start):
            return [(h_ref[pl.ds(start, 2 * own), :], w_buf, slice(None))]

        total = scatter_rows(terms, bufs, s_send, s_receive, lambda: hear(3))
        loaded.wait()
        middle = total + x_buf[...].astype(F32)
        mid_buf[...] = middle
        stored.start()
        _, hat = norm_parts(middle)
        rows_ref[pl.ds(pl.multiple_of((2 * c + t) * own, own), own), :] = hat.astype(BF16)
        gather_rows(rows_ref, rows_out, g_send, g_receive, store)
        stored.wait()

    vmem, hbm = pl.BlockSpec(memory_space=pltpu.VMEM), pl.BlockSpec(memory_space=pl.ANY)
    return call(
        kernel, "to_middle", 3, (heads_out, w_attn, x),
        [jax.ShapeDtypeStruct((own, width), F32), jax.ShapeDtypeStruct((tokens, width), BF16)],
        [
            pltpu.VMEM((width, wide), BF16),
            pltpu.VMEM((own, width), BF16),
            pltpu.VMEM((own, width), F32),
            pltpu.SemaphoreType.DMA((3,)),
        ]
        + scatter_scratch(own, width) + sems(SCATTER_COPIES) + gather_scratch(tokens, width),
        [vmem, hbm, hbm],
        [hbm, hbm],
        flops=2 * tokens * width * heads_out.shape[1],
    )


def gate_up(rows_two, w_both, cot, cot_low):
    tokens, width = rows_two.shape
    own = tokens // 8
    units = w_both.shape[1] // 2
    main = units // 128 * 128
    count = tokens // BLOCK
    tile = 256

    def kernel(
        x_ref, w_ref, cot_ref, low_ref, hid_out, slope_out, silu_out, rows_out, down_out,
        x_buf, w_buf, low_buf, hid_ref, slope_ref, silu_ref, down_buf, load, store, down_store,
        rows_ref, send, receive, row_store,
    ):
        d, c, t = place_of()

        def fetch(i):
            rows = pl.ds(pl.multiple_of(i * BLOCK, BLOCK), BLOCK)
            slot = lax.rem(i, 2)
            return pltpu.make_async_copy(x_ref.at[rows], x_buf.at[slot], load.at[slot])

        def given(i):
            rows = pl.ds(pl.multiple_of(i * BLOCK, BLOCK), BLOCK)
            slot = lax.rem(i, 2)
            return [
                pltpu.make_async_copy(source, target.at[rows], store.at[n, slot])
                for n, (source, target) in enumerate(
                    (
                        (hid_ref.at[rows], hid_out),
                        (slope_ref.at[slot], slope_out),
                        (silu_ref.at[slot], silu_out),
                    )
                )
            ]

        weights = pltpu.make_async_copy(w_ref, w_buf, load.at[2])
        weights.start()
        fetch(0).start()
        low_copy = pltpu.make_async_copy(low_ref, low_buf, load.at[3])
        low_copy.start()
        greet(around())
        mine = pl.multiple_of((2 * c + t) * own, own)
        rows_ref[pl.ds(mine, own), :] = cot_ref[
            pl.ds(pl.multiple_of(t * own, own), own), width // 2 :
        ]

        def blocks(first, last):
            @pl.loop(first, last)
            def _(i):
                slot = lax.rem(i, 2)

                @pl.when(i + 1 < count)
                def _():
                    fetch(i + 1).start()

                fetch(i).wait()
                both = dot(x_buf[slot], w_buf[...], 1, 0)

                @pl.when(i >= 2)
                def _():
                    for copy in given(i - 2):
                        copy.wait()

                def act(gate, up, part):
                    sig = jax.nn.sigmoid(gate)
                    silu = gate * sig
                    hid_ref[pl.ds(pl.multiple_of(i * BLOCK, BLOCK), BLOCK), part] = (
                        silu * up
                    ).astype(BF16)
                    slope_ref[slot, :, part] = (up * sig * (1.0 + gate * (1.0 - sig))).astype(BF16)
                    silu_ref[slot, :, part] = silu.astype(BF16)

                act(both[:, :main], both[:, main : 2 * main], slice(0, main))
                if main < units:
                    act(
                        both[:, 2 * main : main + units],
                        both[:, main + units :],
                        slice(main, units),
                    )
                for copy in given(i):
                    copy.start()

        per = width // 2 // tile

        def down_given(base, n):
            slot = lax.rem(n, 2)
            rows = pl.ds(pl.multiple_of(base + n * tile, tile), tile)
            return pltpu.make_async_copy(down_buf.at[slot], down_out.at[rows], down_store.at[slot])

        def down_tiles(source, base, end):
            @pl.loop(0, end)
            def _(n):
                @pl.when(n >= 2)
                def _():
                    down_given(base, n - 2).wait()

                part = pl.ds(pl.multiple_of(n * tile, tile), tile)
                down_buf[lax.rem(n, 2)] = dot(source[:, part], hid_ref[...], 0, 0).astype(BF16)
                down_given(base, n).start()

        def early():
            weights.wait()
            blocks(0, 1)

        def later():
            blocks(count // 2, count)
            low_copy.wait()
            down_tiles(low_buf, 0, per)
            for n in (per - 2, per - 1):
                down_given(0, n).wait()

        gather_rows(
            rows_ref, rows_out, send, receive, row_store, early=early,
            middle=lambda: blocks(1, count // 2), late=later,
        )
        down_tiles(rows_ref, width // 2, per)
        for n in (per - 2, per - 1):
            down_given(width // 2, n).wait()
        for i in (count - 2, count - 1):
            for copy in given(i):
                copy.wait()

    vmem, hbm = pl.BlockSpec(memory_space=pltpu.VMEM), pl.BlockSpec(memory_space=pl.ANY)
    return call(
        kernel, "gate_up", 8, (rows_two, w_both, cot, cot_low),
        [jax.ShapeDtypeStruct((tokens, units), BF16)] * 3
        + [
            jax.ShapeDtypeStruct((tokens, width // 2), BF16),
            jax.ShapeDtypeStruct((width, units), BF16),
        ],
        [
            pltpu.VMEM((2, BLOCK, width), BF16),
            pltpu.VMEM(w_both.shape, BF16),
            pltpu.VMEM(cot_low.shape, BF16),
            pltpu.VMEM((tokens, units), BF16),
            pltpu.VMEM((2, BLOCK, units), BF16),
            pltpu.VMEM((2, BLOCK, units), BF16),
            pltpu.VMEM((2, tile, units), BF16),
            pltpu.SemaphoreType.DMA((4,)),
            pltpu.SemaphoreType.DMA((3, 2)),
            pltpu.SemaphoreType.DMA((2,)),
        ]
        + gather_scratch(tokens, width // 2),
        [hbm, hbm, vmem, hbm],
        [hbm] * 5,
        flops=4 * tokens * width * units,
    )


def feed_forward(slope, silu, cot_low, cot_high, w_down, rows_two):
    tokens, width = rows_two.shape
    units = slope.shape[1]
    main = units // 128 * 128
    tile = 256
    part_width = width // 2
    count = tokens // BLOCK

    def kernel(
        slope_ref, silu_ref, low_ref, high_ref, d_ref, two_ref, g_out, grad_ref,
        slope_buf, silu_buf, low_buf, high_buf, d_buf, rest_buf, d_load, g_ref, here, g_store, cols,
        out, load, store,
    ):
        def rows(i):
            return pl.ds(pl.multiple_of(i * BLOCK, BLOCK), BLOCK)

        def fetch(i):
            slot = lax.rem(i, 2)
            return [
                pltpu.make_async_copy(source.at[rows(i)], target.at[slot], here.at[n, slot])
                for n, (source, target) in enumerate(
                    (
                        (low_ref, low_buf),
                        (high_ref, high_buf),
                        (slope_ref, slope_buf),
                        (silu_ref, silu_buf),
                    )
                )
            ]

        def g_given(i):
            return pltpu.make_async_copy(g_ref.at[rows(i)], g_out.at[rows(i)], g_store.at[i])

        def wanted(n):
            part = pl.ds(pl.multiple_of(n * tile, tile), tile)
            slot = lax.rem(n, 2)
            return pltpu.make_async_copy(two_ref.at[:, part], cols.at[slot], load.at[slot])

        def given(n):
            part = pl.ds(pl.multiple_of(n * tile, tile), tile)
            slot = lax.rem(n, 2)
            return pltpu.make_async_copy(out.at[slot], grad_ref.at[part], store.at[slot])

        weights_there = load_down(d_ref, d_buf, rest_buf, d_load, units)
        for copy in fetch(0):
            copy.start()
        wanted(0).start()
        weights_there()

        @pl.loop(0, count)
        def _(i):
            slot = lax.rem(i, 2)

            @pl.when(i + 1 < count)
            def _():
                for copy in fetch(i + 1):
                    copy.start()

            for copy in fetch(i):
                copy.wait()
            g_hidden = dot(low_buf[slot], down_rows(d_buf, 0, part_width, units), 1, 0) + dot(
                high_buf[slot], down_rows(d_buf, part_width, width, units), 1, 0
            )
            gg = g_hidden * slope_buf[slot].astype(F32)
            gu = g_hidden * silu_buf[slot].astype(F32)
            part = rows(i)
            g_ref[part, :main] = gg[:, :main].astype(BF16)
            g_ref[part, main : 2 * main] = gu[:, :main].astype(BF16)
            if main < units:
                g_ref[part, 2 * main :] = jnp.concatenate(
                    [gg[:, main:], gu[:, main:]], axis=1
                ).astype(BF16)
            g_given(i).start()

        last = width // tile

        @pl.loop(0, last)
        def _(n):
            @pl.when(n + 1 < last)
            def _():
                wanted(n + 1).start()

            wanted(n).wait()

            @pl.when(n >= 2)
            def _():
                given(n - 2).wait()

            slot = lax.rem(n, 2)
            out[slot] = dot(cols[slot], g_ref[...], 0, 0).astype(BF16)
            given(n).start()

        given(last - 2).wait()
        given(last - 1).wait()
        for i in range(count):
            g_given(i).wait()

    hbm = pl.BlockSpec(memory_space=pl.ANY)
    moved = 2 * tokens * (2 * width + 4 * units) + 6 * width * units
    return pl.pallas_call(
        kernel,
        in_specs=[hbm] * 6,
        out_specs=[hbm] * 2,
        out_shape=[
            jax.ShapeDtypeStruct((tokens, 2 * units), BF16),
            jax.ShapeDtypeStruct((width, 2 * units), BF16),
        ],
        scratch_shapes=[
            pltpu.VMEM((2, BLOCK, units), BF16),
            pltpu.VMEM((2, BLOCK, units), BF16),
            pltpu.VMEM((2, BLOCK, part_width), BF16),
            pltpu.VMEM((2, BLOCK, part_width), BF16),
            *down_scratch(w_down, units),
            pltpu.VMEM((tokens, 2 * units), BF16),
            pltpu.SemaphoreType.DMA((4, 2)),
            pltpu.SemaphoreType.DMA((count,)),
            pltpu.VMEM((2, tokens, tile), BF16),
            pltpu.VMEM((2, tile, 2 * units), BF16),
            pltpu.SemaphoreType.DMA((3,)),
            pltpu.SemaphoreType.DMA((2,)),
        ],
        compiler_params=pltpu.CompilerParams(vmem_limit_bytes=VMEM_MOST),
        cost_estimate=pl.CostEstimate(
            flops=6 * tokens * width * units, bytes_accessed=moved, transcendentals=0
        ),
        name="feed_forward",
    )(slope, silu, cot_low, cot_high, w_down, rows_two)


def to_branch(g_both, w_both, middle, cot, w_attn, wide, hidden, w_down):
    tokens, width = g_both.shape[0], middle.shape[1]
    own = tokens // 8
    units = hidden.shape[1]
    tile = width // 2

    def kernel(
        g_ref, w_ref, mid_ref, cot_ref, o_ref, hid_ref, d_ref, gm_ref, rows_out, mix_ref, term_ref,
        g_buf, w_buf, hid_buf, d_buf, rest_buf, d_load, term_buf, load, term_store,
        mid_buf, cot_buf, o_buf, gm_buf, large, *rest,
    ):
        bufs, (s_send, s_receive, rows_ref, g_send, g_receive, store) = rest[:6], rest[6:]
        d, c, t = place_of()
        mine = pl.ds(pl.multiple_of(t * own, own), own)
        loads = (
            pltpu.make_async_copy(mid_ref, mid_buf, large.at[0]),
            pltpu.make_async_copy(cot_ref.at[mine], cot_buf, large.at[1]),
            pltpu.make_async_copy(o_ref.at[:, wide : 2 * wide], o_buf, large.at[2]),
        )
        stored = pltpu.make_async_copy(gm_buf, gm_ref, large.at[3])

        def fetch(i):
            part = pl.ds(pl.multiple_of(2 * scatter_order(i) * own, 2 * own), 2 * own)
            slot = lax.rem(i, 2)
            return pltpu.make_async_copy(g_ref.at[part], g_buf.at[slot], load.at[slot])

        weights = pltpu.make_async_copy(w_ref, w_buf, load.at[2])
        weights.start()
        fetch(0).start()
        say(around())
        weights.wait()
        down_there = load_down(d_ref, d_buf, rest_buf, d_load, units)
        for copy in loads:
            copy.start()
        pltpu.make_async_copy(
            hid_ref.at[pl.ds(0, BLOCK)], hid_buf, load.at[4]
        ).start()

        def terms(i, start):
            fetch(i).wait()

            @pl.when(i < 3)
            def _():
                fetch(i + 1).start()

            return [(g_buf[lax.rem(i, 2)], w_buf, slice(None))]

        total = scatter_rows(terms, bufs, s_send, s_receive, lambda: hear(3))
        for copy in loads:
            copy.wait()
        scale, hat = norm_parts(mid_buf[...])
        g_middle = cot_buf[...].astype(F32) + norm_back(total, hat, scale)
        gm_buf[...] = g_middle
        stored.start()
        rows_ref[pl.ds(pl.multiple_of((2 * c + t) * own, own), own), :] = g_middle.astype(BF16)

        def mix(start):
            mix_ref[pl.ds(start, own), :] = dot(
                rows_ref[pl.ds(start, own), :], o_buf[...], 1, 0
            ).astype(BF16)

        def block(i):
            return pl.ds(pl.multiple_of(i * BLOCK, BLOCK), BLOCK)

        def hidden_of(i):
            return pltpu.make_async_copy(hid_ref.at[block(i)], hid_buf, load.at[4])

        def term_given(i):
            return pltpu.make_async_copy(term_buf, term_ref.at[block(i)], term_store.at[0])

        def out_terms(first, last):
            @pl.loop(first, last)
            def _(i):
                hidden_of(i).wait()

                @pl.when(i > 0)
                def _():
                    term_given(i - 1).wait()

                for n in (0, 1):
                    columns = slice(n * tile, (n + 1) * tile)
                    matrix = down_rows(d_buf, n * tile, (n + 1) * tile, units)
                    term_buf[:, columns] = dot(hid_buf[...], matrix, 1, 1).astype(BF16)
                term_given(i).start()

                @pl.when(i + 1 < tokens // BLOCK)
                def _():
                    hidden_of(i + 1).start()

        down_there()
        blocks = tokens // BLOCK
        gather_rows(
            rows_ref, rows_out, g_send, g_receive, store, mix,
            lambda: out_terms(0, blocks // 2),
            lambda: out_terms(blocks // 2, blocks - 1),
            lambda: out_terms(blocks - 1, blocks),
        )
        term_given(blocks - 1).wait()
        stored.wait()

    vmem, hbm = pl.BlockSpec(memory_space=pltpu.VMEM), pl.BlockSpec(memory_space=pl.ANY)
    return call(
        kernel, "to_branch", 5, (g_both, w_both, middle, cot, w_attn, hidden, w_down),
        [
            jax.ShapeDtypeStruct((own, width), F32),
            jax.ShapeDtypeStruct((tokens, width), BF16),
            jax.ShapeDtypeStruct((tokens, wide), BF16),
            jax.ShapeDtypeStruct((tokens, width), BF16),
        ],
        [
            pltpu.VMEM((2, 2 * own, g_both.shape[1]), BF16),
            pltpu.VMEM(w_both.shape, BF16),
            pltpu.VMEM((BLOCK, units), BF16),
            *down_scratch(w_down, units),
            pltpu.VMEM((BLOCK, width), BF16),
            pltpu.SemaphoreType.DMA((5,)),
            pltpu.SemaphoreType.DMA((1,)),
            pltpu.VMEM((own, width), F32),
            pltpu.VMEM((own, width), BF16),
            pltpu.VMEM((width, wide), BF16),
            pltpu.VMEM((own, width), F32),
            pltpu.SemaphoreType.DMA((4,)),
        ]
        + scatter_scratch(own, width) + sems(SCATTER_COPIES) + gather_scratch(tokens, width),
        [hbm] * 7,
        [hbm, hbm, vmem, hbm],
        flops=4 * tokens * width * (g_both.shape[1] // 2 + wide),
    )


def as_row(column):
    return jnp.transpose(jnp.broadcast_to(column, (column.shape[0], 128)), (1, 0))[:8]


def to_input(
    g_qkv, w_attn, x, g_middle, rows_one, branch, heads_out, sum_both, weights, gains, heads
):
    tokens, width = g_qkv.shape[0], x.shape[1]
    own = tokens // 8
    deep = lax.axis_size("dp")
    across = g_qkv.shape[1]
    group = width // deep
    held = group // 4
    wide, narrow = heads * DV, heads * F
    both = sum_both.shape[1]
    units = both // 2
    main = units // 128 * 128

    def kernel(
        g_ref, w_ref, x_ref, gm_ref, one_ref, br_ref, h_ref, both_ref,
        wq_ref, wk_ref, wv_ref, wg_ref, wu_ref, gain_ref, gain_two_ref,
        out_ref, gq_ref, gk_ref, gv_ref, go_ref, gg_ref, gu_ref, row_ref, row_two_ref,
        *rest,
    ):
        bufs, (s_send, s_receive, t_send, t_receive) = rest[:6], rest[6:10]
        (
            came_deep, came_out, sums, sums_out, parts_a, parts_o, parts_b, scalar, back_ref, back_out,
            cols, load, d_send, d_receive, p_send, p_receive, local, x_buf, gm_buf, in_buf, gate_buf,
            up_buf, large,
        ) = rest[10:]
        d, c, t = place_of()
        hand_on, landed = exchange(
            ((sums, parts_a), (both_ref, parts_b), (sums_out, parts_o)), held, p_send, p_receive, local
        )

        def fetch(j):
            part = pl.ds(pl.multiple_of(depth(d, j % deep + 1) * group, group), group)
            source = br_ref if j < deep else one_ref
            return pltpu.make_async_copy(source.at[:, part], cols.at[j % 2], load.at[j % 2])

        def deeper(j):
            n = j % deep
            source, target = (back_out, came_out) if j < deep else (back_ref, came_deep)
            return remote(
                source.at[n], target.at[n], d_send, d_receive, j, (depth(d, n + 1), c, t)
            )

        def plane(j):
            n = j % deep
            if j + 1 < 2 * deep:
                fetch(j + 1).start()
            fetch(j).wait()
            if j < deep:
                back_out[n] = dot(cols[j % 2], h_ref[...], 0, 0).astype(BF16)
            else:
                back_ref[n] = dot(cols[j % 2], g_ref[...], 0, 0).astype(BF16)

        def sum_of(back, came, first):
            total = back[deep - 1].astype(F32)
            for n in range(deep - 1):
                deeper(first + n).wait_recv()
                total = total + came[n].astype(F32)
            return total.astype(BF16)

        fetch(0).start()
        mine = pl.ds(pl.multiple_of(t * own, own), own)
        loads = (
            pltpu.make_async_copy(x_ref.at[mine], x_buf, large.at[0]),
            pltpu.make_async_copy(gm_ref, gm_buf, large.at[1]),
        )
        stored = pltpu.make_async_copy(in_buf, out_ref.at[mine], large.at[2])
        wide_stores = (
            pltpu.make_async_copy(gate_buf, gg_ref, large.at[3]),
            pltpu.make_async_copy(up_buf, gu_ref, large.at[4]),
        )
        for copy in loads:
            copy.start()
        met = (
            around()
            + [(d, beside(c, 3), t)]
            + [(depth(d, k), c, t) for k in range(1, deep)]
        )
        say(met)

        early = deep // 2
        for j in range(early):
            plane(j)

        def enter():
            hear(len(met))
            hand_on(1)
            for j in range(early):
                deeper(j).start()

        def terms(i, start):
            part = pl.ds(start, 2 * own)
            return [
                (g_ref[part, :wide], w_ref, slice(0, wide)),
                (g_ref[part, wide:], w_ref, slice(2 * wide, None)),
            ]

        def fill(n):
            if n == 0:
                for j in range(early, 2 * deep):
                    plane(j)
                    if j % deep != deep - 1:
                        deeper(j).start()
                return
            landed(1)
            whole = [parts_b[b].astype(F32) for b in range(4)]
            term = jnp.zeros((held, 1), F32)
            for ref, weight, first, rest_of in (
                (gate_buf, wg_ref, 0, 2 * main),
                (up_buf, wu_ref, main, main + units),
            ):
                pieces = []
                for b in range(4):
                    pieces.append(whole[b][:, first : first + main])
                    if main < units:
                        pieces.append(whole[b][:, rest_of : rest_of + units - main])
                s = jnp.concatenate(pieces, axis=1)
                term = term + jnp.sum(s * weight[...].astype(F32), axis=1, keepdims=True)
                ref[...] = s * as_column(gain_two_ref[...].astype(F32))
            for copy in wide_stores:
                copy.start()
            scalar[0, 1] = as_row(term)

        e_one = scatter_rows(terms, bufs, s_send, s_receive, enter, fill)
        for copy in loads:
            copy.wait()
        scale, hat = norm_parts(x_buf[...].astype(F32))
        in_buf[...] = gm_buf[...] + norm_back(e_one, hat, scale)
        copy = remote(in_buf, out_ref.at[mine], t_send, t_receive, 0, (d, c, 1 - t))
        copy.start()
        stored.start()
        sums_out[...] = sum_of(back_out, came_out, 0)
        hand_on(2)
        sums[...] = sum_of(back_ref, came_deep, deep)
        hand_on(0)
        landed(2)
        for b in range(4):
            go_ref[:, b * wide : (b + 1) * wide] = parts_o[b].astype(F32)
        landed(0)

        gain_one = as_column(gain_ref[...].astype(F32))
        term_one = jnp.zeros((held, 1), F32)
        for ref, weight, start, count in (
            (gv_ref, wv_ref, 0, wide),
            (gq_ref, wq_ref, wide, narrow),
            (gk_ref, wk_ref, wide + narrow, narrow),
        ):
            s = jnp.concatenate(
                [parts_a[b][:, start : start + count].astype(F32) for b in range(4)], axis=1
            )
            term_one = term_one + jnp.sum(s * weight[...].astype(F32), axis=1, keepdims=True)
            ref[...] = s * gain_one
        scalar[0, 0] = as_row(term_one)
        swap = remote(scalar.at[0], scalar.at[1], t_send, t_receive, 1, (d, c, 1 - t))
        swap.start()
        swap.wait()
        row_ref[...] = (scalar[0, 0] + scalar[1, 0])[:1]
        row_two_ref[...] = (scalar[0, 1] + scalar[1, 1])[:1]
        copy.wait_send()
        there = out_ref.at[pl.ds(pl.multiple_of((1 - t) * own, own), own)]
        remote(there, there, t_send, t_receive, 0, (d, c, 1 - t)).wait_recv()
        for n in range(deep - 1):
            deeper(n).wait_send()
            deeper(deep + n).wait_send()
        stored.wait()
        for copy in wide_stores:
            copy.wait()

    w_q, w_k, w_v, w_gate, w_up = weights
    vmem, hbm = pl.BlockSpec(memory_space=pltpu.VMEM), pl.BlockSpec(memory_space=pl.ANY)
    return call(
        kernel, "to_input", 6,
        (g_qkv, w_attn, x, g_middle, rows_one, branch, heads_out, sum_both) + tuple(weights)
        + tuple(gains),
        [jax.ShapeDtypeStruct((2 * own, width), F32)]
        + [jax.ShapeDtypeStruct(w.shape, F32) for w in (w_q, w_k, w_v, w_v, w_gate, w_up)]
        + [jax.ShapeDtypeStruct((1, held), F32)] * 2,
        scatter_scratch(own, width) + sems(SCATTER_COPIES) + sems(2)
        + [
            pltpu.VMEM((deep - 1, group, across), BF16),
            pltpu.VMEM((deep - 1, group, wide), BF16),
            pltpu.VMEM((group, across), BF16),
            pltpu.VMEM((group, wide), BF16),
            pltpu.VMEM((4, held, across), BF16),
            pltpu.VMEM((4, held, wide), BF16),
            pltpu.VMEM((4, held, both), BF16),
            pltpu.VMEM((2, 2, 8, held), F32),
            pltpu.VMEM((deep, group, across), BF16),
            pltpu.VMEM((deep, group, wide), BF16),
            pltpu.VMEM((2, tokens, group), BF16),
            pltpu.SemaphoreType.DMA((2,)),
        ]
        + sems(2 * deep) + sems(9)
        + [
            pltpu.SemaphoreType.DMA((3,)),
            pltpu.VMEM((own, width), BF16),
            pltpu.VMEM((own, width), F32),
            pltpu.VMEM((own, width), F32),
            pltpu.VMEM(w_gate.shape, F32),
            pltpu.VMEM(w_up.shape, F32),
            pltpu.SemaphoreType.DMA((5,)),
        ],
        [vmem] * 2 + [hbm] * 4 + [vmem, hbm] + [vmem] * 7,
        [hbm] + [vmem] * 4 + [hbm] * 2 + [vmem] * 2,
        flops=2 * tokens * width * g_qkv.shape[1],
    )


def plane_shards(
    activations,
    seg_ids,
    cotangent,
    q_weight,
    k_weight,
    v_weight,
    o_weight,
    gate_weight,
    up_weight,
    down_weight,
    attn_gain,
    mlp_gain,
):
    parts = lax.axis_size("ctx")
    heads = q_weight.shape[1] // F // parts
    tokens = activations.shape[1] * parts
    x, cot_block = activations[0], cotangent[0]
    gain_one, gain_two = attn_gain[None], mlp_gain[None]
    rows_low, own_high, segments, w_attn, cut_both, cut_down = front(
        x,
        seg_ids,
        (q_weight, k_weight, v_weight, o_weight, gate_weight, up_weight, down_weight),
        (gain_one, gain_two),
        tokens,
        heads,
    )
    w_attn = w_attn.reshape(-1, w_attn.shape[3])
    w_both = lax.all_gather(cut_both, "dp", axis=0, tiled=True).reshape(-1, cut_both.shape[2])
    seg_rows, seg_cols = segments.reshape(tokens, 1), segments.reshape(1, tokens)
    qkv, mixed, denom, heads_out, cot_low, rows_one = attend(
        rows_low, own_high, w_attn, seg_rows, seg_cols, cot_block, heads
    )
    cut_down, heads_out = lax.optimization_barrier((cut_down, heads_out))
    w_down = lax.all_gather(cut_down, "dp", axis=0, tiled=True)
    middle, rows_two = to_middle(heads_out, w_attn, x)
    hidden, slope, silu, cot_high, back_down = gate_up(rows_two, w_both, cot_block, cot_low)
    sum_down = lax.psum_scatter(back_down, "dp", scatter_dimension=0, tiled=True)
    g_both, back_both = feed_forward(slope, silu, cot_low, cot_high, w_down, rows_two)
    sum_both = lax.psum_scatter(back_both, "dp", scatter_dimension=0, tiled=True)
    g_middle, branch, g_mixed, out_terms = to_branch(
        g_both, w_both, middle, cot_block, w_attn, heads * DV, hidden, w_down
    )
    g_qkv, out, s_down = attend_back(
        qkv, g_mixed, mixed, denom, seg_rows, seg_cols, out_terms, middle, sum_down, heads
    )
    g_input, s_q, s_k, s_v, s_o, s_gate, s_up, attn_row, mlp_row = to_input(
        g_qkv,
        w_attn,
        x,
        g_middle,
        rows_one,
        branch,
        heads_out,
        sum_both,
        (q_weight, k_weight, v_weight, gate_weight, up_weight),
        (gain_one, gain_two),
        heads,
    )
    return (
        out[None],
        g_input[None],
        s_q,
        s_k,
        s_v,
        s_o,
        s_gate,
        s_up,
        s_down,
        attn_row[0],
        mlp_row[0],
    )


def layer(*arrays):
    heads, units = arrays[3].shape[1] // F, arrays[7].shape[1]
    fits = lax.axis_size("ctx") == 4 and lax.axis_size("tp") == 2
    fits = fits and heads % 4 == 0 and units % 256 == 0
    plan = plane_shards if fits else shards
    return plan(*arrays)


def solution(mesh):
    placed = (
        P("dp", "ctx", None),
        P("dp", "ctx"),
        P("dp", "ctx", None),
        P(("dp", "ctx"), "tp"),
        P(("dp", "ctx"), "tp"),
        P(("dp", "ctx"), "tp"),
        P(("dp", "ctx"), "tp"),
        P(("dp", "ctx"), "tp"),
        P(("dp", "ctx"), "tp"),
        P(("dp", "ctx"), "tp"),
        P(("dp", "ctx")),
        P(("dp", "ctx")),
    )
    return jax.shard_map(
        layer,
        mesh=mesh,
        in_specs=placed,
        out_specs=(
            P("dp", "ctx", None),
            P("dp", "ctx", None),
            P(("dp", "ctx"), "tp"),
            P(("dp", "ctx"), "tp"),
            P(("dp", "ctx"), "tp"),
            P(("dp", "ctx"), "tp"),
            P(("dp", "ctx"), "tp"),
            P(("dp", "ctx"), "tp"),
            P(("dp", "ctx"), "tp"),
            P(("dp", "ctx")),
            P(("dp", "ctx")),
        ),
        check_vma=False,
    )
```
